128 devices in a mesh: seq: 2 (over core), batch: 64 (over z, y, x).
Axes of the slice: x: 4, y: 4, z: 4, core: 2. Of those that a mesh axis runs over, the one named last changes fastest.
Arguments:
- text_input: bfloat16 [128, 128, 768], P('batch', 'seq'), may hold values from -6 to 6
- image_tokens: bfloat16 [512, 188, 768], P(('seq', 'batch')), may hold values from -6 to 6
- output_grad: bfloat16 [128, 128, 768], P('batch', 'seq'), may hold values from -6 to 6
- segment_starts: int32 [128, 4], P('batch'), may hold values from 0 to 127, as said below
- caption_image: int32 [128, 4], replicated, may hold values from 0 to 511, as said below
- image_counts: int32 [512], replicated, may hold values from 94 to 188, as said below
- norm_gain: bfloat16 [4, 768], P(None, ('seq', 'batch')), may hold values from 0.099609375 to 1.8984375
- norm_bias: bfloat16 [4, 768], P(None, ('seq', 'batch')), may hold values from -1.796875 to 1.796875
- self_qkv: bfloat16 [768, 2304], P(('seq', 'batch')), may hold values from -0.21875 to 0.21875
- self_out: bfloat16 [768, 768], P(('seq', 'batch')), may hold values from -0.875 to 0.875
- cross_q: bfloat16 [768, 768], P(('seq', 'batch')), may hold values from -0.21875 to 0.21875
- cross_kv: bfloat16 [768, 1536], P(('seq', 'batch')), may hold values from -0.21875 to 0.21875
- cross_out: bfloat16 [768, 768], P(('seq', 'batch')), may hold values from -1.75 to 1.75
- up_weight: bfloat16 [768, 3072], P(('seq', 'batch')), may hold values from -0.21875 to 0.21875
- up_bias: bfloat16 [3072], P(('seq', 'batch')), may hold values from -1.796875 to 1.796875
- down_weight: bfloat16 [3072, 768], P(('seq', 'batch')), may hold values from -0.109375 to 0.109375
- down_bias: bfloat16 [768], P(('seq', 'batch')), may hold values from -1.796875 to 1.796875
Outputs:
- text_output: float32 [128, 128, 768], P('batch', 'seq')
- text_grad: float32 [128, 128, 768], P('batch', 'seq')
- image_grad: float32 [512, 188, 768], P(('seq', 'batch'))
- norm_gain_grad: float32 [4, 768], P(None, ('seq', 'batch'))
- norm_bias_grad: float32 [4, 768], P(None, ('seq', 'batch'))
- self_qkv_grad: float32 [768, 2304], P(('seq', 'batch'))
- self_out_grad: float32 [768, 768], P(('seq', 'batch'))
- cross_q_grad: float32 [768, 768], P(('seq', 'batch'))
- cross_kv_grad: float32 [768, 1536], P(('seq', 'batch'))
- cross_out_grad: float32 [768, 768], P(('seq', 'batch'))
- up_weight_grad: float32 [768, 3072], P(('seq', 'batch'))
- up_bias_grad: float32 [3072], P(('seq', 'batch'))
- down_weight_grad: float32 [3072, 768], P(('seq', 'batch'))
- down_bias_grad: float32 [768], P(('seq', 'batch'))
The draws below stay inside these ranges and needn't reach their ends.
Inputs may be any that keep to these rules, and one draw needn't show every extreme that they name: `segment_starts`: in every row the first start is 0 and the starts rise strictly. `caption_image`: A permutation: every image belongs to exactly one caption. Image i lies on device i // 4 of seq+batch (seq slowest). Number the 8 captions of the rows of batch index g as k = 0 to 7, row by row; caption k uses an image of the device with seq index k % 2 and batch index (g + (k // 2) * (64 // 4)) mod 64, where 64 is the size of the batch axis; the four turns k // 2 = 0 to 3 of a group use that device's four images in an order drawn at random, each image once. `image_counts`: tokens of an image at or beyond its count are padding.
All inputs are finite; a program needn't handle non-finite values.
Results may differ from the reference program's by a relative error of at most 0.018.
Values may be sent and summed in bfloat16 or wider, within the bound.
No kernel may reach another device: no remote copies, remote signals or barrier semaphores. Data moves between devices by JAX's collectives and lax.ppermute only.
A program may use at most 256 MiB of HBM per device.

```python
import math
import jax
import jax.numpy as jnp
from jax import lax

D = 768
HEADS = 12
HEAD_DIM = 64
FF = 3072
ROW_LEN = 128
SEGS = 4
IMG_TOK = 188
ROWS_DEV = 2
ROWS = 128
CAP_GROUP = 8
IMG_DEV = 4
IMAGES = 512


def draw_segment_starts(key, part):
    key = jax.random.fold_in(key, 11)
    keys = jax.random.split(key, 4)
    quarter = ROW_LEN // 16
    middle = ROW_LEN // 2
    across = jax.random.randint(keys[0], (ROWS, 1), 0, SEGS)
    begin = jax.random.randint(keys[1], (ROWS, 1), across * quarter, middle - quarter + 1)
    begin = jnp.where(across == 0, 0, begin)
    finish = jax.random.randint(keys[2], (ROWS, 1), middle + quarter, ROW_LEN - (SEGS - 1 - across) * quarter + 1)
    finish = jnp.where(across == SEGS - 1, ROW_LEN, finish)
    jitter = jax.random.randint(keys[3], (ROWS, SEGS), -2, 3)
    index = jnp.arange(SEGS)[None, :]
    before = index * begin // jnp.maximum(across, 1) + jnp.where(index > 0, jitter, 0)
    after = finish + (index - across - 1) * (ROW_LEN - finish) // jnp.maximum(SEGS - 1 - across, 1) + jnp.where(index > across + 1, jitter, 0)
    starts = jnp.where(index < across, before, jnp.where(index == across, begin, after))
    return starts.astype(jnp.int32)


def draw_caption_image(key, part):
    key = jax.random.fold_in(key, 23)
    groups_total = ROWS // ROWS_DEV
    devices = IMAGES // IMG_DEV
    stride = groups_total // IMG_DEV
    device_keys = jax.random.split(key, devices)
    local_order = jax.vmap(lambda one_key: jax.random.permutation(one_key, IMG_DEV))(device_keys)
    group = jnp.arange(groups_total)[:, None]
    slot = jnp.arange(CAP_GROUP)[None, :]
    turn = slot // 2
    holder = slot % 2 * groups_total + (group + turn * stride) % groups_total
    image = holder * IMG_DEV + local_order[holder, turn]
    return image.reshape(ROWS, SEGS).astype(jnp.int32)


def draw_image_counts(key, part):
    key = jax.random.fold_in(key, 37)
    keys = jax.random.split(key, 3)
    counts = jax.random.randint(keys[0], (IMAGES,), IMG_TOK // 2, IMG_TOK + 1)
    longest = jax.random.randint(keys[1], (), 0, IMAGES)
    shortest = (longest + 1 + jax.random.randint(keys[2], (), 0, IMAGES - 1)) % IMAGES
    counts = counts.at[longest].set(IMG_TOK).at[shortest].set(IMG_TOK // 2)
    return counts.astype(jnp.int32)


def steps_of(stream_key, dims, cuts, smallest, largest):
    factor_of, own = 1.0, jax.random.fold_in(stream_key, 6)
    for dim, shards_of in cuts:
        steps = jnp.exp(jax.random.uniform(jax.random.fold_in(own, dim), (shards_of,), jnp.float32, smallest / len(cuts), largest / len(cuts)))
        factor_of = factor_of * jnp.repeat(steps, dims[dim] // shards_of).reshape([-1 if axis == dim else 1 for axis in range(len(dims))])
    return factor_of


def bell_draw(rng, extent, deviation, bound, shards=(), held_as=jnp.bfloat16):
    drawn = jax.random.normal(rng, extent, jnp.float32) * deviation
    if len(shards) > 0:
        drawn = steps_of(rng, extent, shards, -0.22, 0.18) * drawn
    return jnp.clip(drawn, min=-bound, max=bound).astype(held_as)


def setup_inputs(seed: int = 0) -> dict:
    arg_keys = jax.random.split(jax.random.key(seed), 18)
    return {
        "text_input": bell_draw(arg_keys[0], (ROWS, ROW_LEN, D), 1.0, 6.0, ((0, 64), (1, 2))),
        "image_tokens": bell_draw(arg_keys[1], (IMAGES, IMG_TOK, D), 1.0, 6.0, ((0, 128),)),
        "output_grad": bell_draw(arg_keys[2], (ROWS, ROW_LEN, D), 1.0, 6.0, ((0, 64), (1, 2))),
        "segment_starts": draw_segment_starts(jax.random.fold_in(arg_keys[17], 71), 0),
        "caption_image": draw_caption_image(jax.random.fold_in(arg_keys[17], 71), 0),
        "image_counts": draw_image_counts(jax.random.fold_in(arg_keys[17], 71), 0),
        "norm_gain": jnp.clip(1.0 + 0.18 * jax.random.normal(arg_keys[6], (4, D), jnp.float32), 0.099609375, 1.8984375).astype(jnp.bfloat16),
        "norm_bias": bell_draw(arg_keys[7], (4, D), 0.3, 1.796875, ((1, 128),)),
        "self_qkv": bell_draw(arg_keys[8], (D, 3 * D), D ** -0.5, 0.21875, ((0, 128),)),
        "self_out": bell_draw(arg_keys[9], (D, D), (D // 16) ** -0.5, 0.875, ((0, 128),)),
        "cross_q": bell_draw(arg_keys[10], (D, D), D ** -0.5, 0.21875, ((0, 128),)),
        "cross_kv": bell_draw(arg_keys[11], (D, 2 * D), D ** -0.5, 0.21875, ((0, 128),)),
        "cross_out": bell_draw(arg_keys[12], (D, D), (D // 64) ** -0.5, 1.75, ((0, 128),)),
        "up_weight": bell_draw(arg_keys[13], (D, FF), D ** -0.5, 0.21875, ((0, 128),)),
        "up_bias": bell_draw(arg_keys[14], (FF,), 0.3, 1.796875, ((0, 128),)),
        "down_weight": bell_draw(arg_keys[15], (FF, D), FF ** -0.5, 0.109375, ((0, 128),)),
        "down_bias": bell_draw(arg_keys[16], (D,), 0.3, 1.796875, ((0, 128),)),
    }


@jax.custom_vjp
def low(v):
    return lax.optimization_barrier(v.astype(jnp.bfloat16)).astype(jnp.float32)

@jax.custom_vjp
def low_back(v):
    return v

def low_keep(v):
    return (low(v), None)

def low_pass(kept, grad):
    return (grad,)

def back_keep(v):
    return (v, None)

def back_low(kept, grad):
    return (low(grad),)
low.defvjp(low_keep, low_pass)
low_back.defvjp(back_keep, back_low)
EPSILON = 1e-05
HIGHEST = lax.Precision.HIGHEST
MASKED_SCORE = -1e+30

def layer_norm(values, scales, shifts):
    center = lax.optimization_barrier(jnp.mean(values, -1, keepdims=True))
    centred = values - center
    spread = lax.optimization_barrier(jnp.mean(centred * centred, -1, keepdims=True))
    return centred * lax.rsqrt(spread + EPSILON) * scales + shifts

def project(left_side, right_side):
    return jnp.einsum('rtd,de->rte', left_side, right_side, precision=HIGHEST)

def attend(queries, keys_in, values_in, allowed):
    scores = jnp.einsum('rthc,rshc->rhts', queries, keys_in, precision=HIGHEST) * HEAD_DIM ** (-0.5)
    scores = low_back(scores)
    scores = jnp.where(allowed[:, None], scores, MASKED_SCORE)
    row_top = lax.optimization_barrier(jnp.max(scores, -1, keepdims=True))
    weights = jnp.exp(scores - row_top)
    probs_full = low(weights / lax.optimization_barrier(jnp.sum(weights, -1, keepdims=True)))
    mixed_out = low_back(low(jnp.einsum('rhts,rshc->rthc', probs_full, values_in, precision=HIGHEST)))
    return mixed_out.reshape(mixed_out.shape[0], mixed_out.shape[1], D)

def heads_of(tensor):
    return tensor.reshape(tensor.shape[0], tensor.shape[1], HEADS, HEAD_DIM)

def layer_block(params, rows_in, images_in, starts, counts):
    norm_gain, norm_bias, self_qkv, self_out, cross_q, cross_kv, cross_out, up_weight, up_bias, down_weight, down_bias = params
    block_rows = rows_in.shape[0]
    places = jnp.arange(ROW_LEN)
    segment = lax.optimization_barrier(jnp.sum((starts[:, :, None] <= places[None, None, :]).astype(jnp.int32), axis=1)) - 1
    normed = low(layer_norm(rows_in, norm_gain[0], norm_bias[0]))
    joined = low_back(low(project(normed, self_qkv)))
    queries = heads_of(joined[..., :D])
    keys_self = heads_of(joined[..., D:2 * D])
    values_self = heads_of(joined[..., 2 * D:])
    causal = (segment[:, :, None] == segment[:, None, :]) & (places[:, None] >= places[None, :])[None]
    branch = low_back(project(attend(queries, keys_self, values_self, causal), self_out))
    after_self = rows_in + branch
    image_normed = low(layer_norm(images_in, norm_gain[2], norm_bias[2]))
    image_kv = low_back(low(jnp.einsum('ntd,de->nte', image_normed, cross_kv, precision=HIGHEST)))
    keys_cross = image_kv[..., :D].reshape(block_rows, SEGS * IMG_TOK, HEADS, HEAD_DIM)
    values_cross = image_kv[..., D:].reshape(block_rows, SEGS * IMG_TOK, HEADS, HEAD_DIM)
    normed_two = low(layer_norm(after_self, norm_gain[1], norm_bias[1]))
    queries_cross = heads_of(low_back(low(project(normed_two, cross_q))))
    key_index = jnp.arange(SEGS * IMG_TOK)
    key_caption = key_index // IMG_TOK
    key_token = key_index % IMG_TOK
    limits = jnp.take(counts, key_caption, axis=1)
    visible = (segment[:, :, None] == key_caption[None, None, :]) & (key_token[None, None, :] < limits[:, None, :])
    branch_two = low_back(project(attend(queries_cross, keys_cross, values_cross, visible), cross_out))
    after_cross = after_self + branch_two
    normed_three = low(layer_norm(after_cross, norm_gain[3], norm_bias[3]))
    hidden = low_back(project(normed_three, up_weight) + up_bias)
    active = low(jax.nn.gelu(hidden, approximate=False))
    return after_cross + low_back(project(active, down_weight) + down_bias)

def reference(text_input, image_tokens, output_grad, segment_starts, caption_image, image_counts, norm_gain, norm_bias, self_qkv, self_out, cross_q, cross_kv, cross_out, up_weight, up_bias, down_weight, down_bias):
    block_rows = math.gcd(ROWS, 32)
    blocks = ROWS // block_rows
    image_order = caption_image.reshape(-1).astype(jnp.int32)
    counts = jnp.take(image_counts, image_order).reshape(blocks, block_rows, SEGS)
    starts = segment_starts.reshape(blocks, block_rows, SEGS)

    def forward(text_f, images_f, gain_f, bias_f, qkv_f, sout_f, cq_f, ckv_f, cout_f, upw_f, upb_f, downw_f, downb_f):
        params = (gain_f, bias_f, qkv_f, sout_f, cq_f, ckv_f, cout_f, upw_f, upb_f, downw_f, downb_f)
        ordered = jnp.take(images_f, image_order, axis=0).reshape(blocks, block_rows * SEGS, IMG_TOK, D)
        rows_all = text_f.reshape(blocks, block_rows, ROW_LEN, D)

        def one_block(pieces):
            return layer_block(params, pieces[0], pieces[1], pieces[2], pieces[3])
        outputs = lax.map(jax.checkpoint(one_block), (rows_all, ordered, starts, counts))
        return outputs.reshape(ROWS, ROW_LEN, D)
    result, pullback = jax.vjp(forward, text_input.astype(jnp.float32), image_tokens.astype(jnp.float32), norm_gain.astype(jnp.float32), norm_bias.astype(jnp.float32), self_qkv.astype(jnp.float32), self_out.astype(jnp.float32), cross_q.astype(jnp.float32), cross_kv.astype(jnp.float32), cross_out.astype(jnp.float32), up_weight.astype(jnp.float32), up_bias.astype(jnp.float32), down_weight.astype(jnp.float32), down_bias.astype(jnp.float32))
    gradients = pullback(output_grad.astype(jnp.float32))
    return (result, gradients[0], gradients[1], gradients[2], gradients[3], gradients[4], gradients[5], gradients[6], gradients[7], gradients[8], gradients[9], gradients[10], gradients[11], gradients[12])
```

```python
import jax
import jax.numpy as jnp
from jax import lax
from jax.sharding import PartitionSpec as P

HEADS = 12
HEAD_DIM = 64
EPSILON = 1e-05
MASKED_SCORE = -1e30
BF = jnp.bfloat16
F32 = jnp.float32
BOTH = ("seq", "batch")
STRIDE = {"z": 16, "y": 4, "x": 1}
ORDERS = (("x", "z", "y"), ("y", "x", "z"), ("z", "y", "x"))


def xor_pairs(axis, value0, value1):
    step, out = STRIDE[axis], []
    for core, value in ((0, value0), (1, value1)):
        for chip in range(64):
            at = chip // step % 4
            out.append((core * 64 + chip, core * 64 + chip + ((at ^ value) - at) * step))
    return out


def reduce_scatter_parts(parts, orders):
    for phase in range(3):
        for step, (v0, v1) in enumerate(((1, 3), (3, 1))):
            last = phase == 2 and step == 1
            sends = [p[p.shape[0] // 2 :] for p in parts]
            keeps = [p[: p.shape[0] // 2] for p in parts]
            got = [lax.ppermute(v, BOTH, xor_pairs(o[phase], v0, v1)) for v, o in zip(sends, orders)]
            parts = [k.astype(F32) + g.astype(F32) for k, g in zip(keeps, got)]
            if not last:
                parts = [p.astype(BF) for p in parts]
    return parts


def swap(value):
    return lax.ppermute(value, "seq", [(0, 1), (1, 0)])


def mm(a, b):
    return jnp.dot(a, b, preferred_element_type=F32)


def mm_t(a, b):
    return lax.dot_general(a, b, (((1,), (1,)), ((), ())), preferred_element_type=F32)


def t_mm(a, b):
    return lax.dot_general(a, b, (((0,), (0,)), ((), ())), preferred_element_type=F32)


def normalize(values):
    center = jnp.mean(values, -1, keepdims=True)
    centred = values - center
    spread = jnp.mean(centred * centred, -1, keepdims=True)
    inv = lax.rsqrt(spread + EPSILON)
    return centred * inv, inv


def norm_back(grad, gain, xhat, inv):
    scaled = grad * gain
    return inv * (
        scaled
        - jnp.mean(scaled, -1, keepdims=True)
        - xhat * jnp.mean(scaled * xhat, -1, keepdims=True)
    )


def one_hot(index, size):
    return (jnp.arange(size)[:, None] == index[None, :]).astype(BF)


def attend_forward(queries, keys_in, values_in, allowed):
    scores = jnp.einsum("rthc,rshc->rhts", queries, keys_in, preferred_element_type=F32) * 0.125
    scores = jnp.where(allowed[:, None], scores, MASKED_SCORE)
    weights = jnp.exp(scores - jnp.max(scores, -1, keepdims=True))
    probs = weights / jnp.sum(weights, -1, keepdims=True)
    low = probs.astype(BF)
    mixed = jnp.einsum("rhts,rshc->rthc", low, values_in, preferred_element_type=F32)
    return mixed.astype(BF), probs, low


def attend_backward(grad, queries, keys_in, values_in, probs, low):
    dv = jnp.einsum("rhts,rthc->rshc", low, grad, preferred_element_type=F32)
    dp = jnp.einsum("rthc,rshc->rhts", grad, values_in, preferred_element_type=F32)
    ds = (probs * (dp - jnp.sum(probs * dp, -1, keepdims=True))).astype(BF)
    dq = jnp.einsum("rhts,rshc->rthc", ds, keys_in, preferred_element_type=F32) * 0.125
    dk = jnp.einsum("rhts,rthc->rshc", ds, queries, preferred_element_type=F32) * 0.125
    return dq.astype(BF), dk.astype(BF), dv.astype(BF)


def on_device(
    text_input,
    image_tokens,
    output_grad,
    segment_starts,
    caption_image,
    image_counts,
    norm_gain,
    norm_bias,
    self_qkv,
    self_out,
    cross_q,
    cross_kv,
    cross_out,
    up_weight,
    up_bias,
    down_weight,
    down_bias,
):
    core = lax.axis_index("seq")
    chip = lax.axis_index("batch")
    first = core == 0

    def ordered(own, other, axis):
        return jnp.where(
            first, jnp.concatenate([own, other], axis), jnp.concatenate([other, own], axis)
        )

    halves = [
        self_qkv.reshape(6, 3, 2, 384),
        cross_q.reshape(6, 1, 2, 384),
        cross_kv.reshape(6, 2, 2, 384),
        up_weight.reshape(6, 2, 64, 3, 8).transpose(0, 3, 1, 2, 4).reshape(6, 3, 2, 512),
    ]
    low_half = jnp.concatenate([h[:, :, 0].reshape(6, -1) for h in halves], 1)
    high_half = jnp.concatenate([h[:, :, 1].reshape(6, -1) for h in halves], 1)
    vectors = jnp.concatenate(
        [norm_gain.T, norm_bias.T, down_bias[:, None], jnp.zeros((6, 247), BF)], 1
    )
    mine = jnp.where(first, low_half, high_half)
    theirs = jnp.where(first, high_half, low_half)
    got = swap(jnp.concatenate([theirs, vectors], 1))
    columns = ordered(mine, got[:, :3840], 0)
    vector_rows = ordered(vectors, got[:, 3840:], 0)
    vector_rows = jnp.concatenate(
        [vector_rows[:, :9], up_bias.reshape(2, 12).T, vector_rows[:, 11:]], 1
    )
    outs = jnp.concatenate([self_out, cross_out], 0)
    twelve = jnp.concatenate([columns, outs, vector_rows], 1)
    down_slabs = down_weight.reshape(3, 8, 768).transpose(1, 0, 2).reshape(8, 2304)
    slot = jnp.concatenate(
        [
            twelve[:8],
            jnp.concatenate([twelve[8:, :2432], twelve[8:, 2432:]], 0),
            down_slabs,
        ],
        1,
    )
    gathered = lax.all_gather(slot, "batch", axis=0, tiled=True)

    own_text = text_input.astype(F32)
    text_full = ordered(text_input, swap(text_input), 1).reshape(256, 768).astype(F32)
    grad_full = ordered(output_grad, swap(output_grad), 1).reshape(256, 768)

    group_images = caption_image.reshape(64, 8)
    my_captions = lax.dynamic_index_in_dim(group_images, chip, 0, keepdims=False)
    limits = jnp.take(image_counts, my_captions)
    turns = jnp.arange(4)
    targets = (chip - turns * 16) % 64
    wanted = group_images[targets, 2 * turns + core]
    local_pick = wanted - (core * 64 + chip) * 4
    inverse = jnp.sum(jnp.where(local_pick[:, None] == turns[None, :], turns[:, None], 0), axis=0)
    outgoing = jnp.take(image_tokens, local_pick, axis=0)
    received = [outgoing[0]]
    for turn in range(1, 4):
        route = [(i, (i - 16 * turn) % 64) for i in range(64)]
        received.append(lax.ppermute(outgoing[turn], "batch", route))
    own_images = jnp.stack(received)
    all_images = jnp.concatenate([own_images, swap(own_images)], 0)

    places = jnp.arange(128)
    segment = (
        jnp.sum((segment_starts[:, :, None] <= places[None, None, :]).astype(jnp.int32), axis=1) - 1
    )
    causal = (segment[:, :, None] == segment[:, None, :]) & (
        places[None, :, None] >= places[None, None, :]
    )
    which = jnp.arange(752) // 188
    token = jnp.arange(752) % 188
    key_caption = 2 * (which % 2) + jnp.where(which < 2, core, 1 - core)
    limit_of = jnp.take(limits.reshape(2, 4), key_caption, axis=1)
    visible = (segment[:, :, None] == key_caption[None, None, :]) & (
        token[None, None, :] < limit_of[:, None, :]
    )

    slots = jnp.arange(512) // 8
    eight = jnp.arange(512) % 8

    def natural_row(at_slot, twelfth):
        return twelfth // 6 * 384 + at_slot * 6 + twelfth % 6

    pick_a = one_hot(natural_row(slots, eight), 768)
    pick_b0 = one_hot(jnp.where(eight < 4, natural_row(slots, 8 + eight), -1), 768)
    pick_b1 = one_hot(jnp.where(eight >= 4, natural_row(slots, 4 + eight), -1), 768)
    w_low = mm(
        jnp.concatenate([pick_a, pick_b0], 1),
        jnp.concatenate([gathered[:, :2432], gathered[:, 4864:7296]], 0),
    ).astype(BF)
    w_high = mm(
        jnp.concatenate([pick_a, pick_b1], 1),
        jnp.concatenate([gathered[:, 2432:4864], gathered[:, 4864:7296]], 0),
    ).astype(BF)
    w_qkv, w_query, w_kv = w_low[:, :1152], w_low[:, 1152:1536], w_low[:, 1536:2304]
    w_up = jnp.concatenate([w_low[:, 2304:], w_high[:, :1408]], 1)
    w_self, w_cross = w_high[:384, 1408:2176], w_high[384:, 1408:2176]
    w_down = jnp.concatenate([gathered[:, 7296 + 768 * k : 8064 + 768 * k] for k in range(3)], 0)
    vec = w_high[:, 2176:2192].T.astype(F32)
    gain, bias, b_down = vec[0:4], vec[4:8], vec[8]
    b_up = (
        vec[9:11].reshape(2, 2, 64, 6).transpose(2, 0, 1, 3).reshape(64, 3, 8)
        .transpose(1, 0, 2).reshape(1536)
    )

    tau = jnp.where(first, jnp.array([0, 3, 1, 2]), jnp.array([0, 1, 3, 2]))
    seq768 = jnp.arange(768)
    slot_of, twelfth = seq768 // 12, seq768 % 12
    order_q, order_f, order_o = [], [], []
    for order in ORDERS:
        digits = (slot_of // 16, slot_of // 4 % 4, slot_of % 4)
        target = 0
        for axis, digit in zip(order, digits):
            step = STRIDE[axis]
            target = target + ((chip // step % 4) ^ tau[digit]) * step
        order_q.append(one_hot(natural_row(target, twelfth), 768))
        ff = []
        for l in range(2):
            row = l * 12 + twelfth
            ff.append(one_hot(row // 8 * 512 + target * 8 + row % 8, 1536))
        order_f.append(ff)
        order_o.append(
            [
                one_hot(jnp.where(twelfth // 6 == l, target * 6 + twelfth % 6, -1), 384)
                for l in range(2)
            ]
        )

    def put(value, pick):
        return mm(value, pick).astype(BF)

    heads = lambda t: t.reshape(2, -1, 6, 64)
    xhat_one, inv_one = normalize(text_full)
    normed_one = (xhat_one * gain[0] + bias[0]).astype(BF)
    joined = mm(normed_one, w_qkv).astype(BF)
    q_self, k_self, v_self = (heads(joined[:, 384 * i : 384 * i + 384]) for i in range(3))
    mixed_self, probs_self, low_self = attend_forward(q_self, k_self, v_self, causal)
    mixed_self = mixed_self.reshape(256, 384)
    part = mm(mixed_self, w_self)
    after_self = text_full + (part + swap(part))
    xhat_two, inv_two = normalize(after_self)
    normed_two = (xhat_two * gain[1] + bias[1]).astype(BF)
    q_cross = heads(mm(normed_two, w_query).astype(BF))

    xhat_image, inv_image = normalize(all_images.reshape(1504, 768).astype(F32))
    image_normed = (xhat_image * gain[2] + bias[2]).astype(BF)
    kv = mm(image_normed, w_kv).astype(BF)

    def by_row(t):
        t = t.reshape(2, 2, 2, 188, 384).transpose(1, 0, 2, 3, 4)
        return t.reshape(2, 752, 6, 64)

    def by_image(t):
        t = t.reshape(2, 2, 2, 188, 384).transpose(1, 0, 2, 3, 4)
        return t.reshape(1504, 384)

    k_cross, v_cross = by_row(kv[:, :384]), by_row(kv[:, 384:])
    mixed_cross, probs_cross, low_cross = attend_forward(q_cross, k_cross, v_cross, visible)
    mixed_cross = mixed_cross.reshape(256, 384)
    part = mm(mixed_cross, w_cross)
    after_cross = after_self + (part + swap(part))

    xhat_three, inv_three = normalize(after_cross)
    normed_three = (xhat_three * gain[3] + bias[3]).astype(BF)
    hidden = mm(normed_three, w_up) + b_up
    cdf = 0.5 * (1.0 + lax.erf(hidden * 0.7071067811865476))
    active = (hidden * cdf).astype(BF)
    slope = cdf + hidden * (jnp.exp(-0.5 * hidden * hidden) * 0.3989422804014327)
    part = mm(active, w_down)

    def mine_of(t):
        t = t.reshape(2, 2, 64, 768)
        return jnp.where(first, t[:, 0], t[:, 1])

    def theirs_of(t):
        t = t.reshape(2, 2, 64, 768)
        return jnp.where(first, t[:, 1], t[:, 0])

    text_output = mine_of(after_cross) + (mine_of(part) + swap(theirs_of(part)) + b_down)

    hidden_low = (mm_t(grad_full, w_down) * slope).astype(BF)
    group_one = []
    for p in range(3):
        rows = put(normed_three, order_q[p])
        pieces = [t_mm(rows, hidden_low[:, 512 * p : 512 * p + 512])]
        for l in range(2):
            rows = put(active, order_f[p][l])
            pieces.append(t_mm(rows, grad_full[:, 256 * p : 256 * p + 256]))
        group_one.append(jnp.concatenate(pieces, 1).astype(BF))
    group_one = reduce_scatter_parts(group_one, ORDERS)
    up_bias_sum = jnp.sum(hidden_low.astype(F32), 0)
    down_bias_sum = jnp.sum(output_grad.astype(F32), (0, 1))
    part = mm_t(hidden_low, w_up)
    d_three = part + swap(part)
    half = jnp.where(first, 1.0, 0.0)
    gain_three = jnp.sum(d_three * xhat_three, 0) * half
    bias_three = jnp.sum(d_three, 0) * half
    stream_two = grad_full.astype(F32) + norm_back(d_three, gain[3], xhat_three, inv_three)

    cross_low = stream_two.astype(BF)
    mixed_grad = heads(mm_t(cross_low, w_cross).astype(BF))
    dq, dk, dv = attend_backward(mixed_grad, q_cross, k_cross, v_cross, probs_cross, low_cross)
    dq = dq.reshape(256, 384)
    d_kv = jnp.concatenate([by_image(dk), by_image(dv)], 1)
    group_two = []
    for p in range(3):
        pieces = []
        if p < 2:
            rows = put(image_normed, order_q[p])
            pieces.append(t_mm(rows, d_kv[:, 384 * p : 384 * p + 384]))
        else:
            pieces.append(
                sum(
                    t_mm(put(mixed_cross, order_o[p][l]), cross_low[:, 384 * l : 384 * l + 384])
                    for l in range(2)
                )
            )
        rows = put(normed_two, order_q[p])
        pieces.append(t_mm(rows, dq[:, 128 * p : 128 * p + 128]))
        group_two.append(jnp.concatenate(pieces, 1).astype(BF))
    group_two = reduce_scatter_parts(group_two, ORDERS)

    part = mm_t(dq, w_query)
    d_two = part + swap(part)
    gain_two = jnp.sum(d_two * xhat_two, 0) * half
    bias_two = jnp.sum(d_two, 0) * half
    stream_one = stream_two + norm_back(d_two, gain[1], xhat_two, inv_two)

    part = mm_t(d_kv, w_kv)
    d_image = part[:752] + swap(part[752:])
    gain_image = jnp.sum(d_image * xhat_image[:752], 0)
    bias_image = jnp.sum(d_image, 0)
    row_grad = norm_back(d_image, gain[2], xhat_image[:752], inv_image[:752]).reshape(4, 188, 768)
    returned = [row_grad[0]]
    for turn in range(1, 4):
        route = [(i, (i + 16 * turn) % 64) for i in range(64)]
        returned.append(lax.ppermute(row_grad[turn].astype(BF), "batch", route).astype(F32))
    image_grad = jnp.take(jnp.stack(returned), inverse, axis=0)

    self_low = stream_one.astype(BF)
    mixed_grad = heads(mm_t(self_low, w_self).astype(BF))
    d_joined = attend_backward(mixed_grad, q_self, k_self, v_self, probs_self, low_self)
    d_joined = [t.reshape(256, 384) for t in d_joined]
    part = mm_t(jnp.concatenate(d_joined, 1), w_qkv)
    d_one = mine_of(part) + swap(theirs_of(part))
    xhat_mine, inv_mine = normalize(own_text)
    gain_one = jnp.sum(d_one * xhat_mine, (0, 1))
    bias_one = jnp.sum(d_one, (0, 1))
    text_grad = mine_of(stream_one) + norm_back(d_one, gain[0], xhat_mine, inv_mine)
    group_three = []
    sums = jnp.stack(
        [gain_one, gain_two, gain_image, gain_three, bias_one, bias_two, bias_image, bias_three]
        + [down_bias_sum]
        + [jnp.zeros((768,), F32)] * 7,
        1,
    ).astype(BF)
    up_sums = jnp.concatenate([up_bias_sum[:, None], jnp.zeros((1536, 15), F32)], 1).astype(BF)
    for p in range(3):
        pieces = [t_mm(put(normed_one, order_q[p]), d_joined[p])]
        pieces.append(
            sum(
                t_mm(
                    put(mixed_self, order_o[p][l]),
                    self_low[:, 384 * l + 128 * p : 384 * l + 128 * p + 128],
                )
                for l in range(2)
            )
        )
        if p == 2:
            pieces.append(t_mm(order_q[p], sums))
            pieces.append(t_mm(order_f[p][0], up_sums))
            pieces.append(t_mm(order_f[p][1], up_sums))
            pieces.append(jnp.zeros((768, 80), F32))
        group_three.append(jnp.concatenate(pieces, 1).astype(BF))
    group_three = reduce_scatter_parts(group_three, ORDERS)

    def own_rows(t):
        return jnp.where(first, t[:6], t[6:])

    def other_rows(t):
        return jnp.where(first, t[6:], t[:6])

    def columns_of(t, blocks):
        got = swap(other_rows(t)).reshape(6, blocks, 1, -1)
        own = own_rows(t).reshape(6, blocks, 1, -1)
        return ordered(own, got, 2).reshape(6, -1)

    up_grad = columns_of(jnp.concatenate([g[:, :512] for g in group_one], 1), 1)
    up_grad = up_grad.reshape(6, 2, 3, 64, 8).transpose(0, 1, 3, 2, 4).reshape(6, 3072)
    down_grad = jnp.concatenate(
        [
            jnp.concatenate([g[:, 512 + 256 * l : 768 + 256 * l] for g in group_one], 1)
            for l in range(2)
        ],
        0,
    )
    kv_grad = columns_of(jnp.concatenate([g[:, :384] for g in group_two[:2]], 1), 2)
    query_grad = columns_of(jnp.concatenate([g[:, 384:] for g in group_two], 1), 1)
    cross_grad = jnp.concatenate([group_two[2][:6, :384], group_two[2][6:, :384]], 1)
    qkv_grad = columns_of(jnp.concatenate([g[:, :384] for g in group_three], 1), 3)
    self_grad = jnp.concatenate([g[:, 384:512] for g in group_three], 1)
    self_grad = jnp.concatenate([self_grad[:6], self_grad[6:]], 1)
    vec_grad = group_three[2][:, 512:]
    vec_sum = own_rows(vec_grad[:, :16]) + swap(other_rows(vec_grad[:, :16]))
    up_bias_grad = jnp.concatenate([vec_grad[:, 16], vec_grad[:, 32]])
    return (
        text_output,
        text_grad,
        image_grad,
        vec_sum[:, 0:4].T,
        vec_sum[:, 4:8].T,
        qkv_grad,
        self_grad,
        query_grad,
        kv_grad,
        cross_grad,
        up_grad,
        up_bias_grad,
        down_grad,
        vec_sum[:, 8],
    )


def solution(mesh):
    rows = P("batch", "seq", None)
    shard = P(BOTH, None)
    wide = P(None, BOTH)
    return jax.shard_map(
        on_device,
        mesh=mesh,
        in_specs=(
            rows, P(BOTH, None, None), rows, P("batch", None), P(), P(), wide, wide,
            shard, shard, shard, shard, shard, shard, P(BOTH), shard, P(BOTH),
        ),
        out_specs=(
            rows, rows, P(BOTH, None, None), wide, wide,
            shard, shard, shard, shard, shard, shard, P(BOTH), shard, P(BOTH),
        ),
        check_vma=False,
    )
```

```python
import math

import jax
import jax.numpy as jnp
from jax import lax
from jax.experimental import pallas as pl
from jax.experimental.pallas import tpu as pltpu
from jax.sharding import PartitionSpec as P

HEADS = 12
HEAD_DIM = 64
EPSILON = 1e-05
MASKED_SCORE = -1e30
BF = jnp.bfloat16
F32 = jnp.float32
BOTH = ("seq", "batch")
STRIDE = {"z": 16, "y": 4, "x": 1}
ORDERS = (("x", "z", "y"), ("y", "x", "z"), ("z", "y", "x"))
GATHER_ORDERS = (("z", "y", "x"), ("z", "x", "y"))


def xor_pairs(axis, value0, value1):
    step, out = STRIDE[axis], []
    for core, value in ((0, value0), (1, value1)):
        for chip in range(64):
            at = chip // step % 4
            out.append((core * 64 + chip, core * 64 + chip + ((at ^ value) - at) * step))
    return out


def swap(value):
    return lax.ppermute(value, "seq", [(0, 1), (1, 0)])


def mm(a, b):
    return jnp.dot(a, b, preferred_element_type=F32)


def mm_t(a, b):
    return lax.dot_general(a, b, (((1,), (1,)), ((), ())), preferred_element_type=F32)


def t_mm(a, b):
    return lax.dot_general(a, b, (((0,), (0,)), ((), ())), preferred_element_type=F32)


def normalize(values):
    center = jnp.mean(values, -1, keepdims=True)
    centred = values - center
    spread = jnp.mean(centred * centred, -1, keepdims=True)
    inv = lax.rsqrt(spread + EPSILON)
    return centred * inv, inv


def norm_back(grad, gain, xhat, inv):
    scaled = grad * gain
    return inv * (
        scaled
        - jnp.mean(scaled, -1, keepdims=True)
        - xhat * jnp.mean(scaled * xhat, -1, keepdims=True)
    )


VMEM = pl.BlockSpec(memory_space=pltpu.VMEM)
SMEM = pl.BlockSpec(memory_space=pltpu.SMEM)
ANY = pl.BlockSpec(memory_space=pl.ANY)


def shape(dims, dtype):
    return jax.ShapeDtypeStruct(dims, dtype)


def cost(flops, moved):
    return pl.CostEstimate(flops=int(flops), bytes_accessed=int(moved), transcendentals=0)


def params(mib):
    return pltpu.CompilerParams(vmem_limit_bytes=mib * 1024 * 1024)


def staged(name, kernel, scalars, ins, outs, work, scratch=(), mib=16):
    moved = sum(math.prod(v.shape) * v.dtype.itemsize for v in (*ins, *outs))
    return pl.pallas_call(
        kernel,
        out_shape=tuple(outs),
        in_specs=[SMEM] * len(scalars) + [VMEM] * len(ins),
        out_specs=(VMEM,) * len(outs),
        scratch_shapes=list(scratch),
        compiler_params=params(mib),
        cost_estimate=cost(work, moved),
        name=name,
    )(*scalars, *ins)


def picked(rows, i, size):
    place = lax.broadcasted_iota(jnp.int32, (size, 512), 0)
    return (place == rows[i : i + 1]).astype(F32).astype(BF)


def placed(columns, i, size):
    place = lax.broadcasted_iota(jnp.int32, (512, size), 1)
    return (place == columns[:, i : i + 1]).astype(F32).astype(BF)


def segment_of(info, row, dims, axis):
    place = lax.broadcasted_iota(jnp.int32, dims, axis)
    total = jnp.full(dims, -1, jnp.int32)
    for j in range(4):
        total = total + (place >= info[1 + 4 * row + j]).astype(jnp.int32)
    return total


def low_lanes():
    return lax.broadcasted_iota(jnp.int32, (1, 128), 1) < 64


def stacked(pair):
    left = low_lanes()
    zero = jnp.zeros_like(pair)
    return jnp.concatenate([jnp.where(left, pair, zero), jnp.where(left, zero, pair)], 0)


def merged(two):
    n = two.shape[0] // 2
    return jnp.where(low_lanes(), two[:n], two[n:])


def softmax(scores, allowed):
    scores = jnp.where(allowed, scores * 0.125, MASKED_SCORE)
    weights = jnp.exp(scores - jnp.max(scores, -1, keepdims=True))
    return weights / jnp.sum(weights, -1, keepdims=True)


def softmax_back(probs, dprobs):
    return (probs * (dprobs - jnp.sum(probs * dprobs, -1, keepdims=True))).astype(BF)


def self_allowed(info, row):
    at = segment_of(info, row, (128, 128), 0)
    key = segment_of(info, row, (128, 128), 1)
    i = lax.broadcasted_iota(jnp.int32, (128, 128), 0)
    j = lax.broadcasted_iota(jnp.int32, (128, 128), 1)
    allowed = (at == key) & (j <= i)
    return jnp.concatenate([allowed, allowed], 0)


def cross_allowed(info, row):
    core = info[0]
    lane = lax.broadcasted_iota(jnp.int32, (1, 768), 1)
    key = jnp.full((1, 768), -1, jnp.int32)
    images = (2 * row, 2 * row + 1, 4 + 2 * row, 5 + 2 * row)
    captions = (core, 2 + core, 1 - core, 3 - core)
    for block in range(4):
        limit = info[9 + images[block]]
        key = jnp.where(
            (lane >= 192 * block) & (lane < 192 * block + limit), captions[block], key
        )
    at = segment_of(info, row, (128, 1), 0)
    return jnp.concatenate([at, at], 0) == key


def row_keys(kv, row, lanes):
    return jnp.concatenate(
        [kv[384 * row : 384 * row + 384, lanes], kv[768 + 384 * row : 1152 + 384 * row, lanes]], 0
    )


def lanes_of():
    lane = lax.broadcasted_iota(jnp.int32, (128, 1536), 0)
    unit = lax.broadcasted_iota(jnp.int32, (128, 1536), 1)
    return (lane == 64 + lax.rem(unit, 24)).astype(F32).astype(BF)


def own_lanes():
    chip = lax.broadcasted_iota(jnp.int32, (64, 1536), 0) * 24
    unit = lax.broadcasted_iota(jnp.int32, (64, 1536), 1)
    return (unit >= chip) & (unit < chip + 24)


def self_forward_kernel(
    info, b_low, b_high, a_low, a_high, index, text,
    part, joined, mixed, normed, w_qkv, w_out, vec, b_up,
):
    xhat, _ = normalize(text[...].astype(F32))
    pick_a, pick_a0, pick_a1 = (picked(index, i, 768) for i in range(3))
    pick_b, pick_b0 = picked(index, 3, 768), picked(index, 4, 768)
    pick_out = picked(index, 6, 384)
    tail = jnp.concatenate([b_low[:, 1920:], b_high[:, 1920:]], 0)
    rows = lax.dot_general(
        tail, pick_b, (((0,), (1,)), ((), ())), preferred_element_type=F32
    )
    rest = lax.dot_general(
        tail, pick_b0, (((0,), (1,)), ((), ())), preferred_element_type=F32
    )
    vec[...] = rows[:16] + rest[16:32]
    of_chip = mm(picked(index, 11, 64), tail).astype(BF)
    b_up[...] = jnp.sum(jnp.where(own_lanes(), mm(of_chip, lanes_of()), 0.0), 0, keepdims=True)
    outs = jnp.concatenate([b_low[:, 1152:1920], b_high[:, 1152:1920]], 0)
    w_out[...] = mm(pick_out, outs).astype(BF)
    normed[...] = (xhat * vec[0:1] + vec[4:5]).astype(BF)
    ga = jnp.concatenate([a_low[...], a_high[...]], 0)
    w_qkv[:, :640] = (
        mm(pick_a, ga[:, :640]) + mm(pick_a0, ga[:, 1152:1792])
    ).astype(BF)
    w_qkv[:, 640:] = (
        mm(pick_a, ga[:, 640:1152]) + mm(pick_a1, ga[:, 1152:1664])
    ).astype(BF)
    joined[...] = mm(normed[...], w_qkv[...]).astype(BF)
    for row in range(2):
        allowed = self_allowed(info, row)
        at = slice(128 * row, 128 * row + 128)
        for j in range(3):
            q = stacked(joined[at, 128 * j : 128 * j + 128])
            k = joined[at, 384 + 128 * j : 512 + 128 * j]
            v = joined[at, 768 + 128 * j : 896 + 128 * j]
            probs = softmax(mm_t(q, k), allowed)
            mixed[at, 128 * j : 128 * j + 128] = merged(mm(probs.astype(BF), v)).astype(BF)
    part[...] = mm(mixed[...], w_out[...])


def self_forward(info, gathered, index, text):
    a_low, a_high, b_low, b_high = gathered
    return staged(
        "self_forward",
        self_forward_kernel,
        (info,),
        (b_low, b_high, a_low, a_high, index, text),
        (
            shape((256, 768), F32),
            shape((256, 1152), BF),
            shape((256, 384), BF),
            shape((256, 768), BF),
            shape((768, 1152), BF),
            shape((384, 768), BF),
            shape((16, 768), F32),
            shape((1, 1536), F32),
        ),
        4e9,
    )


def unpack_kernel(g, index, query, up, cross, down):
    pick, pick0, pick1 = (picked(index, i, 768) for i in range(7, 10))
    left = (mm(pick, g[:, :1024]) + mm(pick0, g[:, 1920:2944])).astype(BF)
    query[...] = left[:, :384]
    up[:, :640] = left[:, 384:]
    up[:, 640:] = (mm(pick, g[:, 1024:1920]) + mm(pick1, g[:, 1920:2816])).astype(BF)
    cross[...] = mm(picked(index, 10, 384), g[:, 2944:3712]).astype(BF)
    slabs = [
        g[:, 3712 + 768 * k : 4480 + 768 * k].astype(F32).reshape(64, 1, 8, 768) for k in range(3)
    ]
    down[...] = jnp.concatenate(slabs, 1).reshape(1536, 768).astype(BF)


def unpack(gathered, index):
    outs = ((768, 384), (768, 1536), (384, 768), (1536, 768))
    return staged(
        "unpack", unpack_kernel, (), (gathered, index), [shape(o, BF) for o in outs], 3.5e9
    )


def natural_row(at_slot, twelfth):
    return at_slot * 6 + twelfth + jnp.where(twelfth >= 6, 378, 0)


def index_kernel(place, rows, columns):
    core, chip = place[0], place[1]

    def target_of(order, slot):
        first = slot * 0 + core == 0
        target = 0
        for axis, digit in zip(order, (slot >> 4, (slot >> 2) & 3, slot & 3)):
            step = STRIDE[axis]
            here = lax.rem(lax.div(chip, step), 4)
            other = jnp.where(
                first, jnp.where(digit == 1, 3, jnp.maximum(digit, 1) - 1), digit ^ (digit >> 1)
            )
            target = target + (here ^ other) * step
        return target

    def picks_of(at_slot, eight):
        return [
            natural_row(at_slot, eight),
            jnp.where(eight < 4, natural_row(at_slot, 8 + eight), -1),
            jnp.where(eight >= 4, natural_row(at_slot, 4 + eight), -1),
        ]

    def out_pick(at_slot, eight):
        return jnp.where(eight < 6, at_slot * 6 + eight, -1)

    at = lax.broadcasted_iota(jnp.int32, (1, 512), 1)
    slot, eight = at >> 3, at & 7
    target_a, target_b = (target_of(order[::-1], slot) for order in GATHER_ORDERS)
    values = picks_of(target_a, eight) + picks_of(target_b, eight) + [out_pick(target_b, eight)]
    values += picks_of(slot, eight) + [out_pick(slot, eight), jnp.where(eight == 0, target_b, -1)]
    for i in range(16):
        rows[i : i + 1] = values[i] if i < len(values) else at * 0
    at = lax.broadcasted_iota(jnp.int32, (512, 1), 0)
    eight = at & 7
    targets = [target_of(order, at >> 3) for order in ORDERS]
    values = []
    for target in targets:
        values += [natural_row(target, eight), natural_row(target, 8 + (eight & 3))]
    values += [out_pick(target, eight) for target in targets]
    values += [target * 8 + eight for target in targets] + [jnp.where(eight == 0, targets[2], -1)]
    for i in range(16):
        columns[:, i : i + 1] = values[i] if i < len(values) else at * 0


def indices(place):
    return staged(
        "indices",
        index_kernel,
        (place,),
        (),
        [shape((16, 512), jnp.int32), shape((512, 16), jnp.int32)],
        1e6,
    )


def image_pick_kernel(pick, tokens, *outs):
    for turn, out in enumerate(outs):
        out[...] = tokens[pick[turn]]


def image_pick(pick, tokens):
    return staged(
        "image_pick", image_pick_kernel, (pick,), (tokens,), [shape((188, 768), BF)] * 4, 1e6
    )


def image_stack_kernel(v0, v1, v2, v3, out, wide):
    wide[188:192] = jnp.zeros((4, 768), F32)
    for turn, value in enumerate((v0, v1, v2, v3)):
        wide[0:188] = value[...].astype(F32)
        out[192 * turn : 192 * turn + 192] = wide[...].astype(BF)


def image_stack(values):
    return staged(
        "image_stack",
        image_stack_kernel,
        (),
        values,
        [shape((768, 768), BF)],
        1e6,
        [pltpu.VMEM((192, 768), F32)],
    )[0]


def image_forward_kernel(
    vec, b_low, b_high, index, own, other, kv, normed, w_kv
):
    g = jnp.concatenate([b_low[:, :1152], b_high[:, :1152]], 0)
    pick = picked(index, 3, 768)
    for i in range(2):
        lanes = slice(384 * i, 384 * i + 384)
        rest = mm(picked(index, 4 + i, 768), g[:, 768:])
        w_kv[:, lanes] = (mm(pick, g[:, lanes]) + rest).astype(BF)
    row = lax.broadcasted_iota(jnp.int32, (192, 1), 0)
    for image in range(8):
        source, here = (own, 192 * image) if image < 4 else (other, 192 * image - 768)
        xhat, _ = normalize(source[here : here + 192].astype(F32))
        at = slice(192 * image, 192 * image + 192)
        normed[at] = jnp.where(row < 188, xhat * vec[2:3] + vec[6:7], 0.0).astype(BF)
        kv[at] = mm(normed[at], w_kv[...]).astype(BF)


def image_forward(vec, b_low, b_high, index, own, other):
    return staged(
        "image_forward",
        image_forward_kernel,
        (),
        (vec, b_low, b_high, index, own, other),
        (shape((1536, 768), BF), shape((1536, 768), BF), shape((768, 768), BF)),
        3.5e9,
    )


def cross_forward_kernel(
    info, vec, text, mine, got, w_query, kv, w_out, after, normed, queries, mixed, part
):
    after[...] = text[...].astype(F32) + (mine[...] + got[...])
    xhat, _ = normalize(after[...])
    normed[...] = (xhat * vec[1:2] + vec[5:6]).astype(BF)
    queries[...] = mm(normed[...], w_query[...]).astype(BF)
    for row in range(2):
        allowed = cross_allowed(info, row)
        at = slice(128 * row, 128 * row + 128)
        for j in range(3):
            lanes = slice(128 * j, 128 * j + 128)
            q = stacked(queries[at, lanes])
            k = row_keys(kv, row, lanes)
            v = row_keys(kv, row, slice(384 + 128 * j, 512 + 128 * j))
            probs = softmax(mm_t(q, k), allowed)
            mixed[at, lanes] = merged(mm(probs.astype(BF), v)).astype(BF)
    part[...] = mm(mixed[...], w_out[...])


def cross_forward(info, vec, text, mine, got, kv, w_query, w_out):
    return staged(
        "cross_forward",
        cross_forward_kernel,
        (info,),
        (vec, text, mine, got, w_query, kv, w_out),
        (shape((256, 768), F32), shape((256, 768), BF), shape((256, 384), BF), shape((256, 384), BF), shape((256, 768), F32)),
        3e9,
    )


def feed_kernel(
    info, vec, b_up, before, mine, got, w_up, w_down, grad,
    after, normed, active, hidden_low, to_mine, to_other, back, sums,
    part,
):
    after[...] = before[...] + (mine[...] + got[...])
    xhat, _ = normalize(after[...])
    normed[...] = (xhat * vec[3:4] + vec[7:8]).astype(BF)
    part[...] = jnp.zeros((256, 768), F32)
    for k in range(3):
        lanes = slice(512 * k, 512 * k + 512)
        down = w_down[lanes]
        hidden = mm(normed[...], w_up[:, lanes]) + b_up[:, lanes]
        cdf = 0.5 * (1.0 + lax.erf(hidden * 0.7071067811865476))
        active[:, lanes] = (hidden * cdf).astype(BF)
        slope = cdf + hidden * (jnp.exp(-0.5 * hidden * hidden) * 0.3989422804014327)
        part[...] += mm(active[:, lanes], down)
        hidden_low[:, lanes] = (mm_t(grad[...], down) * slope).astype(BF)
    back[...] = mm_t(hidden_low[...], w_up[...])
    sums[...] = jnp.concatenate(
        [
            jnp.sum(back[...] * xhat, 0, keepdims=True),
            jnp.sum(back[...], 0, keepdims=True),
            jnp.zeros((6, 768), F32),
        ],
        0,
    )
    core = info[0]
    bias = vec[8:9]
    for row in range(2):
        at = pl.ds(pl.multiple_of(128 * row + 64 * core, 64), 64)
        to_mine[64 * row : 64 * row + 64] = after[at] + part[at] + bias
        at = pl.ds(pl.multiple_of(128 * row + 64 * (1 - core), 64), 64)
        to_other[64 * row : 64 * row + 64] = part[at]


def feed(info, vec, b_up, before, mine, got, w_up, w_down, grad):
    return staged(
        "feed",
        feed_kernel,
        (info,),
        (vec, b_up, before, mine, got, w_up, w_down, grad),
        (shape((256, 768), F32), shape((256, 768), BF), shape((256, 1536), BF), shape((256, 1536), BF), shape((128, 768), F32), shape((128, 768), F32), shape((256, 768), F32), shape((8, 768), F32)),
        3e9,
        [pltpu.VMEM((256, 768), F32)],
    )


def laid_out(weight, qa, qb, width):
    top = mm(qa, weight)
    rest = mm(qb, weight)
    n = weight.shape[1]
    upper = lax.broadcasted_iota(jnp.int32, (512, 1), 0) % 8 < 4
    tail = rest[:, width:]
    if n - width < width:
        tail = jnp.concatenate([tail, jnp.zeros((512, 2 * width - n), F32)], 1)
    return top, jnp.where(upper, rest[:, :width], tail)


def put(keep, send, lanes, value):
    keep[:, lanes] = value[:256].astype(BF)
    send[:, lanes] = value[256:].astype(BF)


def feed_grads_kernel(normed, active, hidden_low, grad, index, *outs):
    keeps, sends, up_rows = outs[0:3], outs[3:6], outs[6]
    d_up = t_mm(normed[...], hidden_low[...]).astype(BF)
    total = jnp.sum(hidden_low[...].astype(F32), 0, keepdims=True)
    of_chip = mm_t(jnp.where(own_lanes(), total, 0.0).astype(BF), lanes_of()).astype(BF)
    up_rows[...] = mm(placed(index, 12, 64), of_chip)
    for p in range(3):
        qa, qb = placed(index, 2 * p, 768), placed(index, 2 * p + 1, 768)
        top, rest = laid_out(d_up[:, 512 * p : 512 * p + 512], qa, qb, 256)
        put(keeps[p], sends[p], slice(0, 512), top)
        put(keeps[p], sends[p], slice(512, 768), rest)
    d_down = t_mm(active[...], grad[...]).reshape(64, 3, 8, 768)
    slabs = [placed(index, 9 + p, 512) for p in range(3)]
    for k in range(3):
        rows = d_down[:, k].reshape(512, 768).astype(BF)
        for p, slab in enumerate(slabs):
            moved = mm(slab, rows[:, 256 * p : 256 * p + 256])
            put(keeps[p], sends[p], slice(768 + 256 * k, 1024 + 256 * k), moved)


def feed_grads(normed, active, hidden_low, grad, index):
    return staged(
        "feed_grads",
        feed_grads_kernel,
        (),
        (normed, active, hidden_low, grad, index),
        (*[shape((256, 1536), BF)] * 6, shape((512, 128), F32)),
        6e9,
    )


def cross_backward_kernel(
    info, vec, grad, mine, got, after, w_out, queries, kv, w_query, before,
    stream, low, dq, dkv, back, sums,
):
    xhat, inv = normalize(after[...])
    step = norm_back(mine[...] + got[...], vec[3:4], xhat, inv)
    stream[...] = grad[...].astype(F32) + step
    low[...] = stream[...].astype(BF)
    mixed_grad = mm_t(low[...], w_out[...]).astype(BF)
    for row in range(2):
        allowed = cross_allowed(info, row)
        at = slice(128 * row, 128 * row + 128)
        for j in range(3):
            lanes = slice(128 * j, 128 * j + 128)
            value_lanes = slice(384 + 128 * j, 512 + 128 * j)
            q = stacked(queries[at, lanes])
            do = stacked(mixed_grad[at, lanes])
            k = row_keys(kv, row, lanes)
            v = row_keys(kv, row, value_lanes)
            probs = softmax(mm_t(q, k), allowed)
            ds = softmax_back(probs, mm_t(do, v))
            dq[at, lanes] = (merged(mm(ds, k)) * 0.125).astype(BF)
            dk = (t_mm(ds, q) * 0.125).astype(BF)
            dv = t_mm(probs.astype(BF), do).astype(BF)
            for value, where in ((dk, lanes), (dv, value_lanes)):
                dkv[384 * row : 384 * row + 384, where] = value[:384]
                dkv[768 + 384 * row : 1152 + 384 * row, where] = value[384:]
    back[...] = mm_t(dq[...], w_query[...])
    xhat, _ = normalize(before[...])
    sums[...] = jnp.concatenate(
        [
            jnp.sum(back[...] * xhat, 0, keepdims=True),
            jnp.sum(back[...], 0, keepdims=True),
            jnp.zeros((6, 768), F32),
        ],
        0,
    )


def cross_backward(info, vec, grad, mine, got, after, w_out, queries, kv, w_query, before):
    return staged(
        "cross_backward",
        cross_backward_kernel,
        (info,),
        (vec, grad, mine, got, after, w_out, queries, kv, w_query, before),
        (shape((256, 768), F32), shape((256, 768), BF), shape((256, 384), BF), shape((1536, 768), BF), shape((256, 768), F32), shape((8, 768), F32)),
        5e9,
    )


def cross_grads_kernel(
    image_normed, dkv, normed, dq, mixed, low, index, *outs
):
    keeps, sends = outs[0:3], outs[3:6]
    d_kv = t_mm(image_normed[...], dkv[...]).astype(BF)
    d_query = t_mm(normed[...], dq[...]).astype(BF)
    pieces = (d_kv[:, :384], d_kv[:, 384:], d_query)
    d_out = t_mm(mixed[...], low[...]).astype(BF)
    for p in range(3):
        qa, qb = placed(index, 2 * p, 768), placed(index, 2 * p + 1, 768)
        o = placed(index, 6 + p, 384)
        top, rest = laid_out(pieces[p], qa, qb, 256)
        put(keeps[p], sends[p], slice(0, 384), top)
        put(keeps[p], sends[p], slice(384, 640), rest)
        put(keeps[p], sends[p], slice(640, 896), mm(o, d_out[:, 256 * p : 256 * p + 256]))


def cross_grads(image_normed, dkv, normed, dq, mixed, low, index):
    return staged(
        "cross_grads",
        cross_grads_kernel,
        (),
        (image_normed, dkv, normed, dq, mixed, low, index),
        (*[shape((256, 896), BF)] * 6,),
        4e9,
    )


def image_part_kernel(dkv, w_kv, out):
    out[...] = mm_t(dkv[768:], w_kv[...]).astype(BF)


def image_part(dkv, w_kv):
    return staged(
        "image_part",
        image_part_kernel,
        (),
        (dkv, w_kv),
        (shape((768, 768), BF),),
        1e9,
    )


def image_backward_kernel(vec, dkv, w_kv, got, own, out, low1, low2, low3, sums):
    total = [jnp.zeros((1, 768), F32)] * 2
    for image, result in enumerate((out, low1, low2, low3)):
        at = slice(192 * image, 192 * image + 192)
        dy = mm_t(dkv[at], w_kv[...]) + got[at].astype(F32)
        xhat, inv = normalize(own[at].astype(F32))
        total = [
            total[0] + jnp.sum(dy * xhat, 0, keepdims=True),
            total[1] + jnp.sum(dy, 0, keepdims=True),
        ]
        result[...] = norm_back(dy, vec[2:3], xhat, inv)[:188].astype(result.dtype)
    sums[...] = jnp.concatenate(total + [jnp.zeros((6, 768), F32)], 0)


def image_backward(vec, dkv, w_kv, got, own):
    return staged(
        "image_backward",
        image_backward_kernel,
        (),
        (vec, dkv, w_kv, got, own),
        (shape((188, 768), F32), *[shape((188, 768), BF)] * 3, shape((8, 768), F32)),
        1e9,
    )


def self_backward_kernel(
    info, vec, stream_in, mine, got, before, w_out, joined, w_qkv, text,
    stream_mine, low, d_joined, to_mine, to_other, sums,
    stream, back,
):
    xhat, inv = normalize(before[...])
    stream[...] = stream_in[...] + norm_back(mine[...] + got[...], vec[1:2], xhat, inv)
    low[...] = stream[...].astype(BF)
    mixed_grad = mm_t(low[...], w_out[...]).astype(BF)
    for row in range(2):
        allowed = self_allowed(info, row)
        at = slice(128 * row, 128 * row + 128)
        for j in range(3):
            lanes = [slice(384 * i + 128 * j, 384 * i + 128 * j + 128) for i in range(3)]
            q = stacked(joined[at, lanes[0]])
            k = joined[at, lanes[1]]
            v = joined[at, lanes[2]]
            do = stacked(mixed_grad[at, lanes[0]])
            probs = softmax(mm_t(q, k), allowed)
            ds = softmax_back(probs, mm_t(do, v))
            d_joined[at, lanes[0]] = (merged(mm(ds, k)) * 0.125).astype(BF)
            d_joined[at, lanes[1]] = (t_mm(ds, q) * 0.125).astype(BF)
            d_joined[at, lanes[2]] = t_mm(probs.astype(BF), do).astype(BF)
    back[...] = mm_t(d_joined[...], w_qkv[...])
    xhat, _ = normalize(text[...].astype(F32))
    sums[...] = jnp.concatenate(
        [
            jnp.sum(back[...] * xhat, 0, keepdims=True),
            jnp.sum(back[...], 0, keepdims=True),
            jnp.zeros((6, 768), F32),
        ],
        0,
    )
    core = info[0]
    for row in range(2):
        at = pl.ds(pl.multiple_of(128 * row + 64 * core, 64), 64)
        stream_mine[64 * row : 64 * row + 64] = stream[at]
        to_mine[64 * row : 64 * row + 64] = back[at]
        at = pl.ds(pl.multiple_of(128 * row + 64 * (1 - core), 64), 64)
        to_other[64 * row : 64 * row + 64] = back[at]


def self_backward(info, vec, stream_in, mine, got, before, w_out, joined, w_qkv, text):
    return staged(
        "self_backward",
        self_backward_kernel,
        (info,),
        (vec, stream_in, mine, got, before, w_out, joined, w_qkv, text),
        (shape((128, 768), F32), shape((256, 768), BF), shape((256, 1152), BF), shape((128, 768), F32), shape((128, 768), F32), shape((8, 768), F32)),
        3e9,
        [pltpu.VMEM((256, 768), F32), pltpu.VMEM((256, 768), F32)],
    )


def self_grads_kernel(
    normed, d_joined, mixed, low, sum0, sum1, sum2, sum3, grad, up_rows,
    index, e0, e1, e2, *outs,
):
    keeps, sends = outs[0:3], outs[3:6]
    for send, early in zip(sends, (e0, e1, e2)):
        send[:, :896] = early[...]
    d_qkv = t_mm(normed[...], d_joined[...]).astype(BF)
    d_out = t_mm(mixed[...], low[...]).astype(BF)
    for p in range(3):
        qa, qb = placed(index, 2 * p, 768), placed(index, 2 * p + 1, 768)
        o = placed(index, 6 + p, 384)
        top, rest = laid_out(d_qkv[:, 384 * p : 384 * p + 384], qa, qb, 256)
        moved = mm(o, d_out[:, 256 * p : 256 * p + 256])
        for at, value in ((0, top), (384, rest), (640, moved)):
            n = value.shape[1]
            keeps[p][:, at : at + n] = value[:256].astype(BF)
            sends[p][:, 896 + at : 896 + at + n] = value[256:].astype(BF)
    down_sum = jnp.sum(grad[...].astype(F32), 0, keepdims=True) * 0.5
    rows = [s[i : i + 1] for i in range(2) for s in (sum0, sum1, sum2, sum3)]
    rows = jnp.concatenate(rows + [down_sum, jnp.zeros((7, 768), F32)], 0).astype(BF)
    zero = jnp.zeros((16, 768), BF)
    first = jnp.concatenate([rows] + [zero] * 7, 0)
    second = jnp.concatenate([zero, rows] + [zero] * 6, 0)
    value = mm_t(qa, first) + mm_t(qb, second) + up_rows[...]
    keeps[2][:, 896:1024] = value[:256].astype(BF)
    sends[2][:, 1792:1920] = value[256:].astype(BF)


def self_grads(normed, d_joined, mixed, low, sums, grad, up_rows, index, early):
    return staged(
        "self_grads",
        self_grads_kernel,
        (),
        (normed, d_joined, mixed, low, *sums, grad, up_rows, index, *early),
        (*[shape((256, n), BF) for n in (896, 896, 1024, 1792, 1792, 1920)],),
        3e9,
    )


def first_core(info, dims):
    return lax.broadcasted_iota(jnp.int32, dims, 0) * 0 + info[0] == 0


def half_columns(refs, low):
    pieces = []
    for ref, blocks, width in refs:
        for i in range(blocks):
            at = 2 * i * width + (0 if low else width)
            pieces.append(ref[:, at : at + width].astype(F32))
    return jnp.concatenate(pieces, 1)


def weight_blocks(qkv, kv, query, up):
    return ((qkv, 3, 384), (kv, 2, 384), (query, 1, 384), (up, 1, 1536))


def vector_rows(vectors):
    i = lax.broadcasted_iota(jnp.int32, (16, 128), 0)
    j = lax.broadcasted_iota(jnp.int32, (16, 128), 1)
    spread = ((i == j) | (i + 16 == j)).astype(F32).astype(BF)
    return t_mm(vectors[...], spread)[:6]


def pack_swap_kernel(info, qkv, kv, query, up, vectors, send):
    refs = weight_blocks(qkv, kv, query, up)
    theirs = jnp.where(
        first_core(info, (6, 3840)), half_columns(refs, False), half_columns(refs, True)
    )
    send[:, :3840] = theirs.astype(BF)
    send[:, 3840:] = vector_rows(vectors).astype(BF)


def pack_slots_kernel(
    info, qkv, kv, query, up, vectors, got, self_out, cross_out, down, up_bias,
    slot, part_a, part_b, twelve, rest,
):
    refs = weight_blocks(qkv, kv, query, up)
    first = first_core(info, (6, 3968))
    mine = jnp.concatenate(
        [
            jnp.where(first[:, :3840], half_columns(refs, True), half_columns(refs, False)),
            vector_rows(vectors),
        ],
        1,
    )
    other = got[...].astype(F32)
    twelve[0:6] = jnp.where(first, mine, other)
    twelve[6:12] = jnp.where(first, other, mine)
    twelve[12:16] = jnp.zeros((4, 3968), F32)

    def lay(out, at, begin, n, width):
        out[:, at : at + n] = twelve[0:8, begin : begin + n].astype(BF)
        rest[0:4, :width] = twelve[8:12, begin : begin + width]
        rest[4:8, : n - width] = twelve[8:12, begin + width : begin + n]
        if n < 2 * width:
            rest[4:8, n - width : width] = jnp.zeros((4, 2 * width - n), F32)
        out[:, at + n : at + n + width] = rest[:, :width].astype(BF)

    def padded(out, at, ref):
        rest[0:6, :768] = ref[...].astype(F32)
        rest[6:8, :768] = jnp.zeros((2, 768), F32)
        out[:, at : at + 768] = rest[:, :768].astype(BF)

    lay(part_a, 0, 0, 1152, 640)
    lay(part_b, 0, 1152, 768, 384)
    padded(part_b, 1152, self_out)
    lane = lax.broadcasted_iota(jnp.int32, (8, 128), 1)
    vec = jnp.where(lane < 16, twelve[0:8, 3840:], 0.0)
    vec = vec + jnp.where((lane >= 16) & (lane < 32), twelve[8:16, 3840:], 0.0)
    part_b[:, 1920:] = (vec + up_bias[...].astype(F32)).astype(BF)
    lay(slot, 0, 1920, 1920, 1024)
    padded(slot, 2944, cross_out)
    slabs = down[...].astype(F32)
    for k in range(3):
        at = 3712 + 768 * k
        slot[:, at : at + 768] = slabs[8 * k : 8 * k + 8].astype(BF)


def pack_swap(info, weights, vectors):
    return staged(
        "pack_swap",
        pack_swap_kernel,
        (info,),
        (*weights, vectors),
        (shape((6, 3968), BF),),
        1e6,
        mib=8,
    )[0]


def pack_slots(info, weights, vectors, got, self_out, cross_out, down, up_bias):
    return staged(
        "pack_slots",
        pack_slots_kernel,
        (info,),
        (*weights, vectors, got, self_out, cross_out, down, up_bias),
        (shape((8, 6016), BF), shape((8, 1792), BF), shape((8, 2048), BF)),
        1e6,
        [pltpu.VMEM((16, 3968), F32), pltpu.VMEM((8, 1024), F32)],
        mib=8,
    )


TWELVES = (
    [(0, 512, 256)] * 3 + [(1536, 384, 256)] * 3 + [(2432, 384, 256)] * 3
)


def finish_send_kernel(info, *refs):
    keeps, gots, (s0, s1, s2, send, own, twelve) = refs[:3], refs[3:6], refs[6:]
    sums = (s0, s1, s2)
    for p in range(3):
        sums[p][...] = keeps[p][...].astype(F32) + gots[p][...].astype(F32)
    here = 0
    for i, (at, n, width) in enumerate(TWELVES):
        ref = sums[i % 3]
        twelve[0:8, here : here + n] = ref[:, at : at + n]
        twelve[8:12, here : here + width] = ref[0:4, at + n : at + n + width]
        twelve[8:12, here + width : here + n] = ref[4:8, at + n : at + n + n - width]
        here += n
    vec = s2[:, 3328:]
    twelve[0:8, 3840:] = vec
    twelve[8:12, 3840:] = pltpu.roll(vec, 112, 1)[0:4]
    first = first_core(info, (6, 3968))
    send[...] = jnp.where(first, twelve[6:12], twelve[0:6])
    own[...] = jnp.where(first, twelve[0:6], twelve[6:12])


def finish_kernel(info, s0, s1, s2, own, got, qkv, out_self, query, kv, out_cross, up, down, vec):
    sums = (s0, s1, s2)
    first = first_core(info, (6, 3840))
    low = jnp.where(first, own[:, :3840], got[:, :3840])
    high = jnp.where(first, got[:, :3840], own[:, :3840])
    for ref, begin, blocks, width in (
        (up, 0, 1, 1536), (kv, 1536, 2, 384), (query, 2304, 1, 384), (qkv, 2688, 3, 384),
    ):
        for i in range(blocks):
            at = begin + i * width
            ref[:, 2 * i * width : (2 * i + 1) * width] = low[:, at : at + width]
            ref[:, (2 * i + 1) * width : (2 * i + 2) * width] = high[:, at : at + width]
    for p in range(3):
        lanes = slice(256 * p, 256 * p + 256)
        out_self[:, lanes] = sums[p][0:6, 3072:3328]
        out_cross[:, lanes] = sums[p][0:6, 2176:2432]
        for k in range(3):
            at = 768 + 256 * k
            down[8 * k : 8 * k + 8, lanes] = sums[p][:, at : at + 256]
    vec[...] = own[:, 3840:] + got[:, 3840:]


def finish_send(info, keeps, gots):
    widths = [k.shape[1] for k in keeps]
    return staged(
        "finish_send",
        finish_send_kernel,
        (info,),
        (*keeps, *gots),
        [shape((8, n), F32) for n in widths] + [shape((6, 3968), F32)] * 2,
        1e6,
        [pltpu.VMEM((16, 3968), F32)],
        mib=8,
    )


def finish(info, sums, own, got):
    return staged(
        "finish",
        finish_kernel,
        (info,),
        (*sums, own, got),
        [
            shape(dims, F32)
            for dims in (
                (6, 2304), (6, 768), (6, 768), (6, 1536), (6, 768), (6, 3072), (24, 768), (6, 128),
            )
        ],
        1e6,
        mib=8,
    )


def text_finish_kernel(vec, text, stream, mine, got, out_mine, out_got, grad, out):
    xhat, inv = normalize(text[...].astype(F32))
    grad[...] = stream[...] + norm_back(mine[...] + got[...], vec[0:1], xhat, inv)
    out[...] = out_mine[...] + out_got[...]


def text_finish(vec, text, stream, mine, got, out_mine, out_got):
    return staged(
        "text_finish",
        text_finish_kernel,
        (),
        (vec, text, stream, mine, got, out_mine, out_got),
        [shape((128, 768), F32)] * 2,
        1e6,
        mib=8,
    )


def image_finish_kernel(pick, v0, v1, v2, v3, out):
    values = [v[...].astype(F32) for v in (v0, v1, v2, v3)]
    for image in range(4):
        total = values[3]
        for turn in range(3):
            total = jnp.where(pick[turn] == image, values[turn], total)
        out[:, image, :] = total


def image_finish(pick, values):
    out = staged(
        "image_finish",
        image_finish_kernel,
        (pick,),
        values,
        [shape((188, 4, 768), F32)],
        1e6,
    )[0]
    return jnp.transpose(out, (1, 0, 2))


def combine_kernel(plan, *refs):
    at = 0
    ins = []
    for keeps, gots in plan:
        ins.append((refs[at : at + len(keeps)], refs[at + len(keeps) : at + len(keeps) + len(gots)]))
        at += len(keeps) + len(gots)
    outs = refs[at:]
    for p, (keeps, gots) in enumerate(ins):
        here = 0
        edges = []
        for ref in keeps:
            edges.append((here, here + ref.shape[1], ref))
            here += ref.shape[1]
        here = 0
        for ref in gots:
            for low, high, keep in edges:
                a, b = max(low, here), min(high, here + ref.shape[1])
                if a >= b:
                    continue
                total = keep[:, a - low : b - low].astype(F32) + ref[:, a - here : b - here].astype(F32)
                half = total.shape[0] // 2
                outs[2 * p][:, a:b] = total[:half].astype(BF)
                outs[2 * p + 1][:, a:b] = total[half:].astype(BF)
            here += ref.shape[1]


def combine(parts):
    plan, args, outs = [], [], []
    for keeps, gots in parts:
        plan.append(([k.shape[1] for k in keeps], [g.shape[1] for g in gots]))
        args += [*keeps, *gots]
        rows, width = keeps[0].shape[0], sum(k.shape[1] for k in keeps)
        outs += [shape((rows // 2, width), BF)] * 2
    got = staged(
        "combine", lambda *refs: combine_kernel(plan, *refs), (), args, outs, 1e6
    )
    return [(got[2 * p], got[2 * p + 1]) for p in range(len(parts))]


def send_step(step, values, parts=(0, 1, 2)):
    v0, v1 = ((1, 3), (3, 1))[step % 2]
    return [
        lax.ppermute(v, BOTH, xor_pairs(ORDERS[p][step // 2], v0, v1)) for v, p in zip(values, parts)
    ]


def after(value, *others):
    return lax.optimization_barrier((value, *others))[0]


def gather_parts(parts, orders):
    ticks = []
    for phase in range(3):
        for step, (v0, v1) in enumerate(((3, 1), (1, 3))):
            got = [lax.ppermute(v, BOTH, xor_pairs(o[phase], v0, v1)) for v, o in zip(parts, orders)]
            if phase == 2 and step == 1:
                return list(zip(parts, got)), ticks
            got, parts = lax.optimization_barrier((got, parts))
            ticks.append(got[0])
            parts = [jnp.concatenate([p, g], 0) for p, g in zip(parts, got)]


def on_device(
    text_input,
    image_tokens,
    output_grad,
    segment_starts,
    caption_image,
    image_counts,
    norm_gain,
    norm_bias,
    self_qkv,
    self_out,
    cross_q,
    cross_kv,
    cross_out,
    up_weight,
    up_bias,
    down_weight,
    down_bias,
):
    core = lax.axis_index("seq")
    chip = lax.axis_index("batch")
    first = core == 0

    def ordered(own, other, axis):
        return jnp.where(
            first, jnp.concatenate([own, other], axis), jnp.concatenate([other, own], axis)
        )

    place = jnp.stack([core, chip]).astype(jnp.int32)
    weights = (self_qkv, cross_kv, cross_q, up_weight)
    vectors = jnp.concatenate([norm_gain, norm_bias, down_bias[None]], 0)
    vectors = jnp.pad(vectors, ((0, 7), (0, 122)))
    bias_row = jnp.pad(up_bias[None], ((0, 7), (64, 40)))
    got = swap(pack_swap(place, weights, vectors))
    slot, part_a, part_b = pack_slots(
        place, weights, vectors, got, self_out, cross_out, down_weight, bias_row
    )
    gathered = lax.all_gather(slot, "batch", axis=0, tiled=True)
    ((a_low, a_high), (b_low, b_high)), ticks = gather_parts([part_a, part_b], GATHER_ORDERS)

    late_text, late_grad = after(text_input, ticks[1]), after(output_grad, ticks[3])
    text = ordered(late_text, swap(late_text), 1).reshape(256, 768)
    grad = ordered(late_grad, swap(late_grad), 1).reshape(256, 768)

    group_images = caption_image.reshape(64, 8)
    my_captions = lax.dynamic_index_in_dim(group_images, chip, 0, keepdims=False)
    limits = jnp.take(image_counts, my_captions).reshape(4, 2)
    limits = jnp.where(first, jnp.concatenate([limits[:, 0], limits[:, 1]]), jnp.concatenate([limits[:, 1], limits[:, 0]]))
    turns = jnp.arange(4)
    targets = (chip - turns * 16) % 64
    wanted = group_images[targets, 2 * turns + core]
    local_pick = wanted - (core * 64 + chip) * 4
    outgoing = image_pick(after(local_pick, ticks[0]), image_tokens)
    received = [outgoing[0]]
    for turn in range(1, 4):
        route = [(i, (i - 16 * turn) % 64) for i in range(64)]
        received.append(lax.ppermute(outgoing[turn], "batch", route))
    own_images = image_stack([after(received[0], ticks[4]), *received[1:]])
    other_images = swap(own_images)
    info = jnp.concatenate(
        [core[None], segment_starts.reshape(8), limits, jnp.zeros((15,), jnp.int32)]
    ).astype(jnp.int32)

    row_index, column_index = indices(after(place, ticks[2]))

    info = after(info, grad, text, column_index, other_images)
    part, joined, mixed_self, normed_one, w_qkv, w_self, vec, b_up = self_forward(
        info, (a_low, a_high, b_low, b_high), row_index, text
    )
    got = swap(part)
    kv, image_normed, w_kv = image_forward(vec, b_low, b_high, row_index, own_images, other_images)
    w_query, w_up, w_cross, w_down = unpack(gathered, row_index)
    after_self, normed_two, q_cross, mixed_cross, part = cross_forward(
        info, vec, text, part, got, kv, w_query, w_cross
    )
    after_cross, normed_three, active, hidden_low, text_mine, text_other, part, sum3 = feed(
        info, vec, b_up, after_self, part, swap(part), w_up, w_down, grad
    )
    text_got = swap(text_other)
    got = swap(part)

    grads = feed_grads(normed_three, active, hidden_low, grad, column_index)
    keep_one, up_rows = grads[0:3], grads[6]
    got_one = send_step(0, grads[3:6])
    stream_two, cross_low, dq, dkv, part, sum1 = cross_backward(
        info, vec, after(grad, keep_one[0]), part, got, after_cross, w_cross, q_cross, kv, w_query, after_self
    )
    got = swap(part)
    image_send = image_part(dkv, w_kv)[0]
    image_got = swap(image_send)
    grads = cross_grads(
        image_normed, dkv, normed_two, after(dq, image_send), mixed_cross, cross_low, column_index
    )
    keep_two, early = grads[0:3], grads[3:6]
    *rows_back, sum2 = image_backward(
        vec, dkv, w_kv, after(image_got, keep_two[0]), own_images
    )
    returned = [rows_back[0]]
    for turn in range(1, 4):
        route = [(i, (i + 16 * turn) % 64) for i in range(64)]
        returned.append(lax.ppermute(rows_back[turn], "batch", route))
    stream_one, self_low, d_joined, one_mine, one_other, sum0 = self_backward(
        info, vec, after(stream_two, sum2, *got_one), part, got, after_self, w_self, joined, w_qkv, text
    )
    self_low, *late = lax.optimization_barrier((self_low, *returned[1:]))
    returned = returned[:1] + late
    grads = self_grads(
        normed_one, d_joined, mixed_self, self_low, (sum0, sum1, sum2, sum3), grad, up_rows,
        column_index, early,
    )
    keep_three = grads[0:3]
    got_two = send_step(0, grads[3:6])
    pairs = []
    for p in range(3):
        pairs += combine([([keep_one[p], keep_two[p], keep_three[p]], [got_one[p], got_two[p]])])
    for step in range(1, 6):
        got_step = send_step(step, [s for _, s in pairs])
        step_parts = [([k], [g]) for (k, _), g in zip(pairs, got_step)]
        if step == 5:
            *sums, send, own = finish_send(place, [k for k, _ in pairs], got_step)
        elif step == 1:
            pairs = [combine([one])[0] for one in step_parts]
        else:
            pairs = combine(step_parts)

    image_grad = image_finish(local_pick, returned)
    text_grad, text_output = text_finish(
        vec, text_input.reshape(128, 768), stream_one, one_mine, swap(one_other), text_mine, text_got
    )
    text_grad, text_output = text_grad.reshape(2, 64, 768), text_output.reshape(2, 64, 768)

    qkv_grad, self_grad, query_grad, kv_grad, cross_grad, up_grad, down_grad, vec_sum = finish(
        place, sums, own, swap(send)
    )
    up_bias_grad = sums[2][0, 3392:3416]
    return (
        text_output,
        text_grad,
        image_grad,
        vec_sum[:, 0:4].T,
        vec_sum[:, 4:8].T,
        qkv_grad,
        self_grad,
        query_grad,
        kv_grad,
        cross_grad,
        up_grad,
        up_bias_grad,
        down_grad,
        vec_sum[:, 8],
    )


def solution(mesh):
    rows = P("batch", "seq", None)
    shard = P(BOTH, None)
    wide = P(None, BOTH)
    return jax.shard_map(
        on_device,
        mesh=mesh,
        in_specs=(
            rows, P(BOTH, None, None), rows, P("batch", None), P(), P(), wide, wide,
            shard, shard, shard, shard, shard, shard, P(BOTH), shard, P(BOTH),
        ),
        out_specs=(
            rows, rows, P(BOTH, None, None), wide, wide,
            shard, shard, shard, shard, shard, shard, P(BOTH), shard, P(BOTH),
        ),
        check_vma=False,
    )
```

```python
import math

import jax
import jax.numpy as jnp
from jax import lax
from jax.experimental import pallas as pl
from jax.experimental.pallas import tpu as pltpu
from jax.sharding import PartitionSpec as P

HEADS = 12
HEAD_DIM = 64
EPSILON = 1e-05
MASKED_SCORE = -1e30
BF = jnp.bfloat16
F32 = jnp.float32
BOTH = ("seq", "batch")
STRIDE = {"z": 16, "y": 4, "x": 1}
ORDERS = (("x", "z", "y"), ("y", "x", "z"), ("z", "y", "x"))


def xor_pairs(axis, value0, value1):
    step, out = STRIDE[axis], []
    for core, value in ((0, value0), (1, value1)):
        for chip in range(64):
            at = chip // step % 4
            out.append((core * 64 + chip, core * 64 + chip + ((at ^ value) - at) * step))
    return out


def swap(value):
    return lax.ppermute(value, "seq", [(0, 1), (1, 0)])


def mm(a, b):
    return jnp.dot(a, b, preferred_element_type=F32)


def mm_t(a, b):
    return lax.dot_general(a, b, (((1,), (1,)), ((), ())), preferred_element_type=F32)


def t_mm(a, b):
    return lax.dot_general(a, b, (((0,), (0,)), ((), ())), preferred_element_type=F32)


def normalize(values):
    center = jnp.mean(values, -1, keepdims=True)
    centred = values - center
    spread = jnp.mean(centred * centred, -1, keepdims=True)
    inv = lax.rsqrt(spread + EPSILON)
    return centred * inv, inv


def norm_back(grad, gain, xhat, inv):
    scaled = grad * gain
    return inv * (
        scaled
        - jnp.mean(scaled, -1, keepdims=True)
        - xhat * jnp.mean(scaled * xhat, -1, keepdims=True)
    )


VMEM = pl.BlockSpec(memory_space=pltpu.VMEM)
SMEM = pl.BlockSpec(memory_space=pltpu.SMEM)
HBM = pl.BlockSpec(memory_space=pltpu.HBM)


def shape(dims, dtype):
    return jax.ShapeDtypeStruct(dims, dtype)


def cost(flops, moved):
    return pl.CostEstimate(flops=int(flops), bytes_accessed=int(moved), transcendentals=0)


def params(mib):
    return pltpu.CompilerParams(vmem_limit_bytes=mib * 1024 * 1024)


def staged(name, kernel, scalars, ins, outs, work, scratch=(), mib=16):
    moved = sum(math.prod(v.shape) * v.dtype.itemsize for v in (*ins, *outs))
    return pl.pallas_call(
        kernel,
        out_shape=tuple(outs),
        in_specs=[SMEM] * len(scalars) + [VMEM] * len(ins),
        out_specs=(VMEM,) * len(outs),
        scratch_shapes=list(scratch),
        compiler_params=params(mib),
        cost_estimate=cost(work, moved),
        name=name,
    )(*scalars, *ins)


def placed(columns, i, size):
    place = lax.broadcasted_iota(jnp.int32, (512, size), 1)
    return (place == columns[:, i : i + 1]).astype(F32).astype(BF)


def segment_of(info, row, dims, axis):
    place = lax.broadcasted_iota(jnp.int32, dims, axis)
    total = jnp.full(dims, -1, jnp.int32)
    for j in range(4):
        total = total + (place >= info[1 + 4 * row + j]).astype(jnp.int32)
    return total


def low_lanes():
    return lax.broadcasted_iota(jnp.int32, (1, 128), 1) < 64


def stacked(pair):
    left = low_lanes()
    zero = jnp.zeros_like(pair)
    return jnp.concatenate([jnp.where(left, pair, zero), jnp.where(left, zero, pair)], 0)


def merged(two):
    n = two.shape[0] // 2
    return jnp.where(low_lanes(), two[:n], two[n:])


def softmax(scores, allowed):
    scores = jnp.where(allowed, scores, MASKED_SCORE)
    weights = jnp.exp(scores - jnp.max(scores, -1, keepdims=True))
    return weights * (1.0 / jnp.sum(weights, -1, keepdims=True))


def softmax_back(probs, dprobs):
    return (probs * (dprobs - jnp.sum(probs * dprobs, -1, keepdims=True))).astype(BF)


def self_allowed(info, row):
    at = segment_of(info, row, (128, 128), 0)
    key = segment_of(info, row, (128, 128), 1)
    i = lax.broadcasted_iota(jnp.int32, (128, 128), 0)
    j = lax.broadcasted_iota(jnp.int32, (128, 128), 1)
    allowed = (at == key) & (j <= i)
    return jnp.concatenate([allowed, allowed], 0)


def cross_allowed(info, row):
    core = info[0]
    lane = lax.broadcasted_iota(jnp.int32, (1, 768), 1)
    key = jnp.full((1, 768), -1, jnp.int32)
    images = (2 * row, 2 * row + 1, 4 + 2 * row, 5 + 2 * row)
    captions = (core, 2 + core, 1 - core, 3 - core)
    for block in range(4):
        limit = info[9 + images[block]]
        key = jnp.where(
            (lane >= 192 * block) & (lane < 192 * block + limit), captions[block], key
        )
    at = segment_of(info, row, (128, 1), 0)
    return jnp.concatenate([at, at], 0) == key


def row_keys(kv, row, lanes):
    return jnp.concatenate(
        [kv[384 * row : 384 * row + 384, lanes], kv[768 + 384 * row : 1152 + 384 * row, lanes]], 0
    )


def lanes_of():
    lane = lax.broadcasted_iota(jnp.int32, (128, 1536), 0)
    unit = lax.broadcasted_iota(jnp.int32, (128, 1536), 1)
    return (lane == 64 + lax.rem(unit, 24)).astype(F32).astype(BF)


def own_lanes():
    chip = lax.broadcasted_iota(jnp.int32, (64, 1536), 0) * 24
    unit = lax.broadcasted_iota(jnp.int32, (64, 1536), 1)
    return (unit >= chip) & (unit < chip + 24)


def self_forward_kernel(info, vec, w_qkv, w_out, text, part, joined, mixed, normed):
    xhat, _ = normalize(text[...].astype(F32))
    normed[...] = (xhat * vec[0:1] + vec[4:5]).astype(BF)
    joined[...] = mm(normed[...], w_qkv[...]).astype(BF)
    for row in range(2):
        allowed = self_allowed(info, row)
        at = slice(128 * row, 128 * row + 128)
        for j in range(3):
            q = stacked(joined[at, 128 * j : 128 * j + 128]) * 0.125
            k = joined[at, 384 + 128 * j : 512 + 128 * j]
            v = joined[at, 768 + 128 * j : 896 + 128 * j]
            probs = softmax(mm_t(q, k), allowed)
            mixed[at, 128 * j : 128 * j + 128] = merged(mm(probs.astype(BF), v)).astype(BF)
    part[...] = mm(mixed[...], w_out[...])


def self_forward(info, vec, w_qkv, w_out, text):
    return staged(
        "self_forward",
        self_forward_kernel,
        (info,),
        (vec, w_qkv, w_out, text),
        (
            shape((256, 768), F32),
            shape((256, 1152), BF),
            shape((256, 384), BF),
            shape((256, 768), BF),
        ),
        2e9,
    )


def rows_of_six(first, last, shift):
    row = lax.broadcasted_iota(jnp.int32, (192, 256), 0)
    place = lax.broadcasted_iota(jnp.int32, (192, 256), 1)
    chip = lax.div(row, 6)
    r = row - 6 * chip
    hit = (place == 8 * chip + r + shift) & (r >= first) & (r <= last)
    return hit.astype(F32).astype(BF)


def unpack_kernel(
    gathered, w_qkv, w_kv, w_query, w_up, w_self, w_cross, w_down, vec, b_up, g, sems
):
    spans = ((4608, 2304), (0, 2304), (2304, 2304), (6912, 2432))
    loads = [
        pltpu.make_async_copy(gathered.at[:, pl.ds(at, n)], g.at[:, pl.ds(at, n)], sems.at[i])
        for i, (at, n) in enumerate(spans)
    ]
    for c in loads:
        c.start()
    low, high = rows_of_six(0, 5, 0), rows_of_six(0, 1, 6)
    left, right = rows_of_six(2, 5, -2), rows_of_six(2, 5, 2)

    def natural(at, n, begin, rest, outs):
        for half in range(2):
            here = slice(256 * half, 256 * half + 256)
            there = slice(192 * half, 192 * half + 192)
            a = g[here, at : at + n]
            outs[0][there] = mm(low, a).astype(BF)
            there = slice(outs[2] + 192 * half, outs[2] + 192 * half + 192)
            outs[1][there] = (mm(high, a) + mm(rest, g[here, begin : begin + n])).astype(BF)

    loads[0].wait()
    loads[1].wait()
    natural(0, 1152, 4608, left, (w_qkv, w_qkv, 384))
    natural(1152, 768, 5760, left, (w_kv, w_kv, 384))
    natural(1920, 384, 6528, left, (w_query, w_query, 384))
    loads[2].wait()
    natural(2304, 1536, 4608, right, (w_up, w_up, 384))
    natural(3840, 768, 6144, right, (w_self, w_cross, 0))
    loads[3].wait()
    tail = g[:, 6912:7040]
    lane = lax.broadcasted_iota(jnp.int32, (1, 128), 1)
    one = jnp.where(lane < 16, tail.astype(F32), 0.0).astype(BF)
    two = jnp.where((lane >= 16) & (lane < 32), tail.astype(F32), 0.0).astype(BF)
    halves = [slice(0, 256), slice(256, 512)]
    rows = [mm(low, one[h]) for h in halves]
    rows += [mm(high, one[h]) + mm(left, two[h]) for h in halves]
    across = jnp.transpose(jnp.concatenate(rows, 0))
    vec[...] = across[:16] + across[16:32]
    chip = lax.broadcasted_iota(jnp.int32, (64, 512), 0)
    place = lax.broadcasted_iota(jnp.int32, (64, 512), 1)
    of_chip = mm((place == 8 * chip).astype(F32).astype(BF), tail).astype(BF)
    b_up[...] = jnp.sum(jnp.where(own_lanes(), mm(of_chip, lanes_of()), 0.0), 0, keepdims=True)
    slabs = [
        g[:, 7040 + 768 * k : 7808 + 768 * k].astype(F32).reshape(64, 1, 8, 768) for k in range(3)
    ]
    w_down[...] = jnp.concatenate(slabs, 1).reshape(1536, 768).astype(BF)


def unpack(gathered):
    outs = ((768, 1152), (768, 768), (768, 384), (768, 1536), (384, 768), (384, 768), (1536, 768))
    return pl.pallas_call(
        unpack_kernel,
        out_shape=(
            *[shape(o, BF) for o in outs],
            shape((16, 768), F32),
            shape((1, 1536), F32),
        ),
        in_specs=[HBM],
        out_specs=(VMEM,) * 9,
        scratch_shapes=[pltpu.VMEM((512, 9344), BF), pltpu.SemaphoreType.DMA((4,))],
        compiler_params=params(46),
        cost_estimate=cost(4e9, 20e6),
        name="unpack",
    )(gathered)


def natural_row(at_slot, twelfth):
    return at_slot * 6 + twelfth + jnp.where(twelfth >= 6, 378, 0)


def index_kernel(place, columns):
    core, chip = place[0], place[1]

    def target_of(order, slot):
        first = slot * 0 + core == 0
        target = 0
        for axis, digit in zip(order, (slot >> 4, (slot >> 2) & 3, slot & 3)):
            step = STRIDE[axis]
            here = lax.rem(lax.div(chip, step), 4)
            other = jnp.where(
                first, jnp.where(digit == 1, 3, jnp.maximum(digit, 1) - 1), digit ^ (digit >> 1)
            )
            target = target + (here ^ other) * step
        return target

    def out_pick(at_slot, eight):
        return jnp.where(eight < 6, at_slot * 6 + eight, -1)

    at = lax.broadcasted_iota(jnp.int32, (512, 1), 0)
    eight = at & 7
    targets = [target_of(order, at >> 3) for order in ORDERS]
    values = []
    for target in targets:
        values += [natural_row(target, eight), natural_row(target, 8 + (eight & 3))]
    values += [out_pick(target, eight) for target in targets]
    values += [target * 8 + eight for target in targets] + [jnp.where(eight == 0, targets[2], -1)]
    for i in range(16):
        columns[:, i : i + 1] = values[i] if i < len(values) else at * 0


def indices(place):
    return staged(
        "indices",
        index_kernel,
        (place,),
        (),
        [shape((512, 16), jnp.int32)],
        1e6,
    )[0]


def image_pick_kernel(pick, tokens, *outs):
    for turn, out in enumerate(outs):
        out[...] = tokens[pick[turn]]


def image_pick(pick, tokens):
    return staged(
        "image_pick", image_pick_kernel, (pick,), (tokens,), [shape((188, 768), BF)] * 4, 1e6
    )


def image_stack_kernel(v0, v1, v2, v3, out, wide):
    wide[188:192] = jnp.zeros((4, 768), F32)
    for turn, value in enumerate((v0, v1, v2, v3)):
        wide[0:188] = value[...].astype(F32)
        out[192 * turn : 192 * turn + 192] = wide[...].astype(BF)


def image_stack(values):
    return staged(
        "image_stack",
        image_stack_kernel,
        (),
        values,
        [shape((768, 768), BF)],
        1e6,
        [pltpu.VMEM((192, 768), F32)],
    )[0]


def image_forward_kernel(vec, w_kv, own, other, kv, normed):
    row = lax.broadcasted_iota(jnp.int32, (192, 1), 0)
    for image in range(8):
        source, here = (own, 192 * image) if image < 4 else (other, 192 * image - 768)
        xhat, _ = normalize(source[here : here + 192].astype(F32))
        at = slice(192 * image, 192 * image + 192)
        normed[at] = jnp.where(row < 188, xhat * vec[2:3] + vec[6:7], 0.0).astype(BF)
        kv[at] = mm(normed[at], w_kv[...]).astype(BF)


def image_forward(vec, w_kv, own, other):
    return staged(
        "image_forward",
        image_forward_kernel,
        (),
        (vec, w_kv, own, other),
        (shape((1536, 768), BF), shape((1536, 768), BF)),
        2e9,
    )


def cross_forward_kernel(
    info, vec, text, mine, got, w_query, kv, w_out, after, normed, queries, mixed, part
):
    after[...] = text[...].astype(F32) + (mine[...] + got[...])
    xhat, _ = normalize(after[...])
    normed[...] = (xhat * vec[1:2] + vec[5:6]).astype(BF)
    queries[...] = mm(normed[...], w_query[...]).astype(BF)
    for row in range(2):
        allowed = cross_allowed(info, row)
        at = slice(128 * row, 128 * row + 128)
        for j in range(3):
            lanes = slice(128 * j, 128 * j + 128)
            q = stacked(queries[at, lanes]) * 0.125
            k = row_keys(kv, row, lanes)
            v = row_keys(kv, row, slice(384 + 128 * j, 512 + 128 * j))
            probs = softmax(mm_t(q, k), allowed)
            mixed[at, lanes] = merged(mm(probs.astype(BF), v)).astype(BF)
    part[...] = mm(mixed[...], w_out[...])


def cross_forward(info, vec, text, mine, got, kv, w_query, w_out):
    return staged(
        "cross_forward",
        cross_forward_kernel,
        (info,),
        (vec, text, mine, got, w_query, kv, w_out),
        (shape((256, 768), F32), shape((256, 768), BF), shape((256, 384), BF), shape((256, 384), BF), shape((256, 768), F32)),
        3e9,
    )


def feed_kernel(
    info, vec, b_up, before, mine, got, w_up, w_down, grad,
    after, normed, active, hidden_low, to_mine, to_other, back, sums,
    part,
):
    after[...] = before[...] + (mine[...] + got[...])
    xhat, _ = normalize(after[...])
    normed[...] = (xhat * vec[3:4] + vec[7:8]).astype(BF)
    part[...] = jnp.zeros((256, 768), F32)
    for k in range(3):
        lanes = slice(512 * k, 512 * k + 512)
        down = w_down[lanes]
        hidden = mm(normed[...], w_up[:, lanes]) + b_up[:, lanes]
        cdf = 0.5 * (1.0 + lax.erf(hidden * 0.7071067811865476))
        active[:, lanes] = (hidden * cdf).astype(BF)
        slope = cdf + hidden * (jnp.exp(-0.5 * hidden * hidden) * 0.3989422804014327)
        part[...] += mm(active[:, lanes], down)
        hidden_low[:, lanes] = (mm_t(grad[...], down) * slope).astype(BF)
    back[...] = mm_t(hidden_low[...], w_up[...])
    sums[...] = jnp.concatenate(
        [
            jnp.sum(back[...] * xhat, 0, keepdims=True),
            jnp.sum(back[...], 0, keepdims=True),
            jnp.zeros((6, 768), F32),
        ],
        0,
    )
    core = info[0]
    bias = vec[8:9]
    for row in range(2):
        at = pl.ds(pl.multiple_of(128 * row + 64 * core, 64), 64)
        to_mine[64 * row : 64 * row + 64] = after[at] + part[at] + bias
        at = pl.ds(pl.multiple_of(128 * row + 64 * (1 - core), 64), 64)
        to_other[64 * row : 64 * row + 64] = part[at]


def feed(info, vec, b_up, before, mine, got, w_up, w_down, grad):
    return staged(
        "feed",
        feed_kernel,
        (info,),
        (vec, b_up, before, mine, got, w_up, w_down, grad),
        (shape((256, 768), F32), shape((256, 768), BF), shape((256, 1536), BF), shape((256, 1536), BF), shape((128, 768), F32), shape((128, 768), F32), shape((256, 768), F32), shape((8, 768), F32)),
        3e9,
        [pltpu.VMEM((256, 768), F32)],
    )


def laid_out(weight, qa, qb, width):
    top = mm(qa, weight)
    rest = mm(qb, weight)
    n = weight.shape[1]
    upper = lax.broadcasted_iota(jnp.int32, (512, 1), 0) % 8 < 4
    tail = rest[:, width:]
    if n - width < width:
        tail = jnp.concatenate([tail, jnp.zeros((512, 2 * width - n), F32)], 1)
    return top, jnp.where(upper, rest[:, :width], tail)


def put(keep, send, lanes, value):
    keep[:, lanes] = value[:256].astype(BF)
    send[:, lanes] = value[256:].astype(BF)


def feed_grads_kernel(normed, active, hidden_low, grad, index, *outs):
    keeps, sends, up_rows = outs[0:3], outs[3:6], outs[6]
    d_up = t_mm(normed[...], hidden_low[...]).astype(BF)
    total = jnp.sum(hidden_low[...].astype(F32), 0, keepdims=True)
    of_chip = mm_t(jnp.where(own_lanes(), total, 0.0).astype(BF), lanes_of()).astype(BF)
    up_rows[...] = mm(placed(index, 12, 64), of_chip)
    for p in range(3):
        qa, qb = placed(index, 2 * p, 768), placed(index, 2 * p + 1, 768)
        top, rest = laid_out(d_up[:, 512 * p : 512 * p + 512], qa, qb, 256)
        put(keeps[p], sends[p], slice(0, 512), top)
        put(keeps[p], sends[p], slice(512, 768), rest)
    d_down = t_mm(active[...], grad[...]).reshape(64, 3, 8, 768)
    slabs = [placed(index, 9 + p, 512) for p in range(3)]
    for k in range(3):
        rows = d_down[:, k].reshape(512, 768).astype(BF)
        for p, slab in enumerate(slabs):
            moved = mm(slab, rows[:, 256 * p : 256 * p + 256])
            put(keeps[p], sends[p], slice(768 + 256 * k, 1024 + 256 * k), moved)


def feed_grads(normed, active, hidden_low, grad, index):
    return staged(
        "feed_grads",
        feed_grads_kernel,
        (),
        (normed, active, hidden_low, grad, index),
        (*[shape((256, 1536), BF)] * 6, shape((512, 128), F32)),
        6e9,
    )


def cross_backward_kernel(
    info, vec, grad, mine, got, after, w_out, queries, kv, w_query, before,
    stream, low, dq, dkv, back, sums,
):
    xhat, inv = normalize(after[...])
    step = norm_back(mine[...] + got[...], vec[3:4], xhat, inv)
    stream[...] = grad[...].astype(F32) + step
    low[...] = stream[...].astype(BF)
    mixed_grad = mm_t(low[...], w_out[...]).astype(BF)
    for row in range(2):
        allowed = cross_allowed(info, row)
        at = slice(128 * row, 128 * row + 128)
        for j in range(3):
            lanes = slice(128 * j, 128 * j + 128)
            value_lanes = slice(384 + 128 * j, 512 + 128 * j)
            q = stacked(queries[at, lanes]) * 0.125
            do = stacked(mixed_grad[at, lanes])
            k = row_keys(kv, row, lanes)
            v = row_keys(kv, row, value_lanes)
            probs = softmax(mm_t(q, k), allowed)
            ds = softmax_back(probs, mm_t(do, v))
            dq[at, lanes] = (merged(mm(ds, k)) * 0.125).astype(BF)
            dk = t_mm(ds, q).astype(BF)
            dv = t_mm(probs.astype(BF), do).astype(BF)
            for value, where in ((dk, lanes), (dv, value_lanes)):
                dkv[384 * row : 384 * row + 384, where] = value[:384]
                dkv[768 + 384 * row : 1152 + 384 * row, where] = value[384:]
    back[...] = mm_t(dq[...], w_query[...])
    xhat, _ = normalize(before[...])
    sums[...] = jnp.concatenate(
        [
            jnp.sum(back[...] * xhat, 0, keepdims=True),
            jnp.sum(back[...], 0, keepdims=True),
            jnp.zeros((6, 768), F32),
        ],
        0,
    )


def cross_backward(info, vec, grad, mine, got, after, w_out, queries, kv, w_query, before):
    return staged(
        "cross_backward",
        cross_backward_kernel,
        (info,),
        (vec, grad, mine, got, after, w_out, queries, kv, w_query, before),
        (shape((256, 768), F32), shape((256, 768), BF), shape((256, 384), BF), shape((1536, 768), BF), shape((256, 768), F32), shape((8, 768), F32)),
        5e9,
    )


def cross_grads_kernel(
    image_normed, dkv, normed, dq, mixed, low, index, *outs
):
    keeps, sends = outs[0:3], outs[3:6]
    d_kv = t_mm(image_normed[...], dkv[...]).astype(BF)
    d_query = t_mm(normed[...], dq[...]).astype(BF)
    pieces = (d_kv[:, :384], d_kv[:, 384:], d_query)
    d_out = t_mm(mixed[...], low[...]).astype(BF)
    for p in range(3):
        qa, qb = placed(index, 2 * p, 768), placed(index, 2 * p + 1, 768)
        o = placed(index, 6 + p, 384)
        top, rest = laid_out(pieces[p], qa, qb, 256)
        put(keeps[p], sends[p], slice(0, 384), top)
        put(keeps[p], sends[p], slice(384, 640), rest)
        put(keeps[p], sends[p], slice(640, 896), mm(o, d_out[:, 256 * p : 256 * p + 256]))


def cross_grads(image_normed, dkv, normed, dq, mixed, low, index):
    return staged(
        "cross_grads",
        cross_grads_kernel,
        (),
        (image_normed, dkv, normed, dq, mixed, low, index),
        (*[shape((256, 896), BF)] * 6,),
        4e9,
    )


def image_part_kernel(dkv, w_kv, out):
    out[...] = mm_t(dkv[768:], w_kv[...]).astype(BF)


def image_part(dkv, w_kv):
    return staged(
        "image_part",
        image_part_kernel,
        (),
        (dkv, w_kv),
        (shape((768, 768), BF),),
        1e9,
    )


def image_backward_kernel(vec, dkv, w_kv, got, own, out, low1, low2, low3, sums):
    total = [jnp.zeros((1, 768), F32)] * 2
    for image, result in enumerate((out, low1, low2, low3)):
        at = slice(192 * image, 192 * image + 192)
        dy = mm_t(dkv[at], w_kv[...]) + got[at].astype(F32)
        xhat, inv = normalize(own[at].astype(F32))
        total = [
            total[0] + jnp.sum(dy * xhat, 0, keepdims=True),
            total[1] + jnp.sum(dy, 0, keepdims=True),
        ]
        result[...] = norm_back(dy, vec[2:3], xhat, inv)[:188].astype(result.dtype)
    sums[...] = jnp.concatenate(total + [jnp.zeros((6, 768), F32)], 0)


def image_backward(vec, dkv, w_kv, got, own):
    return staged(
        "image_backward",
        image_backward_kernel,
        (),
        (vec, dkv, w_kv, got, own),
        (shape((188, 768), F32), *[shape((188, 768), BF)] * 3, shape((8, 768), F32)),
        1e9,
    )


def self_backward_kernel(
    info, vec, stream_in, mine, got, before, w_out, joined, w_qkv, text,
    stream_mine, low, d_joined, to_mine, to_other, sums,
    stream, back,
):
    xhat, inv = normalize(before[...])
    stream[...] = stream_in[...] + norm_back(mine[...] + got[...], vec[1:2], xhat, inv)
    low[...] = stream[...].astype(BF)
    mixed_grad = mm_t(low[...], w_out[...]).astype(BF)
    for row in range(2):
        allowed = self_allowed(info, row)
        at = slice(128 * row, 128 * row + 128)
        for j in range(3):
            lanes = [slice(384 * i + 128 * j, 384 * i + 128 * j + 128) for i in range(3)]
            q = stacked(joined[at, lanes[0]]) * 0.125
            k = joined[at, lanes[1]]
            v = joined[at, lanes[2]]
            do = stacked(mixed_grad[at, lanes[0]])
            probs = softmax(mm_t(q, k), allowed)
            ds = softmax_back(probs, mm_t(do, v))
            d_joined[at, lanes[0]] = (merged(mm(ds, k)) * 0.125).astype(BF)
            d_joined[at, lanes[1]] = t_mm(ds, q).astype(BF)
            d_joined[at, lanes[2]] = t_mm(probs.astype(BF), do).astype(BF)
    back[...] = mm_t(d_joined[...], w_qkv[...])
    xhat, _ = normalize(text[...].astype(F32))
    sums[...] = jnp.concatenate(
        [
            jnp.sum(back[...] * xhat, 0, keepdims=True),
            jnp.sum(back[...], 0, keepdims=True),
            jnp.zeros((6, 768), F32),
        ],
        0,
    )
    core = info[0]
    for row in range(2):
        at = pl.ds(pl.multiple_of(128 * row + 64 * core, 64), 64)
        stream_mine[64 * row : 64 * row + 64] = stream[at]
        to_mine[64 * row : 64 * row + 64] = back[at]
        at = pl.ds(pl.multiple_of(128 * row + 64 * (1 - core), 64), 64)
        to_other[64 * row : 64 * row + 64] = back[at]


def self_backward(info, vec, stream_in, mine, got, before, w_out, joined, w_qkv, text):
    return staged(
        "self_backward",
        self_backward_kernel,
        (info,),
        (vec, stream_in, mine, got, before, w_out, joined, w_qkv, text),
        (shape((128, 768), F32), shape((256, 768), BF), shape((256, 1152), BF), shape((128, 768), F32), shape((128, 768), F32), shape((8, 768), F32)),
        3e9,
        [pltpu.VMEM((256, 768), F32), pltpu.VMEM((256, 768), F32)],
    )


def self_grads_kernel(
    normed, d_joined, mixed, low, sum0, sum1, sum2, sum3, grad, up_rows,
    index, e0, e1, e2, *outs,
):
    keeps, sends = outs[0:3], outs[3:6]
    for send, early in zip(sends, (e0, e1, e2)):
        send[:, :896] = early[...]
    d_qkv = t_mm(normed[...], d_joined[...]).astype(BF)
    d_out = t_mm(mixed[...], low[...]).astype(BF)
    for p in range(3):
        qa, qb = placed(index, 2 * p, 768), placed(index, 2 * p + 1, 768)
        o = placed(index, 6 + p, 384)
        top, rest = laid_out(d_qkv[:, 384 * p : 384 * p + 384], qa, qb, 256)
        moved = mm(o, d_out[:, 256 * p : 256 * p + 256])
        for at, value in ((0, top), (384, rest), (640, moved)):
            n = value.shape[1]
            keeps[p][:, at : at + n] = value[:256].astype(BF)
            sends[p][:, 896 + at : 896 + at + n] = value[256:].astype(BF)
    down_sum = jnp.sum(grad[...].astype(F32), 0, keepdims=True) * 0.5
    rows = [s[i : i + 1] for i in range(2) for s in (sum0, sum1, sum2, sum3)]
    rows = jnp.concatenate(rows + [down_sum, jnp.zeros((7, 768), F32)], 0).astype(BF)
    zero = jnp.zeros((16, 768), BF)
    first = jnp.concatenate([rows] + [zero] * 7, 0)
    second = jnp.concatenate([zero, rows] + [zero] * 6, 0)
    value = mm_t(qa, first) + mm_t(qb, second) + up_rows[...]
    keeps[2][:, 896:1024] = value[:256].astype(BF)
    sends[2][:, 1792:1920] = value[256:].astype(BF)


def self_grads(normed, d_joined, mixed, low, sums, grad, up_rows, index, early):
    return staged(
        "self_grads",
        self_grads_kernel,
        (),
        (normed, d_joined, mixed, low, *sums, grad, up_rows, index, *early),
        (*[shape((256, n), BF) for n in (896, 896, 1024, 1792, 1792, 1920)],),
        3e9,
    )


def first_core(info, dims):
    return lax.broadcasted_iota(jnp.int32, dims, 0) * 0 + info[0] == 0


BLOCKS = ((0, 3, 384), (1, 2, 384), (2, 1, 384), (3, 1, 1536))


def halves_into(core, refs, target, sem):
    copies, here = [], 0
    for which, blocks, width in BLOCKS:
        for i in range(blocks):
            at = pl.multiple_of(2 * i * width + core * width, 128)
            copies.append(
                pltpu.make_async_copy(
                    refs[which].at[:, pl.ds(at, width)], target.at[:, pl.ds(here, width)],
                    sem.at[len(copies)],
                )
            )
            here += width
    return copies


def vector_rows(gain, bias, down_bias):
    total = jnp.zeros((6, 128), F32)
    for at, ref in ((0, gain), (4, bias), (8, down_bias)):
        n = ref.shape[0]
        i = lax.broadcasted_iota(jnp.int32, (n, 128), 0) + at
        j = lax.broadcasted_iota(jnp.int32, (n, 128), 1)
        total = total + t_mm(ref[...], ((i == j) | (i + 16 == j)).astype(F32).astype(BF))
    return total


def pack_swap_kernel(info, qkv, kv, query, up, gain, bias, down_bias, send, half, sem):
    copies = halves_into(1 - info[0], (qkv, kv, query, up), half, sem)
    for c in copies:
        c.start()
    send[:, 3840:] = vector_rows(gain, bias, down_bias).astype(BF)
    for c in copies:
        c.wait()
    send[:, :3840] = half[...]


def pack_slots_kernel(
    info, qkv, kv, query, up, self_out, cross_out, down, gain, bias, down_bias, up_bias, got,
    slot, twelve, half, outs, slabs, sem, sems,
):
    copies = halves_into(info[0], (qkv, kv, query, up), half, sem)
    others = [
        pltpu.make_async_copy(self_out, outs.at[0], sems.at[0]),
        pltpu.make_async_copy(cross_out, outs.at[1], sems.at[1]),
        pltpu.make_async_copy(down, slabs, sems.at[2]),
    ]
    for c in copies + others:
        c.start()
    first = first_core(info, (6, 128))
    mine = vector_rows(gain, bias, down_bias)
    other = got[:, 3840:].astype(F32)
    twelve[0:6, 4608:] = jnp.where(first, mine, other)
    twelve[6:12, 4608:] = jnp.where(first, other, mine)
    twelve[12:16, 4608:] = jnp.zeros((4, 128), F32)
    lane = lax.broadcasted_iota(jnp.int32, (8, 128), 1)
    row = lax.broadcasted_iota(jnp.int32, (8, 128), 0)
    vec = jnp.where(lane < 16, twelve[0:8, 4608:], 0.0)
    vec = vec + jnp.where((lane >= 16) & (lane < 32), twelve[8:16, 4608:], 0.0)
    i = lax.broadcasted_iota(jnp.int32, (24, 128), 0)
    j = lax.broadcasted_iota(jnp.int32, (24, 128), 1)
    units = mm(up_bias[...], (i + 64 == j).astype(F32).astype(BF))
    slot[:, 6912:7040] = (vec + jnp.where(row == 0, units, 0.0)).astype(BF)
    for c in copies:
        c.wait()
    first = first_core(info, (6, 3840))
    mine = half[...].astype(F32)
    other = got[:, :3840].astype(F32)
    twelve[0:6, :3840] = jnp.where(first, mine, other)
    twelve[6:12, :3840] = jnp.where(first, other, mine)
    for c in others:
        c.wait()
    twelve[0:6, 3840:4608] = outs[0].astype(F32)
    twelve[6:12, 3840:4608] = outs[1].astype(F32)
    slot[:, :4608] = twelve[0:8, :4608].astype(BF)
    twelve[0:4, :2304] = twelve[8:12, :2304]
    twelve[4:8, :2304] = twelve[8:12, 2304:4608]
    slot[:, 4608:6912] = twelve[0:8, :2304].astype(BF)
    wide = slabs[...].astype(F32)
    for k in range(3):
        at = 7040 + 768 * k
        slot[:, at : at + 768] = wide[8 * k : 8 * k + 8].astype(BF)


def packed(name, kernel, info, far, near, out, scratch):
    return pl.pallas_call(
        kernel,
        out_shape=out,
        in_specs=[SMEM] + [HBM] * len(far) + [VMEM] * len(near),
        out_specs=VMEM,
        scratch_shapes=scratch,
        compiler_params=params(60),
        cost_estimate=cost(1e6, 1e6),
        name=name,
    )(info, *far, *near)


def pack_swap(info, weights, vectors):
    return packed(
        "pack_swap",
        pack_swap_kernel,
        info,
        weights,
        vectors,
        shape((6, 3968), BF),
        [pltpu.VMEM((6, 3840), BF), pltpu.SemaphoreType.DMA((7,))],
    )


def pack_slots(info, weights, vectors, got, self_out, cross_out, down, up_bias):
    return packed(
        "pack_slots",
        pack_slots_kernel,
        info,
        (*weights, self_out, cross_out, down),
        (*vectors, up_bias, got),
        shape((8, 9344), BF),
        [
            pltpu.VMEM((16, 4736), F32),
            pltpu.VMEM((6, 3840), BF),
            pltpu.VMEM((2, 6, 768), BF),
            pltpu.VMEM((24, 768), BF),
            pltpu.SemaphoreType.DMA((7,)),
            pltpu.SemaphoreType.DMA((3,)),
        ],
    )


TWELVES = (
    [(0, 512, 256)] * 3 + [(1536, 384, 256)] * 3 + [(2432, 384, 256)] * 3
)


def finish_send_kernel(info, *refs):
    keeps, gots, (s0, s1, s2, send, own, twelve) = refs[:3], refs[3:6], refs[6:]
    sums = (s0, s1, s2)
    for p in range(3):
        sums[p][...] = keeps[p][...].astype(F32) + gots[p][...].astype(F32)
    here = 0
    for i, (at, n, width) in enumerate(TWELVES):
        ref = sums[i % 3]
        twelve[0:8, here : here + n] = ref[:, at : at + n]
        twelve[8:12, here : here + width] = ref[0:4, at + n : at + n + width]
        twelve[8:12, here + width : here + n] = ref[4:8, at + n : at + n + n - width]
        here += n
    vec = s2[:, 3328:]
    twelve[0:8, 3840:] = vec
    twelve[8:12, 3840:] = pltpu.roll(vec, 112, 1)[0:4]
    first = first_core(info, (6, 3968))
    send[...] = jnp.where(first, twelve[6:12], twelve[0:6])
    own[...] = jnp.where(first, twelve[0:6], twelve[6:12])


def finish_kernel(
    info, s0, s1, s2, own, got, qkv, out_self, query, kv, out_cross, up, down, gain, bias, down_bias
):
    sums = (s0, s1, s2)
    first = first_core(info, (6, 3840))
    low = jnp.where(first, own[:, :3840], got[:, :3840])
    high = jnp.where(first, got[:, :3840], own[:, :3840])
    for ref, begin, blocks, width in (
        (up, 0, 1, 1536), (kv, 1536, 2, 384), (query, 2304, 1, 384), (qkv, 2688, 3, 384),
    ):
        for i in range(blocks):
            at = begin + i * width
            ref[:, 2 * i * width : (2 * i + 1) * width] = low[:, at : at + width]
            ref[:, (2 * i + 1) * width : (2 * i + 2) * width] = high[:, at : at + width]
    for p in range(3):
        lanes = slice(256 * p, 256 * p + 256)
        out_self[:, lanes] = sums[p][0:6, 3072:3328]
        out_cross[:, lanes] = sums[p][0:6, 2176:2432]
        for k in range(3):
            at = 768 + 256 * k
            down[8 * k : 8 * k + 8, lanes] = sums[p][:, at : at + 256]
    total = jnp.concatenate([own[:, 3840:] + got[:, 3840:], jnp.zeros((122, 128), F32)], 0)
    across = jnp.transpose(total)
    gain[...] = across[0:4, 0:6]
    bias[...] = across[4:8, 0:6]
    down_bias[...] = across[8:9, 0:6]


def finish_send(info, keeps, gots):
    widths = [k.shape[1] for k in keeps]
    return staged(
        "finish_send",
        finish_send_kernel,
        (info,),
        (*keeps, *gots),
        [shape((8, n), F32) for n in widths] + [shape((6, 3968), F32)] * 2,
        1e6,
        [pltpu.VMEM((16, 3968), F32)],
        mib=8,
    )


def finish(info, sums, own, got):
    return staged(
        "finish",
        finish_kernel,
        (info,),
        (*sums, own, got),
        [
            shape(dims, F32)
            for dims in (
                (6, 2304), (6, 768), (6, 768), (6, 1536), (6, 768), (6, 3072), (24, 768), (4, 6), (4, 6),
                (1, 6),
            )
        ],
        1e6,
        mib=8,
    )


def text_finish_kernel(vec, text, stream, mine, got, out_mine, out_got, grad, out):
    xhat, inv = normalize(text[...].astype(F32))
    grad[...] = stream[...] + norm_back(mine[...] + got[...], vec[0:1], xhat, inv)
    out[...] = out_mine[...] + out_got[...]


def text_finish(vec, text, stream, mine, got, out_mine, out_got):
    return staged(
        "text_finish",
        text_finish_kernel,
        (),
        (vec, text, stream, mine, got, out_mine, out_got),
        [shape((128, 768), F32)] * 2,
        1e6,
        mib=8,
    )


def image_finish_kernel(pick, v0, v1, v2, v3, out):
    values = [v[...].astype(F32) for v in (v0, v1, v2, v3)]
    for image in range(4):
        total = values[3]
        for turn in range(3):
            total = jnp.where(pick[turn] == image, values[turn], total)
        out[:, image, :] = total


def image_finish(pick, values):
    out = staged(
        "image_finish",
        image_finish_kernel,
        (pick,),
        values,
        [shape((188, 4, 768), F32)],
        1e6,
    )[0]
    return jnp.transpose(out, (1, 0, 2))


def combine_kernel(plan, *refs):
    at = 0
    ins = []
    for keeps, gots in plan:
        ins.append((refs[at : at + len(keeps)], refs[at + len(keeps) : at + len(keeps) + len(gots)]))
        at += len(keeps) + len(gots)
    outs = refs[at:]
    for p, (keeps, gots) in enumerate(ins):
        here = 0
        edges = []
        for ref in keeps:
            edges.append((here, here + ref.shape[1], ref))
            here += ref.shape[1]
        here = 0
        for ref in gots:
            for low, high, keep in edges:
                a, b = max(low, here), min(high, here + ref.shape[1])
                if a >= b:
                    continue
                total = keep[:, a - low : b - low].astype(F32) + ref[:, a - here : b - here].astype(F32)
                half = total.shape[0] // 2
                outs[2 * p][:, a:b] = total[:half].astype(BF)
                outs[2 * p + 1][:, a:b] = total[half:].astype(BF)
            here += ref.shape[1]


def combine(parts):
    plan, args, outs = [], [], []
    for keeps, gots in parts:
        plan.append(([k.shape[1] for k in keeps], [g.shape[1] for g in gots]))
        args += [*keeps, *gots]
        rows, width = keeps[0].shape[0], sum(k.shape[1] for k in keeps)
        outs += [shape((rows // 2, width), BF)] * 2
    got = staged(
        "combine", lambda *refs: combine_kernel(plan, *refs), (), args, outs, 1e6
    )
    return [(got[2 * p], got[2 * p + 1]) for p in range(len(parts))]


def send_step(step, values, parts=(0, 1, 2)):
    v0, v1 = ((1, 3), (3, 1))[step % 2]
    return [
        lax.ppermute(v, BOTH, xor_pairs(ORDERS[p][step // 2], v0, v1)) for v, p in zip(values, parts)
    ]


def after(value, *others):
    return lax.optimization_barrier((value, *others))[0]


def on_device(
    text_input,
    image_tokens,
    output_grad,
    segment_starts,
    caption_image,
    image_counts,
    norm_gain,
    norm_bias,
    self_qkv,
    self_out,
    cross_q,
    cross_kv,
    cross_out,
    up_weight,
    up_bias,
    down_weight,
    down_bias,
):
    core = lax.axis_index("seq")
    chip = lax.axis_index("batch")
    first = core == 0

    def ordered(own, other, axis):
        return jnp.where(
            first, jnp.concatenate([own, other], axis), jnp.concatenate([other, own], axis)
        )

    place = jnp.stack([core, chip]).astype(jnp.int32)
    weights = (self_qkv, cross_kv, cross_q, up_weight)
    vectors = (norm_gain, norm_bias, down_bias[None])
    got = swap(pack_swap(place, weights, vectors))
    slot = pack_slots(
        place, weights, vectors, got, self_out, cross_out, down_weight, up_bias[None]
    )
    gathered = lax.all_gather(slot, "batch", axis=0, tiled=True)

    late_text, late_grad = after(text_input, slot), after(output_grad, slot)
    text = ordered(late_text, swap(late_text), 1).reshape(256, 768)
    grad = ordered(late_grad, swap(late_grad), 1).reshape(256, 768)

    group_images = after(caption_image, slot).reshape(64, 8)
    my_captions = lax.dynamic_index_in_dim(group_images, chip, 0, keepdims=False)
    limits = jnp.take(image_counts, my_captions).reshape(4, 2)
    limits = jnp.where(first, jnp.concatenate([limits[:, 0], limits[:, 1]]), jnp.concatenate([limits[:, 1], limits[:, 0]]))
    turns = jnp.arange(4)
    targets = (chip - turns * 16) % 64
    wanted = group_images[targets, 2 * turns + core]
    local_pick = wanted - (core * 64 + chip) * 4
    outgoing = image_pick(after(local_pick, slot), image_tokens)
    received = [outgoing[0]]
    for turn in range(1, 4):
        route = [(i, (i - 16 * turn) % 64) for i in range(64)]
        received.append(lax.ppermute(outgoing[turn], "batch", route))
    own_images = image_stack(received)
    other_images = swap(own_images)
    info = jnp.concatenate(
        [core[None], segment_starts.reshape(8), limits, jnp.zeros((15,), jnp.int32)]
    ).astype(jnp.int32)

    column_index = indices(after(place, slot))

    gathered, info, grad, text, column_index, own_images, other_images = lax.optimization_barrier(
        (gathered, info, grad, text, column_index, own_images, other_images)
    )
    w_qkv, w_kv, w_query, w_up, w_self, w_cross, w_down, vec, b_up = unpack(gathered)
    part, joined, mixed_self, normed_one = self_forward(info, vec, w_qkv, w_self, text)
    got = swap(part)
    kv, image_normed = image_forward(vec, w_kv, own_images, other_images)
    after_self, normed_two, q_cross, mixed_cross, part = cross_forward(
        info, vec, text, part, got, kv, w_query, w_cross
    )
    after_cross, normed_three, active, hidden_low, text_mine, text_other, part, sum3 = feed(
        info, vec, b_up, after_self, part, swap(part), w_up, w_down, grad
    )
    text_got = swap(text_other)
    got = swap(part)

    grads = feed_grads(normed_three, active, hidden_low, grad, column_index)
    keep_one, up_rows = grads[0:3], grads[6]
    got_one = send_step(0, grads[3:6])
    stream_two, cross_low, dq, dkv, part, sum1 = cross_backward(
        info, vec, after(grad, keep_one[0]), part, got, after_cross, w_cross, q_cross, kv, w_query, after_self
    )
    got = swap(part)
    image_send = image_part(dkv, w_kv)[0]
    *rows_back, sum2 = image_backward(vec, dkv, w_kv, swap(image_send), own_images)
    returned = [rows_back[0]]
    for turn in range(1, 4):
        route = [(i, (i + 16 * turn) % 64) for i in range(64)]
        returned.append(lax.ppermute(rows_back[turn], "batch", route))
    grads = cross_grads(
        image_normed, dkv, normed_two, after(dq, sum2), mixed_cross, cross_low, column_index
    )
    keep_two, early = grads[0:3], grads[3:6]
    stream_one, self_low, d_joined, one_mine, one_other, sum0 = self_backward(
        info, vec, after(stream_two, keep_two[0]), part, got, after_self, w_self, joined,
        w_qkv, text,
    )
    self_low, *late = lax.optimization_barrier((self_low, *returned[1:], *got_one))
    returned, got_one = returned[:1] + late[:3], late[3:]
    grads = self_grads(
        normed_one, d_joined, mixed_self, self_low, (sum0, sum1, sum2, sum3), grad, up_rows,
        column_index, early,
    )
    keep_three = grads[0:3]
    got_two = send_step(0, grads[3:6])
    one_got = swap(one_other)
    image_grad = image_finish(after(local_pick, grads[3]), returned)
    text_grad, text_output = text_finish(
        after(vec, grads[3]), text_input.reshape(128, 768), stream_one, one_mine, one_got, text_mine,
        text_got,
    )
    got_two, image_grad, text_grad = lax.optimization_barrier((got_two, image_grad, text_grad))
    pairs = []
    for p in range(3):
        pairs += combine([([keep_one[p], keep_two[p], keep_three[p]], [got_one[p], got_two[p]])])
    for step in range(1, 6):
        got_step = send_step(step, [s for _, s in pairs])
        step_parts = [([k], [g]) for (k, _), g in zip(pairs, got_step)]
        if step == 5:
            *sums, send, own = finish_send(place, [k for k, _ in pairs], got_step)
        elif step == 1:
            pairs = [combine([one])[0] for one in step_parts]
        else:
            pairs = combine(step_parts)

    text_grad, text_output = text_grad.reshape(2, 64, 768), text_output.reshape(2, 64, 768)

    (
        qkv_grad, self_grad, query_grad, kv_grad, cross_grad, up_grad, down_grad, gain_grad, bias_grad,
        down_bias_grad,
    ) = finish(place, sums, own, swap(send))
    up_bias_grad = sums[2][0, 3392:3416]
    return (
        text_output,
        text_grad,
        image_grad,
        gain_grad,
        bias_grad,
        qkv_grad,
        self_grad,
        query_grad,
        kv_grad,
        cross_grad,
        up_grad,
        up_bias_grad,
        down_grad,
        down_bias_grad[0],
    )


def solution(mesh):
    rows = P("batch", "seq", None)
    shard = P(BOTH, None)
    wide = P(None, BOTH)
    return jax.shard_map(
        on_device,
        mesh=mesh,
        in_specs=(
            rows, P(BOTH, None, None), rows, P("batch", None), P(), P(), wide, wide,
            shard, shard, shard, shard, shard, shard, P(BOTH), shard, P(BOTH),
        ),
        out_specs=(
            rows, rows, P(BOTH, None, None), wide, wide,
            shard, shard, shard, shard, shard, shard, P(BOTH), shard, P(BOTH),
        ),
        check_vma=False,
    )
```

```python
import math

import jax
import jax.numpy as jnp
from jax import lax
from jax.experimental import pallas as pl
from jax.experimental.pallas import tpu as pltpu
from jax.sharding import PartitionSpec as P

HEADS = 12
HEAD_DIM = 64
EPSILON = 1e-05
MASKED_SCORE = -1e30
BF = jnp.bfloat16
F32 = jnp.float32
BOTH = ("seq", "batch")
STRIDE = {"z": 16, "y": 4, "x": 1}
ORDERS = (("x", "z", "y"), ("y", "x", "z"), ("z", "y", "x"))


def xor_pairs(axis, value0, value1):
    step, out = STRIDE[axis], []
    for core, value in ((0, value0), (1, value1)):
        for chip in range(64):
            at = chip // step % 4
            out.append((core * 64 + chip, core * 64 + chip + ((at ^ value) - at) * step))
    return out


def swap(value):
    return lax.ppermute(value, "seq", [(0, 1), (1, 0)])


def mm(a, b):
    return jnp.dot(a, b, preferred_element_type=F32)


def mm_t(a, b):
    return lax.dot_general(a, b, (((1,), (1,)), ((), ())), preferred_element_type=F32)


def t_mm(a, b):
    return lax.dot_general(a, b, (((0,), (0,)), ((), ())), preferred_element_type=F32)


def normalize(values):
    center = jnp.mean(values, -1, keepdims=True)
    centred = values - center
    spread = jnp.mean(centred * centred, -1, keepdims=True)
    inv = lax.rsqrt(spread + EPSILON)
    return centred * inv, inv


def norm_back(grad, gain, xhat, inv):
    scaled = grad * gain
    return inv * (
        scaled
        - jnp.mean(scaled, -1, keepdims=True)
        - xhat * jnp.mean(scaled * xhat, -1, keepdims=True)
    )


VMEM = pl.BlockSpec(memory_space=pltpu.VMEM)
SMEM = pl.BlockSpec(memory_space=pltpu.SMEM)
HBM = pl.BlockSpec(memory_space=pltpu.HBM)


def shape(dims, dtype):
    return jax.ShapeDtypeStruct(dims, dtype)


def cost(flops, moved):
    return pl.CostEstimate(
        flops=int(flops / 64), bytes_accessed=int(moved / 64), transcendentals=0
    )


def params(mib):
    return pltpu.CompilerParams(vmem_limit_bytes=mib * 1024 * 1024)


def staged(name, kernel, scalars, ins, outs, work, scratch=(), mib=16):
    moved = sum(math.prod(v.shape) * v.dtype.itemsize for v in (*ins, *outs))
    return pl.pallas_call(
        kernel,
        out_shape=tuple(outs),
        in_specs=[SMEM] * len(scalars) + [VMEM] * len(ins),
        out_specs=(VMEM,) * len(outs),
        scratch_shapes=list(scratch),
        compiler_params=params(mib),
        cost_estimate=cost(work, moved),
        name=name,
    )(*scalars, *ins)


def placed(columns, i, size):
    place = lax.broadcasted_iota(jnp.int32, (512, size), 1)
    return (place == columns[:, i : i + 1]).astype(F32).astype(BF)


def segment_of(info, row, dims, axis):
    place = lax.broadcasted_iota(jnp.int32, dims, axis)
    total = jnp.full(dims, -1, jnp.int32)
    for j in range(4):
        total = total + (place >= info[1 + 4 * row + j]).astype(jnp.int32)
    return total


def low_lanes():
    return lax.broadcasted_iota(jnp.int32, (1, 128), 1) < 64


def stacked(pair):
    left = low_lanes()
    zero = jnp.zeros_like(pair)
    return jnp.concatenate([jnp.where(left, pair, zero), jnp.where(left, zero, pair)], 0)


def merged(two):
    n = two.shape[0] // 2
    return jnp.where(low_lanes(), two[:n], two[n:])


def softmax(scores, allowed):
    scores = jnp.where(allowed, scores, MASKED_SCORE)
    weights = jnp.exp(scores - jnp.max(scores, -1, keepdims=True))
    return weights * (1.0 / jnp.sum(weights, -1, keepdims=True))


def softmax_back(probs, dprobs):
    return (probs * (dprobs - jnp.sum(probs * dprobs, -1, keepdims=True))).astype(BF)


def self_allowed(info, row):
    at = segment_of(info, row, (128, 128), 0)
    key = segment_of(info, row, (128, 128), 1)
    i = lax.broadcasted_iota(jnp.int32, (128, 128), 0)
    j = lax.broadcasted_iota(jnp.int32, (128, 128), 1)
    allowed = (at == key) & (j <= i)
    return jnp.concatenate([allowed, allowed], 0)


def cross_allowed(info, row):
    core = info[0]
    lane = lax.broadcasted_iota(jnp.int32, (1, 768), 1)
    key = jnp.full((1, 768), -1, jnp.int32)
    images = (2 * row, 2 * row + 1, 4 + 2 * row, 5 + 2 * row)
    captions = (core, 2 + core, 1 - core, 3 - core)
    for block in range(4):
        limit = info[9 + images[block]]
        key = jnp.where(
            (lane >= 192 * block) & (lane < 192 * block + limit), captions[block], key
        )
    at = segment_of(info, row, (128, 1), 0)
    return jnp.concatenate([at, at], 0) == key


def row_keys(kv, row, lanes):
    return jnp.concatenate(
        [kv[384 * row : 384 * row + 384, lanes], kv[768 + 384 * row : 1152 + 384 * row, lanes]], 0
    )


def lanes_of():
    lane = lax.broadcasted_iota(jnp.int32, (128, 1536), 0)
    unit = lax.broadcasted_iota(jnp.int32, (128, 1536), 1)
    return (lane == 64 + lax.rem(unit, 24)).astype(F32).astype(BF)


def own_lanes():
    chip = lax.broadcasted_iota(jnp.int32, (64, 1536), 0) * 24
    unit = lax.broadcasted_iota(jnp.int32, (64, 1536), 1)
    return (unit >= chip) & (unit < chip + 24)


def self_forward_kernel(info, vec, w_qkv, w_out, text, part, joined, mixed, normed):
    xhat, _ = normalize(text[...].astype(F32))
    normed[...] = (xhat * vec[0:1] + vec[4:5]).astype(BF)
    joined[...] = mm(normed[...], w_qkv[...]).astype(BF)
    for row in range(2):
        allowed = self_allowed(info, row)
        at = slice(128 * row, 128 * row + 128)
        for j in range(3):
            q = stacked(joined[at, 128 * j : 128 * j + 128]) * 0.125
            k = joined[at, 384 + 128 * j : 512 + 128 * j]
            v = joined[at, 768 + 128 * j : 896 + 128 * j]
            probs = softmax(mm_t(q, k), allowed)
            mixed[at, 128 * j : 128 * j + 128] = merged(mm(probs.astype(BF), v)).astype(BF)
    part[...] = mm(mixed[...], w_out[...])


def self_forward(info, vec, w_qkv, w_out, text):
    return staged(
        "self_forward",
        self_forward_kernel,
        (info,),
        (vec, w_qkv, w_out, text),
        (
            shape((256, 768), F32),
            shape((256, 1152), BF),
            shape((256, 384), BF),
            shape((256, 768), BF),
        ),
        2e9,
    )


def rows_of_six(first, last, shift):
    row = lax.broadcasted_iota(jnp.int32, (192, 256), 0)
    place = lax.broadcasted_iota(jnp.int32, (192, 256), 1)
    chip = lax.div(row, 6)
    r = row - 6 * chip
    hit = (place == 8 * chip + r + shift) & (r >= first) & (r <= last)
    return hit.astype(F32).astype(BF)


def unpack_kernel(
    gathered, w_qkv, w_kv, w_query, w_up, w_self, w_cross, w_down, vec, b_up, g, sems
):
    spans = ((4608, 1152), (0, 1152), (6912, 2432), (5760, 1152), (1152, 1152), (2304, 2304))
    loads = [
        pltpu.make_async_copy(gathered.at[:, pl.ds(at, n)], g.at[:, pl.ds(at, n)], sems.at[i])
        for i, (at, n) in enumerate(spans)
    ]
    loads[0].start()
    loads[1].start()
    low, high = rows_of_six(0, 5, 0), rows_of_six(0, 1, 6)
    left, right = rows_of_six(2, 5, -2), rows_of_six(2, 5, 2)

    def natural(at, n, begin, rest, outs):
        for half in range(2):
            here = slice(256 * half, 256 * half + 256)
            there = slice(192 * half, 192 * half + 192)
            a = g[here, at : at + n]
            outs[0][there] = mm(low, a).astype(BF)
            there = slice(outs[2] + 192 * half, outs[2] + 192 * half + 192)
            outs[1][there] = (mm(high, a) + mm(rest, g[here, begin : begin + n])).astype(BF)

    loads[0].wait()
    loads[1].wait()
    for i in (2, 3, 4):
        loads[i].start()
    natural(0, 1152, 4608, left, (w_qkv, w_qkv, 384))
    loads[2].wait()
    loads[5].start()
    tail = g[:, 6912:7040]
    lane = lax.broadcasted_iota(jnp.int32, (1, 128), 1)
    one = jnp.where(lane < 16, tail.astype(F32), 0.0).astype(BF)
    two = jnp.where((lane >= 16) & (lane < 32), tail.astype(F32), 0.0).astype(BF)
    halves = [slice(0, 256), slice(256, 512)]
    rows = [mm(low, one[h]) for h in halves]
    rows += [mm(high, one[h]) + mm(left, two[h]) for h in halves]
    across = jnp.transpose(jnp.concatenate(rows, 0))
    vec[...] = across[:16] + across[16:32]
    chip = lax.broadcasted_iota(jnp.int32, (64, 512), 0)
    place = lax.broadcasted_iota(jnp.int32, (64, 512), 1)
    of_chip = mm((place == 8 * chip).astype(F32).astype(BF), tail).astype(BF)
    b_up[...] = jnp.sum(jnp.where(own_lanes(), mm(of_chip, lanes_of()), 0.0), 0, keepdims=True)
    slabs = [
        g[:, 7040 + 768 * k : 7808 + 768 * k].astype(F32).reshape(64, 1, 8, 768) for k in range(3)
    ]
    w_down[...] = jnp.concatenate(slabs, 1).reshape(1536, 768).astype(BF)
    loads[3].wait()
    loads[4].wait()
    natural(1152, 768, 5760, left, (w_kv, w_kv, 384))
    natural(1920, 384, 6528, left, (w_query, w_query, 384))
    loads[5].wait()
    natural(2304, 1536, 4608, right, (w_up, w_up, 384))
    natural(3840, 768, 6144, right, (w_self, w_cross, 0))


def unpack(gathered):
    outs = ((768, 1152), (768, 768), (768, 384), (768, 1536), (384, 768), (384, 768), (1536, 768))
    return pl.pallas_call(
        unpack_kernel,
        out_shape=(
            *[shape(o, BF) for o in outs],
            shape((16, 768), F32),
            shape((1, 1536), F32),
        ),
        in_specs=[HBM],
        out_specs=(VMEM,) * 9,
        scratch_shapes=[pltpu.VMEM((512, 9344), BF), pltpu.SemaphoreType.DMA((6,))],
        compiler_params=params(46),
        cost_estimate=cost(4e9, 20e6),
        name="unpack",
    )(gathered)


def natural_row(at_slot, twelfth):
    return at_slot * 6 + twelfth + jnp.where(twelfth >= 6, 378, 0)


def index_kernel(place, columns):
    core, chip = place[0], place[1]

    def target_of(order, slot):
        first = slot * 0 + core == 0
        target = 0
        for axis, digit in zip(order, (slot >> 4, (slot >> 2) & 3, slot & 3)):
            step = STRIDE[axis]
            here = lax.rem(lax.div(chip, step), 4)
            other = jnp.where(
                first, jnp.where(digit == 1, 3, jnp.maximum(digit, 1) - 1), digit ^ (digit >> 1)
            )
            target = target + (here ^ other) * step
        return target

    def out_pick(at_slot, eight):
        return jnp.where(eight < 6, at_slot * 6 + eight, -1)

    at = lax.broadcasted_iota(jnp.int32, (512, 1), 0)
    eight = at & 7
    targets = [target_of(order, at >> 3) for order in ORDERS]
    values = []
    for target in targets:
        values += [natural_row(target, eight), natural_row(target, 8 + (eight & 3)) - 384]
    values += [out_pick(target, eight) for target in targets]
    values += [target * 8 + eight for target in targets] + [jnp.where(eight == 0, targets[2], -1)]
    for i in range(16):
        columns[:, i : i + 1] = values[i] if i < len(values) else at * 0


def indices(place):
    return staged(
        "indices",
        index_kernel,
        (place,),
        (),
        [shape((512, 16), jnp.int32)],
        1e6,
    )[0]


def image_pick_kernel(pick, tokens, *outs):
    for turn, out in enumerate(outs):
        out[...] = tokens[pick[turn]]


def image_pick(pick, tokens):
    return staged(
        "image_pick", image_pick_kernel, (pick,), (tokens,), [shape((188, 768), BF)] * 4, 1e6
    )


def image_stack_kernel(v0, v1, v2, v3, out, wide):
    wide[188:192] = jnp.zeros((4, 768), F32)
    for turn, value in enumerate((v0, v1, v2, v3)):
        wide[0:188] = value[...].astype(F32)
        out[192 * turn : 192 * turn + 192] = wide[...].astype(BF)


def image_stack(values):
    return staged(
        "image_stack",
        image_stack_kernel,
        (),
        values,
        [shape((768, 768), BF)],
        1e6,
        [pltpu.VMEM((192, 768), F32)],
    )[0]


def image_forward_kernel(vec, w_kv, own, other, kv, normed):
    row = lax.broadcasted_iota(jnp.int32, (192, 1), 0)
    for image in range(8):
        source, here = (own, 192 * image) if image < 4 else (other, 192 * image - 768)
        xhat, _ = normalize(source[here : here + 192].astype(F32))
        at = slice(192 * image, 192 * image + 192)
        normed[at] = jnp.where(row < 188, xhat * vec[2:3] + vec[6:7], 0.0).astype(BF)
        kv[at] = mm(normed[at], w_kv[...]).astype(BF)


def image_forward(vec, w_kv, own, other):
    return staged(
        "image_forward",
        image_forward_kernel,
        (),
        (vec, w_kv, own, other),
        (shape((1536, 768), BF), shape((1536, 768), BF)),
        2e9,
    )


def cross_forward_kernel(
    info, vec, text, mine, got, w_query, kv, w_out, after, normed, queries, mixed, part
):
    after[...] = text[...].astype(F32) + (mine[...] + got[...])
    xhat, _ = normalize(after[...])
    normed[...] = (xhat * vec[1:2] + vec[5:6]).astype(BF)
    queries[...] = mm(normed[...], w_query[...]).astype(BF)
    for row in range(2):
        allowed = cross_allowed(info, row)
        at = slice(128 * row, 128 * row + 128)
        for j in range(3):
            lanes = slice(128 * j, 128 * j + 128)
            q = stacked(queries[at, lanes]) * 0.125
            k = row_keys(kv, row, lanes)
            v = row_keys(kv, row, slice(384 + 128 * j, 512 + 128 * j))
            probs = softmax(mm_t(q, k), allowed)
            mixed[at, lanes] = merged(mm(probs.astype(BF), v)).astype(BF)
    part[...] = mm(mixed[...], w_out[...])


def cross_forward(info, vec, text, mine, got, kv, w_query, w_out):
    return staged(
        "cross_forward",
        cross_forward_kernel,
        (info,),
        (vec, text, mine, got, w_query, kv, w_out),
        (shape((256, 768), F32), shape((256, 768), BF), shape((256, 384), BF), shape((256, 384), BF), shape((256, 768), F32)),
        3e9,
    )


def feed_kernel(
    info, vec, b_up, before, mine, got, w_up, w_down, grad,
    after, normed, active, hidden_low, to_mine, to_other, back, sums,
    part,
):
    after[...] = before[...] + (mine[...] + got[...])
    xhat, _ = normalize(after[...])
    normed[...] = (xhat * vec[3:4] + vec[7:8]).astype(BF)
    part[...] = jnp.zeros((256, 768), F32)
    for k in range(3):
        lanes = slice(512 * k, 512 * k + 512)
        down = w_down[lanes]
        hidden = mm(normed[...], w_up[:, lanes]) + b_up[:, lanes]
        cdf = 0.5 * (1.0 + lax.erf(hidden * 0.7071067811865476))
        active[:, lanes] = (hidden * cdf).astype(BF)
        slope = cdf + hidden * (jnp.exp(-0.5 * hidden * hidden) * 0.3989422804014327)
        part[...] += mm(active[:, lanes], down)
        hidden_low[:, lanes] = (mm_t(grad[...], down) * slope).astype(BF)
    back[...] = mm_t(hidden_low[...], w_up[...])
    sums[...] = jnp.concatenate(
        [
            jnp.sum(back[...] * xhat, 0, keepdims=True),
            jnp.sum(back[...], 0, keepdims=True),
            jnp.zeros((6, 768), F32),
        ],
        0,
    )
    core = info[0]
    bias = vec[8:9]
    for row in range(2):
        at = pl.ds(pl.multiple_of(128 * row + 64 * core, 64), 64)
        to_mine[64 * row : 64 * row + 64] = after[at] + part[at] + bias
        at = pl.ds(pl.multiple_of(128 * row + 64 * (1 - core), 64), 64)
        to_other[64 * row : 64 * row + 64] = part[at]


def feed(info, vec, b_up, before, mine, got, w_up, w_down, grad):
    return staged(
        "feed",
        feed_kernel,
        (info,),
        (vec, b_up, before, mine, got, w_up, w_down, grad),
        (shape((256, 768), F32), shape((256, 768), BF), shape((256, 1536), BF), shape((256, 1536), BF), shape((128, 768), F32), shape((128, 768), F32), shape((256, 768), F32), shape((8, 768), F32)),
        3e9,
        [pltpu.VMEM((256, 768), F32)],
    )


def laid_out(weight, qa, qb, width):
    top = mm(qa, weight)
    rest = mm(qb, weight[384:])
    n = weight.shape[1]
    upper = lax.broadcasted_iota(jnp.int32, (512, 1), 0) % 8 < 4
    tail = rest[:, width:]
    if n - width < width:
        tail = jnp.concatenate([tail, jnp.zeros((512, 2 * width - n), F32)], 1)
    return top, jnp.where(upper, rest[:, :width], tail)


def put(keep, send, lanes, value):
    keep[:, lanes] = value[:256].astype(BF)
    send[:, lanes] = value[256:].astype(BF)


def feed_grads_kernel(normed, active, hidden_low, grad, index, *outs):
    keeps, sends, up_rows = outs[0:3], outs[3:6], outs[6]
    d_up = t_mm(normed[...], hidden_low[...]).astype(BF)
    total = jnp.sum(hidden_low[...].astype(F32), 0, keepdims=True)
    of_chip = mm_t(jnp.where(own_lanes(), total, 0.0).astype(BF), lanes_of()).astype(BF)
    up_rows[...] = mm(placed(index, 12, 64), of_chip)
    for p in range(3):
        qa, qb = placed(index, 2 * p, 768), placed(index, 2 * p + 1, 384)
        top, rest = laid_out(d_up[:, 512 * p : 512 * p + 512], qa, qb, 256)
        put(keeps[p], sends[p], slice(0, 512), top)
        put(keeps[p], sends[p], slice(512, 768), rest)
    d_down = t_mm(active[...], grad[...]).reshape(64, 3, 8, 768)
    slabs = [placed(index, 9 + p, 512) for p in range(3)]
    for k in range(3):
        rows = d_down[:, k].reshape(512, 768).astype(BF)
        for p, slab in enumerate(slabs):
            moved = mm(slab, rows[:, 256 * p : 256 * p + 256])
            put(keeps[p], sends[p], slice(768 + 256 * k, 1024 + 256 * k), moved)


def feed_grads(normed, active, hidden_low, grad, index):
    return staged(
        "feed_grads",
        feed_grads_kernel,
        (),
        (normed, active, hidden_low, grad, index),
        (*[shape((256, 1536), BF)] * 6, shape((512, 128), F32)),
        6e9,
    )


def cross_backward_kernel(
    info, vec, grad, mine, got, after, w_out, queries, kv, w_query, before,
    stream, low, dq, dkv, back, sums,
):
    xhat, inv = normalize(after[...])
    step = norm_back(mine[...] + got[...], vec[3:4], xhat, inv)
    stream[...] = grad[...].astype(F32) + step
    low[...] = stream[...].astype(BF)
    mixed_grad = mm_t(low[...], w_out[...]).astype(BF)
    for row in range(2):
        allowed = cross_allowed(info, row)
        at = slice(128 * row, 128 * row + 128)
        for j in range(3):
            lanes = slice(128 * j, 128 * j + 128)
            value_lanes = slice(384 + 128 * j, 512 + 128 * j)
            q = stacked(queries[at, lanes]) * 0.125
            do = stacked(mixed_grad[at, lanes])
            k = row_keys(kv, row, lanes)
            v = row_keys(kv, row, value_lanes)
            probs = softmax(mm_t(q, k), allowed)
            ds = softmax_back(probs, mm_t(do, v))
            dq[at, lanes] = (merged(mm(ds, k)) * 0.125).astype(BF)
            dk = t_mm(ds, q).astype(BF)
            dv = t_mm(probs.astype(BF), do).astype(BF)
            for value, where in ((dk, lanes), (dv, value_lanes)):
                dkv[384 * row : 384 * row + 384, where] = value[:384]
                dkv[768 + 384 * row : 1152 + 384 * row, where] = value[384:]
    back[...] = mm_t(dq[...], w_query[...])
    xhat, _ = normalize(before[...])
    sums[...] = jnp.concatenate(
        [
            jnp.sum(back[...] * xhat, 0, keepdims=True),
            jnp.sum(back[...], 0, keepdims=True),
            jnp.zeros((6, 768), F32),
        ],
        0,
    )


def cross_backward(info, vec, grad, mine, got, after, w_out, queries, kv, w_query, before):
    return staged(
        "cross_backward",
        cross_backward_kernel,
        (info,),
        (vec, grad, mine, got, after, w_out, queries, kv, w_query, before),
        (shape((256, 768), F32), shape((256, 768), BF), shape((256, 384), BF), shape((1536, 768), BF), shape((256, 768), F32), shape((8, 768), F32)),
        5e9,
    )


def cross_part(p, weight, mixed, low, index, keep, send):
    qa, qb = placed(index, 2 * p, 768), placed(index, 2 * p + 1, 384)
    top, rest = laid_out(weight, qa, qb, 256)
    put(keep, send, slice(0, 384), top)
    put(keep, send, slice(384, 640), rest)
    d_out = t_mm(mixed[...], low[:, 256 * p : 256 * p + 256]).astype(BF)
    put(keep, send, slice(640, 896), mm(placed(index, 6 + p, 384), d_out))


def image_grads_kernel(image_normed, dkv, mixed, low, index, keep0, keep1, send0, send1):
    d_kv = t_mm(image_normed[...], dkv[...]).astype(BF)
    cross_part(0, d_kv[:, :384], mixed, low, index, keep0, send0)
    cross_part(1, d_kv[:, 384:], mixed, low, index, keep1, send1)


def image_grads(image_normed, dkv, mixed, low, index):
    return staged(
        "image_grads",
        image_grads_kernel,
        (),
        (image_normed, dkv, mixed, low, index),
        [shape((256, 896), BF)] * 4,
        4e9,
    )


def query_grads_kernel(normed, dq, mixed, low, index, keep, send):
    d_query = t_mm(normed[...], dq[...]).astype(BF)
    cross_part(2, d_query, mixed, low, index, keep, send)


def query_grads(normed, dq, mixed, low, index):
    return staged(
        "query_grads",
        query_grads_kernel,
        (),
        (normed, dq, mixed, low, index),
        [shape((256, 896), BF)] * 2,
        1e9,
    )


def image_part_kernel(dkv, w_kv, out):
    out[...] = mm_t(dkv[768:], w_kv[...]).astype(BF)


def image_part(dkv, w_kv):
    return staged(
        "image_part",
        image_part_kernel,
        (),
        (dkv, w_kv),
        (shape((768, 768), BF),),
        1e9,
    )


def image_backward_kernel(vec, dkv, w_kv, got, own, out, low1, low2, low3, sums):
    total = [jnp.zeros((1, 768), F32)] * 2
    for image, result in enumerate((out, low1, low2, low3)):
        at = slice(192 * image, 192 * image + 192)
        dy = mm_t(dkv[at], w_kv[...]) + got[at].astype(F32)
        xhat, inv = normalize(own[at].astype(F32))
        total = [
            total[0] + jnp.sum(dy * xhat, 0, keepdims=True),
            total[1] + jnp.sum(dy, 0, keepdims=True),
        ]
        result[...] = norm_back(dy, vec[2:3], xhat, inv)[:188].astype(result.dtype)
    sums[...] = jnp.concatenate(total + [jnp.zeros((6, 768), F32)], 0)


def image_backward(vec, dkv, w_kv, got, own):
    return staged(
        "image_backward",
        image_backward_kernel,
        (),
        (vec, dkv, w_kv, got, own),
        (shape((188, 768), F32), *[shape((188, 768), BF)] * 3, shape((8, 768), F32)),
        1e9,
    )


def self_backward_kernel(
    info, vec, stream_in, mine, got, before, w_out, joined, w_qkv, text,
    stream_mine, low, d_joined, to_mine, to_other, sums,
    stream, back,
):
    xhat, inv = normalize(before[...])
    stream[...] = stream_in[...] + norm_back(mine[...] + got[...], vec[1:2], xhat, inv)
    low[...] = stream[...].astype(BF)
    mixed_grad = mm_t(low[...], w_out[...]).astype(BF)
    for row in range(2):
        allowed = self_allowed(info, row)
        at = slice(128 * row, 128 * row + 128)
        for j in range(3):
            lanes = [slice(384 * i + 128 * j, 384 * i + 128 * j + 128) for i in range(3)]
            q = stacked(joined[at, lanes[0]]) * 0.125
            k = joined[at, lanes[1]]
            v = joined[at, lanes[2]]
            do = stacked(mixed_grad[at, lanes[0]])
            probs = softmax(mm_t(q, k), allowed)
            ds = softmax_back(probs, mm_t(do, v))
            d_joined[at, lanes[0]] = (merged(mm(ds, k)) * 0.125).astype(BF)
            d_joined[at, lanes[1]] = t_mm(ds, q).astype(BF)
            d_joined[at, lanes[2]] = t_mm(probs.astype(BF), do).astype(BF)
    back[...] = mm_t(d_joined[...], w_qkv[...])
    xhat, _ = normalize(text[...].astype(F32))
    sums[...] = jnp.concatenate(
        [
            jnp.sum(back[...] * xhat, 0, keepdims=True),
            jnp.sum(back[...], 0, keepdims=True),
            jnp.zeros((6, 768), F32),
        ],
        0,
    )
    core = info[0]
    for row in range(2):
        at = pl.ds(pl.multiple_of(128 * row + 64 * core, 64), 64)
        stream_mine[64 * row : 64 * row + 64] = stream[at]
        to_mine[64 * row : 64 * row + 64] = back[at]
        at = pl.ds(pl.multiple_of(128 * row + 64 * (1 - core), 64), 64)
        to_other[64 * row : 64 * row + 64] = back[at]


def self_backward(info, vec, stream_in, mine, got, before, w_out, joined, w_qkv, text):
    return staged(
        "self_backward",
        self_backward_kernel,
        (info,),
        (vec, stream_in, mine, got, before, w_out, joined, w_qkv, text),
        (shape((128, 768), F32), shape((256, 768), BF), shape((256, 1152), BF), shape((128, 768), F32), shape((128, 768), F32), shape((8, 768), F32)),
        3e9,
        [pltpu.VMEM((256, 768), F32), pltpu.VMEM((256, 768), F32)],
    )


def self_grads_kernel(
    normed, d_joined, mixed, low, sum0, sum1, sum2, sum3, grad, up_rows,
    index, e0, e1, e2, *outs,
):
    keeps, sends = outs[0:3], outs[3:6]
    for send, early in zip(sends, (e0, e1, e2)):
        send[:, :896] = early[...]
    d_qkv = t_mm(normed[...], d_joined[...]).astype(BF)
    d_out = t_mm(mixed[...], low[...]).astype(BF)
    for p in range(3):
        qa, qb = placed(index, 2 * p, 768), placed(index, 2 * p + 1, 384)
        o = placed(index, 6 + p, 384)
        top, rest = laid_out(d_qkv[:, 384 * p : 384 * p + 384], qa, qb, 256)
        moved = mm(o, d_out[:, 256 * p : 256 * p + 256])
        for at, value in ((0, top), (384, rest), (640, moved)):
            n = value.shape[1]
            keeps[p][:, at : at + n] = value[:256].astype(BF)
            sends[p][:, 896 + at : 896 + at + n] = value[256:].astype(BF)
    down_sum = jnp.sum(grad[...].astype(F32), 0, keepdims=True) * 0.5
    rows = [s[i : i + 1] for i in range(2) for s in (sum0, sum1, sum2, sum3)]
    rows = jnp.concatenate(rows + [down_sum, jnp.zeros((7, 768), F32)], 0).astype(BF)
    zero = jnp.zeros((16, 768), BF)
    first = jnp.concatenate([rows] + [zero] * 7, 0)
    second = jnp.concatenate([zero, rows] + [zero] * 6, 0)
    value = mm_t(qa, first) + mm_t(qb, second[:, 384:]) + up_rows[...]
    keeps[2][:, 896:1024] = value[:256].astype(BF)
    sends[2][:, 1792:1920] = value[256:].astype(BF)


def self_grads(normed, d_joined, mixed, low, sums, grad, up_rows, index, early):
    return staged(
        "self_grads",
        self_grads_kernel,
        (),
        (normed, d_joined, mixed, low, *sums, grad, up_rows, index, *early),
        (*[shape((256, n), BF) for n in (896, 896, 1024, 1792, 1792, 1920)],),
        3e9,
    )


def first_core(info, dims):
    return lax.broadcasted_iota(jnp.int32, dims, 0) * 0 + info[0] == 0


BLOCKS = ((0, 3, 384), (1, 2, 384), (2, 1, 384), (3, 1, 1536))


def halves_into(core, refs, target, sem):
    copies, here = [], 0
    for which, blocks, width in BLOCKS:
        for i in range(blocks):
            at = pl.multiple_of(2 * i * width + core * width, 128)
            copies.append(
                pltpu.make_async_copy(
                    refs[which].at[:, pl.ds(at, width)], target.at[:, pl.ds(here, width)],
                    sem.at[len(copies)],
                )
            )
            here += width
    return copies


def vector_rows(gain, bias, down_bias):
    total = jnp.zeros((6, 128), F32)
    for at, ref in ((0, gain), (4, bias), (8, down_bias)):
        n = ref.shape[0]
        i = lax.broadcasted_iota(jnp.int32, (n, 128), 0) + at
        j = lax.broadcasted_iota(jnp.int32, (n, 128), 1)
        total = total + t_mm(ref[...], ((i == j) | (i + 16 == j)).astype(F32).astype(BF))
    return total


def pack_swap_kernel(info, qkv, kv, query, up, gain, bias, down_bias, send, half, sem):
    copies = halves_into(1 - info[0], (qkv, kv, query, up), half, sem)
    for c in copies:
        c.start()
    send[:, 3840:] = vector_rows(gain, bias, down_bias).astype(BF)
    for c in copies:
        c.wait()
    send[:, :3840] = half[...]


def pack_slots_kernel(
    info, qkv, kv, query, up, self_out, cross_out, down, gain, bias, down_bias, up_bias, got,
    slot, twelve, half, outs, slabs, sem, sems,
):
    copies = halves_into(info[0], (qkv, kv, query, up), half, sem)
    others = [
        pltpu.make_async_copy(self_out, outs.at[0], sems.at[0]),
        pltpu.make_async_copy(cross_out, outs.at[1], sems.at[1]),
        pltpu.make_async_copy(down, slabs, sems.at[2]),
    ]
    for c in copies + others:
        c.start()
    first = first_core(info, (6, 128))
    mine = vector_rows(gain, bias, down_bias)
    other = got[:, 3840:].astype(F32)
    twelve[0:6, 4608:] = jnp.where(first, mine, other)
    twelve[6:12, 4608:] = jnp.where(first, other, mine)
    twelve[12:16, 4608:] = jnp.zeros((4, 128), F32)
    lane = lax.broadcasted_iota(jnp.int32, (8, 128), 1)
    row = lax.broadcasted_iota(jnp.int32, (8, 128), 0)
    vec = jnp.where(lane < 16, twelve[0:8, 4608:], 0.0)
    vec = vec + jnp.where((lane >= 16) & (lane < 32), twelve[8:16, 4608:], 0.0)
    i = lax.broadcasted_iota(jnp.int32, (24, 128), 0)
    j = lax.broadcasted_iota(jnp.int32, (24, 128), 1)
    units = mm(up_bias[...], (i + 64 == j).astype(F32).astype(BF))
    slot[:, 6912:7040] = (vec + jnp.where(row == 0, units, 0.0)).astype(BF)
    for c in copies:
        c.wait()
    first = first_core(info, (6, 3840))
    mine = half[...].astype(F32)
    other = got[:, :3840].astype(F32)
    twelve[0:6, :3840] = jnp.where(first, mine, other)
    twelve[6:12, :3840] = jnp.where(first, other, mine)
    for c in others:
        c.wait()
    twelve[0:6, 3840:4608] = outs[0].astype(F32)
    twelve[6:12, 3840:4608] = outs[1].astype(F32)
    slot[:, :4608] = twelve[0:8, :4608].astype(BF)
    twelve[0:4, :2304] = twelve[8:12, :2304]
    twelve[4:8, :2304] = twelve[8:12, 2304:4608]
    slot[:, 4608:6912] = twelve[0:8, :2304].astype(BF)
    wide = slabs[...].astype(F32)
    for k in range(3):
        at = 7040 + 768 * k
        slot[:, at : at + 768] = wide[8 * k : 8 * k + 8].astype(BF)


def packed(name, kernel, info, far, near, out, scratch):
    return pl.pallas_call(
        kernel,
        out_shape=out,
        in_specs=[SMEM] + [HBM] * len(far) + [VMEM] * len(near),
        out_specs=VMEM,
        scratch_shapes=scratch,
        compiler_params=params(60),
        cost_estimate=cost(1e6, 1e6),
        name=name,
    )(info, *far, *near)


def pack_swap(info, weights, vectors):
    return packed(
        "pack_swap",
        pack_swap_kernel,
        info,
        weights,
        vectors,
        shape((6, 3968), BF),
        [pltpu.VMEM((6, 3840), BF), pltpu.SemaphoreType.DMA((7,))],
    )


def pack_slots(info, weights, vectors, got, self_out, cross_out, down, up_bias):
    return packed(
        "pack_slots",
        pack_slots_kernel,
        info,
        (*weights, self_out, cross_out, down),
        (*vectors, up_bias, got),
        shape((8, 9344), BF),
        [
            pltpu.VMEM((16, 4736), F32),
            pltpu.VMEM((6, 3840), BF),
            pltpu.VMEM((2, 6, 768), BF),
            pltpu.VMEM((24, 768), BF),
            pltpu.SemaphoreType.DMA((7,)),
            pltpu.SemaphoreType.DMA((3,)),
        ],
    )


TWELVES = (
    [(0, 512, 256)] * 3 + [(1536, 384, 256)] * 3 + [(2432, 384, 256)] * 3
)


def finish_send_kernel(info, *refs):
    keeps, gots, (s0, s1, s2, send, own, twelve) = refs[:3], refs[3:6], refs[6:]
    sums = (s0, s1, s2)
    for p in range(3):
        sums[p][...] = keeps[p][...].astype(F32) + gots[p][...].astype(F32)
    here = 0
    for i, (at, n, width) in enumerate(TWELVES):
        ref = sums[i % 3]
        twelve[0:8, here : here + n] = ref[:, at : at + n]
        twelve[8:12, here : here + width] = ref[0:4, at + n : at + n + width]
        twelve[8:12, here + width : here + n] = ref[4:8, at + n : at + n + n - width]
        here += n
    vec = s2[:, 3328:]
    twelve[0:8, 3840:] = vec
    twelve[8:12, 3840:] = pltpu.roll(vec, 112, 1)[0:4]
    first = first_core(info, (6, 3968))
    send[...] = jnp.where(first, twelve[6:12], twelve[0:6])
    own[...] = jnp.where(first, twelve[0:6], twelve[6:12])


def finish_kernel(
    info, s0, s1, s2, own, got, qkv, out_self, query, kv, out_cross, up, down, gain, bias, down_bias
):
    sums = (s0, s1, s2)
    first = first_core(info, (6, 3840))
    low = jnp.where(first, own[:, :3840], got[:, :3840])
    high = jnp.where(first, got[:, :3840], own[:, :3840])
    for ref, begin, blocks, width in (
        (up, 0, 1, 1536), (kv, 1536, 2, 384), (query, 2304, 1, 384), (qkv, 2688, 3, 384),
    ):
        for i in range(blocks):
            at = begin + i * width
            ref[:, 2 * i * width : (2 * i + 1) * width] = low[:, at : at + width]
            ref[:, (2 * i + 1) * width : (2 * i + 2) * width] = high[:, at : at + width]
    for p in range(3):
        lanes = slice(256 * p, 256 * p + 256)
        out_self[:, lanes] = sums[p][0:6, 3072:3328]
        out_cross[:, lanes] = sums[p][0:6, 2176:2432]
        for k in range(3):
            at = 768 + 256 * k
            down[8 * k : 8 * k + 8, lanes] = sums[p][:, at : at + 256]
    total = jnp.concatenate([own[:, 3840:] + got[:, 3840:], jnp.zeros((122, 128), F32)], 0)
    across = jnp.transpose(total)
    gain[...] = across[0:4, 0:6]
    bias[...] = across[4:8, 0:6]
    down_bias[...] = across[8:9, 0:6]


def finish_send(info, keeps, gots):
    widths = [k.shape[1] for k in keeps]
    return staged(
        "finish_send",
        finish_send_kernel,
        (info,),
        (*keeps, *gots),
        [shape((8, n), F32) for n in widths] + [shape((6, 3968), F32)] * 2,
        1e6,
        [pltpu.VMEM((16, 3968), F32)],
        mib=8,
    )


def finish(info, sums, own, got):
    return staged(
        "finish",
        finish_kernel,
        (info,),
        (*sums, own, got),
        [
            shape(dims, F32)
            for dims in (
                (6, 2304), (6, 768), (6, 768), (6, 1536), (6, 768), (6, 3072), (24, 768), (4, 6), (4, 6),
                (1, 6),
            )
        ],
        1e6,
        mib=8,
    )


def text_finish_kernel(vec, text, stream, mine, got, out_mine, out_got, grad, out):
    xhat, inv = normalize(text[...].astype(F32))
    grad[...] = stream[...] + norm_back(mine[...] + got[...], vec[0:1], xhat, inv)
    out[...] = out_mine[...] + out_got[...]


def text_finish(vec, text, stream, mine, got, out_mine, out_got):
    return staged(
        "text_finish",
        text_finish_kernel,
        (),
        (vec, text, stream, mine, got, out_mine, out_got),
        [shape((128, 768), F32)] * 2,
        1e6,
        mib=8,
    )


def image_finish_kernel(pick, v0, v1, v2, v3, out):
    values = [v[...].astype(F32) for v in (v0, v1, v2, v3)]
    for image in range(4):
        total = values[3]
        for turn in range(3):
            total = jnp.where(pick[turn] == image, values[turn], total)
        out[:, image, :] = total


def image_finish(pick, values):
    out = staged(
        "image_finish",
        image_finish_kernel,
        (pick,),
        values,
        [shape((188, 4, 768), F32)],
        1e6,
    )[0]
    return jnp.transpose(out, (1, 0, 2))


def combine_kernel(plan, *refs):
    at = 0
    ins = []
    for keeps, gots in plan:
        ins.append((refs[at : at + len(keeps)], refs[at + len(keeps) : at + len(keeps) + len(gots)]))
        at += len(keeps) + len(gots)
    outs = refs[at:]
    for p, (keeps, gots) in enumerate(ins):
        here = 0
        edges = []
        for ref in keeps:
            edges.append((here, here + ref.shape[1], ref))
            here += ref.shape[1]
        here = 0
        for ref in gots:
            for low, high, keep in edges:
                a, b = max(low, here), min(high, here + ref.shape[1])
                if a >= b:
                    continue
                total = keep[:, a - low : b - low].astype(F32) + ref[:, a - here : b - here].astype(F32)
                half = total.shape[0] // 2
                outs[2 * p][:, a:b] = total[:half].astype(BF)
                outs[2 * p + 1][:, a:b] = total[half:].astype(BF)
            here += ref.shape[1]


def combine(parts):
    plan, args, outs = [], [], []
    for keeps, gots in parts:
        plan.append(([k.shape[1] for k in keeps], [g.shape[1] for g in gots]))
        args += [*keeps, *gots]
        rows, width = keeps[0].shape[0], sum(k.shape[1] for k in keeps)
        outs += [shape((rows // 2, width), BF)] * 2
    got = staged(
        "combine", lambda *refs: combine_kernel(plan, *refs), (), args, outs, 1e6
    )
    return [(got[2 * p], got[2 * p + 1]) for p in range(len(parts))]


def send_step(step, values, parts=(0, 1, 2)):
    v0, v1 = ((1, 3), (3, 1))[step % 2]
    return [
        lax.ppermute(v, BOTH, xor_pairs(ORDERS[p][step // 2], v0, v1)) for v, p in zip(values, parts)
    ]


def after(value, *others):
    return lax.optimization_barrier((value, *others))[0]


def on_device(
    text_input,
    image_tokens,
    output_grad,
    segment_starts,
    caption_image,
    image_counts,
    norm_gain,
    norm_bias,
    self_qkv,
    self_out,
    cross_q,
    cross_kv,
    cross_out,
    up_weight,
    up_bias,
    down_weight,
    down_bias,
):
    core = lax.axis_index("seq")
    chip = lax.axis_index("batch")
    first = core == 0

    def ordered(own, other, axis):
        return jnp.where(
            first, jnp.concatenate([own, other], axis), jnp.concatenate([other, own], axis)
        )

    place = jnp.stack([core, chip]).astype(jnp.int32)
    weights = (self_qkv, cross_kv, cross_q, up_weight)
    vectors = (norm_gain, norm_bias, down_bias[None])
    got = swap(pack_swap(place, weights, vectors))
    slot = pack_slots(
        place, weights, vectors, got, self_out, cross_out, down_weight, up_bias[None]
    )
    gathered = lax.all_gather(slot, "batch", axis=0, tiled=True)

    late_text, late_grad = after(text_input, slot), after(output_grad, slot)
    text = ordered(late_text, swap(late_text), 1).reshape(256, 768)
    grad = ordered(late_grad, swap(late_grad), 1).reshape(256, 768)

    group_images = after(caption_image, slot).reshape(64, 8)
    my_captions = lax.dynamic_index_in_dim(group_images, chip, 0, keepdims=False)
    limits = jnp.take(image_counts, my_captions).reshape(4, 2)
    limits = jnp.where(first, jnp.concatenate([limits[:, 0], limits[:, 1]]), jnp.concatenate([limits[:, 1], limits[:, 0]]))
    turns = jnp.arange(4)
    targets = (chip - turns * 16) % 64
    wanted = group_images[targets, 2 * turns + core]
    local_pick = wanted - (core * 64 + chip) * 4
    outgoing = image_pick(after(local_pick, slot), image_tokens)
    received = [outgoing[0]]
    for turn in range(1, 4):
        route = [(i, (i - 16 * turn) % 64) for i in range(64)]
        received.append(lax.ppermute(outgoing[turn], "batch", route))
    own_images = image_stack(received)
    other_images = swap(own_images)
    info = jnp.concatenate(
        [core[None], segment_starts.reshape(8), limits, jnp.zeros((15,), jnp.int32)]
    ).astype(jnp.int32)

    column_index = indices(after(place, slot))

    gathered, info, grad, text, column_index, own_images, other_images = lax.optimization_barrier(
        (gathered, info, grad, text, column_index, own_images, other_images)
    )
    w_qkv, w_kv, w_query, w_up, w_self, w_cross, w_down, vec, b_up = unpack(gathered)
    part, joined, mixed_self, normed_one = self_forward(info, vec, w_qkv, w_self, text)
    got = swap(part)
    kv, image_normed = image_forward(vec, w_kv, own_images, other_images)
    after_self, normed_two, q_cross, mixed_cross, part = cross_forward(
        info, vec, text, part, got, kv, w_query, w_cross
    )
    after_cross, normed_three, active, hidden_low, text_mine, text_other, part, sum3 = feed(
        info, vec, b_up, after_self, part, swap(part), w_up, w_down, grad
    )
    text_got = swap(text_other)
    got = swap(part)

    grads = feed_grads(normed_three, active, hidden_low, grad, column_index)
    keep_one, up_rows = grads[0:3], grads[6]
    got_one = send_step(0, grads[3:6])
    stream_two, cross_low, dq, dkv, part, sum1 = cross_backward(
        info, vec, after(grad, keep_one[0]), part, got, after_cross, w_cross, q_cross, kv, w_query, after_self
    )
    got = swap(part)
    image_send = image_part(dkv, w_kv)[0]
    image_got = swap(image_send)
    k_keep, v_keep, k_send, v_send = image_grads(
        image_normed, after(dkv, image_send), mixed_cross, cross_low, column_index
    )
    *rows_back, sum2 = image_backward(vec, dkv, w_kv, after(image_got, k_keep), own_images)
    returned = [rows_back[0]]
    for turn in range(1, 4):
        route = [(i, (i + 16 * turn) % 64) for i in range(64)]
        returned.append(lax.ppermute(rows_back[turn], "batch", route))
    q_keep, q_send = query_grads(
        normed_two, after(dq, sum2), mixed_cross, cross_low, column_index
    )
    keep_two, early = [k_keep, v_keep, q_keep], [k_send, v_send, q_send]
    stream_one, self_low, d_joined, one_mine, one_other, sum0 = self_backward(
        info, vec, after(stream_two, q_keep), part, got, after_self, w_self, joined,
        w_qkv, text,
    )
    self_low, *late = lax.optimization_barrier((self_low, *returned[1:], *got_one))
    returned, got_one = returned[:1] + late[:3], late[3:]
    grads = self_grads(
        normed_one, d_joined, mixed_self, self_low, (sum0, sum1, sum2, sum3), grad, up_rows,
        column_index, early,
    )
    keep_three = grads[0:3]
    got_two = send_step(0, grads[3:6])
    one_got = swap(one_other)
    image_grad = image_finish(after(local_pick, grads[3]), returned)
    text_grad, text_output = text_finish(
        after(vec, grads[3]), text_input.reshape(128, 768), stream_one, one_mine, one_got, text_mine,
        text_got,
    )
    got_two, image_grad, text_grad = lax.optimization_barrier((got_two, image_grad, text_grad))
    pairs = []
    for p in range(3):
        pairs += combine([([keep_one[p], keep_two[p], keep_three[p]], [got_one[p], got_two[p]])])
    for step in range(1, 6):
        got_step = send_step(step, [s for _, s in pairs])
        step_parts = [([k], [g]) for (k, _), g in zip(pairs, got_step)]
        if step == 5:
            *sums, send, own = finish_send(place, [k for k, _ in pairs], got_step)
        elif step == 1:
            pairs = [combine([one])[0] for one in step_parts]
        else:
            pairs = combine(step_parts)

    text_grad, text_output = text_grad.reshape(2, 64, 768), text_output.reshape(2, 64, 768)

    (
        qkv_grad, self_grad, query_grad, kv_grad, cross_grad, up_grad, down_grad, gain_grad, bias_grad,
        down_bias_grad,
    ) = finish(place, sums, own, swap(send))
    up_bias_grad = sums[2][0, 3392:3416]
    return (
        text_output,
        text_grad,
        image_grad,
        gain_grad,
        bias_grad,
        qkv_grad,
        self_grad,
        query_grad,
        kv_grad,
        cross_grad,
        up_grad,
        up_bias_grad,
        down_grad,
        down_bias_grad[0],
    )


def solution(mesh):
    rows = P("batch", "seq", None)
    shard = P(BOTH, None)
    wide = P(None, BOTH)
    return jax.shard_map(
        on_device,
        mesh=mesh,
        in_specs=(
            rows, P(BOTH, None, None), rows, P("batch", None), P(), P(), wide, wide,
            shard, shard, shard, shard, shard, shard, P(BOTH), shard, P(BOTH),
        ),
        out_specs=(
            rows, rows, P(BOTH, None, None), wide, wide,
            shard, shard, shard, shard, shard, shard, P(BOTH), shard, P(BOTH),
        ),
        check_vma=False,
    )
```

```python
import math

import jax
import jax.numpy as jnp
from jax import lax
from jax.experimental import pallas as pl
from jax.experimental.pallas import tpu as pltpu
from jax.sharding import PartitionSpec as P

HEADS = 12
HEAD_DIM = 64
EPSILON = 1e-05
MASKED_SCORE = -1e30
BF = jnp.bfloat16
F32 = jnp.float32
BOTH = ("seq", "batch")
STRIDE = {"z": 16, "y": 4, "x": 1}
ORDERS = (("x", "z", "y"), ("y", "x", "z"), ("z", "y", "x"))


def xor_pairs(axis, value0, value1):
    step, out = STRIDE[axis], []
    for core, value in ((0, value0), (1, value1)):
        for chip in range(64):
            at = chip // step % 4
            out.append((core * 64 + chip, core * 64 + chip + ((at ^ value) - at) * step))
    return out


def swap(value):
    return lax.ppermute(value, "seq", [(0, 1), (1, 0)])


def mm(a, b):
    return jnp.dot(a, b, preferred_element_type=F32)


def mm_t(a, b):
    return lax.dot_general(a, b, (((1,), (1,)), ((), ())), preferred_element_type=F32)


def t_mm(a, b):
    return lax.dot_general(a, b, (((0,), (0,)), ((), ())), preferred_element_type=F32)


def normalize(values):
    center = jnp.mean(values, -1, keepdims=True)
    centred = values - center
    spread = jnp.mean(centred * centred, -1, keepdims=True)
    inv = lax.rsqrt(spread + EPSILON)
    return centred * inv, inv


def norm_back(grad, gain, xhat, inv):
    scaled = grad * gain
    return inv * (
        scaled
        - jnp.mean(scaled, -1, keepdims=True)
        - xhat * jnp.mean(scaled * xhat, -1, keepdims=True)
    )


VMEM = pl.BlockSpec(memory_space=pltpu.VMEM)
SMEM = pl.BlockSpec(memory_space=pltpu.SMEM)
HBM = pl.BlockSpec(memory_space=pltpu.HBM)


def shape(dims, dtype):
    return jax.ShapeDtypeStruct(dims, dtype)


def cost(flops, moved):
    return pl.CostEstimate(
        flops=int(flops / 64), bytes_accessed=int(moved / 64), transcendentals=0
    )


def params(mib):
    return pltpu.CompilerParams(vmem_limit_bytes=mib * 1024 * 1024)


def staged(name, kernel, scalars, ins, outs, work, scratch=(), mib=16):
    moved = sum(math.prod(v.shape) * v.dtype.itemsize for v in (*ins, *outs))
    return pl.pallas_call(
        kernel,
        out_shape=tuple(outs),
        in_specs=[SMEM] * len(scalars) + [VMEM] * len(ins),
        out_specs=(VMEM,) * len(outs),
        scratch_shapes=list(scratch),
        compiler_params=params(mib),
        cost_estimate=cost(work, moved),
        name=name,
    )(*scalars, *ins)


def placed(columns, i, size):
    place = lax.broadcasted_iota(jnp.int32, (512, size), 1)
    return (place == columns[:, i : i + 1]).astype(F32).astype(BF)


def segment_of(info, row, dims, axis):
    place = lax.broadcasted_iota(jnp.int32, dims, axis)
    total = jnp.full(dims, -1, jnp.int32)
    for j in range(4):
        total = total + (place >= info[1 + 4 * row + j]).astype(jnp.int32)
    return total


def low_lanes():
    return lax.broadcasted_iota(jnp.int32, (1, 128), 1) < 64


def stacked(pair):
    left = low_lanes()
    zero = jnp.zeros_like(pair)
    return jnp.concatenate([jnp.where(left, pair, zero), jnp.where(left, zero, pair)], 0)


def merged(two):
    n = two.shape[0] // 2
    return jnp.where(low_lanes(), two[:n], two[n:])


def softmax(scores, allowed):
    scores = jnp.where(allowed, scores, MASKED_SCORE)
    weights = jnp.exp(scores - jnp.max(scores, -1, keepdims=True))
    return weights * (1.0 / jnp.sum(weights, -1, keepdims=True))


def softmax_back(probs, dprobs):
    return (probs * (dprobs - jnp.sum(probs * dprobs, -1, keepdims=True))).astype(BF)


def self_allowed(info, row):
    at = segment_of(info, row, (128, 128), 0)
    key = segment_of(info, row, (128, 128), 1)
    i = lax.broadcasted_iota(jnp.int32, (128, 128), 0)
    j = lax.broadcasted_iota(jnp.int32, (128, 128), 1)
    allowed = (at == key) & (j <= i)
    return jnp.concatenate([allowed, allowed], 0)


def cross_allowed(info, row):
    core = info[0]
    lane = lax.broadcasted_iota(jnp.int32, (1, 768), 1)
    key = jnp.full((1, 768), -1, jnp.int32)
    images = (2 * row, 2 * row + 1, 4 + 2 * row, 5 + 2 * row)
    captions = (core, 2 + core, 1 - core, 3 - core)
    for block in range(4):
        limit = info[9 + images[block]]
        key = jnp.where(
            (lane >= 192 * block) & (lane < 192 * block + limit), captions[block], key
        )
    at = segment_of(info, row, (128, 1), 0)
    return jnp.concatenate([at, at], 0) == key


def row_keys(kv, row, lanes):
    return jnp.concatenate(
        [kv[384 * row : 384 * row + 384, lanes], kv[768 + 384 * row : 1152 + 384 * row, lanes]], 0
    )


def lanes_of():
    lane = lax.broadcasted_iota(jnp.int32, (128, 1536), 0)
    unit = lax.broadcasted_iota(jnp.int32, (128, 1536), 1)
    return (lane == 64 + lax.rem(unit, 24)).astype(F32).astype(BF)


def own_lanes():
    chip = lax.broadcasted_iota(jnp.int32, (64, 1536), 0) * 24
    unit = lax.broadcasted_iota(jnp.int32, (64, 1536), 1)
    return (unit >= chip) & (unit < chip + 24)


def self_forward_kernel(info, vec, w_qkv, w_out, text, part, joined, mixed, normed):
    xhat, _ = normalize(text[...].astype(F32))
    normed[...] = (xhat * vec[0:1] + vec[4:5]).astype(BF)
    joined[...] = mm(normed[...], w_qkv[...]).astype(BF)
    for row in range(2):
        allowed = self_allowed(info, row)
        at = slice(128 * row, 128 * row + 128)
        for j in range(3):
            q = stacked(joined[at, 128 * j : 128 * j + 128]) * 0.125
            k = joined[at, 384 + 128 * j : 512 + 128 * j]
            v = joined[at, 768 + 128 * j : 896 + 128 * j]
            probs = softmax(mm_t(q, k), allowed)
            mixed[at, 128 * j : 128 * j + 128] = merged(mm(probs.astype(BF), v)).astype(BF)
    part[...] = mm(mixed[...], w_out[...])


def self_forward(info, vec, w_qkv, w_out, text):
    return staged(
        "self_forward",
        self_forward_kernel,
        (info,),
        (vec, w_qkv, w_out, text),
        (
            shape((256, 768), F32),
            shape((256, 1152), BF),
            shape((256, 384), BF),
            shape((256, 768), BF),
        ),
        2e9,
    )


def rows_of_six(first, last, shift):
    row = lax.broadcasted_iota(jnp.int32, (192, 256), 0)
    place = lax.broadcasted_iota(jnp.int32, (192, 256), 1)
    chip = lax.div(row, 6)
    r = row - 6 * chip
    hit = (place == 8 * chip + r + shift) & (r >= first) & (r <= last)
    return hit.astype(F32).astype(BF)


def unpack_kernel(
    gathered, w_qkv, w_kv, w_query, w_up, w_self, w_cross, w_down, vec, b_up, g, sems
):
    spans = ((4608, 1152), (0, 1152), (6912, 2432), (5760, 1152), (1152, 1152), (2304, 2304))
    loads = [
        pltpu.make_async_copy(gathered.at[:, pl.ds(at, n)], g.at[:, pl.ds(at, n)], sems.at[i])
        for i, (at, n) in enumerate(spans)
    ]
    loads[0].start()
    loads[1].start()
    low, high = rows_of_six(0, 5, 0), rows_of_six(0, 1, 6)
    left, right = rows_of_six(2, 5, -2), rows_of_six(2, 5, 2)

    def natural(at, n, begin, rest, outs):
        for half in range(2):
            here = slice(256 * half, 256 * half + 256)
            there = slice(192 * half, 192 * half + 192)
            a = g[here, at : at + n]
            outs[0][there] = mm(low, a).astype(BF)
            there = slice(outs[2] + 192 * half, outs[2] + 192 * half + 192)
            outs[1][there] = (mm(high, a) + mm(rest, g[here, begin : begin + n])).astype(BF)

    loads[0].wait()
    loads[1].wait()
    for i in (2, 3, 4):
        loads[i].start()
    natural(0, 1152, 4608, left, (w_qkv, w_qkv, 384))
    loads[2].wait()
    loads[5].start()
    tail = g[:, 6912:7040]
    lane = lax.broadcasted_iota(jnp.int32, (1, 128), 1)
    one = jnp.where(lane < 16, tail.astype(F32), 0.0).astype(BF)
    two = jnp.where((lane >= 16) & (lane < 32), tail.astype(F32), 0.0).astype(BF)
    halves = [slice(0, 256), slice(256, 512)]
    rows = [mm(low, one[h]) for h in halves]
    rows += [mm(high, one[h]) + mm(left, two[h]) for h in halves]
    across = jnp.transpose(jnp.concatenate(rows, 0))
    vec[...] = across[:16] + across[16:32]
    chip = lax.broadcasted_iota(jnp.int32, (64, 512), 0)
    place = lax.broadcasted_iota(jnp.int32, (64, 512), 1)
    of_chip = mm((place == 8 * chip).astype(F32).astype(BF), tail).astype(BF)
    b_up[...] = jnp.sum(jnp.where(own_lanes(), mm(of_chip, lanes_of()), 0.0), 0, keepdims=True)
    slabs = [
        g[:, 7040 + 768 * k : 7808 + 768 * k].astype(F32).reshape(64, 1, 8, 768) for k in range(3)
    ]
    w_down[...] = jnp.concatenate(slabs, 1).reshape(1536, 768).astype(BF)
    loads[3].wait()
    loads[4].wait()
    natural(1152, 768, 5760, left, (w_kv, w_kv, 384))
    natural(1920, 384, 6528, left, (w_query, w_query, 384))
    loads[5].wait()
    natural(2304, 1536, 4608, right, (w_up, w_up, 384))
    natural(3840, 768, 6144, right, (w_self, w_cross, 0))


def unpack(gathered):
    outs = ((768, 1152), (768, 768), (768, 384), (768, 1536), (384, 768), (384, 768), (1536, 768))
    return pl.pallas_call(
        unpack_kernel,
        out_shape=(
            *[shape(o, BF) for o in outs],
            shape((16, 768), F32),
            shape((1, 1536), F32),
        ),
        in_specs=[HBM],
        out_specs=(VMEM,) * 9,
        scratch_shapes=[pltpu.VMEM((512, 9344), BF), pltpu.SemaphoreType.DMA((6,))],
        compiler_params=params(46),
        cost_estimate=cost(4e9, 20e6),
        name="unpack",
    )(gathered)


def natural_row(at_slot, twelfth):
    return at_slot * 6 + twelfth + jnp.where(twelfth >= 6, 378, 0)


def index_kernel(place, columns):
    core, chip = place[0], place[1]

    def target_of(order, slot):
        first = slot * 0 + core == 0
        target = 0
        for axis, digit in zip(order, (slot >> 4, (slot >> 2) & 3, slot & 3)):
            step = STRIDE[axis]
            here = lax.rem(lax.div(chip, step), 4)
            other = jnp.where(
                first, jnp.where(digit == 1, 3, jnp.maximum(digit, 1) - 1), digit ^ (digit >> 1)
            )
            target = target + (here ^ other) * step
        return target

    def out_pick(at_slot, eight):
        return jnp.where(eight < 6, at_slot * 6 + eight, -1)

    at = lax.broadcasted_iota(jnp.int32, (512, 1), 0)
    eight = at & 7
    targets = [target_of(order, at >> 3) for order in ORDERS]
    values = []
    for target in targets:
        values += [natural_row(target, eight), natural_row(target, 8 + (eight & 3)) - 384]
    values += [out_pick(target, eight) for target in targets]
    values += [target * 8 + eight for target in targets] + [jnp.where(eight == 0, targets[2], -1)]
    for i in range(16):
        columns[:, i : i + 1] = values[i] if i < len(values) else at * 0


def indices(place):
    return staged(
        "indices",
        index_kernel,
        (place,),
        (),
        [shape((512, 16), jnp.int32)],
        1e6,
    )[0]


def image_pick_kernel(pick, tokens, *outs):
    for turn, out in enumerate(outs):
        out[...] = tokens[pick[turn]]


def image_pick(pick, tokens):
    return staged(
        "image_pick", image_pick_kernel, (pick,), (tokens,), [shape((188, 768), BF)] * 4, 1e6
    )


def image_stack_kernel(v0, v1, v2, v3, out, wide):
    wide[188:192] = jnp.zeros((4, 768), F32)
    for turn, value in enumerate((v0, v1, v2, v3)):
        wide[0:188] = value[...].astype(F32)
        out[192 * turn : 192 * turn + 192] = wide[...].astype(BF)


def image_stack(values):
    return staged(
        "image_stack",
        image_stack_kernel,
        (),
        values,
        [shape((768, 768), BF)],
        1e6,
        [pltpu.VMEM((192, 768), F32)],
    )[0]


def image_forward_kernel(vec, w_kv, own, other, kv, normed):
    row = lax.broadcasted_iota(jnp.int32, (192, 1), 0)
    for image in range(8):
        source, here = (own, 192 * image) if image < 4 else (other, 192 * image - 768)
        xhat, _ = normalize(source[here : here + 192].astype(F32))
        at = slice(192 * image, 192 * image + 192)
        normed[at] = jnp.where(row < 188, xhat * vec[2:3] + vec[6:7], 0.0).astype(BF)
        kv[at] = mm(normed[at], w_kv[...]).astype(BF)


def image_forward(vec, w_kv, own, other):
    return staged(
        "image_forward",
        image_forward_kernel,
        (),
        (vec, w_kv, own, other),
        (shape((1536, 768), BF), shape((1536, 768), BF)),
        2e9,
    )


def cross_forward_kernel(
    info, vec, text, mine, got, w_query, kv, w_out, after, normed, queries, mixed, part
):
    after[...] = text[...].astype(F32) + (mine[...] + got[...])
    xhat, _ = normalize(after[...])
    normed[...] = (xhat * vec[1:2] + vec[5:6]).astype(BF)
    queries[...] = mm(normed[...], w_query[...]).astype(BF)
    for row in range(2):
        allowed = cross_allowed(info, row)
        at = slice(128 * row, 128 * row + 128)
        for j in range(3):
            lanes = slice(128 * j, 128 * j + 128)
            q = stacked(queries[at, lanes]) * 0.125
            k = row_keys(kv, row, lanes)
            v = row_keys(kv, row, slice(384 + 128 * j, 512 + 128 * j))
            probs = softmax(mm_t(q, k), allowed)
            mixed[at, lanes] = merged(mm(probs.astype(BF), v)).astype(BF)
    part[...] = mm(mixed[...], w_out[...])


def cross_forward(info, vec, text, mine, got, kv, w_query, w_out):
    return staged(
        "cross_forward",
        cross_forward_kernel,
        (info,),
        (vec, text, mine, got, w_query, kv, w_out),
        (shape((256, 768), F32), shape((256, 768), BF), shape((256, 384), BF), shape((256, 384), BF), shape((256, 768), F32)),
        3e9,
    )


def feed_kernel(
    info, vec, b_up, before, mine, got, w_up, w_down, grad,
    after, normed, active, hidden_low, to_mine, to_other, back, sums,
    part,
):
    after[...] = before[...] + (mine[...] + got[...])
    xhat, _ = normalize(after[...])
    normed[...] = (xhat * vec[3:4] + vec[7:8]).astype(BF)
    part[...] = jnp.zeros((256, 768), F32)
    for k in range(3):
        lanes = slice(512 * k, 512 * k + 512)
        down = w_down[lanes]
        hidden = mm(normed[...], w_up[:, lanes]) + b_up[:, lanes]
        cdf = 0.5 * (1.0 + lax.erf(hidden * 0.7071067811865476))
        active[:, lanes] = (hidden * cdf).astype(BF)
        slope = cdf + hidden * (jnp.exp(-0.5 * hidden * hidden) * 0.3989422804014327)
        part[...] += mm(active[:, lanes], down)
        hidden_low[:, lanes] = (mm_t(grad[...], down) * slope).astype(BF)
    back[...] = mm_t(hidden_low[...], w_up[...])
    sums[...] = jnp.concatenate(
        [
            jnp.sum(back[...] * xhat, 0, keepdims=True),
            jnp.sum(back[...], 0, keepdims=True),
            jnp.zeros((6, 768), F32),
        ],
        0,
    )
    core = info[0]
    bias = vec[8:9]
    for row in range(2):
        at = pl.ds(pl.multiple_of(128 * row + 64 * core, 64), 64)
        to_mine[64 * row : 64 * row + 64] = after[at] + part[at] + bias
        at = pl.ds(pl.multiple_of(128 * row + 64 * (1 - core), 64), 64)
        to_other[64 * row : 64 * row + 64] = part[at]


def feed(info, vec, b_up, before, mine, got, w_up, w_down, grad):
    return staged(
        "feed",
        feed_kernel,
        (info,),
        (vec, b_up, before, mine, got, w_up, w_down, grad),
        (shape((256, 768), F32), shape((256, 768), BF), shape((256, 1536), BF), shape((256, 1536), BF), shape((128, 768), F32), shape((128, 768), F32), shape((256, 768), F32), shape((8, 768), F32)),
        3e9,
        [pltpu.VMEM((256, 768), F32)],
    )


def laid_out(weight, qa, qb, width):
    top = mm(qa, weight)
    rest = mm(qb, weight[384:])
    n = weight.shape[1]
    upper = lax.broadcasted_iota(jnp.int32, (512, 1), 0) % 8 < 4
    tail = rest[:, width:]
    if n - width < width:
        tail = jnp.concatenate([tail, jnp.zeros((512, 2 * width - n), F32)], 1)
    return top, jnp.where(upper, rest[:, :width], tail)


def put(keep, send, lanes, value):
    keep[:, lanes] = value[:256].astype(BF)
    send[:, lanes] = value[256:].astype(BF)


def feed_grads_kernel(normed, active, hidden_low, grad, index, *outs):
    keeps, sends, up_rows = outs[0:3], outs[3:6], outs[6]
    d_up = t_mm(normed[...], hidden_low[...]).astype(BF)
    total = jnp.sum(hidden_low[...].astype(F32), 0, keepdims=True)
    of_chip = mm_t(jnp.where(own_lanes(), total, 0.0).astype(BF), lanes_of()).astype(BF)
    up_rows[...] = mm(placed(index, 12, 64), of_chip)
    for p in range(3):
        qa, qb = placed(index, 2 * p, 768), placed(index, 2 * p + 1, 384)
        top, rest = laid_out(d_up[:, 512 * p : 512 * p + 512], qa, qb, 256)
        put(keeps[p], sends[p], slice(0, 512), top)
        put(keeps[p], sends[p], slice(512, 768), rest)
    d_down = t_mm(active[...], grad[...]).reshape(64, 3, 8, 768)
    slabs = [placed(index, 9 + p, 512) for p in range(3)]
    for k in range(3):
        rows = d_down[:, k].reshape(512, 768).astype(BF)
        for p, slab in enumerate(slabs):
            moved = mm(slab, rows[:, 256 * p : 256 * p + 256])
            put(keeps[p], sends[p], slice(768 + 256 * k, 1024 + 256 * k), moved)


def feed_grads(normed, active, hidden_low, grad, index):
    return staged(
        "feed_grads",
        feed_grads_kernel,
        (),
        (normed, active, hidden_low, grad, index),
        (*[shape((256, 1536), BF)] * 6, shape((512, 128), F32)),
        6e9,
    )


def cross_backward_kernel(
    info, vec, grad, mine, got, after, w_out, queries, kv, w_query, before,
    stream, low, dq, dkv, back, sums,
):
    xhat, inv = normalize(after[...])
    step = norm_back(mine[...] + got[...], vec[3:4], xhat, inv)
    stream[...] = grad[...].astype(F32) + step
    low[...] = stream[...].astype(BF)
    mixed_grad = mm_t(low[...], w_out[...]).astype(BF)
    for row in range(2):
        allowed = cross_allowed(info, row)
        at = slice(128 * row, 128 * row + 128)
        for j in range(3):
            lanes = slice(128 * j, 128 * j + 128)
            value_lanes = slice(384 + 128 * j, 512 + 128 * j)
            q = stacked(queries[at, lanes]) * 0.125
            do = stacked(mixed_grad[at, lanes])
            k = row_keys(kv, row, lanes)
            v = row_keys(kv, row, value_lanes)
            probs = softmax(mm_t(q, k), allowed)
            ds = softmax_back(probs, mm_t(do, v))
            dq[at, lanes] = (merged(mm(ds, k)) * 0.125).astype(BF)
            dk = t_mm(ds, q).astype(BF)
            dv = t_mm(probs.astype(BF), do).astype(BF)
            for value, where in ((dk, lanes), (dv, value_lanes)):
                dkv[384 * row : 384 * row + 384, where] = value[:384]
                dkv[768 + 384 * row : 1152 + 384 * row, where] = value[384:]
    back[...] = mm_t(dq[...], w_query[...])
    xhat, _ = normalize(before[...])
    sums[...] = jnp.concatenate(
        [
            jnp.sum(back[...] * xhat, 0, keepdims=True),
            jnp.sum(back[...], 0, keepdims=True),
            jnp.zeros((6, 768), F32),
        ],
        0,
    )


def cross_backward(info, vec, grad, mine, got, after, w_out, queries, kv, w_query, before):
    return staged(
        "cross_backward",
        cross_backward_kernel,
        (info,),
        (vec, grad, mine, got, after, w_out, queries, kv, w_query, before),
        (shape((256, 768), F32), shape((256, 768), BF), shape((256, 384), BF), shape((1536, 768), BF), shape((256, 768), F32), shape((8, 768), F32)),
        5e9,
    )


def cross_part(p, weight, mixed, low, index, keep, send):
    qa, qb = placed(index, 2 * p, 768), placed(index, 2 * p + 1, 384)
    top, rest = laid_out(weight, qa, qb, 256)
    put(keep, send, slice(0, 384), top)
    put(keep, send, slice(384, 640), rest)
    d_out = t_mm(mixed[...], low[:, 256 * p : 256 * p + 256]).astype(BF)
    put(keep, send, slice(640, 896), mm(placed(index, 6 + p, 384), d_out))


def image_grads_kernel(image_normed, dkv, mixed, low, index, keep0, keep1, send0, send1):
    d_kv = t_mm(image_normed[...], dkv[...]).astype(BF)
    cross_part(0, d_kv[:, :384], mixed, low, index, keep0, send0)
    cross_part(1, d_kv[:, 384:], mixed, low, index, keep1, send1)


def image_grads(image_normed, dkv, mixed, low, index):
    return staged(
        "image_grads",
        image_grads_kernel,
        (),
        (image_normed, dkv, mixed, low, index),
        [shape((256, 896), BF)] * 4,
        4e9,
    )


def query_grads_kernel(normed, dq, mixed, low, index, keep, send):
    d_query = t_mm(normed[...], dq[...]).astype(BF)
    cross_part(2, d_query, mixed, low, index, keep, send)


def query_grads(normed, dq, mixed, low, index):
    return staged(
        "query_grads",
        query_grads_kernel,
        (),
        (normed, dq, mixed, low, index),
        [shape((256, 896), BF)] * 2,
        1e9,
    )


def image_part_kernel(dkv, w_kv, out):
    out[...] = mm_t(dkv[768:], w_kv[...]).astype(BF)


def image_part(dkv, w_kv):
    return staged(
        "image_part",
        image_part_kernel,
        (),
        (dkv, w_kv),
        (shape((768, 768), BF),),
        1e9,
    )


def image_backward_kernel(vec, dkv, w_kv, got, own, out, low1, low2, low3, sums):
    total = [jnp.zeros((1, 768), F32)] * 2
    for image, result in enumerate((out, low1, low2, low3)):
        at = slice(192 * image, 192 * image + 192)
        dy = mm_t(dkv[at], w_kv[...]) + got[at].astype(F32)
        xhat, inv = normalize(own[at].astype(F32))
        total = [
            total[0] + jnp.sum(dy * xhat, 0, keepdims=True),
            total[1] + jnp.sum(dy, 0, keepdims=True),
        ]
        result[...] = norm_back(dy, vec[2:3], xhat, inv)[:188].astype(result.dtype)
    sums[...] = jnp.concatenate(total + [jnp.zeros((6, 768), F32)], 0)


def image_backward(vec, dkv, w_kv, got, own):
    return staged(
        "image_backward",
        image_backward_kernel,
        (),
        (vec, dkv, w_kv, got, own),
        (shape((188, 768), F32), *[shape((188, 768), BF)] * 3, shape((8, 768), F32)),
        1e9,
    )


def self_backward_kernel(
    info, vec, stream_in, mine, got, before, w_out, joined, w_qkv, text,
    stream_mine, low, d_joined, to_mine, to_other, sums,
    stream, back,
):
    xhat, inv = normalize(before[...])
    stream[...] = stream_in[...] + norm_back(mine[...] + got[...], vec[1:2], xhat, inv)
    low[...] = stream[...].astype(BF)
    mixed_grad = mm_t(low[...], w_out[...]).astype(BF)
    for row in range(2):
        allowed = self_allowed(info, row)
        at = slice(128 * row, 128 * row + 128)
        for j in range(3):
            lanes = [slice(384 * i + 128 * j, 384 * i + 128 * j + 128) for i in range(3)]
            q = stacked(joined[at, lanes[0]]) * 0.125
            k = joined[at, lanes[1]]
            v = joined[at, lanes[2]]
            do = stacked(mixed_grad[at, lanes[0]])
            probs = softmax(mm_t(q, k), allowed)
            ds = softmax_back(probs, mm_t(do, v))
            d_joined[at, lanes[0]] = (merged(mm(ds, k)) * 0.125).astype(BF)
            d_joined[at, lanes[1]] = t_mm(ds, q).astype(BF)
            d_joined[at, lanes[2]] = t_mm(probs.astype(BF), do).astype(BF)
    back[...] = mm_t(d_joined[...], w_qkv[...])
    xhat, _ = normalize(text[...].astype(F32))
    sums[...] = jnp.concatenate(
        [
            jnp.sum(back[...] * xhat, 0, keepdims=True),
            jnp.sum(back[...], 0, keepdims=True),
            jnp.zeros((6, 768), F32),
        ],
        0,
    )
    core = info[0]
    for row in range(2):
        at = pl.ds(pl.multiple_of(128 * row + 64 * core, 64), 64)
        stream_mine[64 * row : 64 * row + 64] = stream[at]
        to_mine[64 * row : 64 * row + 64] = back[at]
        at = pl.ds(pl.multiple_of(128 * row + 64 * (1 - core), 64), 64)
        to_other[64 * row : 64 * row + 64] = back[at]


def self_backward(info, vec, stream_in, mine, got, before, w_out, joined, w_qkv, text):
    return staged(
        "self_backward",
        self_backward_kernel,
        (info,),
        (vec, stream_in, mine, got, before, w_out, joined, w_qkv, text),
        (shape((128, 768), F32), shape((256, 768), BF), shape((256, 1152), BF), shape((128, 768), F32), shape((128, 768), F32), shape((8, 768), F32)),
        3e9,
        [pltpu.VMEM((256, 768), F32), pltpu.VMEM((256, 768), F32)],
    )


def self_grads_kernel(
    normed, d_joined, mixed, low, sum0, sum1, sum2, sum3, grad, up_rows,
    index, e0, e1, e2, *outs,
):
    keeps, sends = outs[0:3], outs[3:6]
    for send, early in zip(sends, (e0, e1, e2)):
        send[:, :896] = early[...]
    d_qkv = t_mm(normed[...], d_joined[...]).astype(BF)
    d_out = t_mm(mixed[...], low[...]).astype(BF)
    for p in range(3):
        qa, qb = placed(index, 2 * p, 768), placed(index, 2 * p + 1, 384)
        o = placed(index, 6 + p, 384)
        top, rest = laid_out(d_qkv[:, 384 * p : 384 * p + 384], qa, qb, 256)
        moved = mm(o, d_out[:, 256 * p : 256 * p + 256])
        for at, value in ((0, top), (384, rest), (640, moved)):
            n = value.shape[1]
            keeps[p][:, at : at + n] = value[:256].astype(BF)
            sends[p][:, 896 + at : 896 + at + n] = value[256:].astype(BF)
    down_sum = jnp.sum(grad[...].astype(F32), 0, keepdims=True) * 0.5
    rows = [s[i : i + 1] for i in range(2) for s in (sum0, sum1, sum2, sum3)]
    rows = jnp.concatenate(rows + [down_sum, jnp.zeros((7, 768), F32)], 0).astype(BF)
    zero = jnp.zeros((16, 768), BF)
    first = jnp.concatenate([rows] + [zero] * 7, 0)
    second = jnp.concatenate([zero, rows] + [zero] * 6, 0)
    value = mm_t(qa, first) + mm_t(qb, second[:, 384:]) + up_rows[...]
    keeps[2][:, 896:1024] = value[:256].astype(BF)
    sends[2][:, 1792:1920] = value[256:].astype(BF)


def self_grads(normed, d_joined, mixed, low, sums, grad, up_rows, index, early):
    return staged(
        "self_grads",
        self_grads_kernel,
        (),
        (normed, d_joined, mixed, low, *sums, grad, up_rows, index, *early),
        (*[shape((256, n), BF) for n in (896, 896, 1024, 1792, 1792, 1920)],),
        3e9,
    )


def first_core(info, dims):
    return lax.broadcasted_iota(jnp.int32, dims, 0) * 0 + info[0] == 0


BLOCKS = ((0, 3, 384), (1, 2, 384), (2, 1, 384), (3, 1, 1536))


def halves_into(core, refs, target, sem):
    copies, here = [], 0
    for which, blocks, width in BLOCKS:
        for i in range(blocks):
            at = pl.multiple_of(2 * i * width + core * width, 128)
            copies.append(
                pltpu.make_async_copy(
                    refs[which].at[:, pl.ds(at, width)], target.at[:, pl.ds(here, width)],
                    sem.at[len(copies)],
                )
            )
            here += width
    return copies


def vector_rows(gain, bias, down_bias):
    total = jnp.zeros((6, 128), F32)
    for at, ref in ((0, gain), (4, bias), (8, down_bias)):
        n = ref.shape[0]
        i = lax.broadcasted_iota(jnp.int32, (n, 128), 0) + at
        j = lax.broadcasted_iota(jnp.int32, (n, 128), 1)
        total = total + t_mm(ref[...], ((i == j) | (i + 16 == j)).astype(F32).astype(BF))
    return total


def pack_swap_kernel(info, qkv, kv, query, up, gain, bias, down_bias, send, half, sem):
    copies = halves_into(1 - info[0], (qkv, kv, query, up), half, sem)
    for c in copies:
        c.start()
    send[:, 3840:] = vector_rows(gain, bias, down_bias).astype(BF)
    for c in copies:
        c.wait()
    send[:, :3840] = half[...]


def pack_slots_kernel(
    info, qkv, kv, query, up, self_out, cross_out, down, gain, bias, down_bias, up_bias, got,
    slot, twelve, half, outs, slabs, sem, sems,
):
    copies = halves_into(info[0], (qkv, kv, query, up), half, sem)
    others = [
        pltpu.make_async_copy(self_out, outs.at[0], sems.at[0]),
        pltpu.make_async_copy(cross_out, outs.at[1], sems.at[1]),
        pltpu.make_async_copy(down, slabs, sems.at[2]),
    ]
    for c in copies + others:
        c.start()
    first = first_core(info, (6, 128))
    mine = vector_rows(gain, bias, down_bias)
    other = got[:, 3840:].astype(F32)
    twelve[0:6, 4608:] = jnp.where(first, mine, other)
    twelve[6:12, 4608:] = jnp.where(first, other, mine)
    twelve[12:16, 4608:] = jnp.zeros((4, 128), F32)
    lane = lax.broadcasted_iota(jnp.int32, (8, 128), 1)
    row = lax.broadcasted_iota(jnp.int32, (8, 128), 0)
    vec = jnp.where(lane < 16, twelve[0:8, 4608:], 0.0)
    vec = vec + jnp.where((lane >= 16) & (lane < 32), twelve[8:16, 4608:], 0.0)
    i = lax.broadcasted_iota(jnp.int32, (24, 128), 0)
    j = lax.broadcasted_iota(jnp.int32, (24, 128), 1)
    units = mm(up_bias[...], (i + 64 == j).astype(F32).astype(BF))
    slot[:, 6912:7040] = (vec + jnp.where(row == 0, units, 0.0)).astype(BF)
    for c in copies:
        c.wait()
    first = first_core(info, (6, 3840))
    mine = half[...].astype(F32)
    other = got[:, :3840].astype(F32)
    twelve[0:6, :3840] = jnp.where(first, mine, other)
    twelve[6:12, :3840] = jnp.where(first, other, mine)
    for c in others:
        c.wait()
    twelve[0:6, 3840:4608] = outs[0].astype(F32)
    twelve[6:12, 3840:4608] = outs[1].astype(F32)
    slot[:, :4608] = twelve[0:8, :4608].astype(BF)
    twelve[0:4, :2304] = twelve[8:12, :2304]
    twelve[4:8, :2304] = twelve[8:12, 2304:4608]
    slot[:, 4608:6912] = twelve[0:8, :2304].astype(BF)
    wide = slabs[...].astype(F32)
    for k in range(3):
        at = 7040 + 768 * k
        slot[:, at : at + 768] = wide[8 * k : 8 * k + 8].astype(BF)


def packed(name, kernel, info, far, near, out, scratch):
    return pl.pallas_call(
        kernel,
        out_shape=out,
        in_specs=[SMEM] + [HBM] * len(far) + [VMEM] * len(near),
        out_specs=VMEM,
        scratch_shapes=scratch,
        compiler_params=params(60),
        cost_estimate=cost(1e6, 1e6),
        name=name,
    )(info, *far, *near)


def pack_swap(info, weights, vectors):
    return packed(
        "pack_swap",
        pack_swap_kernel,
        info,
        weights,
        vectors,
        shape((6, 3968), BF),
        [pltpu.VMEM((6, 3840), BF), pltpu.SemaphoreType.DMA((7,))],
    )


def pack_slots(info, weights, vectors, got, self_out, cross_out, down, up_bias):
    return packed(
        "pack_slots",
        pack_slots_kernel,
        info,
        (*weights, self_out, cross_out, down),
        (*vectors, up_bias, got),
        shape((8, 9344), BF),
        [
            pltpu.VMEM((16, 4736), F32),
            pltpu.VMEM((6, 3840), BF),
            pltpu.VMEM((2, 6, 768), BF),
            pltpu.VMEM((24, 768), BF),
            pltpu.SemaphoreType.DMA((7,)),
            pltpu.SemaphoreType.DMA((3,)),
        ],
    )


TWELVES = (
    [(0, 512, 256)] * 3 + [(1536, 384, 256)] * 3 + [(2432, 384, 256)] * 3
)


def finish_send_kernel(info, *refs):
    keeps, gots, (s0, s1, s2, send, own, twelve) = refs[:3], refs[3:6], refs[6:]
    sums = (s0, s1, s2)
    for p in range(3):
        sums[p][...] = keeps[p][...].astype(F32) + gots[p][...].astype(F32)
    here = 0
    for i, (at, n, width) in enumerate(TWELVES):
        ref = sums[i % 3]
        twelve[0:8, here : here + n] = ref[:, at : at + n]
        twelve[8:12, here : here + width] = ref[0:4, at + n : at + n + width]
        twelve[8:12, here + width : here + n] = ref[4:8, at + n : at + n + n - width]
        here += n
    vec = s2[:, 3328:]
    twelve[0:8, 3840:] = vec
    twelve[8:12, 3840:] = pltpu.roll(vec, 112, 1)[0:4]
    first = first_core(info, (6, 3968))
    send[...] = jnp.where(first, twelve[6:12], twelve[0:6])
    own[...] = jnp.where(first, twelve[0:6], twelve[6:12])


def finish_kernel(
    info, s0, s1, s2, own, got, qkv, out_self, query, kv, out_cross, up, down, gain, bias, down_bias
):
    sums = (s0, s1, s2)
    first = first_core(info, (6, 3840))
    low = jnp.where(first, own[:, :3840], got[:, :3840])
    high = jnp.where(first, got[:, :3840], own[:, :3840])
    for ref, begin, blocks, width in (
        (up, 0, 1, 1536), (kv, 1536, 2, 384), (query, 2304, 1, 384), (qkv, 2688, 3, 384),
    ):
        for i in range(blocks):
            at = begin + i * width
            ref[:, 2 * i * width : (2 * i + 1) * width] = low[:, at : at + width]
            ref[:, (2 * i + 1) * width : (2 * i + 2) * width] = high[:, at : at + width]
    for p in range(3):
        lanes = slice(256 * p, 256 * p + 256)
        out_self[:, lanes] = sums[p][0:6, 3072:3328]
        out_cross[:, lanes] = sums[p][0:6, 2176:2432]
        for k in range(3):
            at = 768 + 256 * k
            down[8 * k : 8 * k + 8, lanes] = sums[p][:, at : at + 256]
    total = jnp.concatenate([own[:, 3840:] + got[:, 3840:], jnp.zeros((122, 128), F32)], 0)
    across = jnp.transpose(total)
    gain[...] = across[0:4, 0:6]
    bias[...] = across[4:8, 0:6]
    down_bias[...] = across[8:9, 0:6]


def finish_send(info, keeps, gots):
    widths = [k.shape[1] for k in keeps]
    return staged(
        "finish_send",
        finish_send_kernel,
        (info,),
        (*keeps, *gots),
        [shape((8, n), F32) for n in widths] + [shape((6, 3968), F32)] * 2,
        1e6,
        [pltpu.VMEM((16, 3968), F32)],
        mib=8,
    )


def finish(info, sums, own, got):
    return staged(
        "finish",
        finish_kernel,
        (info,),
        (*sums, own, got),
        [
            shape(dims, F32)
            for dims in (
                (6, 2304), (6, 768), (6, 768), (6, 1536), (6, 768), (6, 3072), (24, 768), (4, 6), (4, 6),
                (1, 6),
            )
        ],
        1e6,
        mib=8,
    )


def text_finish_kernel(vec, text, stream, mine, got, out_mine, out_got, grad, out):
    xhat, inv = normalize(text[...].astype(F32))
    grad[...] = stream[...] + norm_back(mine[...] + got[...], vec[0:1], xhat, inv)
    out[...] = out_mine[...] + out_got[...]


def text_finish(vec, text, stream, mine, got, out_mine, out_got):
    return staged(
        "text_finish",
        text_finish_kernel,
        (),
        (vec, text, stream, mine, got, out_mine, out_got),
        [shape((128, 768), F32)] * 2,
        1e6,
        mib=8,
    )


def image_finish_kernel(pick, v0, v1, v2, v3, out):
    values = [v[...].astype(F32) for v in (v0, v1, v2, v3)]
    for image in range(4):
        total = values[3]
        for turn in range(3):
            total = jnp.where(pick[turn] == image, values[turn], total)
        out[:, image, :] = total


def image_finish(pick, values):
    out = staged(
        "image_finish",
        image_finish_kernel,
        (pick,),
        values,
        [shape((188, 4, 768), F32)],
        1e6,
    )[0]
    return jnp.transpose(out, (1, 0, 2))


def combine_kernel(plan, *refs):
    at = 0
    ins = []
    for keeps, gots in plan:
        ins.append((refs[at : at + len(keeps)], refs[at + len(keeps) : at + len(keeps) + len(gots)]))
        at += len(keeps) + len(gots)
    outs = refs[at:]
    for p, (keeps, gots) in enumerate(ins):
        here = 0
        edges = []
        for ref in keeps:
            edges.append((here, here + ref.shape[1], ref))
            here += ref.shape[1]
        here = 0
        for ref in gots:
            for low, high, keep in edges:
                a, b = max(low, here), min(high, here + ref.shape[1])
                if a >= b:
                    continue
                total = keep[:, a - low : b - low].astype(F32) + ref[:, a - here : b - here].astype(F32)
                half = total.shape[0] // 2
                outs[2 * p][:, a:b] = total[:half].astype(BF)
                outs[2 * p + 1][:, a:b] = total[half:].astype(BF)
            here += ref.shape[1]


def combine(parts):
    plan, args, outs = [], [], []
    for keeps, gots in parts:
        plan.append(([k.shape[1] for k in keeps], [g.shape[1] for g in gots]))
        args += [*keeps, *gots]
        rows, width = keeps[0].shape[0], sum(k.shape[1] for k in keeps)
        outs += [shape((rows // 2, width), BF)] * 2
    got = staged(
        "combine", lambda *refs: combine_kernel(plan, *refs), (), args, outs, 1e6
    )
    return [(got[2 * p], got[2 * p + 1]) for p in range(len(parts))]


def send_step(step, values, parts=(0, 1, 2)):
    v0, v1 = ((1, 3), (3, 1))[step % 2]
    return [
        lax.ppermute(v, BOTH, xor_pairs(ORDERS[p][step // 2], v0, v1)) for v, p in zip(values, parts)
    ]


def after(value, *others):
    return lax.optimization_barrier((value, *others))[0]


def image_moves(images, way):
    once, around = [], []
    for core, sign in ((0, 1), (64, -1)):
        once += [(core + i, core + (i + 16 * way) % 64) for i in range(64)]
        around += [(core + i, core + (i + 16 * sign) % 64) for i in range(64)]
    first, second, third = images
    return [
        lax.ppermute(first, BOTH, once),
        lax.ppermute(lax.ppermute(second, BOTH, around), BOTH, around),
        lax.ppermute(third, BOTH, [(j, i) for i, j in once]),
    ]


def on_device(
    text_input,
    image_tokens,
    output_grad,
    segment_starts,
    caption_image,
    image_counts,
    norm_gain,
    norm_bias,
    self_qkv,
    self_out,
    cross_q,
    cross_kv,
    cross_out,
    up_weight,
    up_bias,
    down_weight,
    down_bias,
):
    core = lax.axis_index("seq")
    chip = lax.axis_index("batch")
    first = core == 0

    def ordered(own, other, axis):
        return jnp.where(
            first, jnp.concatenate([own, other], axis), jnp.concatenate([other, own], axis)
        )

    place = jnp.stack([core, chip]).astype(jnp.int32)
    weights = (self_qkv, cross_kv, cross_q, up_weight)
    vectors = (norm_gain, norm_bias, down_bias[None])
    got = swap(pack_swap(place, weights, vectors))
    slot = pack_slots(
        place, weights, vectors, got, self_out, cross_out, down_weight, up_bias[None]
    )
    gathered = lax.all_gather(slot, "batch", axis=0, tiled=True)

    late_text, late_grad = after(text_input, slot), after(output_grad, slot)
    text = ordered(late_text, swap(late_text), 1).reshape(256, 768)
    grad = ordered(late_grad, swap(late_grad), 1).reshape(256, 768)

    group_images = after(caption_image, slot).reshape(64, 8)
    my_captions = lax.dynamic_index_in_dim(group_images, chip, 0, keepdims=False)
    limits = jnp.take(image_counts, my_captions).reshape(4, 2)
    limits = jnp.where(first, jnp.concatenate([limits[:, 0], limits[:, 1]]), jnp.concatenate([limits[:, 1], limits[:, 0]]))
    turns = jnp.arange(4)
    targets = (chip - turns * 16) % 64
    wanted = group_images[targets, 2 * turns + core]
    local_pick = wanted - (core * 64 + chip) * 4
    outgoing = image_pick(after(local_pick, slot), image_tokens)
    received = [outgoing[0], *image_moves(outgoing[1:], -1)]
    own_images = image_stack(received)
    other_images = swap(own_images)
    info = jnp.concatenate(
        [core[None], segment_starts.reshape(8), limits, jnp.zeros((15,), jnp.int32)]
    ).astype(jnp.int32)

    column_index = indices(after(place, slot))

    gathered, info, grad, text, column_index, own_images, other_images = lax.optimization_barrier(
        (gathered, info, grad, text, column_index, own_images, other_images)
    )
    w_qkv, w_kv, w_query, w_up, w_self, w_cross, w_down, vec, b_up = unpack(gathered)
    part, joined, mixed_self, normed_one = self_forward(info, vec, w_qkv, w_self, text)
    got = swap(part)
    kv, image_normed = image_forward(vec, w_kv, own_images, other_images)
    after_self, normed_two, q_cross, mixed_cross, part = cross_forward(
        info, vec, text, part, got, kv, w_query, w_cross
    )
    after_cross, normed_three, active, hidden_low, text_mine, text_other, part, sum3 = feed(
        info, vec, b_up, after_self, part, swap(part), w_up, w_down, grad
    )
    text_got = swap(text_other)
    got = swap(part)

    grads = feed_grads(normed_three, active, hidden_low, grad, column_index)
    keep_one, up_rows = grads[0:3], grads[6]
    got_one = send_step(0, grads[3:6])
    stream_two, cross_low, dq, dkv, part, sum1 = cross_backward(
        info, vec, after(grad, keep_one[0]), part, got, after_cross, w_cross, q_cross, kv, w_query, after_self
    )
    got = swap(part)
    dkv, z_got = lax.optimization_barrier((dkv, got_one[2]))
    got_one = [*got_one[:2], z_got]
    image_send = image_part(dkv, w_kv)[0]
    *rows_back, sum2 = image_backward(vec, dkv, w_kv, swap(image_send), own_images)
    returned = [rows_back[0], *image_moves(rows_back[1:], 1)]
    k_keep, v_keep, k_send, v_send = image_grads(
        image_normed, after(dkv, sum2), mixed_cross, cross_low, column_index
    )
    q_keep, q_send = query_grads(
        normed_two, after(dq, k_keep), mixed_cross, cross_low, column_index
    )
    keep_two, early = [k_keep, v_keep, q_keep], [k_send, v_send, q_send]
    stream_one, self_low, d_joined, one_mine, one_other, sum0 = self_backward(
        info, vec, after(stream_two, q_keep), part, got, after_self, w_self, joined,
        w_qkv, text,
    )
    self_low, *late = lax.optimization_barrier((self_low, *returned[1:], *got_one))
    returned, got_one = returned[:1] + late[:3], late[3:]
    grads = self_grads(
        normed_one, d_joined, mixed_self, self_low, (sum0, sum1, sum2, sum3), grad, up_rows,
        column_index, early,
    )
    keep_three = grads[0:3]
    got_two = send_step(0, grads[3:6])
    one_got = swap(one_other)
    image_grad = image_finish(after(local_pick, grads[3]), returned)
    text_grad, text_output = text_finish(
        after(vec, grads[3]), text_input.reshape(128, 768), stream_one, one_mine, one_got, text_mine,
        text_got,
    )
    got_two, image_grad, text_grad = lax.optimization_barrier((got_two, image_grad, text_grad))
    pairs = []
    for p in range(3):
        pairs += combine([([keep_one[p], keep_two[p], keep_three[p]], [got_one[p], got_two[p]])])
    for step in range(1, 6):
        got_step = send_step(step, [s for _, s in pairs])
        step_parts = [([k], [g]) for (k, _), g in zip(pairs, got_step)]
        if step == 5:
            *sums, send, own = finish_send(place, [k for k, _ in pairs], got_step)
        elif step == 1:
            pairs = [combine([one])[0] for one in step_parts]
        else:
            pairs = combine(step_parts)

    text_grad, text_output = text_grad.reshape(2, 64, 768), text_output.reshape(2, 64, 768)

    (
        qkv_grad, self_grad, query_grad, kv_grad, cross_grad, up_grad, down_grad, gain_grad, bias_grad,
        down_bias_grad,
    ) = finish(place, sums, own, swap(send))
    up_bias_grad = sums[2][0, 3392:3416]
    return (
        text_output,
        text_grad,
        image_grad,
        gain_grad,
        bias_grad,
        qkv_grad,
        self_grad,
        query_grad,
        kv_grad,
        cross_grad,
        up_grad,
        up_bias_grad,
        down_grad,
        down_bias_grad[0],
    )


def solution(mesh):
    rows = P("batch", "seq", None)
    shard = P(BOTH, None)
    wide = P(None, BOTH)
    return jax.shard_map(
        on_device,
        mesh=mesh,
        in_specs=(
            rows, P(BOTH, None, None), rows, P("batch", None), P(), P(), wide, wide,
            shard, shard, shard, shard, shard, shard, P(BOTH), shard, P(BOTH),
        ),
        out_specs=(
            rows, rows, P(BOTH, None, None), wide, wide,
            shard, shard, shard, shard, shard, shard, P(BOTH), shard, P(BOTH),
        ),
        check_vma=False,
    )
```

```python
import math

import jax
import jax.numpy as jnp
from jax import lax
from jax.experimental import pallas as pl
from jax.experimental.pallas import tpu as pltpu
from jax.sharding import PartitionSpec as P

HEADS = 12
HEAD_DIM = 64
EPSILON = 1e-05
MASKED_SCORE = -1e30
BF = jnp.bfloat16
F32 = jnp.float32
BOTH = ("seq", "batch")
STRIDE = {"z": 16, "y": 4, "x": 1}
ORDERS = (("x", "z", "y"), ("y", "x", "z"), ("z", "y", "x"))


def xor_pairs(axis, value0, value1):
    step, out = STRIDE[axis], []
    for core, value in ((0, value0), (1, value1)):
        for chip in range(64):
            at = chip // step % 4
            out.append((core * 64 + chip, core * 64 + chip + ((at ^ value) - at) * step))
    return out


def swap(value):
    return lax.ppermute(value, "seq", [(0, 1), (1, 0)])


def mm(a, b):
    return jnp.dot(a, b, preferred_element_type=F32)


def mm_t(a, b):
    return lax.dot_general(a, b, (((1,), (1,)), ((), ())), preferred_element_type=F32)


def t_mm(a, b):
    return lax.dot_general(a, b, (((0,), (0,)), ((), ())), preferred_element_type=F32)


def normalize(values):
    center = jnp.mean(values, -1, keepdims=True)
    centred = values - center
    spread = jnp.mean(centred * centred, -1, keepdims=True)
    inv = lax.rsqrt(spread + EPSILON)
    return centred * inv, inv


def norm_back(grad, gain, xhat, inv):
    scaled = grad * gain
    return inv * (
        scaled
        - jnp.mean(scaled, -1, keepdims=True)
        - xhat * jnp.mean(scaled * xhat, -1, keepdims=True)
    )


VMEM = pl.BlockSpec(memory_space=pltpu.VMEM)
SMEM = pl.BlockSpec(memory_space=pltpu.SMEM)
HBM = pl.BlockSpec(memory_space=pltpu.HBM)


def shape(dims, dtype):
    return jax.ShapeDtypeStruct(dims, dtype)


def cost(flops, moved):
    return pl.CostEstimate(
        flops=int(flops / 64), bytes_accessed=int(moved / 64), transcendentals=0
    )


def params(mib):
    return pltpu.CompilerParams(vmem_limit_bytes=mib * 1024 * 1024)


def staged(name, kernel, scalars, ins, outs, work, scratch=(), mib=16):
    moved = sum(math.prod(v.shape) * v.dtype.itemsize for v in (*ins, *outs))
    return pl.pallas_call(
        kernel,
        out_shape=tuple(outs),
        in_specs=[SMEM] * len(scalars) + [VMEM] * len(ins),
        out_specs=(VMEM,) * len(outs),
        scratch_shapes=list(scratch),
        compiler_params=params(mib),
        cost_estimate=cost(work, moved),
        name=name,
    )(*scalars, *ins)


def placed(columns, i, size):
    place = lax.broadcasted_iota(jnp.int32, (512, size), 1)
    return (place == columns[:, i : i + 1]).astype(F32).astype(BF)


def segment_of(info, row, dims, axis):
    place = lax.broadcasted_iota(jnp.int32, dims, axis)
    total = jnp.full(dims, -1, jnp.int32)
    for j in range(4):
        total = total + (place >= info[1 + 4 * row + j]).astype(jnp.int32)
    return total


def low_lanes():
    return lax.broadcasted_iota(jnp.int32, (1, 128), 1) < 64


def stacked(pair):
    left = low_lanes()
    zero = jnp.zeros_like(pair)
    return jnp.concatenate([jnp.where(left, pair, zero), jnp.where(left, zero, pair)], 0)


def merged(two):
    n = two.shape[0] // 2
    return jnp.where(low_lanes(), two[:n], two[n:])


def softmax(scores, allowed):
    scores = jnp.where(allowed, scores, MASKED_SCORE)
    weights = jnp.exp(scores - jnp.max(scores, -1, keepdims=True))
    return weights * (1.0 / jnp.sum(weights, -1, keepdims=True))


def softmax_back(probs, dprobs):
    return (probs * (dprobs - jnp.sum(probs * dprobs, -1, keepdims=True))).astype(BF)


def self_allowed(info, row):
    at = segment_of(info, row, (128, 128), 0)
    key = segment_of(info, row, (128, 128), 1)
    i = lax.broadcasted_iota(jnp.int32, (128, 128), 0)
    j = lax.broadcasted_iota(jnp.int32, (128, 128), 1)
    allowed = (at == key) & (j <= i)
    return jnp.concatenate([allowed, allowed], 0)


def cross_allowed(info, row):
    core = info[0]
    lane = lax.broadcasted_iota(jnp.int32, (1, 768), 1)
    key = jnp.full((1, 768), -1, jnp.int32)
    images = (2 * row, 2 * row + 1, 4 + 2 * row, 5 + 2 * row)
    captions = (core, 2 + core, 1 - core, 3 - core)
    for block in range(4):
        limit = info[9 + images[block]]
        key = jnp.where(
            (lane >= 192 * block) & (lane < 192 * block + limit), captions[block], key
        )
    at = segment_of(info, row, (128, 1), 0)
    return jnp.concatenate([at, at], 0) == key


def row_keys(kv, row, lanes):
    return jnp.concatenate(
        [kv[384 * row : 384 * row + 384, lanes], kv[768 + 384 * row : 1152 + 384 * row, lanes]], 0
    )


def lanes_of():
    lane = lax.broadcasted_iota(jnp.int32, (128, 1536), 0)
    unit = lax.broadcasted_iota(jnp.int32, (128, 1536), 1)
    return (lane == 64 + lax.rem(unit, 24)).astype(F32).astype(BF)


def own_lanes():
    chip = lax.broadcasted_iota(jnp.int32, (64, 1536), 0) * 24
    unit = lax.broadcasted_iota(jnp.int32, (64, 1536), 1)
    return (unit >= chip) & (unit < chip + 24)


def self_forward_kernel(info, vec, w_qkv, w_out, text, part, joined, mixed, normed):
    xhat, _ = normalize(text[...].astype(F32))
    normed[...] = (xhat * vec[0:1] + vec[4:5]).astype(BF)
    joined[...] = mm(normed[...], w_qkv[...]).astype(BF)
    for row in range(2):
        allowed = self_allowed(info, row)
        at = slice(128 * row, 128 * row + 128)
        for j in range(3):
            q = stacked(joined[at, 128 * j : 128 * j + 128]) * 0.125
            k = joined[at, 384 + 128 * j : 512 + 128 * j]
            v = joined[at, 768 + 128 * j : 896 + 128 * j]
            probs = softmax(mm_t(q, k), allowed)
            mixed[at, 128 * j : 128 * j + 128] = merged(mm(probs.astype(BF), v)).astype(BF)
    part[...] = mm(mixed[...], w_out[...])


def self_forward(info, vec, w_qkv, w_out, text):
    return staged(
        "self_forward",
        self_forward_kernel,
        (info,),
        (vec, w_qkv, w_out, text),
        (
            shape((256, 768), F32),
            shape((256, 1152), BF),
            shape((256, 384), BF),
            shape((256, 768), BF),
        ),
        2e9,
    )


def rows_of_six(first, last, shift):
    row = lax.broadcasted_iota(jnp.int32, (192, 256), 0)
    place = lax.broadcasted_iota(jnp.int32, (192, 256), 1)
    chip = lax.div(row, 6)
    r = row - 6 * chip
    hit = (place == 8 * chip + r + shift) & (r >= first) & (r <= last)
    return hit.astype(F32).astype(BF)


def unpack_kernel(
    gathered, w_qkv, w_kv, w_query, w_up, w_self, w_cross, w_down, vec, b_up, g, sems
):
    spans = ((4608, 1152), (0, 1152), (6912, 2432), (5760, 1152), (1152, 1152), (2304, 2304))
    loads = [
        pltpu.make_async_copy(gathered.at[:, pl.ds(at, n)], g.at[:, pl.ds(at, n)], sems.at[i])
        for i, (at, n) in enumerate(spans)
    ]
    loads[0].start()
    loads[1].start()
    low, high = rows_of_six(0, 5, 0), rows_of_six(0, 1, 6)
    left, right = rows_of_six(2, 5, -2), rows_of_six(2, 5, 2)

    def natural(at, n, begin, rest, outs):
        for half in range(2):
            here = slice(256 * half, 256 * half + 256)
            there = slice(192 * half, 192 * half + 192)
            a = g[here, at : at + n]
            outs[0][there] = mm(low, a).astype(BF)
            there = slice(outs[2] + 192 * half, outs[2] + 192 * half + 192)
            outs[1][there] = (mm(high, a) + mm(rest, g[here, begin : begin + n])).astype(BF)

    loads[0].wait()
    loads[1].wait()
    for i in (2, 3, 4):
        loads[i].start()
    natural(0, 1152, 4608, left, (w_qkv, w_qkv, 384))
    loads[2].wait()
    loads[5].start()
    tail = g[:, 6912:7040]
    lane = lax.broadcasted_iota(jnp.int32, (1, 128), 1)
    one = jnp.where(lane < 16, tail.astype(F32), 0.0).astype(BF)
    two = jnp.where((lane >= 16) & (lane < 32), tail.astype(F32), 0.0).astype(BF)
    halves = [slice(0, 256), slice(256, 512)]
    rows = [mm(low, one[h]) for h in halves]
    rows += [mm(high, one[h]) + mm(left, two[h]) for h in halves]
    across = jnp.transpose(jnp.concatenate(rows, 0))
    vec[...] = across[:16] + across[16:32]
    chip = lax.broadcasted_iota(jnp.int32, (64, 512), 0)
    place = lax.broadcasted_iota(jnp.int32, (64, 512), 1)
    of_chip = mm((place == 8 * chip).astype(F32).astype(BF), tail).astype(BF)
    b_up[...] = jnp.sum(jnp.where(own_lanes(), mm(of_chip, lanes_of()), 0.0), 0, keepdims=True)
    slabs = [
        g[:, 7040 + 768 * k : 7808 + 768 * k].astype(F32).reshape(64, 1, 8, 768) for k in range(3)
    ]
    w_down[...] = jnp.concatenate(slabs, 1).reshape(1536, 768).astype(BF)
    loads[3].wait()
    loads[4].wait()
    natural(1152, 768, 5760, left, (w_kv, w_kv, 384))
    natural(1920, 384, 6528, left, (w_query, w_query, 384))
    loads[5].wait()
    natural(2304, 1536, 4608, right, (w_up, w_up, 384))
    natural(3840, 768, 6144, right, (w_self, w_cross, 0))


def unpack(gathered):
    outs = ((768, 1152), (768, 768), (768, 384), (768, 1536), (384, 768), (384, 768), (1536, 768))
    return pl.pallas_call(
        unpack_kernel,
        out_shape=(
            *[shape(o, BF) for o in outs],
            shape((16, 768), F32),
            shape((1, 1536), F32),
        ),
        in_specs=[HBM],
        out_specs=(VMEM,) * 9,
        scratch_shapes=[pltpu.VMEM((512, 9344), BF), pltpu.SemaphoreType.DMA((6,))],
        compiler_params=params(46),
        cost_estimate=cost(4e9, 20e6),
        name="unpack",
    )(gathered)


def natural_row(at_slot, twelfth):
    return at_slot * 6 + twelfth + jnp.where(twelfth >= 6, 378, 0)


def index_kernel(place, columns):
    core, chip = place[0], place[1]

    def target_of(order, slot):
        first = slot * 0 + core == 0
        target = 0
        for axis, digit in zip(order, (slot >> 4, (slot >> 2) & 3, slot & 3)):
            step = STRIDE[axis]
            here = lax.rem(lax.div(chip, step), 4)
            other = jnp.where(
                first, jnp.where(digit == 1, 3, jnp.maximum(digit, 1) - 1), digit ^ (digit >> 1)
            )
            target = target + (here ^ other) * step
        return target

    def out_pick(at_slot, eight):
        return jnp.where(eight < 6, at_slot * 6 + eight, -1)

    at = lax.broadcasted_iota(jnp.int32, (512, 1), 0)
    eight = at & 7
    targets = [target_of(order, at >> 3) for order in ORDERS]
    values = []
    for target in targets:
        values += [natural_row(target, eight), natural_row(target, 8 + (eight & 3)) - 384]
    values += [out_pick(target, eight) for target in targets]
    values += [target * 8 + eight for target in targets] + [jnp.where(eight == 0, targets[2], -1)]
    for i in range(16):
        columns[:, i : i + 1] = values[i] if i < len(values) else at * 0


def indices(place):
    return staged(
        "indices",
        index_kernel,
        (place,),
        (),
        [shape((512, 16), jnp.int32)],
        1e6,
    )[0]


def image_pick_kernel(pick, tokens, *outs):
    for turn, out in enumerate(outs):
        out[...] = tokens[pick[turn]]


def image_pick(pick, tokens):
    return staged(
        "image_pick", image_pick_kernel, (pick,), (tokens,), [shape((188, 768), BF)] * 4, 1e6
    )


def image_stack_kernel(v0, v1, v2, v3, out, wide):
    wide[188:192] = jnp.zeros((4, 768), F32)
    for turn, value in enumerate((v0, v1, v2, v3)):
        wide[0:188] = value[...].astype(F32)
        out[192 * turn : 192 * turn + 192] = wide[...].astype(BF)


def image_stack(values):
    return staged(
        "image_stack",
        image_stack_kernel,
        (),
        values,
        [shape((768, 768), BF)],
        1e6,
        [pltpu.VMEM((192, 768), F32)],
    )[0]


def image_forward_kernel(vec, w_kv, own, other, kv, normed):
    row = lax.broadcasted_iota(jnp.int32, (192, 1), 0)
    for image in range(8):
        source, here = (own, 192 * image) if image < 4 else (other, 192 * image - 768)
        xhat, _ = normalize(source[here : here + 192].astype(F32))
        at = slice(192 * image, 192 * image + 192)
        normed[at] = jnp.where(row < 188, xhat * vec[2:3] + vec[6:7], 0.0).astype(BF)
        kv[at] = mm(normed[at], w_kv[...]).astype(BF)


def image_forward(vec, w_kv, own, other):
    return staged(
        "image_forward",
        image_forward_kernel,
        (),
        (vec, w_kv, own, other),
        (shape((1536, 768), BF), shape((1536, 768), BF)),
        2e9,
    )


def cross_forward_kernel(
    info, vec, text, mine, got, w_query, kv, w_out, after, normed, queries, mixed, part
):
    after[...] = text[...].astype(F32) + (mine[...] + got[...])
    xhat, _ = normalize(after[...])
    normed[...] = (xhat * vec[1:2] + vec[5:6]).astype(BF)
    queries[...] = mm(normed[...], w_query[...]).astype(BF)
    for row in range(2):
        allowed = cross_allowed(info, row)
        at = slice(128 * row, 128 * row + 128)
        for j in range(3):
            lanes = slice(128 * j, 128 * j + 128)
            q = stacked(queries[at, lanes]) * 0.125
            k = row_keys(kv, row, lanes)
            v = row_keys(kv, row, slice(384 + 128 * j, 512 + 128 * j))
            probs = softmax(mm_t(q, k), allowed)
            mixed[at, lanes] = merged(mm(probs.astype(BF), v)).astype(BF)
    part[...] = mm(mixed[...], w_out[...])


def cross_forward(info, vec, text, mine, got, kv, w_query, w_out):
    return staged(
        "cross_forward",
        cross_forward_kernel,
        (info,),
        (vec, text, mine, got, w_query, kv, w_out),
        (shape((256, 768), F32), shape((256, 768), BF), shape((256, 384), BF), shape((256, 384), BF), shape((256, 768), F32)),
        3e9,
    )


def feed_kernel(
    info, vec, b_up, before, mine, got, w_up, w_down, grad,
    after, normed, active, hidden_low, to_mine, to_other, back, sums,
    part,
):
    after[...] = before[...] + (mine[...] + got[...])
    xhat, _ = normalize(after[...])
    normed[...] = (xhat * vec[3:4] + vec[7:8]).astype(BF)
    part[...] = jnp.zeros((256, 768), F32)
    for k in range(3):
        lanes = slice(512 * k, 512 * k + 512)
        down = w_down[lanes]
        hidden = mm(normed[...], w_up[:, lanes]) + b_up[:, lanes]
        cdf = 0.5 * (1.0 + lax.erf(hidden * 0.7071067811865476))
        active[:, lanes] = (hidden * cdf).astype(BF)
        slope = cdf + hidden * (jnp.exp(-0.5 * hidden * hidden) * 0.3989422804014327)
        part[...] += mm(active[:, lanes], down)
        hidden_low[:, lanes] = (mm_t(grad[...], down) * slope).astype(BF)
    back[...] = mm_t(hidden_low[...], w_up[...])
    sums[...] = jnp.concatenate(
        [
            jnp.sum(back[...] * xhat, 0, keepdims=True),
            jnp.sum(back[...], 0, keepdims=True),
            jnp.zeros((6, 768), F32),
        ],
        0,
    )
    core = info[0]
    bias = vec[8:9]
    for row in range(2):
        at = pl.ds(pl.multiple_of(128 * row + 64 * core, 64), 64)
        to_mine[64 * row : 64 * row + 64] = after[at] + part[at] + bias
        at = pl.ds(pl.multiple_of(128 * row + 64 * (1 - core), 64), 64)
        to_other[64 * row : 64 * row + 64] = part[at]


def feed(info, vec, b_up, before, mine, got, w_up, w_down, grad):
    return staged(
        "feed",
        feed_kernel,
        (info,),
        (vec, b_up, before, mine, got, w_up, w_down, grad),
        (shape((256, 768), F32), shape((256, 768), BF), shape((256, 1536), BF), shape((256, 1536), BF), shape((128, 768), F32), shape((128, 768), F32), shape((256, 768), F32), shape((8, 768), F32)),
        3e9,
        [pltpu.VMEM((256, 768), F32)],
    )


def laid_out(weight, qa, qb, width):
    top = mm(qa, weight)
    rest = mm(qb, weight[384:])
    n = weight.shape[1]
    upper = lax.broadcasted_iota(jnp.int32, (512, 1), 0) % 8 < 4
    tail = rest[:, width:]
    if n - width < width:
        tail = jnp.concatenate([tail, jnp.zeros((512, 2 * width - n), F32)], 1)
    return top, jnp.where(upper, rest[:, :width], tail)


def put(keep, send, lanes, value):
    keep[:, lanes] = value[:256].astype(BF)
    send[:, lanes] = value[256:].astype(BF)


def feed_grads_kernel(normed, active, hidden_low, grad, index, *outs):
    keeps, sends, up_rows = outs[0:3], outs[3:6], outs[6]
    d_up = t_mm(normed[...], hidden_low[...]).astype(BF)
    total = jnp.sum(hidden_low[...].astype(F32), 0, keepdims=True)
    of_chip = mm_t(jnp.where(own_lanes(), total, 0.0).astype(BF), lanes_of()).astype(BF)
    up_rows[...] = mm(placed(index, 12, 64), of_chip)
    for p in range(3):
        qa, qb = placed(index, 2 * p, 768), placed(index, 2 * p + 1, 384)
        top, rest = laid_out(d_up[:, 512 * p : 512 * p + 512], qa, qb, 256)
        put(keeps[p], sends[p], slice(0, 512), top)
        put(keeps[p], sends[p], slice(512, 768), rest)
    d_down = t_mm(active[...], grad[...]).reshape(64, 3, 8, 768)
    slabs = [placed(index, 9 + p, 512) for p in range(3)]
    for k in range(3):
        rows = d_down[:, k].reshape(512, 768).astype(BF)
        for p, slab in enumerate(slabs):
            moved = mm(slab, rows[:, 256 * p : 256 * p + 256])
            put(keeps[p], sends[p], slice(768 + 256 * k, 1024 + 256 * k), moved)


def feed_grads(normed, active, hidden_low, grad, index):
    return staged(
        "feed_grads",
        feed_grads_kernel,
        (),
        (normed, active, hidden_low, grad, index),
        (*[shape((256, 1536), BF)] * 6, shape((512, 128), F32)),
        6e9,
    )


def cross_backward_kernel(
    info, vec, grad, mine, got, after, w_out, queries, kv, w_query, before,
    stream, low, dq, dkv, back, sums,
):
    xhat, inv = normalize(after[...])
    step = norm_back(mine[...] + got[...], vec[3:4], xhat, inv)
    stream[...] = grad[...].astype(F32) + step
    low[...] = stream[...].astype(BF)
    mixed_grad = mm_t(low[...], w_out[...]).astype(BF)
    for row in range(2):
        allowed = cross_allowed(info, row)
        at = slice(128 * row, 128 * row + 128)
        for j in range(3):
            lanes = slice(128 * j, 128 * j + 128)
            value_lanes = slice(384 + 128 * j, 512 + 128 * j)
            q = stacked(queries[at, lanes]) * 0.125
            do = stacked(mixed_grad[at, lanes])
            k = row_keys(kv, row, lanes)
            v = row_keys(kv, row, value_lanes)
            probs = softmax(mm_t(q, k), allowed)
            ds = softmax_back(probs, mm_t(do, v))
            dq[at, lanes] = (merged(mm(ds, k)) * 0.125).astype(BF)
            dk = t_mm(ds, q).astype(BF)
            dv = t_mm(probs.astype(BF), do).astype(BF)
            for value, where in ((dk, lanes), (dv, value_lanes)):
                dkv[384 * row : 384 * row + 384, where] = value[:384]
                dkv[768 + 384 * row : 1152 + 384 * row, where] = value[384:]
    back[...] = mm_t(dq[...], w_query[...])
    xhat, _ = normalize(before[...])
    sums[...] = jnp.concatenate(
        [
            jnp.sum(back[...] * xhat, 0, keepdims=True),
            jnp.sum(back[...], 0, keepdims=True),
            jnp.zeros((6, 768), F32),
        ],
        0,
    )


def cross_backward(info, vec, grad, mine, got, after, w_out, queries, kv, w_query, before):
    return staged(
        "cross_backward",
        cross_backward_kernel,
        (info,),
        (vec, grad, mine, got, after, w_out, queries, kv, w_query, before),
        (shape((256, 768), F32), shape((256, 768), BF), shape((256, 384), BF), shape((1536, 768), BF), shape((256, 768), F32), shape((8, 768), F32)),
        5e9,
    )


def cross_part(p, weight, mixed, low, index, keep, send):
    qa, qb = placed(index, 2 * p, 768), placed(index, 2 * p + 1, 384)
    top, rest = laid_out(weight, qa, qb, 256)
    put(keep, send, slice(0, 384), top)
    put(keep, send, slice(384, 640), rest)
    d_out = t_mm(mixed[...], low[:, 256 * p : 256 * p + 256]).astype(BF)
    put(keep, send, slice(640, 896), mm(placed(index, 6 + p, 384), d_out))


def image_grads_kernel(image_normed, dkv, mixed, low, index, keep0, keep1, send0, send1):
    d_kv = t_mm(image_normed[...], dkv[...]).astype(BF)
    cross_part(0, d_kv[:, :384], mixed, low, index, keep0, send0)
    cross_part(1, d_kv[:, 384:], mixed, low, index, keep1, send1)


def image_grads(image_normed, dkv, mixed, low, index):
    return staged(
        "image_grads",
        image_grads_kernel,
        (),
        (image_normed, dkv, mixed, low, index),
        [shape((256, 896), BF)] * 4,
        4e9,
    )


def query_grads_kernel(normed, dq, mixed, low, index, keep, send):
    d_query = t_mm(normed[...], dq[...]).astype(BF)
    cross_part(2, d_query, mixed, low, index, keep, send)


def query_grads(normed, dq, mixed, low, index):
    return staged(
        "query_grads",
        query_grads_kernel,
        (),
        (normed, dq, mixed, low, index),
        [shape((256, 896), BF)] * 2,
        1e9,
    )


def image_part_kernel(dkv, w_kv, out):
    out[...] = mm_t(dkv[768:], w_kv[...]).astype(BF)


def image_part(dkv, w_kv):
    return staged(
        "image_part",
        image_part_kernel,
        (),
        (dkv, w_kv),
        (shape((768, 768), BF),),
        1e9,
    )


def image_backward_kernel(vec, dkv, w_kv, got, own, out, low1, low2, low3, sums):
    total = [jnp.zeros((1, 768), F32)] * 2
    for image, result in enumerate((out, low1, low2, low3)):
        at = slice(192 * image, 192 * image + 192)
        dy = mm_t(dkv[at], w_kv[...]) + got[at].astype(F32)
        xhat, inv = normalize(own[at].astype(F32))
        total = [
            total[0] + jnp.sum(dy * xhat, 0, keepdims=True),
            total[1] + jnp.sum(dy, 0, keepdims=True),
        ]
        result[...] = norm_back(dy, vec[2:3], xhat, inv)[:188].astype(result.dtype)
    sums[...] = jnp.concatenate(total + [jnp.zeros((6, 768), F32)], 0)


def image_backward(vec, dkv, w_kv, got, own):
    return staged(
        "image_backward",
        image_backward_kernel,
        (),
        (vec, dkv, w_kv, got, own),
        (shape((188, 768), F32), *[shape((188, 768), BF)] * 3, shape((8, 768), F32)),
        1e9,
    )


def self_backward_kernel(
    info, vec, stream_in, mine, got, before, w_out, joined, w_qkv, text,
    stream_mine, low, d_joined, to_mine, to_other, sums,
    stream, back,
):
    xhat, inv = normalize(before[...])
    stream[...] = stream_in[...] + norm_back(mine[...] + got[...], vec[1:2], xhat, inv)
    low[...] = stream[...].astype(BF)
    mixed_grad = mm_t(low[...], w_out[...]).astype(BF)
    for row in range(2):
        allowed = self_allowed(info, row)
        at = slice(128 * row, 128 * row + 128)
        for j in range(3):
            lanes = [slice(384 * i + 128 * j, 384 * i + 128 * j + 128) for i in range(3)]
            q = stacked(joined[at, lanes[0]]) * 0.125
            k = joined[at, lanes[1]]
            v = joined[at, lanes[2]]
            do = stacked(mixed_grad[at, lanes[0]])
            probs = softmax(mm_t(q, k), allowed)
            ds = softmax_back(probs, mm_t(do, v))
            d_joined[at, lanes[0]] = (merged(mm(ds, k)) * 0.125).astype(BF)
            d_joined[at, lanes[1]] = t_mm(ds, q).astype(BF)
            d_joined[at, lanes[2]] = t_mm(probs.astype(BF), do).astype(BF)
    back[...] = mm_t(d_joined[...], w_qkv[...])
    xhat, _ = normalize(text[...].astype(F32))
    sums[...] = jnp.concatenate(
        [
            jnp.sum(back[...] * xhat, 0, keepdims=True),
            jnp.sum(back[...], 0, keepdims=True),
            jnp.zeros((6, 768), F32),
        ],
        0,
    )
    core = info[0]
    for row in range(2):
        at = pl.ds(pl.multiple_of(128 * row + 64 * core, 64), 64)
        stream_mine[64 * row : 64 * row + 64] = stream[at]
        to_mine[64 * row : 64 * row + 64] = back[at]
        at = pl.ds(pl.multiple_of(128 * row + 64 * (1 - core), 64), 64)
        to_other[64 * row : 64 * row + 64] = back[at]


def self_backward(info, vec, stream_in, mine, got, before, w_out, joined, w_qkv, text):
    return staged(
        "self_backward",
        self_backward_kernel,
        (info,),
        (vec, stream_in, mine, got, before, w_out, joined, w_qkv, text),
        (shape((128, 768), F32), shape((256, 768), BF), shape((256, 1152), BF), shape((128, 768), F32), shape((128, 768), F32), shape((8, 768), F32)),
        3e9,
        [pltpu.VMEM((256, 768), F32), pltpu.VMEM((256, 768), F32)],
    )


def self_grads_kernel(
    normed, d_joined, mixed, low, sum0, sum1, sum2, sum3, grad, up_rows,
    index, e0, e1, e2, *outs,
):
    keeps, sends = outs[0:3], outs[3:6]
    for send, early in zip(sends, (e0, e1, e2)):
        send[:, :896] = early[...]
    d_qkv = t_mm(normed[...], d_joined[...]).astype(BF)
    d_out = t_mm(mixed[...], low[...]).astype(BF)
    for p in range(3):
        qa, qb = placed(index, 2 * p, 768), placed(index, 2 * p + 1, 384)
        o = placed(index, 6 + p, 384)
        top, rest = laid_out(d_qkv[:, 384 * p : 384 * p + 384], qa, qb, 256)
        moved = mm(o, d_out[:, 256 * p : 256 * p + 256])
        for at, value in ((0, top), (384, rest), (640, moved)):
            n = value.shape[1]
            keeps[p][:, at : at + n] = value[:256].astype(BF)
            sends[p][:, 896 + at : 896 + at + n] = value[256:].astype(BF)
    down_sum = jnp.sum(grad[...].astype(F32), 0, keepdims=True) * 0.5
    rows = [s[i : i + 1] for i in range(2) for s in (sum0, sum1, sum2, sum3)]
    rows = jnp.concatenate(rows + [down_sum, jnp.zeros((7, 768), F32)], 0).astype(BF)
    zero = jnp.zeros((16, 768), BF)
    first = jnp.concatenate([rows] + [zero] * 7, 0)
    second = jnp.concatenate([zero, rows] + [zero] * 6, 0)
    value = mm_t(qa, first) + mm_t(qb, second[:, 384:]) + up_rows[...]
    keeps[2][:, 896:1024] = value[:256].astype(BF)
    sends[2][:, 1792:1920] = value[256:].astype(BF)


def self_grads(normed, d_joined, mixed, low, sums, grad, up_rows, index, early):
    return staged(
        "self_grads",
        self_grads_kernel,
        (),
        (normed, d_joined, mixed, low, *sums, grad, up_rows, index, *early),
        (*[shape((256, n), BF) for n in (896, 896, 1024, 1792, 1792, 1920)],),
        3e9,
    )


def first_core(info, dims):
    return lax.broadcasted_iota(jnp.int32, dims, 0) * 0 + info[0] == 0


BLOCKS = ((0, 3, 384), (1, 2, 384), (2, 1, 384), (3, 1, 1536))


def halves_into(core, refs, target, sem):
    copies, here = [], 0
    for which, blocks, width in BLOCKS:
        for i in range(blocks):
            at = pl.multiple_of(2 * i * width + core * width, 128)
            copies.append(
                pltpu.make_async_copy(
                    refs[which].at[:, pl.ds(at, width)], target.at[:, pl.ds(here, width)],
                    sem.at[len(copies)],
                )
            )
            here += width
    return copies


def vector_rows(gain, bias, down_bias):
    total = jnp.zeros((6, 128), F32)
    for at, ref in ((0, gain), (4, bias), (8, down_bias)):
        n = ref.shape[0]
        i = lax.broadcasted_iota(jnp.int32, (n, 128), 0) + at
        j = lax.broadcasted_iota(jnp.int32, (n, 128), 1)
        total = total + t_mm(ref[...], ((i == j) | (i + 16 == j)).astype(F32).astype(BF))
    return total


def pack_swap_kernel(info, qkv, kv, query, up, gain, bias, down_bias, send, half, sem):
    copies = halves_into(1 - info[0], (qkv, kv, query, up), half, sem)
    for c in copies:
        c.start()
    send[:, 3840:] = vector_rows(gain, bias, down_bias).astype(BF)
    for c in copies:
        c.wait()
    send[:, :3840] = half[...]


def pack_slots_kernel(
    info, qkv, kv, query, up, self_out, cross_out, down, gain, bias, down_bias, up_bias, got,
    slot, twelve, half, outs, slabs, sem, sems,
):
    copies = halves_into(info[0], (qkv, kv, query, up), half, sem)
    others = [
        pltpu.make_async_copy(self_out, outs.at[0], sems.at[0]),
        pltpu.make_async_copy(cross_out, outs.at[1], sems.at[1]),
        pltpu.make_async_copy(down, slabs, sems.at[2]),
    ]
    for c in copies + others:
        c.start()
    first = first_core(info, (6, 128))
    mine = vector_rows(gain, bias, down_bias)
    other = got[:, 3840:].astype(F32)
    twelve[0:6, 4608:] = jnp.where(first, mine, other)
    twelve[6:12, 4608:] = jnp.where(first, other, mine)
    twelve[12:16, 4608:] = jnp.zeros((4, 128), F32)
    lane = lax.broadcasted_iota(jnp.int32, (8, 128), 1)
    row = lax.broadcasted_iota(jnp.int32, (8, 128), 0)
    vec = jnp.where(lane < 16, twelve[0:8, 4608:], 0.0)
    vec = vec + jnp.where((lane >= 16) & (lane < 32), twelve[8:16, 4608:], 0.0)
    i = lax.broadcasted_iota(jnp.int32, (24, 128), 0)
    j = lax.broadcasted_iota(jnp.int32, (24, 128), 1)
    units = mm(up_bias[...], (i + 64 == j).astype(F32).astype(BF))
    slot[:, 6912:7040] = (vec + jnp.where(row == 0, units, 0.0)).astype(BF)
    for c in copies:
        c.wait()
    first = first_core(info, (6, 3840))
    mine = half[...].astype(F32)
    other = got[:, :3840].astype(F32)
    twelve[0:6, :3840] = jnp.where(first, mine, other)
    twelve[6:12, :3840] = jnp.where(first, other, mine)
    for c in others:
        c.wait()
    twelve[0:6, 3840:4608] = outs[0].astype(F32)
    twelve[6:12, 3840:4608] = outs[1].astype(F32)
    slot[:, :4608] = twelve[0:8, :4608].astype(BF)
    twelve[0:4, :2304] = twelve[8:12, :2304]
    twelve[4:8, :2304] = twelve[8:12, 2304:4608]
    slot[:, 4608:6912] = twelve[0:8, :2304].astype(BF)
    wide = slabs[...].astype(F32)
    for k in range(3):
        at = 7040 + 768 * k
        slot[:, at : at + 768] = wide[8 * k : 8 * k + 8].astype(BF)


def packed(name, kernel, info, far, near, out, scratch):
    return pl.pallas_call(
        kernel,
        out_shape=out,
        in_specs=[SMEM] + [HBM] * len(far) + [VMEM] * len(near),
        out_specs=VMEM,
        scratch_shapes=scratch,
        compiler_params=params(60),
        cost_estimate=cost(1e6, 1e6),
        name=name,
    )(info, *far, *near)


def pack_swap(info, weights, vectors):
    return packed(
        "pack_swap",
        pack_swap_kernel,
        info,
        weights,
        vectors,
        shape((6, 3968), BF),
        [pltpu.VMEM((6, 3840), BF), pltpu.SemaphoreType.DMA((7,))],
    )


def pack_slots(info, weights, vectors, got, self_out, cross_out, down, up_bias):
    return packed(
        "pack_slots",
        pack_slots_kernel,
        info,
        (*weights, self_out, cross_out, down),
        (*vectors, up_bias, got),
        shape((8, 9344), BF),
        [
            pltpu.VMEM((16, 4736), F32),
            pltpu.VMEM((6, 3840), BF),
            pltpu.VMEM((2, 6, 768), BF),
            pltpu.VMEM((24, 768), BF),
            pltpu.SemaphoreType.DMA((7,)),
            pltpu.SemaphoreType.DMA((3,)),
        ],
    )


TWELVES = (
    [(0, 512, 256)] * 3 + [(1536, 384, 256)] * 3 + [(2432, 384, 256)] * 3
)


def finish_send_kernel(info, *refs):
    keeps, gots, (s0, s1, s2, send, own, twelve) = refs[:3], refs[3:6], refs[6:]
    sums = (s0, s1, s2)
    for p in range(3):
        sums[p][...] = keeps[p][...].astype(F32) + gots[p][...].astype(F32)
    here = 0
    for i, (at, n, width) in enumerate(TWELVES):
        ref = sums[i % 3]
        twelve[0:8, here : here + n] = ref[:, at : at + n]
        twelve[8:12, here : here + width] = ref[0:4, at + n : at + n + width]
        twelve[8:12, here + width : here + n] = ref[4:8, at + n : at + n + n - width]
        here += n
    vec = s2[:, 3328:]
    twelve[0:8, 3840:] = vec
    twelve[8:12, 3840:] = pltpu.roll(vec, 112, 1)[0:4]
    first = first_core(info, (6, 3968))
    send[...] = jnp.where(first, twelve[6:12], twelve[0:6])
    own[...] = jnp.where(first, twelve[0:6], twelve[6:12])


def finish_kernel(
    info, s0, s1, s2, own, got, qkv, out_self, query, kv, out_cross, up, down, gain, bias, down_bias
):
    sums = (s0, s1, s2)
    first = first_core(info, (6, 3840))
    low = jnp.where(first, own[:, :3840], got[:, :3840])
    high = jnp.where(first, got[:, :3840], own[:, :3840])
    for ref, begin, blocks, width in (
        (up, 0, 1, 1536), (kv, 1536, 2, 384), (query, 2304, 1, 384), (qkv, 2688, 3, 384),
    ):
        for i in range(blocks):
            at = begin + i * width
            ref[:, 2 * i * width : (2 * i + 1) * width] = low[:, at : at + width]
            ref[:, (2 * i + 1) * width : (2 * i + 2) * width] = high[:, at : at + width]
    for p in range(3):
        lanes = slice(256 * p, 256 * p + 256)
        out_self[:, lanes] = sums[p][0:6, 3072:3328]
        out_cross[:, lanes] = sums[p][0:6, 2176:2432]
        for k in range(3):
            at = 768 + 256 * k
            down[8 * k : 8 * k + 8, lanes] = sums[p][:, at : at + 256]
    total = jnp.concatenate([own[:, 3840:] + got[:, 3840:], jnp.zeros((122, 128), F32)], 0)
    across = jnp.transpose(total)
    gain[...] = across[0:4, 0:6]
    bias[...] = across[4:8, 0:6]
    down_bias[...] = across[8:9, 0:6]


def finish_send(info, keeps, gots):
    widths = [k.shape[1] for k in keeps]
    return staged(
        "finish_send",
        finish_send_kernel,
        (info,),
        (*keeps, *gots),
        [shape((8, n), F32) for n in widths] + [shape((6, 3968), F32)] * 2,
        1e6,
        [pltpu.VMEM((16, 3968), F32)],
        mib=8,
    )


def finish(info, sums, own, got):
    return staged(
        "finish",
        finish_kernel,
        (info,),
        (*sums, own, got),
        [
            shape(dims, F32)
            for dims in (
                (6, 2304), (6, 768), (6, 768), (6, 1536), (6, 768), (6, 3072), (24, 768), (4, 6), (4, 6),
                (1, 6),
            )
        ],
        1e6,
        mib=8,
    )


def text_finish_kernel(vec, text, stream, mine, got, out_mine, out_got, grad, out):
    xhat, inv = normalize(text[...].astype(F32))
    grad[...] = stream[...] + norm_back(mine[...] + got[...], vec[0:1], xhat, inv)
    out[...] = out_mine[...] + out_got[...]


def text_finish(vec, text, stream, mine, got, out_mine, out_got):
    return staged(
        "text_finish",
        text_finish_kernel,
        (),
        (vec, text, stream, mine, got, out_mine, out_got),
        [shape((128, 768), F32)] * 2,
        1e6,
        mib=8,
    )


def image_finish_kernel(pick, v0, v1, v2, v3, out):
    values = [v[...].astype(F32) for v in (v0, v1, v2, v3)]
    for image in range(4):
        total = values[3]
        for turn in range(3):
            total = jnp.where(pick[turn] == image, values[turn], total)
        out[:, image, :] = total


def image_finish(pick, values):
    out = staged(
        "image_finish",
        image_finish_kernel,
        (pick,),
        values,
        [shape((188, 4, 768), F32)],
        1e6,
    )[0]
    return jnp.transpose(out, (1, 0, 2))


def combine_kernel(plan, *refs):
    at = 0
    ins = []
    for keeps, gots in plan:
        ins.append((refs[at : at + len(keeps)], refs[at + len(keeps) : at + len(keeps) + len(gots)]))
        at += len(keeps) + len(gots)
    outs = refs[at:]
    for p, (keeps, gots) in enumerate(ins):
        here = 0
        edges = []
        for ref in keeps:
            edges.append((here, here + ref.shape[1], ref))
            here += ref.shape[1]
        here = 0
        for ref in gots:
            for low, high, keep in edges:
                a, b = max(low, here), min(high, here + ref.shape[1])
                if a >= b:
                    continue
                total = keep[:, a - low : b - low].astype(F32) + ref[:, a - here : b - here].astype(F32)
                half = total.shape[0] // 2
                outs[2 * p][:, a:b] = total[:half].astype(BF)
                outs[2 * p + 1][:, a:b] = total[half:].astype(BF)
            here += ref.shape[1]


def combine(parts):
    plan, args, outs = [], [], []
    for keeps, gots in parts:
        plan.append(([k.shape[1] for k in keeps], [g.shape[1] for g in gots]))
        args += [*keeps, *gots]
        rows, width = keeps[0].shape[0], sum(k.shape[1] for k in keeps)
        outs += [shape((rows // 2, width), BF)] * 2
    got = staged(
        "combine", lambda *refs: combine_kernel(plan, *refs), (), args, outs, 1e6
    )
    return [(got[2 * p], got[2 * p + 1]) for p in range(len(parts))]


def send_step(step, values, parts=(0, 1, 2)):
    v0, v1 = ((1, 3), (3, 1))[step % 2]
    return [
        lax.ppermute(v, BOTH, xor_pairs(ORDERS[p][step // 2], v0, v1)) for v, p in zip(values, parts)
    ]


def after(value, *others):
    return lax.optimization_barrier((value, *others))[0]


def image_moves(images, way):
    once = [(core + i, core + (i + 16 * way) % 64) for core in (0, 64) for i in range(64)]
    first, second, third = images
    return [
        lax.ppermute(first, BOTH, once),
        move_on(second),
        lax.ppermute(third, BOTH, [(j, i) for i, j in once]),
    ]


def move_on(image):
    route = [(i, (i + 16) % 64) for i in range(64)]
    return lax.ppermute(image, BOTH, route + [(64 + j, 64 + i) for i, j in route])


def on_device(
    text_input,
    image_tokens,
    output_grad,
    segment_starts,
    caption_image,
    image_counts,
    norm_gain,
    norm_bias,
    self_qkv,
    self_out,
    cross_q,
    cross_kv,
    cross_out,
    up_weight,
    up_bias,
    down_weight,
    down_bias,
):
    core = lax.axis_index("seq")
    chip = lax.axis_index("batch")
    first = core == 0

    def ordered(own, other, axis):
        return jnp.where(
            first, jnp.concatenate([own, other], axis), jnp.concatenate([other, own], axis)
        )

    place = jnp.stack([core, chip]).astype(jnp.int32)
    weights = (self_qkv, cross_kv, cross_q, up_weight)
    vectors = (norm_gain, norm_bias, down_bias[None])
    got = swap(pack_swap(place, weights, vectors))
    slot = pack_slots(
        place, weights, vectors, got, self_out, cross_out, down_weight, up_bias[None]
    )
    gathered = lax.all_gather(slot, "batch", axis=0, tiled=True)

    late_text, late_grad = after(text_input, slot), after(output_grad, slot)
    text = ordered(late_text, swap(late_text), 1).reshape(256, 768)
    grad = ordered(late_grad, swap(late_grad), 1).reshape(256, 768)

    group_images = after(caption_image, slot).reshape(64, 8)
    my_captions = lax.dynamic_index_in_dim(group_images, chip, 0, keepdims=False)
    limits = jnp.take(image_counts, my_captions).reshape(4, 2)
    limits = jnp.where(first, jnp.concatenate([limits[:, 0], limits[:, 1]]), jnp.concatenate([limits[:, 1], limits[:, 0]]))
    turns = jnp.arange(4)
    targets = (chip - turns * 16) % 64
    wanted = group_images[targets, 2 * turns + core]
    local_pick = wanted - (core * 64 + chip) * 4
    outgoing = image_pick(after(local_pick, slot), image_tokens)
    received = [outgoing[0], *image_moves(outgoing[1:], -1)]
    received[2] = move_on(received[2])
    own_images = image_stack(received)
    other_images = swap(own_images)
    info = jnp.concatenate(
        [core[None], segment_starts.reshape(8), limits, jnp.zeros((15,), jnp.int32)]
    ).astype(jnp.int32)

    column_index = indices(after(place, slot))

    gathered, info, grad, text, column_index, own_images, other_images = lax.optimization_barrier(
        (gathered, info, grad, text, column_index, own_images, other_images)
    )
    w_qkv, w_kv, w_query, w_up, w_self, w_cross, w_down, vec, b_up = unpack(gathered)
    part, joined, mixed_self, normed_one = self_forward(info, vec, w_qkv, w_self, text)
    got = swap(part)
    kv, image_normed = image_forward(vec, w_kv, own_images, other_images)
    after_self, normed_two, q_cross, mixed_cross, part = cross_forward(
        info, vec, text, part, got, kv, w_query, w_cross
    )
    after_cross, normed_three, active, hidden_low, text_mine, text_other, part, sum3 = feed(
        info, vec, b_up, after_self, part, swap(part), w_up, w_down, grad
    )
    text_got = swap(text_other)
    got = swap(part)

    grads = feed_grads(normed_three, active, hidden_low, grad, column_index)
    keep_one, up_rows = grads[0:3], grads[6]
    got_one = send_step(0, grads[3:6])
    stream_two, cross_low, dq, dkv, part, sum1 = cross_backward(
        info, vec, after(grad, keep_one[0]), part, got, after_cross, w_cross, q_cross, kv, w_query, after_self
    )
    got = swap(part)
    image_send = image_part(dkv, w_kv)[0]
    *rows_back, sum2 = image_backward(vec, dkv, w_kv, swap(image_send), own_images)
    returned = [rows_back[0], *image_moves(rows_back[1:], 1)]
    k_keep, v_keep, k_send, v_send = image_grads(
        image_normed, after(dkv, sum2), mixed_cross, cross_low, column_index
    )
    returned[2] = move_on(after(returned[2], k_keep))
    q_keep, q_send = query_grads(
        normed_two, after(dq, k_keep), mixed_cross, cross_low, column_index
    )
    keep_two, early = [k_keep, v_keep, q_keep], [k_send, v_send, q_send]
    stream_one, self_low, d_joined, one_mine, one_other, sum0 = self_backward(
        info, vec, after(stream_two, q_keep), part, got, after_self, w_self, joined,
        w_qkv, text,
    )
    self_low, *late = lax.optimization_barrier((self_low, *returned[1:], *got_one))
    returned, got_one = returned[:1] + late[:3], late[3:]
    grads = self_grads(
        normed_one, d_joined, mixed_self, self_low, (sum0, sum1, sum2, sum3), grad, up_rows,
        column_index, early,
    )
    keep_three = grads[0:3]
    got_two = send_step(0, grads[3:6])
    one_got = swap(one_other)
    image_grad = image_finish(after(local_pick, grads[3]), returned)
    text_grad, text_output = text_finish(
        after(vec, grads[3]), text_input.reshape(128, 768), stream_one, one_mine, one_got, text_mine,
        text_got,
    )
    got_two, image_grad, text_grad = lax.optimization_barrier((got_two, image_grad, text_grad))
    pairs = []
    for p in range(3):
        pairs += combine([([keep_one[p], keep_two[p], keep_three[p]], [got_one[p], got_two[p]])])
    for step in range(1, 6):
        got_step = send_step(step, [s for _, s in pairs])
        step_parts = [([k], [g]) for (k, _), g in zip(pairs, got_step)]
        if step == 5:
            *sums, send, own = finish_send(place, [k for k, _ in pairs], got_step)
        elif step == 1:
            pairs = [combine([one])[0] for one in step_parts]
        else:
            pairs = combine(step_parts)

    text_grad, text_output = text_grad.reshape(2, 64, 768), text_output.reshape(2, 64, 768)

    (
        qkv_grad, self_grad, query_grad, kv_grad, cross_grad, up_grad, down_grad, gain_grad, bias_grad,
        down_bias_grad,
    ) = finish(place, sums, own, swap(send))
    up_bias_grad = sums[2][0, 3392:3416]
    return (
        text_output,
        text_grad,
        image_grad,
        gain_grad,
        bias_grad,
        qkv_grad,
        self_grad,
        query_grad,
        kv_grad,
        cross_grad,
        up_grad,
        up_bias_grad,
        down_grad,
        down_bias_grad[0],
    )


def solution(mesh):
    rows = P("batch", "seq", None)
    shard = P(BOTH, None)
    wide = P(None, BOTH)
    return jax.shard_map(
        on_device,
        mesh=mesh,
        in_specs=(
            rows, P(BOTH, None, None), rows, P("batch", None), P(), P(), wide, wide,
            shard, shard, shard, shard, shard, shard, P(BOTH), shard, P(BOTH),
        ),
        out_specs=(
            rows, rows, P(BOTH, None, None), wide, wide,
            shard, shard, shard, shard, shard, shard, P(BOTH), shard, P(BOTH),
        ),
        check_vma=False,
    )
```

```python
import math

import jax
import jax.numpy as jnp
from jax import lax
from jax.experimental import pallas as pl
from jax.experimental.pallas import tpu as pltpu
from jax.sharding import PartitionSpec as P

HEADS = 12
HEAD_DIM = 64
EPSILON = 1e-05
MASKED_SCORE = -1e30
BF = jnp.bfloat16
F32 = jnp.float32
BOTH = ("seq", "batch")
STRIDE = {"z": 16, "y": 4, "x": 1}
ORDERS = (("x", "z", "y"), ("y", "x", "z"), ("z", "y", "x"))


def xor_pairs(axis, value0, value1):
    step, out = STRIDE[axis], []
    for core, value in ((0, value0), (1, value1)):
        for chip in range(64):
            at = chip // step % 4
            out.append((core * 64 + chip, core * 64 + chip + ((at ^ value) - at) * step))
    return out


def swap(value):
    return lax.ppermute(value, "seq", [(0, 1), (1, 0)])


def mm(a, b):
    return jnp.dot(a, b, preferred_element_type=F32)


def mm_t(a, b):
    return lax.dot_general(a, b, (((1,), (1,)), ((), ())), preferred_element_type=F32)


def t_mm(a, b):
    return lax.dot_general(a, b, (((0,), (0,)), ((), ())), preferred_element_type=F32)


def normalize(values):
    center = jnp.mean(values, -1, keepdims=True)
    centred = values - center
    spread = jnp.mean(centred * centred, -1, keepdims=True)
    inv = lax.rsqrt(spread + EPSILON)
    return centred * inv, inv


def norm_back(grad, gain, xhat, inv):
    scaled = grad * gain
    return inv * (
        scaled
        - jnp.mean(scaled, -1, keepdims=True)
        - xhat * jnp.mean(scaled * xhat, -1, keepdims=True)
    )


VMEM = pl.BlockSpec(memory_space=pltpu.VMEM)
SMEM = pl.BlockSpec(memory_space=pltpu.SMEM)
HBM = pl.BlockSpec(memory_space=pltpu.HBM)


def shape(dims, dtype):
    return jax.ShapeDtypeStruct(dims, dtype)


def cost(flops, moved):
    return pl.CostEstimate(
        flops=int(flops / 64), bytes_accessed=int(moved / 64), transcendentals=0
    )


def params(mib):
    return pltpu.CompilerParams(vmem_limit_bytes=mib * 1024 * 1024)


def staged(name, kernel, scalars, ins, outs, work, scratch=(), mib=16):
    moved = sum(math.prod(v.shape) * v.dtype.itemsize for v in (*ins, *outs))
    return pl.pallas_call(
        kernel,
        out_shape=tuple(outs),
        in_specs=[SMEM] * len(scalars) + [VMEM] * len(ins),
        out_specs=(VMEM,) * len(outs),
        scratch_shapes=list(scratch),
        compiler_params=params(mib),
        cost_estimate=cost(work, moved),
        name=name,
    )(*scalars, *ins)


def placed(columns, i, size):
    place = lax.broadcasted_iota(jnp.int32, (512, size), 1)
    return (place == columns[:, i : i + 1]).astype(F32).astype(BF)


def segment_of(info, row, dims, axis):
    place = lax.broadcasted_iota(jnp.int32, dims, axis)
    total = jnp.full(dims, -1, jnp.int32)
    for j in range(4):
        total = total + (place >= info[1 + 4 * row + j]).astype(jnp.int32)
    return total


def low_lanes():
    return lax.broadcasted_iota(jnp.int32, (1, 128), 1) < 64


def stacked(pair):
    left = low_lanes()
    zero = jnp.zeros_like(pair)
    return jnp.concatenate([jnp.where(left, pair, zero), jnp.where(left, zero, pair)], 0)


def merged(two):
    n = two.shape[0] // 2
    return jnp.where(low_lanes(), two[:n], two[n:])


def softmax(scores, allowed):
    scores = jnp.where(allowed, scores, MASKED_SCORE)
    weights = jnp.exp(scores - jnp.max(scores, -1, keepdims=True))
    return weights * (1.0 / jnp.sum(weights, -1, keepdims=True))


def softmax_back(probs, dprobs):
    return (probs * (dprobs - jnp.sum(probs * dprobs, -1, keepdims=True))).astype(BF)


def self_allowed(info, row):
    at = segment_of(info, row, (128, 128), 0)
    key = segment_of(info, row, (128, 128), 1)
    i = lax.broadcasted_iota(jnp.int32, (128, 128), 0)
    j = lax.broadcasted_iota(jnp.int32, (128, 128), 1)
    allowed = (at == key) & (j <= i)
    return jnp.concatenate([allowed, allowed], 0)


def cross_allowed(info, row):
    core = info[0]
    lane = lax.broadcasted_iota(jnp.int32, (1, 768), 1)
    key = jnp.full((1, 768), -1, jnp.int32)
    images = (2 * row, 2 * row + 1, 4 + 2 * row, 5 + 2 * row)
    captions = (core, 2 + core, 1 - core, 3 - core)
    for block in range(4):
        limit = info[9 + images[block]]
        key = jnp.where(
            (lane >= 192 * block) & (lane < 192 * block + limit), captions[block], key
        )
    at = segment_of(info, row, (128, 1), 0)
    return jnp.concatenate([at, at], 0) == key


def row_keys(kv, row, lanes):
    return jnp.concatenate(
        [kv[384 * row : 384 * row + 384, lanes], kv[768 + 384 * row : 1152 + 384 * row, lanes]], 0
    )


def lanes_of():
    lane = lax.broadcasted_iota(jnp.int32, (128, 1536), 0)
    unit = lax.broadcasted_iota(jnp.int32, (128, 1536), 1)
    return (lane == 64 + lax.rem(unit, 24)).astype(F32).astype(BF)


def own_lanes():
    chip = lax.broadcasted_iota(jnp.int32, (64, 1536), 0) * 24
    unit = lax.broadcasted_iota(jnp.int32, (64, 1536), 1)
    return (unit >= chip) & (unit < chip + 24)


def self_forward_kernel(info, vec, w_qkv, w_out, text, part, joined, mixed, normed):
    xhat, _ = normalize(text[...].astype(F32))
    normed[...] = (xhat * vec[0:1] + vec[4:5]).astype(BF)
    joined[...] = mm(normed[...], w_qkv[...]).astype(BF)
    for row in range(2):
        allowed = self_allowed(info, row)
        at = slice(128 * row, 128 * row + 128)
        for j in range(3):
            q = stacked(joined[at, 128 * j : 128 * j + 128]) * 0.125
            k = joined[at, 384 + 128 * j : 512 + 128 * j]
            v = joined[at, 768 + 128 * j : 896 + 128 * j]
            probs = softmax(mm_t(q, k), allowed)
            mixed[at, 128 * j : 128 * j + 128] = merged(mm(probs.astype(BF), v)).astype(BF)
    part[...] = mm(mixed[...], w_out[...])


def self_forward(info, vec, w_qkv, w_out, text):
    return staged(
        "self_forward",
        self_forward_kernel,
        (info,),
        (vec, w_qkv, w_out, text),
        (
            shape((256, 768), F32),
            shape((256, 1152), BF),
            shape((256, 384), BF),
            shape((256, 768), BF),
        ),
        2e9,
    )


def rows_of_six(first, last, shift):
    row = lax.broadcasted_iota(jnp.int32, (192, 256), 0)
    place = lax.broadcasted_iota(jnp.int32, (192, 256), 1)
    chip = lax.div(row, 6)
    r = row - 6 * chip
    hit = (place == 8 * chip + r + shift) & (r >= first) & (r <= last)
    return hit.astype(F32).astype(BF)


def unpack_kernel(
    gathered, w_qkv, w_kv, w_query, w_up, w_self, w_cross, w_down, vec, b_up, g, sems
):
    spans = ((4608, 1152), (0, 1152), (6912, 2432), (5760, 1152), (1152, 1152), (2304, 2304))
    loads = [
        pltpu.make_async_copy(gathered.at[:, pl.ds(at, n)], g.at[:, pl.ds(at, n)], sems.at[i])
        for i, (at, n) in enumerate(spans)
    ]
    loads[0].start()
    loads[1].start()
    low, high = rows_of_six(0, 5, 0), rows_of_six(0, 1, 6)
    left, right = rows_of_six(2, 5, -2), rows_of_six(2, 5, 2)

    def natural(at, n, begin, rest, outs):
        for half in range(2):
            here = slice(256 * half, 256 * half + 256)
            there = slice(192 * half, 192 * half + 192)
            a = g[here, at : at + n]
            outs[0][there] = mm(low, a).astype(BF)
            there = slice(outs[2] + 192 * half, outs[2] + 192 * half + 192)
            outs[1][there] = (mm(high, a) + mm(rest, g[here, begin : begin + n])).astype(BF)

    loads[0].wait()
    loads[1].wait()
    for i in (2, 3, 4):
        loads[i].start()
    natural(0, 1152, 4608, left, (w_qkv, w_qkv, 384))
    loads[2].wait()
    loads[5].start()
    tail = g[:, 6912:7040]
    lane = lax.broadcasted_iota(jnp.int32, (1, 128), 1)
    one = jnp.where(lane < 16, tail.astype(F32), 0.0).astype(BF)
    two = jnp.where((lane >= 16) & (lane < 32), tail.astype(F32), 0.0).astype(BF)
    halves = [slice(0, 256), slice(256, 512)]
    rows = [mm(low, one[h]) for h in halves]
    rows += [mm(high, one[h]) + mm(left, two[h]) for h in halves]
    across = jnp.transpose(jnp.concatenate(rows, 0))
    vec[...] = across[:16] + across[16:32]
    chip = lax.broadcasted_iota(jnp.int32, (64, 512), 0)
    place = lax.broadcasted_iota(jnp.int32, (64, 512), 1)
    of_chip = mm((place == 8 * chip).astype(F32).astype(BF), tail).astype(BF)
    b_up[...] = jnp.sum(jnp.where(own_lanes(), mm(of_chip, lanes_of()), 0.0), 0, keepdims=True)
    slabs = [
        g[:, 7040 + 768 * k : 7808 + 768 * k].astype(F32).reshape(64, 1, 8, 768) for k in range(3)
    ]
    w_down[...] = jnp.concatenate(slabs, 1).reshape(1536, 768).astype(BF)
    loads[3].wait()
    loads[4].wait()
    natural(1152, 768, 5760, left, (w_kv, w_kv, 384))
    natural(1920, 384, 6528, left, (w_query, w_query, 384))
    loads[5].wait()
    natural(2304, 1536, 4608, right, (w_up, w_up, 384))
    natural(3840, 768, 6144, right, (w_self, w_cross, 0))


def unpack(gathered):
    outs = ((768, 1152), (768, 768), (768, 384), (768, 1536), (384, 768), (384, 768), (1536, 768))
    return pl.pallas_call(
        unpack_kernel,
        out_shape=(
            *[shape(o, BF) for o in outs],
            shape((16, 768), F32),
            shape((1, 1536), F32),
        ),
        in_specs=[HBM],
        out_specs=(VMEM,) * 9,
        scratch_shapes=[pltpu.VMEM((512, 9344), BF), pltpu.SemaphoreType.DMA((6,))],
        compiler_params=params(46),
        cost_estimate=cost(4e9, 20e6),
        name="unpack",
    )(gathered)


def natural_row(at_slot, twelfth):
    return at_slot * 6 + twelfth + jnp.where(twelfth >= 6, 378, 0)


def index_kernel(place, columns):
    core, chip = place[0], place[1]

    def target_of(order, slot):
        first = slot * 0 + core == 0
        target = 0
        for axis, digit in zip(order, (slot >> 4, (slot >> 2) & 3, slot & 3)):
            step = STRIDE[axis]
            here = lax.rem(lax.div(chip, step), 4)
            other = jnp.where(
                first, jnp.where(digit == 1, 3, jnp.maximum(digit, 1) - 1), digit ^ (digit >> 1)
            )
            target = target + (here ^ other) * step
        return target

    def out_pick(at_slot, eight):
        return jnp.where(eight < 6, at_slot * 6 + eight, -1)

    at = lax.broadcasted_iota(jnp.int32, (512, 1), 0)
    eight = at & 7
    targets = [target_of(order, at >> 3) for order in ORDERS]
    values = []
    for target in targets:
        values += [natural_row(target, eight), natural_row(target, 8 + (eight & 3)) - 384]
    values += [out_pick(target, eight) for target in targets]
    values += [target * 8 + eight for target in targets] + [jnp.where(eight == 0, targets[2], -1)]
    for i in range(16):
        columns[:, i : i + 1] = values[i] if i < len(values) else at * 0


def indices(place):
    return staged(
        "indices",
        index_kernel,
        (place,),
        (),
        [shape((512, 16), jnp.int32)],
        1e6,
    )[0]


def image_pick_kernel(pick, tokens, *outs):
    for turn, out in enumerate(outs):
        out[...] = tokens[pick[turn]]


def image_pick(pick, tokens):
    return staged(
        "image_pick", image_pick_kernel, (pick,), (tokens,), [shape((188, 768), BF)] * 4, 1e6
    )


def image_stack_kernel(v0, v1, v2, v3, out, wide):
    wide[188:192] = jnp.zeros((4, 768), F32)
    for turn, value in enumerate((v0, v1, v2, v3)):
        wide[0:188] = value[...].astype(F32)
        out[192 * turn : 192 * turn + 192] = wide[...].astype(BF)


def image_stack(values):
    return staged(
        "image_stack",
        image_stack_kernel,
        (),
        values,
        [shape((768, 768), BF)],
        1e6,
        [pltpu.VMEM((192, 768), F32)],
    )[0]


def image_forward_kernel(vec, w_kv, own, other, kv, normed):
    row = lax.broadcasted_iota(jnp.int32, (192, 1), 0)
    for image in range(8):
        source, here = (own, 192 * image) if image < 4 else (other, 192 * image - 768)
        xhat, _ = normalize(source[here : here + 192].astype(F32))
        at = slice(192 * image, 192 * image + 192)
        normed[at] = jnp.where(row < 188, xhat * vec[2:3] + vec[6:7], 0.0).astype(BF)
        kv[at] = mm(normed[at], w_kv[...]).astype(BF)


def image_forward(vec, w_kv, own, other):
    return staged(
        "image_forward",
        image_forward_kernel,
        (),
        (vec, w_kv, own, other),
        (shape((1536, 768), BF), shape((1536, 768), BF)),
        2e9,
    )


def cross_forward_kernel(
    info, vec, text, mine, got, w_query, kv, w_out, after, normed, queries, mixed, part
):
    after[...] = text[...].astype(F32) + (mine[...] + got[...])
    xhat, _ = normalize(after[...])
    normed[...] = (xhat * vec[1:2] + vec[5:6]).astype(BF)
    queries[...] = mm(normed[...], w_query[...]).astype(BF)
    for row in range(2):
        allowed = cross_allowed(info, row)
        at = slice(128 * row, 128 * row + 128)
        for j in range(3):
            lanes = slice(128 * j, 128 * j + 128)
            q = stacked(queries[at, lanes]) * 0.125
            k = row_keys(kv, row, lanes)
            v = row_keys(kv, row, slice(384 + 128 * j, 512 + 128 * j))
            probs = softmax(mm_t(q, k), allowed)
            mixed[at, lanes] = merged(mm(probs.astype(BF), v)).astype(BF)
    part[...] = mm(mixed[...], w_out[...])


def cross_forward(info, vec, text, mine, got, kv, w_query, w_out):
    return staged(
        "cross_forward",
        cross_forward_kernel,
        (info,),
        (vec, text, mine, got, w_query, kv, w_out),
        (shape((256, 768), F32), shape((256, 768), BF), shape((256, 384), BF), shape((256, 384), BF), shape((256, 768), F32)),
        3e9,
    )


def feed_kernel(
    info, vec, b_up, before, mine, got, w_up, w_down, grad,
    after, normed, active, hidden_low, to_mine, to_other, back, sums,
    part,
):
    after[...] = before[...] + (mine[...] + got[...])
    xhat, _ = normalize(after[...])
    normed[...] = (xhat * vec[3:4] + vec[7:8]).astype(BF)
    part[...] = jnp.zeros((256, 768), F32)
    for k in range(3):
        lanes = slice(512 * k, 512 * k + 512)
        down = w_down[lanes]
        hidden = mm(normed[...], w_up[:, lanes]) + b_up[:, lanes]
        cdf = 0.5 * (1.0 + lax.erf(hidden * 0.7071067811865476))
        active[:, lanes] = (hidden * cdf).astype(BF)
        slope = cdf + hidden * (jnp.exp(-0.5 * hidden * hidden) * 0.3989422804014327)
        part[...] += mm(active[:, lanes], down)
        hidden_low[:, lanes] = (mm_t(grad[...], down) * slope).astype(BF)
    back[...] = mm_t(hidden_low[...], w_up[...])
    sums[...] = jnp.concatenate(
        [
            jnp.sum(back[...] * xhat, 0, keepdims=True),
            jnp.sum(back[...], 0, keepdims=True),
            jnp.zeros((6, 768), F32),
        ],
        0,
    )
    core = info[0]
    bias = vec[8:9]
    for row in range(2):
        at = pl.ds(pl.multiple_of(128 * row + 64 * core, 64), 64)
        to_mine[64 * row : 64 * row + 64] = after[at] + part[at] + bias
        at = pl.ds(pl.multiple_of(128 * row + 64 * (1 - core), 64), 64)
        to_other[64 * row : 64 * row + 64] = part[at]


def feed(info, vec, b_up, before, mine, got, w_up, w_down, grad):
    return staged(
        "feed",
        feed_kernel,
        (info,),
        (vec, b_up, before, mine, got, w_up, w_down, grad),
        (shape((256, 768), F32), shape((256, 768), BF), shape((256, 1536), BF), shape((256, 1536), BF), shape((128, 768), F32), shape((128, 768), F32), shape((256, 768), F32), shape((8, 768), F32)),
        3e9,
        [pltpu.VMEM((256, 768), F32)],
    )


def laid_out(weight, qa, qb, width):
    top = mm(qa, weight)
    rest = mm(qb, weight[384:])
    n = weight.shape[1]
    upper = lax.broadcasted_iota(jnp.int32, (512, 1), 0) % 8 < 4
    tail = rest[:, width:]
    if n - width < width:
        tail = jnp.concatenate([tail, jnp.zeros((512, 2 * width - n), F32)], 1)
    return top, jnp.where(upper, rest[:, :width], tail)


def put(keep, send, lanes, value):
    keep[:, lanes] = value[:256].astype(BF)
    send[:, lanes] = value[256:].astype(BF)


def feed_grads_kernel(normed, active, hidden_low, grad, index, *outs):
    keeps, sends, up_rows = outs[0:3], outs[3:6], outs[6]
    d_up = t_mm(normed[...], hidden_low[...]).astype(BF)
    total = jnp.sum(hidden_low[...].astype(F32), 0, keepdims=True)
    of_chip = mm_t(jnp.where(own_lanes(), total, 0.0).astype(BF), lanes_of()).astype(BF)
    up_rows[...] = mm(placed(index, 12, 64), of_chip)
    for p in range(3):
        qa, qb = placed(index, 2 * p, 768), placed(index, 2 * p + 1, 384)
        top, rest = laid_out(d_up[:, 512 * p : 512 * p + 512], qa, qb, 256)
        put(keeps[p], sends[p], slice(0, 512), top)
        put(keeps[p], sends[p], slice(512, 768), rest)
    d_down = t_mm(active[...], grad[...]).reshape(64, 3, 8, 768)
    slabs = [placed(index, 9 + p, 512) for p in range(3)]
    for k in range(3):
        rows = d_down[:, k].reshape(512, 768).astype(BF)
        for p, slab in enumerate(slabs):
            moved = mm(slab, rows[:, 256 * p : 256 * p + 256])
            put(keeps[p], sends[p], slice(768 + 256 * k, 1024 + 256 * k), moved)


def feed_grads(normed, active, hidden_low, grad, index):
    return staged(
        "feed_grads",
        feed_grads_kernel,
        (),
        (normed, active, hidden_low, grad, index),
        (*[shape((256, 1536), BF)] * 6, shape((512, 128), F32)),
        6e9,
    )


def cross_backward_kernel(
    info, vec, grad, mine, got, after, w_out, queries, kv, w_query, before,
    stream, low, dq, dkv, back, sums,
):
    xhat, inv = normalize(after[...])
    step = norm_back(mine[...] + got[...], vec[3:4], xhat, inv)
    stream[...] = grad[...].astype(F32) + step
    low[...] = stream[...].astype(BF)
    mixed_grad = mm_t(low[...], w_out[...]).astype(BF)
    for row in range(2):
        allowed = cross_allowed(info, row)
        at = slice(128 * row, 128 * row + 128)
        for j in range(3):
            lanes = slice(128 * j, 128 * j + 128)
            value_lanes = slice(384 + 128 * j, 512 + 128 * j)
            q = stacked(queries[at, lanes]) * 0.125
            do = stacked(mixed_grad[at, lanes])
            k = row_keys(kv, row, lanes)
            v = row_keys(kv, row, value_lanes)
            probs = softmax(mm_t(q, k), allowed)
            ds = softmax_back(probs, mm_t(do, v))
            dq[at, lanes] = (merged(mm(ds, k)) * 0.125).astype(BF)
            dk = t_mm(ds, q).astype(BF)
            dv = t_mm(probs.astype(BF), do).astype(BF)
            for value, where in ((dk, lanes), (dv, value_lanes)):
                dkv[384 * row : 384 * row + 384, where] = value[:384]
                dkv[768 + 384 * row : 1152 + 384 * row, where] = value[384:]
    back[...] = mm_t(dq[...], w_query[...])
    xhat, _ = normalize(before[...])
    sums[...] = jnp.concatenate(
        [
            jnp.sum(back[...] * xhat, 0, keepdims=True),
            jnp.sum(back[...], 0, keepdims=True),
            jnp.zeros((6, 768), F32),
        ],
        0,
    )


def cross_backward(info, vec, grad, mine, got, after, w_out, queries, kv, w_query, before):
    return staged(
        "cross_backward",
        cross_backward_kernel,
        (info,),
        (vec, grad, mine, got, after, w_out, queries, kv, w_query, before),
        (shape((256, 768), F32), shape((256, 768), BF), shape((256, 384), BF), shape((1536, 768), BF), shape((256, 768), F32), shape((8, 768), F32)),
        5e9,
    )


def cross_part(p, weight, mixed, low, index, keep, send):
    qa, qb = placed(index, 2 * p, 768), placed(index, 2 * p + 1, 384)
    top, rest = laid_out(weight, qa, qb, 256)
    put(keep, send, slice(0, 384), top)
    put(keep, send, slice(384, 640), rest)
    d_out = t_mm(mixed[...], low[:, 256 * p : 256 * p + 256]).astype(BF)
    put(keep, send, slice(640, 896), mm(placed(index, 6 + p, 384), d_out))


def image_grads_kernel(image_normed, dkv, mixed, low, index, keep0, keep1, send0, send1):
    d_kv = t_mm(image_normed[...], dkv[...]).astype(BF)
    cross_part(0, d_kv[:, :384], mixed, low, index, keep0, send0)
    cross_part(1, d_kv[:, 384:], mixed, low, index, keep1, send1)


def image_grads(image_normed, dkv, mixed, low, index):
    return staged(
        "image_grads",
        image_grads_kernel,
        (),
        (image_normed, dkv, mixed, low, index),
        [shape((256, 896), BF)] * 4,
        4e9,
    )


def query_grads_kernel(normed, dq, mixed, low, index, keep, send):
    d_query = t_mm(normed[...], dq[...]).astype(BF)
    cross_part(2, d_query, mixed, low, index, keep, send)


def query_grads(normed, dq, mixed, low, index):
    return staged(
        "query_grads",
        query_grads_kernel,
        (),
        (normed, dq, mixed, low, index),
        [shape((256, 896), BF)] * 2,
        1e9,
    )


def image_part_kernel(dkv, w_kv, out):
    out[...] = mm_t(dkv[768:], w_kv[...]).astype(BF)


def image_part(dkv, w_kv):
    return staged(
        "image_part",
        image_part_kernel,
        (),
        (dkv, w_kv),
        (shape((768, 768), BF),),
        1e9,
    )


def image_backward_kernel(vec, dkv, w_kv, got, own, out, low1, low2, low3, sums):
    total = [jnp.zeros((1, 768), F32)] * 2
    for image, result in enumerate((out, low1, low2, low3)):
        at = slice(192 * image, 192 * image + 192)
        dy = mm_t(dkv[at], w_kv[...]) + got[at].astype(F32)
        xhat, inv = normalize(own[at].astype(F32))
        total = [
            total[0] + jnp.sum(dy * xhat, 0, keepdims=True),
            total[1] + jnp.sum(dy, 0, keepdims=True),
        ]
        result[...] = norm_back(dy, vec[2:3], xhat, inv)[:188].astype(result.dtype)
    sums[...] = jnp.concatenate(total + [jnp.zeros((6, 768), F32)], 0)


def image_backward(vec, dkv, w_kv, got, own):
    return staged(
        "image_backward",
        image_backward_kernel,
        (),
        (vec, dkv, w_kv, got, own),
        (shape((188, 768), F32), *[shape((188, 768), BF)] * 3, shape((8, 768), F32)),
        1e9,
    )


def self_backward_kernel(
    info, vec, stream_in, mine, got, before, w_out, joined, w_qkv, text,
    stream_mine, low, d_joined, to_mine, to_other, sums,
    stream, back,
):
    xhat, inv = normalize(before[...])
    stream[...] = stream_in[...] + norm_back(mine[...] + got[...], vec[1:2], xhat, inv)
    low[...] = stream[...].astype(BF)
    mixed_grad = mm_t(low[...], w_out[...]).astype(BF)
    for row in range(2):
        allowed = self_allowed(info, row)
        at = slice(128 * row, 128 * row + 128)
        for j in range(3):
            lanes = [slice(384 * i + 128 * j, 384 * i + 128 * j + 128) for i in range(3)]
            q = stacked(joined[at, lanes[0]]) * 0.125
            k = joined[at, lanes[1]]
            v = joined[at, lanes[2]]
            do = stacked(mixed_grad[at, lanes[0]])
            probs = softmax(mm_t(q, k), allowed)
            ds = softmax_back(probs, mm_t(do, v))
            d_joined[at, lanes[0]] = (merged(mm(ds, k)) * 0.125).astype(BF)
            d_joined[at, lanes[1]] = t_mm(ds, q).astype(BF)
            d_joined[at, lanes[2]] = t_mm(probs.astype(BF), do).astype(BF)
    back[...] = mm_t(d_joined[...], w_qkv[...])
    xhat, _ = normalize(text[...].astype(F32))
    sums[...] = jnp.concatenate(
        [
            jnp.sum(back[...] * xhat, 0, keepdims=True),
            jnp.sum(back[...], 0, keepdims=True),
            jnp.zeros((6, 768), F32),
        ],
        0,
    )
    core = info[0]
    for row in range(2):
        at = pl.ds(pl.multiple_of(128 * row + 64 * core, 64), 64)
        stream_mine[64 * row : 64 * row + 64] = stream[at]
        to_mine[64 * row : 64 * row + 64] = back[at]
        at = pl.ds(pl.multiple_of(128 * row + 64 * (1 - core), 64), 64)
        to_other[64 * row : 64 * row + 64] = back[at]


def self_backward(info, vec, stream_in, mine, got, before, w_out, joined, w_qkv, text):
    return staged(
        "self_backward",
        self_backward_kernel,
        (info,),
        (vec, stream_in, mine, got, before, w_out, joined, w_qkv, text),
        (shape((128, 768), F32), shape((256, 768), BF), shape((256, 1152), BF), shape((128, 768), F32), shape((128, 768), F32), shape((8, 768), F32)),
        3e9,
        [pltpu.VMEM((256, 768), F32), pltpu.VMEM((256, 768), F32)],
    )


def self_grads_kernel(
    normed, d_joined, mixed, low, sum0, sum1, sum2, sum3, grad, up_rows,
    index, e0, e1, e2, *outs,
):
    keeps, sends = outs[0:3], outs[3:6]
    for send, early in zip(sends, (e0, e1, e2)):
        send[:, :896] = early[...]
    d_qkv = t_mm(normed[...], d_joined[...]).astype(BF)
    d_out = t_mm(mixed[...], low[...]).astype(BF)
    for p in range(3):
        qa, qb = placed(index, 2 * p, 768), placed(index, 2 * p + 1, 384)
        o = placed(index, 6 + p, 384)
        top, rest = laid_out(d_qkv[:, 384 * p : 384 * p + 384], qa, qb, 256)
        moved = mm(o, d_out[:, 256 * p : 256 * p + 256])
        for at, value in ((0, top), (384, rest), (640, moved)):
            n = value.shape[1]
            keeps[p][:, at : at + n] = value[:256].astype(BF)
            sends[p][:, 896 + at : 896 + at + n] = value[256:].astype(BF)
    down_sum = jnp.sum(grad[...].astype(F32), 0, keepdims=True) * 0.5
    rows = [s[i : i + 1] for i in range(2) for s in (sum0, sum1, sum2, sum3)]
    rows = jnp.concatenate(rows + [down_sum, jnp.zeros((7, 768), F32)], 0).astype(BF)
    zero = jnp.zeros((16, 768), BF)
    first = jnp.concatenate([rows] + [zero] * 7, 0)
    second = jnp.concatenate([zero, rows] + [zero] * 6, 0)
    value = mm_t(qa, first) + mm_t(qb, second[:, 384:]) + up_rows[...]
    keeps[2][:, 896:1024] = value[:256].astype(BF)
    sends[2][:, 1792:1920] = value[256:].astype(BF)


def self_grads(normed, d_joined, mixed, low, sums, grad, up_rows, index, early):
    return staged(
        "self_grads",
        self_grads_kernel,
        (),
        (normed, d_joined, mixed, low, *sums, grad, up_rows, index, *early),
        (*[shape((256, n), BF) for n in (896, 896, 1024, 1792, 1792, 1920)],),
        3e9,
    )


def first_core(info, dims):
    return lax.broadcasted_iota(jnp.int32, dims, 0) * 0 + info[0] == 0


BLOCKS = ((0, 3, 384), (1, 2, 384), (2, 1, 384), (3, 1, 1536))


def halves_into(core, refs, target, sem):
    copies, here = [], 0
    for which, blocks, width in BLOCKS:
        for i in range(blocks):
            at = pl.multiple_of(2 * i * width + core * width, 128)
            copies.append(
                pltpu.make_async_copy(
                    refs[which].at[:, pl.ds(at, width)], target.at[:, pl.ds(here, width)],
                    sem.at[len(copies)],
                )
            )
            here += width
    return copies


def vector_rows(gain, bias, down_bias):
    total = jnp.zeros((6, 128), F32)
    for at, ref in ((0, gain), (4, bias), (8, down_bias)):
        n = ref.shape[0]
        i = lax.broadcasted_iota(jnp.int32, (n, 128), 0) + at
        j = lax.broadcasted_iota(jnp.int32, (n, 128), 1)
        total = total + t_mm(ref[...], ((i == j) | (i + 16 == j)).astype(F32).astype(BF))
    return total


def pack_swap_kernel(info, qkv, kv, query, up, gain, bias, down_bias, send, half, sem):
    copies = halves_into(1 - info[0], (qkv, kv, query, up), half, sem)
    for c in copies:
        c.start()
    send[:, 3840:] = vector_rows(gain, bias, down_bias).astype(BF)
    for c in copies:
        c.wait()
    send[:, :3840] = half[...]


def pack_slots_kernel(
    info, qkv, kv, query, up, self_out, cross_out, down, gain, bias, down_bias, up_bias, got,
    slot, twelve, half, outs, slabs, sem, sems,
):
    copies = halves_into(info[0], (qkv, kv, query, up), half, sem)
    others = [
        pltpu.make_async_copy(self_out, outs.at[0], sems.at[0]),
        pltpu.make_async_copy(cross_out, outs.at[1], sems.at[1]),
        pltpu.make_async_copy(down, slabs, sems.at[2]),
    ]
    for c in copies + others:
        c.start()
    first = first_core(info, (6, 128))
    mine = vector_rows(gain, bias, down_bias)
    other = got[:, 3840:].astype(F32)
    twelve[0:6, 4608:] = jnp.where(first, mine, other)
    twelve[6:12, 4608:] = jnp.where(first, other, mine)
    twelve[12:16, 4608:] = jnp.zeros((4, 128), F32)
    lane = lax.broadcasted_iota(jnp.int32, (8, 128), 1)
    row = lax.broadcasted_iota(jnp.int32, (8, 128), 0)
    vec = jnp.where(lane < 16, twelve[0:8, 4608:], 0.0)
    vec = vec + jnp.where((lane >= 16) & (lane < 32), twelve[8:16, 4608:], 0.0)
    i = lax.broadcasted_iota(jnp.int32, (24, 128), 0)
    j = lax.broadcasted_iota(jnp.int32, (24, 128), 1)
    units = mm(up_bias[...], (i + 64 == j).astype(F32).astype(BF))
    slot[:, 6912:7040] = (vec + jnp.where(row == 0, units, 0.0)).astype(BF)
    for c in copies:
        c.wait()
    first = first_core(info, (6, 3840))
    mine = half[...].astype(F32)
    other = got[:, :3840].astype(F32)
    twelve[0:6, :3840] = jnp.where(first, mine, other)
    twelve[6:12, :3840] = jnp.where(first, other, mine)
    for c in others:
        c.wait()
    twelve[0:6, 3840:4608] = outs[0].astype(F32)
    twelve[6:12, 3840:4608] = outs[1].astype(F32)
    slot[:, :4608] = twelve[0:8, :4608].astype(BF)
    twelve[0:4, :2304] = twelve[8:12, :2304]
    twelve[4:8, :2304] = twelve[8:12, 2304:4608]
    slot[:, 4608:6912] = twelve[0:8, :2304].astype(BF)
    wide = slabs[...].astype(F32)
    for k in range(3):
        at = 7040 + 768 * k
        slot[:, at : at + 768] = wide[8 * k : 8 * k + 8].astype(BF)


def packed(name, kernel, info, far, near, out, scratch):
    return pl.pallas_call(
        kernel,
        out_shape=out,
        in_specs=[SMEM] + [HBM] * len(far) + [VMEM] * len(near),
        out_specs=VMEM,
        scratch_shapes=scratch,
        compiler_params=params(60),
        cost_estimate=cost(1e6, 1e6),
        name=name,
    )(info, *far, *near)


def pack_swap(info, weights, vectors):
    return packed(
        "pack_swap",
        pack_swap_kernel,
        info,
        weights,
        vectors,
        shape((6, 3968), BF),
        [pltpu.VMEM((6, 3840), BF), pltpu.SemaphoreType.DMA((7,))],
    )


def pack_slots(info, weights, vectors, got, self_out, cross_out, down, up_bias):
    return packed(
        "pack_slots",
        pack_slots_kernel,
        info,
        (*weights, self_out, cross_out, down),
        (*vectors, up_bias, got),
        shape((8, 9344), BF),
        [
            pltpu.VMEM((16, 4736), F32),
            pltpu.VMEM((6, 3840), BF),
            pltpu.VMEM((2, 6, 768), BF),
            pltpu.VMEM((24, 768), BF),
            pltpu.SemaphoreType.DMA((7,)),
            pltpu.SemaphoreType.DMA((3,)),
        ],
    )


TWELVES = (
    [(0, 512, 256)] * 3 + [(1536, 384, 256)] * 3 + [(2432, 384, 256)] * 3
)


def finish_send_kernel(info, *refs):
    keeps, gots, (s0, s1, s2, send, own, twelve) = refs[:3], refs[3:6], refs[6:]
    sums = (s0, s1, s2)
    for p in range(3):
        sums[p][...] = keeps[p][...].astype(F32) + gots[p][...].astype(F32)
    here = 0
    for i, (at, n, width) in enumerate(TWELVES):
        ref = sums[i % 3]
        twelve[0:8, here : here + n] = ref[:, at : at + n]
        twelve[8:12, here : here + width] = ref[0:4, at + n : at + n + width]
        twelve[8:12, here + width : here + n] = ref[4:8, at + n : at + n + n - width]
        here += n
    vec = s2[:, 3328:]
    twelve[0:8, 3840:] = vec
    twelve[8:12, 3840:] = pltpu.roll(vec, 112, 1)[0:4]
    first = first_core(info, (6, 3968))
    send[...] = jnp.where(first, twelve[6:12], twelve[0:6])
    own[...] = jnp.where(first, twelve[0:6], twelve[6:12])


def finish_kernel(
    info, s0, s1, s2, own, got, qkv, out_self, query, kv, out_cross, up, down, gain, bias, down_bias
):
    sums = (s0, s1, s2)
    first = first_core(info, (6, 3840))
    low = jnp.where(first, own[:, :3840], got[:, :3840])
    high = jnp.where(first, got[:, :3840], own[:, :3840])
    for ref, begin, blocks, width in (
        (up, 0, 1, 1536), (kv, 1536, 2, 384), (query, 2304, 1, 384), (qkv, 2688, 3, 384),
    ):
        for i in range(blocks):
            at = begin + i * width
            ref[:, 2 * i * width : (2 * i + 1) * width] = low[:, at : at + width]
            ref[:, (2 * i + 1) * width : (2 * i + 2) * width] = high[:, at : at + width]
    for p in range(3):
        lanes = slice(256 * p, 256 * p + 256)
        out_self[:, lanes] = sums[p][0:6, 3072:3328]
        out_cross[:, lanes] = sums[p][0:6, 2176:2432]
        for k in range(3):
            at = 768 + 256 * k
            down[8 * k : 8 * k + 8, lanes] = sums[p][:, at : at + 256]
    total = jnp.concatenate([own[:, 3840:] + got[:, 3840:], jnp.zeros((122, 128), F32)], 0)
    across = jnp.transpose(total)
    gain[...] = across[0:4, 0:6]
    bias[...] = across[4:8, 0:6]
    down_bias[...] = across[8:9, 0:6]


def finish_send(info, keeps, gots):
    widths = [k.shape[1] for k in keeps]
    return staged(
        "finish_send",
        finish_send_kernel,
        (info,),
        (*keeps, *gots),
        [shape((8, n), F32) for n in widths] + [shape((6, 3968), F32)] * 2,
        1e6,
        [pltpu.VMEM((16, 3968), F32)],
        mib=8,
    )


def finish(info, sums, own, got):
    return staged(
        "finish",
        finish_kernel,
        (info,),
        (*sums, own, got),
        [
            shape(dims, F32)
            for dims in (
                (6, 2304), (6, 768), (6, 768), (6, 1536), (6, 768), (6, 3072), (24, 768), (4, 6), (4, 6),
                (1, 6),
            )
        ],
        1e6,
        mib=8,
    )


def text_finish_kernel(vec, text, stream, mine, got, out_mine, out_got, grad, out):
    xhat, inv = normalize(text[...].astype(F32))
    grad[...] = stream[...] + norm_back(mine[...] + got[...], vec[0:1], xhat, inv)
    out[...] = out_mine[...] + out_got[...]


def text_finish(vec, text, stream, mine, got, out_mine, out_got):
    return staged(
        "text_finish",
        text_finish_kernel,
        (),
        (vec, text, stream, mine, got, out_mine, out_got),
        [shape((128, 768), F32)] * 2,
        1e6,
        mib=8,
    )


def image_finish_kernel(pick, v0, v1, v2, v3, out):
    values = [v[...].astype(F32) for v in (v0, v1, v2, v3)]
    for image in range(4):
        total = values[3]
        for turn in range(3):
            total = jnp.where(pick[turn] == image, values[turn], total)
        out[:, image, :] = total


def image_finish(pick, values):
    out = staged(
        "image_finish",
        image_finish_kernel,
        (pick,),
        values,
        [shape((188, 4, 768), F32)],
        1e6,
    )[0]
    return jnp.transpose(out, (1, 0, 2))


def combine_kernel(plan, *refs):
    at = 0
    ins = []
    for keeps, gots in plan:
        ins.append((refs[at : at + len(keeps)], refs[at + len(keeps) : at + len(keeps) + len(gots)]))
        at += len(keeps) + len(gots)
    outs = refs[at:]
    for p, (keeps, gots) in enumerate(ins):
        here = 0
        edges = []
        for ref in keeps:
            edges.append((here, here + ref.shape[1], ref))
            here += ref.shape[1]
        here = 0
        for ref in gots:
            for low, high, keep in edges:
                a, b = max(low, here), min(high, here + ref.shape[1])
                if a >= b:
                    continue
                total = keep[:, a - low : b - low].astype(F32) + ref[:, a - here : b - here].astype(F32)
                half = total.shape[0] // 2
                outs[2 * p][:, a:b] = total[:half].astype(BF)
                outs[2 * p + 1][:, a:b] = total[half:].astype(BF)
            here += ref.shape[1]


def combine(parts):
    plan, args, outs = [], [], []
    for keeps, gots in parts:
        plan.append(([k.shape[1] for k in keeps], [g.shape[1] for g in gots]))
        args += [*keeps, *gots]
        rows, width = keeps[0].shape[0], sum(k.shape[1] for k in keeps)
        outs += [shape((rows // 2, width), BF)] * 2
    got = staged(
        "combine", lambda *refs: combine_kernel(plan, *refs), (), args, outs, 1e6
    )
    return [(got[2 * p], got[2 * p + 1]) for p in range(len(parts))]


def send_step(step, values, parts=(0, 1, 2)):
    v0, v1 = ((1, 3), (3, 1))[step % 2]
    return [
        lax.ppermute(v, BOTH, xor_pairs(ORDERS[p][step // 2], v0, v1)) for v, p in zip(values, parts)
    ]


def after(value, *others):
    return lax.optimization_barrier((value, *others))[0]


def image_moves(images, way):
    once = [(core + i, core + (i + 16 * way) % 64) for core in (0, 64) for i in range(64)]
    first, second, third = images
    return [
        lax.ppermute(first, BOTH, once),
        move_on(second),
        lax.ppermute(third, BOTH, [(j, i) for i, j in once]),
    ]


def move_on(image):
    route = [(i, (i + 16) % 64) for i in range(64)]
    return lax.ppermute(image, BOTH, route + [(64 + j, 64 + i) for i, j in route])


def on_device(
    text_input,
    image_tokens,
    output_grad,
    segment_starts,
    caption_image,
    image_counts,
    norm_gain,
    norm_bias,
    self_qkv,
    self_out,
    cross_q,
    cross_kv,
    cross_out,
    up_weight,
    up_bias,
    down_weight,
    down_bias,
):
    core = lax.axis_index("seq")
    chip = lax.axis_index("batch")
    first = core == 0

    def ordered(own, other, axis):
        return jnp.where(
            first, jnp.concatenate([own, other], axis), jnp.concatenate([other, own], axis)
        )

    place = jnp.stack([core, chip]).astype(jnp.int32)
    weights = (self_qkv, cross_kv, cross_q, up_weight)
    vectors = (norm_gain, norm_bias, down_bias[None])
    got = swap(pack_swap(place, weights, vectors))
    slot = pack_slots(
        place, weights, vectors, got, self_out, cross_out, down_weight, up_bias[None]
    )
    gathered = lax.all_gather(slot, "batch", axis=0, tiled=True)

    late_text, late_grad = after(text_input, slot), after(output_grad, slot)
    text = ordered(late_text, swap(late_text), 1).reshape(256, 768)
    grad = ordered(late_grad, swap(late_grad), 1).reshape(256, 768)

    group_images = after(caption_image, slot).reshape(64, 8)
    my_captions = lax.dynamic_index_in_dim(group_images, chip, 0, keepdims=False)
    limits = jnp.take(image_counts, my_captions).reshape(4, 2)
    limits = jnp.where(first, jnp.concatenate([limits[:, 0], limits[:, 1]]), jnp.concatenate([limits[:, 1], limits[:, 0]]))
    turns = jnp.arange(4)
    targets = (chip - turns * 16) % 64
    wanted = group_images[targets, 2 * turns + core]
    local_pick = wanted - (core * 64 + chip) * 4
    outgoing = image_pick(after(local_pick, slot), image_tokens)
    received = [outgoing[0], *image_moves(outgoing[1:], -1)]
    received[2] = move_on(received[2])
    own_images = image_stack(received)
    other_images = swap(own_images)
    info = jnp.concatenate(
        [core[None], segment_starts.reshape(8), limits, jnp.zeros((15,), jnp.int32)]
    ).astype(jnp.int32)

    column_index = indices(after(place, slot))

    gathered, info, grad, text, column_index, own_images, other_images = lax.optimization_barrier(
        (gathered, info, grad, text, column_index, own_images, other_images)
    )
    w_qkv, w_kv, w_query, w_up, w_self, w_cross, w_down, vec, b_up = unpack(gathered)
    part, joined, mixed_self, normed_one = self_forward(info, vec, w_qkv, w_self, text)
    got = swap(part)
    kv, image_normed = image_forward(vec, w_kv, own_images, other_images)
    after_self, normed_two, q_cross, mixed_cross, part = cross_forward(
        info, vec, text, part, got, kv, w_query, w_cross
    )
    after_cross, normed_three, active, hidden_low, text_mine, text_other, part, sum3 = feed(
        info, vec, b_up, after_self, part, swap(part), w_up, w_down, grad
    )
    text_got = swap(text_other)
    got = swap(part)

    grads = feed_grads(normed_three, active, hidden_low, grad, column_index)
    keep_one, up_rows = grads[0:3], grads[6]
    got_one, z_send = send_step(0, grads[3:5], (0, 1)), grads[5]
    stream_two, cross_low, dq, dkv, part, sum1 = cross_backward(
        info, vec, after(grad, keep_one[0]), part, got, after_cross, w_cross, q_cross, kv, w_query, after_self
    )
    got = swap(part)
    image_send = image_part(dkv, w_kv)[0]
    *rows_back, sum2 = image_backward(vec, dkv, w_kv, swap(image_send), own_images)
    returned = [rows_back[0], *image_moves(rows_back[1:], 1)]
    k_keep, v_keep, k_send, v_send = image_grads(
        image_normed, after(dkv, sum2), mixed_cross, cross_low, column_index
    )
    dq, k_keep, *moved = lax.optimization_barrier((dq, k_keep, *returned[1:]))
    returned = [returned[0], moved[0], move_on(moved[1]), moved[2]]
    got_one += send_step(0, [after(z_send, moved[0])], (2,))
    q_keep, q_send = query_grads(normed_two, dq, mixed_cross, cross_low, column_index)
    keep_two, early = [k_keep, v_keep, q_keep], [k_send, v_send, q_send]
    stream_one, self_low, d_joined, one_mine, one_other, sum0 = self_backward(
        info, vec, after(stream_two, q_keep), part, got, after_self, w_self, joined,
        w_qkv, text,
    )
    self_low, late, *got_one[:2] = lax.optimization_barrier((self_low, returned[2], *got_one[:2]))
    returned[2] = late
    grads = self_grads(
        normed_one, d_joined, mixed_self, self_low, (sum0, sum1, sum2, sum3), grad, up_rows,
        column_index, early,
    )
    keep_three = grads[0:3]
    sends, got_one[2] = lax.optimization_barrier((grads[3:6], got_one[2]))
    got_two = send_step(0, sends)
    one_got = swap(one_other)
    image_grad = image_finish(after(local_pick, grads[3]), returned)
    text_grad, text_output = text_finish(
        after(vec, grads[3]), text_input.reshape(128, 768), stream_one, one_mine, one_got, text_mine,
        text_got,
    )
    got_two, image_grad, text_grad = lax.optimization_barrier((got_two, image_grad, text_grad))
    pairs = []
    for p in range(3):
        pairs += combine([([keep_one[p], keep_two[p], keep_three[p]], [got_one[p], got_two[p]])])
    for step in range(1, 6):
        got_step = send_step(step, [s for _, s in pairs])
        step_parts = [([k], [g]) for (k, _), g in zip(pairs, got_step)]
        if step == 5:
            *sums, send, own = finish_send(place, [k for k, _ in pairs], got_step)
        elif step == 1:
            pairs = [combine([one])[0] for one in step_parts]
        else:
            pairs = combine(step_parts)

    text_grad, text_output = text_grad.reshape(2, 64, 768), text_output.reshape(2, 64, 768)

    (
        qkv_grad, self_grad, query_grad, kv_grad, cross_grad, up_grad, down_grad, gain_grad, bias_grad,
        down_bias_grad,
    ) = finish(place, sums, own, swap(send))
    up_bias_grad = sums[2][0, 3392:3416]
    return (
        text_output,
        text_grad,
        image_grad,
        gain_grad,
        bias_grad,
        qkv_grad,
        self_grad,
        query_grad,
        kv_grad,
        cross_grad,
        up_grad,
        up_bias_grad,
        down_grad,
        down_bias_grad[0],
    )


def solution(mesh):
    rows = P("batch", "seq", None)
    shard = P(BOTH, None)
    wide = P(None, BOTH)
    return jax.shard_map(
        on_device,
        mesh=mesh,
        in_specs=(
            rows, P(BOTH, None, None), rows, P("batch", None), P(), P(), wide, wide,
            shard, shard, shard, shard, shard, shard, P(BOTH), shard, P(BOTH),
        ),
        out_specs=(
            rows, rows, P(BOTH, None, None), wide, wide,
            shard, shard, shard, shard, shard, shard, P(BOTH), shard, P(BOTH),
        ),
        check_vma=False,
    )
```

```python
import math

import jax
import jax.numpy as jnp
from jax import lax
from jax.experimental import pallas as pl
from jax.experimental.pallas import tpu as pltpu
from jax.sharding import PartitionSpec as P

HEADS = 12
HEAD_DIM = 64
EPSILON = 1e-05
MASKED_SCORE = -1e30
BF = jnp.bfloat16
F32 = jnp.float32
BOTH = ("seq", "batch")
STRIDE = {"z": 16, "y": 4, "x": 1}
ORDERS = (("x", "z", "y"), ("y", "x", "z"), ("z", "y", "x"))


def xor_pairs(axis, value0, value1):
    step, out = STRIDE[axis], []
    for core, value in ((0, value0), (1, value1)):
        for chip in range(64):
            at = chip // step % 4
            out.append((core * 64 + chip, core * 64 + chip + ((at ^ value) - at) * step))
    return out


def swap(value):
    return lax.ppermute(value, "seq", [(0, 1), (1, 0)])


def mm(a, b):
    return jnp.dot(a, b, preferred_element_type=F32)


def mm_t(a, b):
    return lax.dot_general(a, b, (((1,), (1,)), ((), ())), preferred_element_type=F32)


def t_mm(a, b):
    return lax.dot_general(a, b, (((0,), (0,)), ((), ())), preferred_element_type=F32)


def normalize(values):
    center = jnp.mean(values, -1, keepdims=True)
    centred = values - center
    spread = jnp.mean(centred * centred, -1, keepdims=True)
    inv = lax.rsqrt(spread + EPSILON)
    return centred * inv, inv


def norm_back(grad, gain, xhat, inv):
    scaled = grad * gain
    return inv * (
        scaled
        - jnp.mean(scaled, -1, keepdims=True)
        - xhat * jnp.mean(scaled * xhat, -1, keepdims=True)
    )


VMEM = pl.BlockSpec(memory_space=pltpu.VMEM)
SMEM = pl.BlockSpec(memory_space=pltpu.SMEM)
HBM = pl.BlockSpec(memory_space=pltpu.HBM)


def shape(dims, dtype):
    return jax.ShapeDtypeStruct(dims, dtype)


def cost(flops, moved):
    return pl.CostEstimate(
        flops=int(flops / 64), bytes_accessed=int(moved / 64), transcendentals=0
    )


def params(mib):
    return pltpu.CompilerParams(vmem_limit_bytes=mib * 1024 * 1024)


def staged(name, kernel, scalars, ins, outs, work, scratch=(), mib=16):
    moved = sum(math.prod(v.shape) * v.dtype.itemsize for v in (*ins, *outs))
    return pl.pallas_call(
        kernel,
        out_shape=tuple(outs),
        in_specs=[SMEM] * len(scalars) + [VMEM] * len(ins),
        out_specs=(VMEM,) * len(outs),
        scratch_shapes=list(scratch),
        compiler_params=params(mib),
        cost_estimate=cost(work, moved),
        name=name,
    )(*scalars, *ins)


def placed(columns, i, size):
    place = lax.broadcasted_iota(jnp.int32, (512, size), 1)
    return (place == columns[:, i : i + 1]).astype(F32).astype(BF)


def segment_of(info, row, dims, axis):
    place = lax.broadcasted_iota(jnp.int32, dims, axis)
    total = jnp.full(dims, -1, jnp.int32)
    for j in range(4):
        total = total + (place >= info[1 + 4 * row + j]).astype(jnp.int32)
    return total


def low_lanes():
    return lax.broadcasted_iota(jnp.int32, (1, 128), 1) < 64


def stacked(pair):
    left = low_lanes()
    zero = jnp.zeros_like(pair)
    return jnp.concatenate([jnp.where(left, pair, zero), jnp.where(left, zero, pair)], 0)


def merged(two):
    n = two.shape[0] // 2
    return jnp.where(low_lanes(), two[:n], two[n:])


def softmax(scores, allowed):
    scores = jnp.where(allowed, scores, MASKED_SCORE)
    weights = jnp.exp(scores - jnp.max(scores, -1, keepdims=True))
    return weights * (1.0 / jnp.sum(weights, -1, keepdims=True))


def softmax_back(probs, dprobs):
    return (probs * (dprobs - jnp.sum(probs * dprobs, -1, keepdims=True))).astype(BF)


def self_allowed(info, row):
    at = segment_of(info, row, (128, 128), 0)
    key = segment_of(info, row, (128, 128), 1)
    i = lax.broadcasted_iota(jnp.int32, (128, 128), 0)
    j = lax.broadcasted_iota(jnp.int32, (128, 128), 1)
    allowed = (at == key) & (j <= i)
    return jnp.concatenate([allowed, allowed], 0)


def cross_allowed(info, row):
    core = info[0]
    lane = lax.broadcasted_iota(jnp.int32, (1, 768), 1)
    key = jnp.full((1, 768), -1, jnp.int32)
    images = (2 * row, 2 * row + 1, 4 + 2 * row, 5 + 2 * row)
    captions = (core, 2 + core, 1 - core, 3 - core)
    for block in range(4):
        limit = info[9 + images[block]]
        key = jnp.where(
            (lane >= 192 * block) & (lane < 192 * block + limit), captions[block], key
        )
    at = segment_of(info, row, (128, 1), 0)
    return jnp.concatenate([at, at], 0) == key


def row_keys(kv, row, lanes):
    return jnp.concatenate(
        [kv[384 * row : 384 * row + 384, lanes], kv[768 + 384 * row : 1152 + 384 * row, lanes]], 0
    )


def lanes_of():
    lane = lax.broadcasted_iota(jnp.int32, (128, 1536), 0)
    unit = lax.broadcasted_iota(jnp.int32, (128, 1536), 1)
    return (lane == 64 + lax.rem(unit, 24)).astype(F32).astype(BF)


def own_lanes():
    chip = lax.broadcasted_iota(jnp.int32, (64, 1536), 0) * 24
    unit = lax.broadcasted_iota(jnp.int32, (64, 1536), 1)
    return (unit >= chip) & (unit < chip + 24)


def self_forward_kernel(info, vec, w_qkv, w_out, text, part, joined, mixed, normed):
    xhat, _ = normalize(text[...].astype(F32))
    normed[...] = (xhat * vec[0:1] + vec[4:5]).astype(BF)
    joined[...] = mm(normed[...], w_qkv[...]).astype(BF)
    for row in range(2):
        allowed = self_allowed(info, row)
        at = slice(128 * row, 128 * row + 128)
        for j in range(3):
            q = stacked(joined[at, 128 * j : 128 * j + 128]) * 0.125
            k = joined[at, 384 + 128 * j : 512 + 128 * j]
            v = joined[at, 768 + 128 * j : 896 + 128 * j]
            probs = softmax(mm_t(q, k), allowed)
            mixed[at, 128 * j : 128 * j + 128] = merged(mm(probs.astype(BF), v)).astype(BF)
    part[...] = mm(mixed[...], w_out[...])


def self_forward(info, vec, w_qkv, w_out, text):
    return staged(
        "self_forward",
        self_forward_kernel,
        (info,),
        (vec, w_qkv, w_out, text),
        (
            shape((256, 768), F32),
            shape((256, 1152), BF),
            shape((256, 384), BF),
            shape((256, 768), BF),
        ),
        2e9,
    )


def rows_of_six(first, last, shift):
    row = lax.broadcasted_iota(jnp.int32, (192, 256), 0)
    place = lax.broadcasted_iota(jnp.int32, (192, 256), 1)
    chip = lax.div(row, 6)
    r = row - 6 * chip
    hit = (place == 8 * chip + r + shift) & (r >= first) & (r <= last)
    return hit.astype(F32).astype(BF)


def unpack_kernel(
    gathered, w_qkv, w_kv, w_query, w_up, w_self, w_cross, w_down, vec, b_up, g, sems
):
    spans = ((4608, 1152), (0, 1152), (6912, 2432), (5760, 1152), (1152, 1152), (2304, 2304))
    loads = [
        pltpu.make_async_copy(gathered.at[:, pl.ds(at, n)], g.at[:, pl.ds(at, n)], sems.at[i])
        for i, (at, n) in enumerate(spans)
    ]
    loads[0].start()
    loads[1].start()
    low, high = rows_of_six(0, 5, 0), rows_of_six(0, 1, 6)
    both = jnp.concatenate([low, high], 0)
    left, right = rows_of_six(2, 5, -2), rows_of_six(2, 5, 2)

    def natural(at, n, begin, rest, outs):
        for half in range(2):
            here = slice(256 * half, 256 * half + 256)
            there = slice(192 * half, 192 * half + 192)
            rows = mm(both, g[here, at : at + n])
            outs[0][there] = rows[:192].astype(BF)
            there = slice(outs[2] + 192 * half, outs[2] + 192 * half + 192)
            outs[1][there] = (rows[192:] + mm(rest, g[here, begin : begin + n])).astype(BF)

    loads[0].wait()
    loads[1].wait()
    for i in (2, 3, 4):
        loads[i].start()
    natural(0, 1152, 4608, left, (w_qkv, w_qkv, 384))
    loads[2].wait()
    loads[5].start()
    tail = g[:, 6912:7040]
    lane = lax.broadcasted_iota(jnp.int32, (1, 128), 1)
    one = jnp.where(lane < 16, tail.astype(F32), 0.0).astype(BF)
    two = jnp.where((lane >= 16) & (lane < 32), tail.astype(F32), 0.0).astype(BF)
    halves = [slice(0, 256), slice(256, 512)]
    rows = [mm(low, one[h]) for h in halves]
    rows += [mm(high, one[h]) + mm(left, two[h]) for h in halves]
    across = jnp.transpose(jnp.concatenate(rows, 0))
    vec[...] = across[:16] + across[16:32]
    chip = lax.broadcasted_iota(jnp.int32, (64, 512), 0)
    place = lax.broadcasted_iota(jnp.int32, (64, 512), 1)
    of_chip = mm((place == 8 * chip).astype(F32).astype(BF), tail).astype(BF)
    b_up[...] = jnp.sum(jnp.where(own_lanes(), mm(of_chip, lanes_of()), 0.0), 0, keepdims=True)
    slabs = [
        g[:, 7040 + 768 * k : 7808 + 768 * k].astype(F32).reshape(64, 1, 8, 768) for k in range(3)
    ]
    w_down[...] = jnp.concatenate(slabs, 1).reshape(1536, 768).astype(BF)
    loads[3].wait()
    loads[4].wait()
    natural(1152, 768, 5760, left, (w_kv, w_kv, 384))
    natural(1920, 384, 6528, left, (w_query, w_query, 384))
    loads[5].wait()
    natural(2304, 1536, 4608, right, (w_up, w_up, 384))
    natural(3840, 768, 6144, right, (w_self, w_cross, 0))


def unpack(gathered):
    outs = ((768, 1152), (768, 768), (768, 384), (768, 1536), (384, 768), (384, 768), (1536, 768))
    return pl.pallas_call(
        unpack_kernel,
        out_shape=(
            *[shape(o, BF) for o in outs],
            shape((16, 768), F32),
            shape((1, 1536), F32),
        ),
        in_specs=[HBM],
        out_specs=(VMEM,) * 9,
        scratch_shapes=[pltpu.VMEM((512, 9344), BF), pltpu.SemaphoreType.DMA((6,))],
        compiler_params=params(46),
        cost_estimate=cost(4e9, 20e6),
        name="unpack",
    )(gathered)


def natural_row(at_slot, twelfth):
    return at_slot * 6 + twelfth + jnp.where(twelfth >= 6, 378, 0)


def index_kernel(place, columns):
    core, chip = place[0], place[1]

    def target_of(order, slot):
        first = slot * 0 + core == 0
        target = 0
        for axis, digit in zip(order, (slot >> 4, (slot >> 2) & 3, slot & 3)):
            step = STRIDE[axis]
            here = lax.rem(lax.div(chip, step), 4)
            other = jnp.where(
                first, jnp.where(digit == 1, 3, jnp.maximum(digit, 1) - 1), digit ^ (digit >> 1)
            )
            target = target + (here ^ other) * step
        return target

    def out_pick(at_slot, eight):
        return jnp.where(eight < 6, at_slot * 6 + eight, -1)

    at = lax.broadcasted_iota(jnp.int32, (512, 1), 0)
    eight = at & 7
    targets = [target_of(order, at >> 3) for order in ORDERS]
    values = []
    for target in targets:
        values += [natural_row(target, eight), natural_row(target, 8 + (eight & 3)) - 384]
    values += [out_pick(target, eight) for target in targets]
    values += [target * 8 + eight for target in targets] + [jnp.where(eight == 0, targets[2], -1)]
    for i in range(16):
        columns[:, i : i + 1] = values[i] if i < len(values) else at * 0


def indices(place):
    return staged(
        "indices",
        index_kernel,
        (place,),
        (),
        [shape((512, 16), jnp.int32)],
        1e6,
    )[0]


def image_pick_kernel(pick, tokens, *outs):
    for turn, out in enumerate(outs):
        out[...] = tokens[pick[turn]]


def image_pick(pick, tokens):
    return staged(
        "image_pick", image_pick_kernel, (pick,), (tokens,), [shape((188, 768), BF)] * 4, 1e6
    )


def image_stack_kernel(v0, v1, v2, v3, out, wide):
    wide[188:192] = jnp.zeros((4, 768), F32)
    for turn, value in enumerate((v0, v1, v2, v3)):
        wide[0:188] = value[...].astype(F32)
        out[192 * turn : 192 * turn + 192] = wide[...].astype(BF)


def image_stack(values):
    return staged(
        "image_stack",
        image_stack_kernel,
        (),
        values,
        [shape((768, 768), BF)],
        1e6,
        [pltpu.VMEM((192, 768), F32)],
    )[0]


def image_forward_kernel(vec, w_kv, own, other, kv, normed):
    row = lax.broadcasted_iota(jnp.int32, (192, 1), 0)
    for image in range(8):
        source, here = (own, 192 * image) if image < 4 else (other, 192 * image - 768)
        xhat, _ = normalize(source[here : here + 192].astype(F32))
        at = slice(192 * image, 192 * image + 192)
        normed[at] = jnp.where(row < 188, xhat * vec[2:3] + vec[6:7], 0.0).astype(BF)
        kv[at] = mm(normed[at], w_kv[...]).astype(BF)


def image_forward(vec, w_kv, own, other):
    return staged(
        "image_forward",
        image_forward_kernel,
        (),
        (vec, w_kv, own, other),
        (shape((1536, 768), BF), shape((1536, 768), BF)),
        2e9,
    )


def cross_forward_kernel(
    info, vec, text, mine, got, w_query, kv, w_out, after, normed, queries, mixed, part
):
    after[...] = text[...].astype(F32) + (mine[...] + got[...])
    xhat, _ = normalize(after[...])
    normed[...] = (xhat * vec[1:2] + vec[5:6]).astype(BF)
    queries[...] = mm(normed[...], w_query[...]).astype(BF)
    for row in range(2):
        allowed = cross_allowed(info, row)
        at = slice(128 * row, 128 * row + 128)
        for j in range(3):
            lanes = slice(128 * j, 128 * j + 128)
            q = stacked(queries[at, lanes]) * 0.125
            k = row_keys(kv, row, lanes)
            v = row_keys(kv, row, slice(384 + 128 * j, 512 + 128 * j))
            probs = softmax(mm_t(q, k), allowed)
            mixed[at, lanes] = merged(mm(probs.astype(BF), v)).astype(BF)
    part[...] = mm(mixed[...], w_out[...])


def cross_forward(info, vec, text, mine, got, kv, w_query, w_out):
    return staged(
        "cross_forward",
        cross_forward_kernel,
        (info,),
        (vec, text, mine, got, w_query, kv, w_out),
        (shape((256, 768), F32), shape((256, 768), BF), shape((256, 384), BF), shape((256, 384), BF), shape((256, 768), F32)),
        3e9,
    )


def feed_kernel(
    info, vec, b_up, before, mine, got, w_up, w_down, grad,
    after, normed, active, hidden_low, to_mine, to_other, back, sums,
    part,
):
    after[...] = before[...] + (mine[...] + got[...])
    xhat, _ = normalize(after[...])
    normed[...] = (xhat * vec[3:4] + vec[7:8]).astype(BF)
    part[...] = jnp.zeros((256, 768), F32)
    for k in range(3):
        lanes = slice(512 * k, 512 * k + 512)
        down = w_down[lanes]
        hidden = mm(normed[...], w_up[:, lanes]) + b_up[:, lanes]
        cdf = 0.5 * (1.0 + lax.erf(hidden * 0.7071067811865476))
        active[:, lanes] = (hidden * cdf).astype(BF)
        slope = cdf + hidden * (jnp.exp(-0.5 * hidden * hidden) * 0.3989422804014327)
        part[...] += mm(active[:, lanes], down)
        hidden_low[:, lanes] = (mm_t(grad[...], down) * slope).astype(BF)
    back[...] = mm_t(hidden_low[...], w_up[...])
    sums[...] = jnp.concatenate(
        [
            jnp.sum(back[...] * xhat, 0, keepdims=True),
            jnp.sum(back[...], 0, keepdims=True),
            jnp.zeros((6, 768), F32),
        ],
        0,
    )
    core = info[0]
    bias = vec[8:9]
    for row in range(2):
        at = pl.ds(pl.multiple_of(128 * row + 64 * core, 64), 64)
        to_mine[64 * row : 64 * row + 64] = after[at] + part[at] + bias
        at = pl.ds(pl.multiple_of(128 * row + 64 * (1 - core), 64), 64)
        to_other[64 * row : 64 * row + 64] = part[at]


def feed(info, vec, b_up, before, mine, got, w_up, w_down, grad):
    return staged(
        "feed",
        feed_kernel,
        (info,),
        (vec, b_up, before, mine, got, w_up, w_down, grad),
        (shape((256, 768), F32), shape((256, 768), BF), shape((256, 1536), BF), shape((256, 1536), BF), shape((128, 768), F32), shape((128, 768), F32), shape((256, 768), F32), shape((8, 768), F32)),
        3e9,
        [pltpu.VMEM((256, 768), F32)],
    )


def laid_out(weight, qa, qb, width):
    top = mm(qa, weight)
    rest = mm(qb, weight[384:])
    n = weight.shape[1]
    upper = lax.broadcasted_iota(jnp.int32, (512, 1), 0) % 8 < 4
    tail = rest[:, width:]
    if n - width < width:
        tail = jnp.concatenate([tail, jnp.zeros((512, 2 * width - n), F32)], 1)
    return top, jnp.where(upper, rest[:, :width], tail)


def put(keep, send, lanes, value):
    keep[:, lanes] = value[:256].astype(BF)
    send[:, lanes] = value[256:].astype(BF)


def feed_grads_kernel(normed, active, hidden_low, grad, index, *outs):
    keeps, sends, up_rows = outs[0:2], outs[2:4], outs[4]
    d_up = t_mm(normed[...], hidden_low[...]).astype(BF)
    total = jnp.sum(hidden_low[...].astype(F32), 0, keepdims=True)
    of_chip = mm_t(jnp.where(own_lanes(), total, 0.0).astype(BF), lanes_of()).astype(BF)
    up_rows[...] = mm(placed(index, 12, 64), of_chip)
    for p in range(2):
        qa, qb = placed(index, 2 * p, 768), placed(index, 2 * p + 1, 384)
        top, rest = laid_out(d_up[:, 768 * p : 768 * p + 768], qa, qb, 384)
        put(keeps[p], sends[p], slice(0, 768), top)
        put(keeps[p], sends[p], slice(768, 1152), rest)
    d_down = t_mm(active[...], grad[...]).reshape(64, 3, 8, 768)
    slabs = [placed(index, 9 + p, 512) for p in range(2)]
    for k in range(3):
        rows = d_down[:, k].reshape(512, 768).astype(BF)
        for p, slab in enumerate(slabs):
            moved = mm(slab, rows[:, 384 * p : 384 * p + 384])
            put(keeps[p], sends[p], slice(1152 + 384 * k, 1536 + 384 * k), moved)


def feed_grads(normed, active, hidden_low, grad, index):
    return staged(
        "feed_grads",
        feed_grads_kernel,
        (),
        (normed, active, hidden_low, grad, index),
        (*[shape((256, 2304), BF)] * 4, shape((512, 128), F32)),
        6e9,
    )


def cross_backward_kernel(
    info, vec, grad, mine, got, after, w_out, queries, kv, w_query, before,
    stream, low, dq, dkv, back, sums,
):
    xhat, inv = normalize(after[...])
    step = norm_back(mine[...] + got[...], vec[3:4], xhat, inv)
    stream[...] = grad[...].astype(F32) + step
    low[...] = stream[...].astype(BF)
    mixed_grad = mm_t(low[...], w_out[...]).astype(BF)
    for row in range(2):
        allowed = cross_allowed(info, row)
        at = slice(128 * row, 128 * row + 128)
        for j in range(3):
            lanes = slice(128 * j, 128 * j + 128)
            value_lanes = slice(384 + 128 * j, 512 + 128 * j)
            q = stacked(queries[at, lanes]) * 0.125
            do = stacked(mixed_grad[at, lanes])
            k = row_keys(kv, row, lanes)
            v = row_keys(kv, row, value_lanes)
            probs = softmax(mm_t(q, k), allowed)
            ds = softmax_back(probs, mm_t(do, v))
            dq[at, lanes] = (merged(mm(ds, k)) * 0.125).astype(BF)
            dk = t_mm(ds, q).astype(BF)
            dv = t_mm(probs.astype(BF), do).astype(BF)
            for value, where in ((dk, lanes), (dv, value_lanes)):
                dkv[384 * row : 384 * row + 384, where] = value[:384]
                dkv[768 + 384 * row : 1152 + 384 * row, where] = value[384:]
    back[...] = mm_t(dq[...], w_query[...])
    xhat, _ = normalize(before[...])
    sums[...] = jnp.concatenate(
        [
            jnp.sum(back[...] * xhat, 0, keepdims=True),
            jnp.sum(back[...], 0, keepdims=True),
            jnp.zeros((6, 768), F32),
        ],
        0,
    )


def cross_backward(info, vec, grad, mine, got, after, w_out, queries, kv, w_query, before):
    return staged(
        "cross_backward",
        cross_backward_kernel,
        (info,),
        (vec, grad, mine, got, after, w_out, queries, kv, w_query, before),
        (shape((256, 768), F32), shape((256, 768), BF), shape((256, 384), BF), shape((1536, 768), BF), shape((256, 768), F32), shape((8, 768), F32)),
        5e9,
    )


def cross_part(p, weight, mixed, low, index, keep, send):
    qa, qb = placed(index, 2 * p, 768), placed(index, 2 * p + 1, 384)
    top, rest = laid_out(weight, qa, qb, 256)
    put(keep, send, slice(0, 384), top)
    put(keep, send, slice(384, 640), rest)
    d_out = t_mm(mixed[...], low[:, 256 * p : 256 * p + 256]).astype(BF)
    put(keep, send, slice(640, 896), mm(placed(index, 6 + p, 384), d_out))


def image_grads_kernel(image_normed, dkv, mixed, low, index, keep0, keep1, send0, send1):
    d_kv = t_mm(image_normed[...], dkv[...]).astype(BF)
    cross_part(0, d_kv[:, :384], mixed, low, index, keep0, send0)
    cross_part(1, d_kv[:, 384:], mixed, low, index, keep1, send1)


def image_grads(image_normed, dkv, mixed, low, index):
    return staged(
        "image_grads",
        image_grads_kernel,
        (),
        (image_normed, dkv, mixed, low, index),
        [shape((256, 896), BF)] * 4,
        4e9,
    )


def query_grads_kernel(normed, dq, mixed, low, index, keep, send):
    d_query = t_mm(normed[...], dq[...]).astype(BF)
    cross_part(2, d_query, mixed, low, index, keep, send)


def query_grads(normed, dq, mixed, low, index):
    return staged(
        "query_grads",
        query_grads_kernel,
        (),
        (normed, dq, mixed, low, index),
        [shape((256, 896), BF)] * 2,
        1e9,
    )


def image_part_kernel(dkv, w_kv, out):
    out[...] = mm_t(dkv[768:], w_kv[...]).astype(BF)


def image_part(dkv, w_kv):
    return staged(
        "image_part",
        image_part_kernel,
        (),
        (dkv, w_kv),
        (shape((768, 768), BF),),
        1e9,
    )


def image_backward_kernel(vec, dkv, w_kv, got, own, out, low1, low2, low3, sums):
    total = [jnp.zeros((1, 768), F32)] * 2
    for image, result in enumerate((out, low1, low2, low3)):
        at = slice(192 * image, 192 * image + 192)
        dy = mm_t(dkv[at], w_kv[...]) + got[at].astype(F32)
        xhat, inv = normalize(own[at].astype(F32))
        total = [
            total[0] + jnp.sum(dy * xhat, 0, keepdims=True),
            total[1] + jnp.sum(dy, 0, keepdims=True),
        ]
        result[...] = norm_back(dy, vec[2:3], xhat, inv)[:188].astype(result.dtype)
    sums[...] = jnp.concatenate(total + [jnp.zeros((6, 768), F32)], 0)


def image_backward(vec, dkv, w_kv, got, own):
    return staged(
        "image_backward",
        image_backward_kernel,
        (),
        (vec, dkv, w_kv, got, own),
        (shape((188, 768), F32), *[shape((188, 768), BF)] * 3, shape((8, 768), F32)),
        1e9,
    )


def self_backward_kernel(
    info, vec, stream_in, mine, got, before, w_out, joined, w_qkv, text,
    stream_mine, low, d_joined, to_mine, to_other, sums,
    stream, back,
):
    xhat, inv = normalize(before[...])
    stream[...] = stream_in[...] + norm_back(mine[...] + got[...], vec[1:2], xhat, inv)
    low[...] = stream[...].astype(BF)
    mixed_grad = mm_t(low[...], w_out[...]).astype(BF)
    for row in range(2):
        allowed = self_allowed(info, row)
        at = slice(128 * row, 128 * row + 128)
        for j in range(3):
            lanes = [slice(384 * i + 128 * j, 384 * i + 128 * j + 128) for i in range(3)]
            q = stacked(joined[at, lanes[0]]) * 0.125
            k = joined[at, lanes[1]]
            v = joined[at, lanes[2]]
            do = stacked(mixed_grad[at, lanes[0]])
            probs = softmax(mm_t(q, k), allowed)
            ds = softmax_back(probs, mm_t(do, v))
            d_joined[at, lanes[0]] = (merged(mm(ds, k)) * 0.125).astype(BF)
            d_joined[at, lanes[1]] = t_mm(ds, q).astype(BF)
            d_joined[at, lanes[2]] = t_mm(probs.astype(BF), do).astype(BF)
    back[...] = mm_t(d_joined[...], w_qkv[...])
    xhat, _ = normalize(text[...].astype(F32))
    sums[...] = jnp.concatenate(
        [
            jnp.sum(back[...] * xhat, 0, keepdims=True),
            jnp.sum(back[...], 0, keepdims=True),
            jnp.zeros((6, 768), F32),
        ],
        0,
    )
    core = info[0]
    for row in range(2):
        at = pl.ds(pl.multiple_of(128 * row + 64 * core, 64), 64)
        stream_mine[64 * row : 64 * row + 64] = stream[at]
        to_mine[64 * row : 64 * row + 64] = back[at]
        at = pl.ds(pl.multiple_of(128 * row + 64 * (1 - core), 64), 64)
        to_other[64 * row : 64 * row + 64] = back[at]


def self_backward(info, vec, stream_in, mine, got, before, w_out, joined, w_qkv, text):
    return staged(
        "self_backward",
        self_backward_kernel,
        (info,),
        (vec, stream_in, mine, got, before, w_out, joined, w_qkv, text),
        (shape((128, 768), F32), shape((256, 768), BF), shape((256, 1152), BF), shape((128, 768), F32), shape((128, 768), F32), shape((8, 768), F32)),
        3e9,
        [pltpu.VMEM((256, 768), F32), pltpu.VMEM((256, 768), F32)],
    )


def self_grads_kernel(
    normed, d_joined, mixed, low, sum0, sum1, sum2, sum3, grad, up_rows,
    index, e0, e1, e2, *outs,
):
    keeps, sends = outs[0:3], outs[3:6]
    for send, early in zip(sends, (e0, e1, e2)):
        send[:, :896] = early[...]
    d_qkv = t_mm(normed[...], d_joined[...]).astype(BF)
    d_out = t_mm(mixed[...], low[...]).astype(BF)
    for p in range(3):
        qa, qb = placed(index, 2 * p, 768), placed(index, 2 * p + 1, 384)
        o = placed(index, 6 + p, 384)
        top, rest = laid_out(d_qkv[:, 384 * p : 384 * p + 384], qa, qb, 256)
        moved = mm(o, d_out[:, 256 * p : 256 * p + 256])
        for at, value in ((0, top), (384, rest), (640, moved)):
            n = value.shape[1]
            keeps[p][:, at : at + n] = value[:256].astype(BF)
            sends[p][:, 896 + at : 896 + at + n] = value[256:].astype(BF)
    down_sum = jnp.sum(grad[...].astype(F32), 0, keepdims=True) * 0.5
    rows = [s[i : i + 1] for i in range(2) for s in (sum0, sum1, sum2, sum3)]
    rows = jnp.concatenate(rows + [down_sum, jnp.zeros((7, 768), F32)], 0).astype(BF)
    zero = jnp.zeros((16, 768), BF)
    first = jnp.concatenate([rows] + [zero] * 7, 0)
    second = jnp.concatenate([zero, rows] + [zero] * 6, 0)
    value = mm_t(qa, first) + mm_t(qb, second[:, 384:]) + up_rows[...]
    keeps[2][:, 896:1024] = value[:256].astype(BF)
    sends[2][:, 1792:1920] = value[256:].astype(BF)


def self_grads(normed, d_joined, mixed, low, sums, grad, up_rows, index, early):
    return staged(
        "self_grads",
        self_grads_kernel,
        (),
        (normed, d_joined, mixed, low, *sums, grad, up_rows, index, *early),
        (*[shape((256, n), BF) for n in (896, 896, 1024, 1792, 1792, 1920)],),
        3e9,
    )


def first_core(info, dims):
    return lax.broadcasted_iota(jnp.int32, dims, 0) * 0 + info[0] == 0


BLOCKS = ((0, 3, 384), (1, 2, 384), (2, 1, 384), (3, 1, 1536))


def halves_into(core, refs, target, sem):
    copies, here = [], 0
    for which, blocks, width in BLOCKS:
        for i in range(blocks):
            at = pl.multiple_of(2 * i * width + core * width, 128)
            copies.append(
                pltpu.make_async_copy(
                    refs[which].at[:, pl.ds(at, width)], target.at[:, pl.ds(here, width)],
                    sem.at[len(copies)],
                )
            )
            here += width
    return copies


def vector_rows(gain, bias, down_bias):
    total = jnp.zeros((6, 128), F32)
    for at, ref in ((0, gain), (4, bias), (8, down_bias)):
        n = ref.shape[0]
        i = lax.broadcasted_iota(jnp.int32, (n, 128), 0) + at
        j = lax.broadcasted_iota(jnp.int32, (n, 128), 1)
        total = total + t_mm(ref[...], ((i == j) | (i + 16 == j)).astype(F32).astype(BF))
    return total


def pack_swap_kernel(info, qkv, kv, query, up, gain, bias, down_bias, send, half, sem):
    copies = halves_into(1 - info[0], (qkv, kv, query, up), half, sem)
    for c in copies:
        c.start()
    send[:, 3840:] = vector_rows(gain, bias, down_bias).astype(BF)
    for c in copies:
        c.wait()
    send[:, :3840] = half[...]


def pack_slots_kernel(
    info, qkv, kv, query, up, self_out, cross_out, down, got, gain, bias, down_bias, up_bias,
    slot, twelve, half, outs, slabs, theirs, sem, sems,
):
    copies = halves_into(info[0], (qkv, kv, query, up), half, sem)
    others = [
        pltpu.make_async_copy(self_out, outs.at[0], sems.at[0]),
        pltpu.make_async_copy(cross_out, outs.at[1], sems.at[1]),
        pltpu.make_async_copy(down, slabs, sems.at[2]),
    ]
    sent = pltpu.make_async_copy(got, theirs, sems.at[3])
    sent.start()
    for c in copies + others:
        c.start()
    first = first_core(info, (6, 128))
    mine = vector_rows(gain, bias, down_bias)
    sent.wait()
    other = theirs[:, 3840:].astype(F32)
    twelve[0:6, 4608:] = jnp.where(first, mine, other)
    twelve[6:12, 4608:] = jnp.where(first, other, mine)
    twelve[12:16, 4608:] = jnp.zeros((4, 128), F32)
    lane = lax.broadcasted_iota(jnp.int32, (8, 128), 1)
    row = lax.broadcasted_iota(jnp.int32, (8, 128), 0)
    vec = jnp.where(lane < 16, twelve[0:8, 4608:], 0.0)
    vec = vec + jnp.where((lane >= 16) & (lane < 32), twelve[8:16, 4608:], 0.0)
    i = lax.broadcasted_iota(jnp.int32, (24, 128), 0)
    j = lax.broadcasted_iota(jnp.int32, (24, 128), 1)
    units = mm(up_bias[...], (i + 64 == j).astype(F32).astype(BF))
    slot[:, 6912:7040] = (vec + jnp.where(row == 0, units, 0.0)).astype(BF)
    for c in copies:
        c.wait()
    first = first_core(info, (6, 3840))
    mine = half[...].astype(F32)
    other = theirs[:, :3840].astype(F32)
    twelve[0:6, :3840] = jnp.where(first, mine, other)
    twelve[6:12, :3840] = jnp.where(first, other, mine)
    for c in others:
        c.wait()
    twelve[0:6, 3840:4608] = outs[0].astype(F32)
    twelve[6:12, 3840:4608] = outs[1].astype(F32)
    slot[:, :4608] = twelve[0:8, :4608].astype(BF)
    twelve[0:4, :2304] = twelve[8:12, :2304]
    twelve[4:8, :2304] = twelve[8:12, 2304:4608]
    slot[:, 4608:6912] = twelve[0:8, :2304].astype(BF)
    wide = slabs[...].astype(F32)
    for k in range(3):
        at = 7040 + 768 * k
        slot[:, at : at + 768] = wide[8 * k : 8 * k + 8].astype(BF)


def packed(name, kernel, info, far, near, out, scratch):
    return pl.pallas_call(
        kernel,
        out_shape=out,
        in_specs=[SMEM] + [HBM] * len(far) + [VMEM] * len(near),
        out_specs=VMEM,
        scratch_shapes=scratch,
        compiler_params=params(60),
        cost_estimate=cost(1e6, 1e6),
        name=name,
    )(info, *far, *near)


def pack_swap(info, weights, vectors):
    return packed(
        "pack_swap",
        pack_swap_kernel,
        info,
        weights,
        vectors,
        shape((6, 3968), BF),
        [pltpu.VMEM((6, 3840), BF), pltpu.SemaphoreType.DMA((7,))],
    )


def pack_slots(info, weights, vectors, got, self_out, cross_out, down, up_bias):
    return packed(
        "pack_slots",
        pack_slots_kernel,
        info,
        (*weights, self_out, cross_out, down, got),
        (*vectors, up_bias),
        shape((8, 9344), BF),
        [
            pltpu.VMEM((16, 4736), F32),
            pltpu.VMEM((6, 3840), BF),
            pltpu.VMEM((2, 6, 768), BF),
            pltpu.VMEM((24, 768), BF),
            pltpu.VMEM((6, 3968), BF),
            pltpu.SemaphoreType.DMA((7,)),
            pltpu.SemaphoreType.DMA((4,)),
        ],
    )


BASE = (2304, 2304, 0)
TWELVES = [(p, 0, 768, 384) for p in range(2)] + [
    (p, BASE[p] + at, 384, 256) for at in (0, 896) for p in range(3)
]


def finish_send_kernel(info, *refs):
    keeps, gots, (s0, s1, s2, send, own, twelve) = refs[:3], refs[3:6], refs[6:]
    sums = (s0, s1, s2)
    for p in range(3):
        sums[p][...] = keeps[p][...].astype(F32) + gots[p][...].astype(F32)
    here = 0
    for p, at, n, width in TWELVES:
        ref = sums[p]
        twelve[0:8, here : here + n] = ref[:, at : at + n]
        twelve[8:12, here : here + width] = ref[0:4, at + n : at + n + width]
        twelve[8:12, here + width : here + n] = ref[4:8, at + n : at + n + n - width]
        here += n
    vec = s2[:, 1792:]
    twelve[0:8, 3840:] = vec
    twelve[8:12, 3840:] = pltpu.roll(vec, 112, 1)[0:4]
    first = first_core(info, (6, 3968))
    send[...] = jnp.where(first, twelve[6:12], twelve[0:6])
    own[...] = jnp.where(first, twelve[0:6], twelve[6:12])


def finish_kernel(
    info, s0, s1, s2, own, got, qkv, out_self, query, kv, out_cross, up, down, gain, bias, down_bias
):
    sums = (s0, s1, s2)
    first = first_core(info, (6, 3840))
    low = jnp.where(first, own[:, :3840], got[:, :3840])
    high = jnp.where(first, got[:, :3840], own[:, :3840])
    for ref, begin, blocks, width in (
        (up, 0, 1, 1536), (kv, 1536, 2, 384), (query, 2304, 1, 384), (qkv, 2688, 3, 384),
    ):
        for i in range(blocks):
            at = begin + i * width
            ref[:, 2 * i * width : (2 * i + 1) * width] = low[:, at : at + width]
            ref[:, (2 * i + 1) * width : (2 * i + 2) * width] = high[:, at : at + width]
    for p in range(3):
        lanes = slice(256 * p, 256 * p + 256)
        out_cross[:, lanes] = sums[p][0:6, BASE[p] + 640 : BASE[p] + 896]
        out_self[:, lanes] = sums[p][0:6, BASE[p] + 1536 : BASE[p] + 1792]
    for p in range(2):
        for k in range(3):
            at = 1152 + 384 * k
            down[8 * k : 8 * k + 8, 384 * p : 384 * p + 384] = sums[p][:, at : at + 384]
    total = jnp.concatenate([own[:, 3840:] + got[:, 3840:], jnp.zeros((122, 128), F32)], 0)
    across = jnp.transpose(total)
    gain[...] = across[0:4, 0:6]
    bias[...] = across[4:8, 0:6]
    down_bias[...] = across[8:9, 0:6]


def finish_send(info, keeps, gots):
    widths = [k.shape[1] for k in keeps]
    return staged(
        "finish_send",
        finish_send_kernel,
        (info,),
        (*keeps, *gots),
        [shape((8, n), F32) for n in widths] + [shape((6, 3968), F32)] * 2,
        1e6,
        [pltpu.VMEM((16, 3968), F32)],
        mib=8,
    )


def finish(info, sums, own, got):
    return staged(
        "finish",
        finish_kernel,
        (info,),
        (*sums, own, got),
        [
            shape(dims, F32)
            for dims in (
                (6, 2304), (6, 768), (6, 768), (6, 1536), (6, 768), (6, 3072), (24, 768), (4, 6), (4, 6),
                (1, 6),
            )
        ],
        1e6,
        mib=8,
    )


def text_finish_kernel(vec, text, stream, mine, got, out_mine, out_got, grad, out):
    xhat, inv = normalize(text[...].astype(F32))
    grad[...] = stream[...] + norm_back(mine[...] + got[...], vec[0:1], xhat, inv)
    out[...] = out_mine[...] + out_got[...]


def text_finish(vec, text, stream, mine, got, out_mine, out_got):
    return staged(
        "text_finish",
        text_finish_kernel,
        (),
        (vec, text, stream, mine, got, out_mine, out_got),
        [shape((128, 768), F32)] * 2,
        1e6,
        mib=8,
    )


def image_finish_kernel(pick, v0, v1, v2, v3, out):
    values = [v[...].astype(F32) for v in (v0, v1, v2, v3)]
    for image in range(4):
        total = values[3]
        for turn in range(3):
            total = jnp.where(pick[turn] == image, values[turn], total)
        out[:, image, :] = total


def image_finish(pick, values):
    out = staged(
        "image_finish",
        image_finish_kernel,
        (pick,),
        values,
        [shape((188, 4, 768), F32)],
        1e6,
    )[0]
    return jnp.transpose(out, (1, 0, 2))


def combine_kernel(plan, *refs):
    at = 0
    ins = []
    for keeps, gots in plan:
        ins.append((refs[at : at + len(keeps)], refs[at + len(keeps) : at + len(keeps) + len(gots)]))
        at += len(keeps) + len(gots)
    outs = refs[at:]
    for p, (keeps, gots) in enumerate(ins):
        here = 0
        edges = []
        for ref in keeps:
            edges.append((here, here + ref.shape[1], ref))
            here += ref.shape[1]
        here = 0
        for ref in gots:
            for low, high, keep in edges:
                a, b = max(low, here), min(high, here + ref.shape[1])
                if a >= b:
                    continue
                total = keep[:, a - low : b - low].astype(F32) + ref[:, a - here : b - here].astype(F32)
                half = total.shape[0] // 2
                outs[2 * p][:, a:b] = total[:half].astype(BF)
                outs[2 * p + 1][:, a:b] = total[half:].astype(BF)
            here += ref.shape[1]


def combine(parts):
    plan, args, outs = [], [], []
    for keeps, gots in parts:
        plan.append(([k.shape[1] for k in keeps], [g.shape[1] for g in gots]))
        args += [*keeps, *gots]
        rows, width = keeps[0].shape[0], sum(k.shape[1] for k in keeps)
        outs += [shape((rows // 2, width), BF)] * 2
    got = staged(
        "combine", lambda *refs: combine_kernel(plan, *refs), (), args, outs, 1e6
    )
    return [(got[2 * p], got[2 * p + 1]) for p in range(len(parts))]


def send_step(step, values, parts=(0, 1, 2)):
    v0, v1 = ((1, 3), (3, 1))[step % 2]
    return [
        lax.ppermute(v, BOTH, xor_pairs(ORDERS[p][step // 2], v0, v1)) for v, p in zip(values, parts)
    ]


def after(value, *others):
    return lax.optimization_barrier((value, *others))[0]


def image_moves(images, way):
    once = [(core + i, core + (i + 16 * way) % 64) for core in (0, 64) for i in range(64)]
    first, second, third = images
    return [
        lax.ppermute(first, BOTH, once),
        move_on(second),
        lax.ppermute(third, BOTH, [(j, i) for i, j in once]),
    ]


def move_on(image):
    route = [(i, (i + 16) % 64) for i in range(64)]
    return lax.ppermute(image, BOTH, route + [(64 + j, 64 + i) for i, j in route])


def on_device(
    text_input,
    image_tokens,
    output_grad,
    segment_starts,
    caption_image,
    image_counts,
    norm_gain,
    norm_bias,
    self_qkv,
    self_out,
    cross_q,
    cross_kv,
    cross_out,
    up_weight,
    up_bias,
    down_weight,
    down_bias,
):
    core = lax.axis_index("seq")
    chip = lax.axis_index("batch")
    first = core == 0

    def ordered(own, other, axis):
        return jnp.where(
            first, jnp.concatenate([own, other], axis), jnp.concatenate([other, own], axis)
        )

    place = jnp.stack([core, chip]).astype(jnp.int32)
    weights = (self_qkv, cross_kv, cross_q, up_weight)
    vectors = (norm_gain, norm_bias, down_bias[None])
    got = swap(pack_swap(place, weights, vectors))
    slot = pack_slots(
        place, weights, vectors, got, self_out, cross_out, down_weight, up_bias[None]
    )
    gathered = lax.all_gather(slot, "batch", axis=0, tiled=True)

    late_text, late_grad = after(text_input, slot), after(output_grad, slot)
    text = ordered(late_text, swap(late_text), 1).reshape(256, 768)
    grad = ordered(late_grad, swap(late_grad), 1).reshape(256, 768)

    group_images = after(caption_image, slot).reshape(64, 8)
    my_captions = lax.dynamic_index_in_dim(group_images, chip, 0, keepdims=False)
    limits = jnp.take(image_counts, my_captions).reshape(4, 2)
    limits = jnp.where(first, jnp.concatenate([limits[:, 0], limits[:, 1]]), jnp.concatenate([limits[:, 1], limits[:, 0]]))
    turns = jnp.arange(4)
    targets = (chip - turns * 16) % 64
    wanted = group_images[targets, 2 * turns + core]
    local_pick = wanted - (core * 64 + chip) * 4
    outgoing = image_pick(after(local_pick, slot), image_tokens)
    received = [outgoing[0], *image_moves(outgoing[1:], -1)]
    received[2] = move_on(received[2])
    own_images = image_stack(received)
    other_images = swap(own_images)
    info = jnp.concatenate(
        [core[None], segment_starts.reshape(8), limits, jnp.zeros((15,), jnp.int32)]
    ).astype(jnp.int32)

    column_index = indices(after(place, slot))

    gathered, info, grad, text, column_index, own_images, other_images = lax.optimization_barrier(
        (gathered, info, grad, text, column_index, own_images, other_images)
    )
    w_qkv, w_kv, w_query, w_up, w_self, w_cross, w_down, vec, b_up = unpack(gathered)
    part, joined, mixed_self, normed_one = self_forward(info, vec, w_qkv, w_self, text)
    got = swap(part)
    kv, image_normed = image_forward(vec, w_kv, own_images, other_images)
    after_self, normed_two, q_cross, mixed_cross, part = cross_forward(
        info, vec, text, part, got, kv, w_query, w_cross
    )
    after_cross, normed_three, active, hidden_low, text_mine, text_other, part, sum3 = feed(
        info, vec, b_up, after_self, part, swap(part), w_up, w_down, grad
    )
    text_got = swap(text_other)
    got = swap(part)

    grads = feed_grads(normed_three, active, hidden_low, grad, column_index)
    keep_one, up_rows = grads[0:2], grads[4]
    got_one = send_step(0, grads[2:4], (0, 1))
    stream_two, cross_low, dq, dkv, part, sum1 = cross_backward(
        info, vec, after(grad, keep_one[0]), part, got, after_cross, w_cross, q_cross, kv, w_query, after_self
    )
    got = swap(part)
    image_send = image_part(dkv, w_kv)[0]
    *rows_back, sum2 = image_backward(vec, dkv, w_kv, swap(image_send), own_images)
    returned = [rows_back[0], *image_moves(rows_back[1:], 1)]
    k_keep, v_keep, k_send, v_send = image_grads(
        image_normed, after(dkv, sum2), mixed_cross, cross_low, column_index
    )
    returned[2] = move_on(after(returned[2], k_keep))
    q_keep, q_send = query_grads(
        normed_two, after(dq, k_keep), mixed_cross, cross_low, column_index
    )
    keep_two, early = [k_keep, v_keep, q_keep], [k_send, v_send, q_send]
    stream_one, self_low, d_joined, one_mine, one_other, sum0 = self_backward(
        info, vec, after(stream_two, q_keep), part, got, after_self, w_self, joined,
        w_qkv, text,
    )
    self_low, *late = lax.optimization_barrier((self_low, *returned[1:], *got_one))
    returned, got_one = returned[:1] + late[:3], late[3:]
    grads = self_grads(
        normed_one, d_joined, mixed_self, self_low, (sum0, sum1, sum2, sum3), grad, up_rows,
        column_index, early,
    )
    keep_three = grads[0:3]
    got_two = send_step(0, grads[3:6])
    one_got = swap(one_other)
    image_grad = image_finish(after(local_pick, grads[3]), returned)
    text_grad, text_output = text_finish(
        after(vec, grads[3]), text_input.reshape(128, 768), stream_one, one_mine, one_got, text_mine,
        text_got,
    )
    got_two, image_grad, text_grad = lax.optimization_barrier((got_two, image_grad, text_grad))
    pairs = []
    for p in range(3):
        keeps, gots = [keep_two[p], keep_three[p]], [got_two[p]]
        if p < 2:
            keeps, gots = [keep_one[p], *keeps], [got_one[p], *gots]
        pairs += combine([(keeps, gots)])
    for step in range(1, 6):
        got_step = send_step(step, [s for _, s in pairs])
        step_parts = [([k], [g]) for (k, _), g in zip(pairs, got_step)]
        if step == 5:
            *sums, send, own = finish_send(place, [k for k, _ in pairs], got_step)
        elif step == 1:
            pairs = [combine([one])[0] for one in step_parts]
        else:
            pairs = combine(step_parts)

    text_grad, text_output = text_grad.reshape(2, 64, 768), text_output.reshape(2, 64, 768)

    (
        qkv_grad, self_grad, query_grad, kv_grad, cross_grad, up_grad, down_grad, gain_grad, bias_grad,
        down_bias_grad,
    ) = finish(place, sums, own, swap(send))
    up_bias_grad = sums[2][0, 1856:1880]
    return (
        text_output,
        text_grad,
        image_grad,
        gain_grad,
        bias_grad,
        qkv_grad,
        self_grad,
        query_grad,
        kv_grad,
        cross_grad,
        up_grad,
        up_bias_grad,
        down_grad,
        down_bias_grad[0],
    )


def solution(mesh):
    rows = P("batch", "seq", None)
    shard = P(BOTH, None)
    wide = P(None, BOTH)
    return jax.shard_map(
        on_device,
        mesh=mesh,
        in_specs=(
            rows, P(BOTH, None, None), rows, P("batch", None), P(), P(), wide, wide,
            shard, shard, shard, shard, shard, shard, P(BOTH), shard, P(BOTH),
        ),
        out_specs=(
            rows, rows, P(BOTH, None, None), wide, wide,
            shard, shard, shard, shard, shard, shard, P(BOTH), shard, P(BOTH),
        ),
        check_vma=False,
    )
```

```python
import math

import jax
import jax.numpy as jnp
from jax import lax
from jax.experimental import pallas as pl
from jax.experimental.pallas import tpu as pltpu
from jax.sharding import PartitionSpec as P

HEADS = 12
HEAD_DIM = 64
EPSILON = 1e-05
MASKED_SCORE = -1e30
BF = jnp.bfloat16
F32 = jnp.float32
BOTH = ("seq", "batch")
STRIDE = {"z": 16, "y": 4, "x": 1}
ORDERS = (("x", "z", "y"), ("y", "x", "z"), ("z", "x", "y"))


def xor_pairs(axis, value0, value1):
    step, out = STRIDE[axis], []
    for core, value in ((0, value0), (1, value1)):
        for chip in range(64):
            at = chip // step % 4
            out.append((core * 64 + chip, core * 64 + chip + ((at ^ value) - at) * step))
    return out


def swap(value):
    return lax.ppermute(value, "seq", [(0, 1), (1, 0)])


def mm(a, b):
    return jnp.dot(a, b, preferred_element_type=F32)


def mm_t(a, b):
    return lax.dot_general(a, b, (((1,), (1,)), ((), ())), preferred_element_type=F32)


def t_mm(a, b):
    return lax.dot_general(a, b, (((0,), (0,)), ((), ())), preferred_element_type=F32)


def normalize(values):
    center = jnp.mean(values, -1, keepdims=True)
    centred = values - center
    spread = jnp.mean(centred * centred, -1, keepdims=True)
    inv = lax.rsqrt(spread + EPSILON)
    return centred * inv, inv


def norm_back(grad, gain, xhat, inv):
    scaled = grad * gain
    return inv * (
        scaled
        - jnp.mean(scaled, -1, keepdims=True)
        - xhat * jnp.mean(scaled * xhat, -1, keepdims=True)
    )


VMEM = pl.BlockSpec(memory_space=pltpu.VMEM)
SMEM = pl.BlockSpec(memory_space=pltpu.SMEM)
HBM = pl.BlockSpec(memory_space=pltpu.HBM)


def shape(dims, dtype):
    return jax.ShapeDtypeStruct(dims, dtype)


def cost(flops, moved):
    return pl.CostEstimate(
        flops=int(flops / 64), bytes_accessed=int(moved / 64), transcendentals=0
    )


def params(mib):
    return pltpu.CompilerParams(vmem_limit_bytes=mib * 1024 * 1024)


def staged(name, kernel, scalars, ins, outs, work, scratch=(), mib=16):
    moved = sum(math.prod(v.shape) * v.dtype.itemsize for v in (*ins, *outs))
    return pl.pallas_call(
        kernel,
        out_shape=tuple(outs),
        in_specs=[SMEM] * len(scalars) + [VMEM] * len(ins),
        out_specs=(VMEM,) * len(outs),
        scratch_shapes=list(scratch),
        compiler_params=params(mib),
        cost_estimate=cost(work, moved),
        name=name,
    )(*scalars, *ins)


def placed(columns, i, size):
    place = lax.broadcasted_iota(jnp.int32, (512, size), 1)
    return (place == columns[:, i : i + 1]).astype(F32).astype(BF)


def segment_of(info, row, dims, axis):
    place = lax.broadcasted_iota(jnp.int32, dims, axis)
    total = jnp.full(dims, -1, jnp.int32)
    for j in range(4):
        total = total + (place >= info[1 + 4 * row + j]).astype(jnp.int32)
    return total


def low_lanes():
    return lax.broadcasted_iota(jnp.int32, (1, 128), 1) < 64


def stacked(pair):
    left = low_lanes()
    zero = jnp.zeros_like(pair)
    return jnp.concatenate([jnp.where(left, pair, zero), jnp.where(left, zero, pair)], 0)


def merged(two):
    n = two.shape[0] // 2
    return jnp.where(low_lanes(), two[:n], two[n:])


def softmax(scores, allowed):
    scores = jnp.where(allowed, scores, MASKED_SCORE)
    weights = jnp.exp(scores - jnp.max(scores, -1, keepdims=True))
    return weights * (1.0 / jnp.sum(weights, -1, keepdims=True))


def softmax_back(probs, dprobs):
    return (probs * (dprobs - jnp.sum(probs * dprobs, -1, keepdims=True))).astype(BF)


def self_allowed(info, row):
    at = segment_of(info, row, (128, 128), 0)
    key = segment_of(info, row, (128, 128), 1)
    i = lax.broadcasted_iota(jnp.int32, (128, 128), 0)
    j = lax.broadcasted_iota(jnp.int32, (128, 128), 1)
    allowed = (at == key) & (j <= i)
    return jnp.concatenate([allowed, allowed], 0)


def cross_allowed(info, row):
    core = info[0]
    lane = lax.broadcasted_iota(jnp.int32, (1, 768), 1)
    key = jnp.full((1, 768), -1, jnp.int32)
    images = (2 * row, 2 * row + 1, 4 + 2 * row, 5 + 2 * row)
    captions = (core, 2 + core, 1 - core, 3 - core)
    for block in range(4):
        limit = info[9 + images[block]]
        key = jnp.where(
            (lane >= 192 * block) & (lane < 192 * block + limit), captions[block], key
        )
    at = segment_of(info, row, (128, 1), 0)
    return jnp.concatenate([at, at], 0) == key


def row_keys(kv, row, lanes):
    return jnp.concatenate(
        [kv[384 * row : 384 * row + 384, lanes], kv[768 + 384 * row : 1152 + 384 * row, lanes]], 0
    )


def lanes_of():
    lane = lax.broadcasted_iota(jnp.int32, (128, 1536), 0)
    unit = lax.broadcasted_iota(jnp.int32, (128, 1536), 1)
    return (lane == 64 + lax.rem(unit, 24)).astype(F32).astype(BF)


def own_lanes():
    chip = lax.broadcasted_iota(jnp.int32, (64, 1536), 0) * 24
    unit = lax.broadcasted_iota(jnp.int32, (64, 1536), 1)
    return (unit >= chip) & (unit < chip + 24)


def self_forward_kernel(info, vec, w_qkv, w_out, text, part, joined, mixed, normed):
    xhat, _ = normalize(text[...].astype(F32))
    normed[...] = (xhat * vec[0:1] + vec[4:5]).astype(BF)
    joined[...] = mm(normed[...], w_qkv[...]).astype(BF)
    for row in range(2):
        allowed = self_allowed(info, row)
        at = slice(128 * row, 128 * row + 128)
        for j in range(3):
            q = stacked(joined[at, 128 * j : 128 * j + 128]) * 0.125
            k = joined[at, 384 + 128 * j : 512 + 128 * j]
            v = joined[at, 768 + 128 * j : 896 + 128 * j]
            probs = softmax(mm_t(q, k), allowed)
            mixed[at, 128 * j : 128 * j + 128] = merged(mm(probs.astype(BF), v)).astype(BF)
    part[...] = mm(mixed[...], w_out[...])


def self_forward(info, vec, w_qkv, w_out, text):
    return staged(
        "self_forward",
        self_forward_kernel,
        (info,),
        (vec, w_qkv, w_out, text),
        (
            shape((256, 768), F32),
            shape((256, 1152), BF),
            shape((256, 384), BF),
            shape((256, 768), BF),
        ),
        2e9,
    )


def rows_of_six(first, last, shift):
    row = lax.broadcasted_iota(jnp.int32, (192, 256), 0)
    place = lax.broadcasted_iota(jnp.int32, (192, 256), 1)
    chip = lax.div(row, 6)
    r = row - 6 * chip
    hit = (place == 8 * chip + r + shift) & (r >= first) & (r <= last)
    return hit.astype(F32).astype(BF)


def unpack_kernel(
    gathered, w_qkv, w_kv, w_query, w_up, w_self, w_cross, w_down, vec, b_up, g, sems
):
    spans = ((4608, 1152), (0, 1152), (6912, 2432), (5760, 1152), (1152, 1152), (2304, 2304))
    loads = [
        pltpu.make_async_copy(gathered.at[:, pl.ds(at, n)], g.at[:, pl.ds(at, n)], sems.at[i])
        for i, (at, n) in enumerate(spans)
    ]
    loads[0].start()
    loads[1].start()
    low, high = rows_of_six(0, 5, 0), rows_of_six(0, 1, 6)
    both = jnp.concatenate([low, high], 0)
    left, right = rows_of_six(2, 5, -2), rows_of_six(2, 5, 2)

    def natural(at, n, begin, rest, outs):
        for half in range(2):
            here = slice(256 * half, 256 * half + 256)
            there = slice(192 * half, 192 * half + 192)
            rows = mm(both, g[here, at : at + n])
            outs[0][there] = rows[:192].astype(BF)
            there = slice(outs[2] + 192 * half, outs[2] + 192 * half + 192)
            outs[1][there] = (rows[192:] + mm(rest, g[here, begin : begin + n])).astype(BF)

    loads[0].wait()
    loads[1].wait()
    for i in (2, 3, 4):
        loads[i].start()
    natural(0, 1152, 4608, left, (w_qkv, w_qkv, 384))
    loads[2].wait()
    loads[5].start()
    tail = g[:, 6912:7040]
    lane = lax.broadcasted_iota(jnp.int32, (1, 128), 1)
    one = jnp.where(lane < 16, tail.astype(F32), 0.0).astype(BF)
    two = jnp.where((lane >= 16) & (lane < 32), tail.astype(F32), 0.0).astype(BF)
    halves = [slice(0, 256), slice(256, 512)]
    rows = [mm(low, one[h]) for h in halves]
    rows += [mm(high, one[h]) + mm(left, two[h]) for h in halves]
    across = jnp.transpose(jnp.concatenate(rows, 0))
    vec[...] = across[:16] + across[16:32]
    chip = lax.broadcasted_iota(jnp.int32, (64, 512), 0)
    place = lax.broadcasted_iota(jnp.int32, (64, 512), 1)
    of_chip = mm((place == 8 * chip).astype(F32).astype(BF), tail).astype(BF)
    b_up[...] = jnp.sum(jnp.where(own_lanes(), mm(of_chip, lanes_of()), 0.0), 0, keepdims=True)
    slabs = [
        g[:, 7040 + 768 * k : 7808 + 768 * k].astype(F32).reshape(64, 1, 8, 768) for k in range(3)
    ]
    w_down[...] = jnp.concatenate(slabs, 1).reshape(1536, 768).astype(BF)
    loads[3].wait()
    loads[4].wait()
    natural(1152, 768, 5760, left, (w_kv, w_kv, 384))
    natural(1920, 384, 6528, left, (w_query, w_query, 384))
    loads[5].wait()
    natural(2304, 1536, 4608, right, (w_up, w_up, 384))
    natural(3840, 768, 6144, right, (w_self, w_cross, 0))


def unpack(gathered):
    outs = ((768, 1152), (768, 768), (768, 384), (768, 1536), (384, 768), (384, 768), (1536, 768))
    return pl.pallas_call(
        unpack_kernel,
        out_shape=(
            *[shape(o, BF) for o in outs],
            shape((16, 768), F32),
            shape((1, 1536), F32),
        ),
        in_specs=[HBM],
        out_specs=(VMEM,) * 9,
        scratch_shapes=[pltpu.VMEM((512, 9344), BF), pltpu.SemaphoreType.DMA((6,))],
        compiler_params=params(46),
        cost_estimate=cost(4e9, 20e6),
        name="unpack",
    )(gathered)


def natural_row(at_slot, twelfth):
    return at_slot * 6 + twelfth + jnp.where(twelfth >= 6, 378, 0)


def index_kernel(place, columns):
    core, chip = place[0], place[1]

    def target_of(order, slot):
        first = slot * 0 + core == 0
        target = 0
        for axis, digit in zip(order, (slot >> 4, (slot >> 2) & 3, slot & 3)):
            step = STRIDE[axis]
            here = lax.rem(lax.div(chip, step), 4)
            other = jnp.where(
                first, jnp.where(digit == 1, 3, jnp.maximum(digit, 1) - 1), digit ^ (digit >> 1)
            )
            target = target + (here ^ other) * step
        return target

    def out_pick(at_slot, eight):
        return jnp.where(eight < 6, at_slot * 6 + eight, -1)

    at = lax.broadcasted_iota(jnp.int32, (512, 1), 0)
    eight = at & 7
    targets = [target_of(order, at >> 3) for order in ORDERS]
    values = []
    for target in targets:
        values += [natural_row(target, eight), natural_row(target, 8 + (eight & 3)) - 384]
    values += [out_pick(target, eight) for target in targets]
    values += [target * 8 + eight for target in targets] + [jnp.where(eight == 0, targets[2], -1)]
    for i in range(16):
        columns[:, i : i + 1] = values[i] if i < len(values) else at * 0


def indices(place):
    return staged(
        "indices",
        index_kernel,
        (place,),
        (),
        [shape((512, 16), jnp.int32)],
        1e6,
    )[0]


def image_pick_kernel(pick, tokens, *outs):
    for turn, out in enumerate(outs):
        out[...] = tokens[pick[turn]]


def image_pick(pick, tokens):
    return staged(
        "image_pick", image_pick_kernel, (pick,), (tokens,), [shape((188, 768), BF)] * 4, 1e6
    )


def image_stack_kernel(v0, v1, v2, v3, out, wide):
    wide[188:192] = jnp.zeros((4, 768), F32)
    for turn, value in enumerate((v0, v1, v2, v3)):
        wide[0:188] = value[...].astype(F32)
        out[192 * turn : 192 * turn + 192] = wide[...].astype(BF)


def image_stack(values):
    return staged(
        "image_stack",
        image_stack_kernel,
        (),
        values,
        [shape((768, 768), BF)],
        1e6,
        [pltpu.VMEM((192, 768), F32)],
    )[0]


def image_forward_kernel(vec, w_kv, own, other, kv, normed):
    row = lax.broadcasted_iota(jnp.int32, (192, 1), 0)
    for image in range(8):
        source, here = (own, 192 * image) if image < 4 else (other, 192 * image - 768)
        xhat, _ = normalize(source[here : here + 192].astype(F32))
        at = slice(192 * image, 192 * image + 192)
        normed[at] = jnp.where(row < 188, xhat * vec[2:3] + vec[6:7], 0.0).astype(BF)
        kv[at] = mm(normed[at], w_kv[...]).astype(BF)


def image_forward(vec, w_kv, own, other):
    return staged(
        "image_forward",
        image_forward_kernel,
        (),
        (vec, w_kv, own, other),
        (shape((1536, 768), BF), shape((1536, 768), BF)),
        2e9,
    )


def cross_forward_kernel(
    info, vec, text, mine, got, w_query, kv, w_out, after, normed, queries, mixed, part
):
    after[...] = text[...].astype(F32) + (mine[...] + got[...])
    xhat, _ = normalize(after[...])
    normed[...] = (xhat * vec[1:2] + vec[5:6]).astype(BF)
    queries[...] = mm(normed[...], w_query[...]).astype(BF)
    for row in range(2):
        allowed = cross_allowed(info, row)
        at = slice(128 * row, 128 * row + 128)
        for j in range(3):
            lanes = slice(128 * j, 128 * j + 128)
            q = stacked(queries[at, lanes]) * 0.125
            k = row_keys(kv, row, lanes)
            v = row_keys(kv, row, slice(384 + 128 * j, 512 + 128 * j))
            probs = softmax(mm_t(q, k), allowed)
            mixed[at, lanes] = merged(mm(probs.astype(BF), v)).astype(BF)
    part[...] = mm(mixed[...], w_out[...])


def cross_forward(info, vec, text, mine, got, kv, w_query, w_out):
    return staged(
        "cross_forward",
        cross_forward_kernel,
        (info,),
        (vec, text, mine, got, w_query, kv, w_out),
        (shape((256, 768), F32), shape((256, 768), BF), shape((256, 384), BF), shape((256, 384), BF), shape((256, 768), F32)),
        3e9,
    )


def feed_kernel(
    info, vec, b_up, before, mine, got, w_up, w_down, grad,
    after, normed, active, hidden_low, to_mine, to_other, back, sums,
    part,
):
    after[...] = before[...] + (mine[...] + got[...])
    xhat, _ = normalize(after[...])
    normed[...] = (xhat * vec[3:4] + vec[7:8]).astype(BF)
    part[...] = jnp.zeros((256, 768), F32)
    for k in range(3):
        lanes = slice(512 * k, 512 * k + 512)
        down = w_down[lanes]
        hidden = mm(normed[...], w_up[:, lanes]) + b_up[:, lanes]
        cdf = 0.5 * (1.0 + lax.erf(hidden * 0.7071067811865476))
        active[:, lanes] = (hidden * cdf).astype(BF)
        slope = cdf + hidden * (jnp.exp(-0.5 * hidden * hidden) * 0.3989422804014327)
        part[...] += mm(active[:, lanes], down)
        hidden_low[:, lanes] = (mm_t(grad[...], down) * slope).astype(BF)
    back[...] = mm_t(hidden_low[...], w_up[...])
    sums[...] = jnp.concatenate(
        [
            jnp.sum(back[...] * xhat, 0, keepdims=True),
            jnp.sum(back[...], 0, keepdims=True),
            jnp.zeros((6, 768), F32),
        ],
        0,
    )
    core = info[0]
    bias = vec[8:9]
    for row in range(2):
        at = pl.ds(pl.multiple_of(128 * row + 64 * core, 64), 64)
        to_mine[64 * row : 64 * row + 64] = after[at] + part[at] + bias
        at = pl.ds(pl.multiple_of(128 * row + 64 * (1 - core), 64), 64)
        to_other[64 * row : 64 * row + 64] = part[at]


def feed(info, vec, b_up, before, mine, got, w_up, w_down, grad):
    return staged(
        "feed",
        feed_kernel,
        (info,),
        (vec, b_up, before, mine, got, w_up, w_down, grad),
        (shape((256, 768), F32), shape((256, 768), BF), shape((256, 1536), BF), shape((256, 1536), BF), shape((128, 768), F32), shape((128, 768), F32), shape((256, 768), F32), shape((8, 768), F32)),
        3e9,
        [pltpu.VMEM((256, 768), F32)],
    )


def laid_out(weight, qa, qb, width):
    top = mm(qa, weight)
    rest = mm(qb, weight[384:])
    n = weight.shape[1]
    upper = lax.broadcasted_iota(jnp.int32, (512, 1), 0) % 8 < 4
    tail = rest[:, width:]
    if n - width < width:
        tail = jnp.concatenate([tail, jnp.zeros((512, 2 * width - n), F32)], 1)
    return top, jnp.where(upper, rest[:, :width], tail)


def put(keep, send, lanes, value):
    keep[:, lanes] = value[:256].astype(BF)
    send[:, lanes] = value[256:].astype(BF)


def feed_grads_kernel(normed, active, hidden_low, grad, index, *outs):
    keeps, sends, up_rows = outs[0:2], outs[2:4], outs[4]
    d_up = t_mm(normed[...], hidden_low[...]).astype(BF)
    total = jnp.sum(hidden_low[...].astype(F32), 0, keepdims=True)
    of_chip = mm_t(jnp.where(own_lanes(), total, 0.0).astype(BF), lanes_of()).astype(BF)
    up_rows[...] = mm(placed(index, 12, 64), of_chip)
    for p in range(2):
        qa, qb = placed(index, 2 * p, 768), placed(index, 2 * p + 1, 384)
        top, rest = laid_out(d_up[:, 768 * p : 768 * p + 768], qa, qb, 384)
        put(keeps[p], sends[p], slice(0, 768), top)
        put(keeps[p], sends[p], slice(768, 1152), rest)
    d_down = t_mm(active[...], grad[...]).reshape(64, 3, 8, 768)
    slabs = [placed(index, 9 + p, 512) for p in range(2)]
    for k in range(3):
        rows = d_down[:, k].reshape(512, 768).astype(BF)
        for p, slab in enumerate(slabs):
            moved = mm(slab, rows[:, 384 * p : 384 * p + 384])
            put(keeps[p], sends[p], slice(1152 + 384 * k, 1536 + 384 * k), moved)


def feed_grads(normed, active, hidden_low, grad, index):
    return staged(
        "feed_grads",
        feed_grads_kernel,
        (),
        (normed, active, hidden_low, grad, index),
        (*[shape((256, 2304), BF)] * 4, shape((512, 128), F32)),
        6e9,
    )


def cross_backward_kernel(
    info, vec, grad, mine, got, after, w_out, queries, kv, w_query, before,
    stream, low, dq, dkv, back, sums,
):
    xhat, inv = normalize(after[...])
    step = norm_back(mine[...] + got[...], vec[3:4], xhat, inv)
    stream[...] = grad[...].astype(F32) + step
    low[...] = stream[...].astype(BF)
    mixed_grad = mm_t(low[...], w_out[...]).astype(BF)
    for row in range(2):
        allowed = cross_allowed(info, row)
        at = slice(128 * row, 128 * row + 128)
        for j in range(3):
            lanes = slice(128 * j, 128 * j + 128)
            value_lanes = slice(384 + 128 * j, 512 + 128 * j)
            q = stacked(queries[at, lanes]) * 0.125
            do = stacked(mixed_grad[at, lanes])
            k = row_keys(kv, row, lanes)
            v = row_keys(kv, row, value_lanes)
            probs = softmax(mm_t(q, k), allowed)
            ds = softmax_back(probs, mm_t(do, v))
            dq[at, lanes] = (merged(mm(ds, k)) * 0.125).astype(BF)
            dk = t_mm(ds, q).astype(BF)
            dv = t_mm(probs.astype(BF), do).astype(BF)
            for value, where in ((dk, lanes), (dv, value_lanes)):
                dkv[384 * row : 384 * row + 384, where] = value[:384]
                dkv[768 + 384 * row : 1152 + 384 * row, where] = value[384:]
    back[...] = mm_t(dq[...], w_query[...])
    xhat, _ = normalize(before[...])
    sums[...] = jnp.concatenate(
        [
            jnp.sum(back[...] * xhat, 0, keepdims=True),
            jnp.sum(back[...], 0, keepdims=True),
            jnp.zeros((6, 768), F32),
        ],
        0,
    )


def cross_backward(info, vec, grad, mine, got, after, w_out, queries, kv, w_query, before):
    return staged(
        "cross_backward",
        cross_backward_kernel,
        (info,),
        (vec, grad, mine, got, after, w_out, queries, kv, w_query, before),
        (shape((256, 768), F32), shape((256, 768), BF), shape((256, 384), BF), shape((1536, 768), BF), shape((256, 768), F32), shape((8, 768), F32)),
        5e9,
    )


def cross_part(p, weight, mixed, low, index, keep, send):
    qa, qb = placed(index, 2 * p, 768), placed(index, 2 * p + 1, 384)
    top, rest = laid_out(weight, qa, qb, 256)
    put(keep, send, slice(0, 384), top)
    put(keep, send, slice(384, 640), rest)
    d_out = t_mm(mixed[...], low[:, 256 * p : 256 * p + 256]).astype(BF)
    put(keep, send, slice(640, 896), mm(placed(index, 6 + p, 384), d_out))


def image_grads_kernel(image_normed, dkv, mixed, low, index, keep0, keep1, send0, send1):
    d_kv = t_mm(image_normed[...], dkv[...]).astype(BF)
    cross_part(0, d_kv[:, :384], mixed, low, index, keep0, send0)
    cross_part(1, d_kv[:, 384:], mixed, low, index, keep1, send1)


def image_grads(image_normed, dkv, mixed, low, index):
    return staged(
        "image_grads",
        image_grads_kernel,
        (),
        (image_normed, dkv, mixed, low, index),
        [shape((256, 896), BF)] * 4,
        4e9,
    )


def query_grads_kernel(normed, dq, mixed, low, index, keep, send):
    d_query = t_mm(normed[...], dq[...]).astype(BF)
    cross_part(2, d_query, mixed, low, index, keep, send)


def query_grads(normed, dq, mixed, low, index):
    return staged(
        "query_grads",
        query_grads_kernel,
        (),
        (normed, dq, mixed, low, index),
        [shape((256, 896), BF)] * 2,
        1e9,
    )


def image_part_kernel(dkv, w_kv, out):
    out[...] = mm_t(dkv[768:], w_kv[...]).astype(BF)


def image_part(dkv, w_kv):
    return staged(
        "image_part",
        image_part_kernel,
        (),
        (dkv, w_kv),
        (shape((768, 768), BF),),
        1e9,
    )


def image_backward_kernel(vec, dkv, w_kv, got, own, out, low1, low2, low3, sums):
    total = [jnp.zeros((1, 768), F32)] * 2
    for image, result in enumerate((out, low1, low2, low3)):
        at = slice(192 * image, 192 * image + 192)
        dy = mm_t(dkv[at], w_kv[...]) + got[at].astype(F32)
        xhat, inv = normalize(own[at].astype(F32))
        total = [
            total[0] + jnp.sum(dy * xhat, 0, keepdims=True),
            total[1] + jnp.sum(dy, 0, keepdims=True),
        ]
        result[...] = norm_back(dy, vec[2:3], xhat, inv)[:188].astype(result.dtype)
    sums[...] = jnp.concatenate(total + [jnp.zeros((6, 768), F32)], 0)


def image_backward(vec, dkv, w_kv, got, own):
    return staged(
        "image_backward",
        image_backward_kernel,
        (),
        (vec, dkv, w_kv, got, own),
        (shape((188, 768), F32), *[shape((188, 768), BF)] * 3, shape((8, 768), F32)),
        1e9,
    )


def self_backward_kernel(
    info, vec, stream_in, mine, got, before, w_out, joined, w_qkv, text,
    stream_mine, low, d_joined, to_mine, to_other, sums,
    stream, back,
):
    xhat, inv = normalize(before[...])
    stream[...] = stream_in[...] + norm_back(mine[...] + got[...], vec[1:2], xhat, inv)
    low[...] = stream[...].astype(BF)
    mixed_grad = mm_t(low[...], w_out[...]).astype(BF)
    for row in range(2):
        allowed = self_allowed(info, row)
        at = slice(128 * row, 128 * row + 128)
        for j in range(3):
            lanes = [slice(384 * i + 128 * j, 384 * i + 128 * j + 128) for i in range(3)]
            q = stacked(joined[at, lanes[0]]) * 0.125
            k = joined[at, lanes[1]]
            v = joined[at, lanes[2]]
            do = stacked(mixed_grad[at, lanes[0]])
            probs = softmax(mm_t(q, k), allowed)
            ds = softmax_back(probs, mm_t(do, v))
            d_joined[at, lanes[0]] = (merged(mm(ds, k)) * 0.125).astype(BF)
            d_joined[at, lanes[1]] = t_mm(ds, q).astype(BF)
            d_joined[at, lanes[2]] = t_mm(probs.astype(BF), do).astype(BF)
    back[...] = mm_t(d_joined[...], w_qkv[...])
    xhat, _ = normalize(text[...].astype(F32))
    sums[...] = jnp.concatenate(
        [
            jnp.sum(back[...] * xhat, 0, keepdims=True),
            jnp.sum(back[...], 0, keepdims=True),
            jnp.zeros((6, 768), F32),
        ],
        0,
    )
    core = info[0]
    for row in range(2):
        at = pl.ds(pl.multiple_of(128 * row + 64 * core, 64), 64)
        stream_mine[64 * row : 64 * row + 64] = stream[at]
        to_mine[64 * row : 64 * row + 64] = back[at]
        at = pl.ds(pl.multiple_of(128 * row + 64 * (1 - core), 64), 64)
        to_other[64 * row : 64 * row + 64] = back[at]


def self_backward(info, vec, stream_in, mine, got, before, w_out, joined, w_qkv, text):
    return staged(
        "self_backward",
        self_backward_kernel,
        (info,),
        (vec, stream_in, mine, got, before, w_out, joined, w_qkv, text),
        (shape((128, 768), F32), shape((256, 768), BF), shape((256, 1152), BF), shape((128, 768), F32), shape((128, 768), F32), shape((8, 768), F32)),
        3e9,
        [pltpu.VMEM((256, 768), F32), pltpu.VMEM((256, 768), F32)],
    )


def self_grads_kernel(
    normed, d_joined, mixed, low, sum0, sum1, sum2, sum3, grad, up_rows,
    index, e0, e1, e2, *outs,
):
    keeps, sends = outs[0:3], outs[3:6]
    for send, early in zip(sends, (e0, e1, e2)):
        send[:, :896] = early[...]
    d_qkv = t_mm(normed[...], d_joined[...]).astype(BF)
    d_out = t_mm(mixed[...], low[...]).astype(BF)
    for p in range(3):
        qa, qb = placed(index, 2 * p, 768), placed(index, 2 * p + 1, 384)
        o = placed(index, 6 + p, 384)
        top, rest = laid_out(d_qkv[:, 384 * p : 384 * p + 384], qa, qb, 256)
        moved = mm(o, d_out[:, 256 * p : 256 * p + 256])
        for at, value in ((0, top), (384, rest), (640, moved)):
            n = value.shape[1]
            keeps[p][:, at : at + n] = value[:256].astype(BF)
            sends[p][:, 896 + at : 896 + at + n] = value[256:].astype(BF)
    down_sum = jnp.sum(grad[...].astype(F32), 0, keepdims=True) * 0.5
    rows = [s[i : i + 1] for i in range(2) for s in (sum0, sum1, sum2, sum3)]
    rows = jnp.concatenate(rows + [down_sum, jnp.zeros((7, 768), F32)], 0).astype(BF)
    zero = jnp.zeros((16, 768), BF)
    first = jnp.concatenate([rows] + [zero] * 7, 0)
    second = jnp.concatenate([zero, rows] + [zero] * 6, 0)
    value = mm_t(qa, first) + mm_t(qb, second[:, 384:]) + up_rows[...]
    keeps[2][:, 896:1024] = value[:256].astype(BF)
    sends[2][:, 1792:1920] = value[256:].astype(BF)


def self_grads(normed, d_joined, mixed, low, sums, grad, up_rows, index, early):
    return staged(
        "self_grads",
        self_grads_kernel,
        (),
        (normed, d_joined, mixed, low, *sums, grad, up_rows, index, *early),
        (*[shape((256, n), BF) for n in (896, 896, 1024, 1792, 1792, 1920)],),
        3e9,
    )


def first_core(info, dims):
    return lax.broadcasted_iota(jnp.int32, dims, 0) * 0 + info[0] == 0


BLOCKS = ((0, 3, 384), (1, 2, 384), (2, 1, 384), (3, 1, 1536))


def halves_into(core, refs, target, sem):
    copies, here = [], 0
    for which, blocks, width in BLOCKS:
        for i in range(blocks):
            at = pl.multiple_of(2 * i * width + core * width, 128)
            copies.append(
                pltpu.make_async_copy(
                    refs[which].at[:, pl.ds(at, width)], target.at[:, pl.ds(here, width)],
                    sem.at[len(copies)],
                )
            )
            here += width
    return copies


def vector_rows(gain, bias, down_bias):
    total = jnp.zeros((6, 128), F32)
    for at, ref in ((0, gain), (4, bias), (8, down_bias)):
        n = ref.shape[0]
        i = lax.broadcasted_iota(jnp.int32, (n, 128), 0) + at
        j = lax.broadcasted_iota(jnp.int32, (n, 128), 1)
        total = total + t_mm(ref[...], ((i == j) | (i + 16 == j)).astype(F32).astype(BF))
    return total


def pack_swap_kernel(info, qkv, kv, query, up, gain, bias, down_bias, send, half, sem):
    copies = halves_into(1 - info[0], (qkv, kv, query, up), half, sem)
    for c in copies:
        c.start()
    send[:, 3840:] = vector_rows(gain, bias, down_bias).astype(BF)
    for c in copies:
        c.wait()
    send[:, :3840] = half[...]


def pack_slots_kernel(
    info, qkv, kv, query, up, self_out, cross_out, down, got, gain, bias, down_bias, up_bias,
    slot, twelve, half, outs, slabs, theirs, sem, sems,
):
    copies = halves_into(info[0], (qkv, kv, query, up), half, sem)
    others = [
        pltpu.make_async_copy(self_out, outs.at[0], sems.at[0]),
        pltpu.make_async_copy(cross_out, outs.at[1], sems.at[1]),
        pltpu.make_async_copy(down, slabs, sems.at[2]),
    ]
    sent = pltpu.make_async_copy(got, theirs, sems.at[3])
    sent.start()
    for c in copies + others:
        c.start()
    first = first_core(info, (6, 128))
    mine = vector_rows(gain, bias, down_bias)
    sent.wait()
    other = theirs[:, 3840:].astype(F32)
    twelve[0:6, 4608:] = jnp.where(first, mine, other)
    twelve[6:12, 4608:] = jnp.where(first, other, mine)
    twelve[12:16, 4608:] = jnp.zeros((4, 128), F32)
    lane = lax.broadcasted_iota(jnp.int32, (8, 128), 1)
    row = lax.broadcasted_iota(jnp.int32, (8, 128), 0)
    vec = jnp.where(lane < 16, twelve[0:8, 4608:], 0.0)
    vec = vec + jnp.where((lane >= 16) & (lane < 32), twelve[8:16, 4608:], 0.0)
    i = lax.broadcasted_iota(jnp.int32, (24, 128), 0)
    j = lax.broadcasted_iota(jnp.int32, (24, 128), 1)
    units = mm(up_bias[...], (i + 64 == j).astype(F32).astype(BF))
    slot[:, 6912:7040] = (vec + jnp.where(row == 0, units, 0.0)).astype(BF)
    for c in copies:
        c.wait()
    first = first_core(info, (6, 3840))
    mine = half[...].astype(F32)
    other = theirs[:, :3840].astype(F32)
    twelve[0:6, :3840] = jnp.where(first, mine, other)
    twelve[6:12, :3840] = jnp.where(first, other, mine)
    for c in others:
        c.wait()
    twelve[0:6, 3840:4608] = outs[0].astype(F32)
    twelve[6:12, 3840:4608] = outs[1].astype(F32)
    slot[:, :4608] = twelve[0:8, :4608].astype(BF)
    twelve[0:4, :2304] = twelve[8:12, :2304]
    twelve[4:8, :2304] = twelve[8:12, 2304:4608]
    slot[:, 4608:6912] = twelve[0:8, :2304].astype(BF)
    wide = slabs[...].astype(F32)
    for k in range(3):
        at = 7040 + 768 * k
        slot[:, at : at + 768] = wide[8 * k : 8 * k + 8].astype(BF)


def packed(name, kernel, info, far, near, out, scratch):
    return pl.pallas_call(
        kernel,
        out_shape=out,
        in_specs=[SMEM] + [HBM] * len(far) + [VMEM] * len(near),
        out_specs=VMEM,
        scratch_shapes=scratch,
        compiler_params=params(60),
        cost_estimate=cost(1e6, 1e6),
        name=name,
    )(info, *far, *near)


def pack_swap(info, weights, vectors):
    return packed(
        "pack_swap",
        pack_swap_kernel,
        info,
        weights,
        vectors,
        shape((6, 3968), BF),
        [pltpu.VMEM((6, 3840), BF), pltpu.SemaphoreType.DMA((7,))],
    )


def pack_slots(info, weights, vectors, got, self_out, cross_out, down, up_bias):
    return packed(
        "pack_slots",
        pack_slots_kernel,
        info,
        (*weights, self_out, cross_out, down, got),
        (*vectors, up_bias),
        shape((8, 9344), BF),
        [
            pltpu.VMEM((16, 4736), F32),
            pltpu.VMEM((6, 3840), BF),
            pltpu.VMEM((2, 6, 768), BF),
            pltpu.VMEM((24, 768), BF),
            pltpu.VMEM((6, 3968), BF),
            pltpu.SemaphoreType.DMA((7,)),
            pltpu.SemaphoreType.DMA((4,)),
        ],
    )


BASE = (2304, 2304, 0)
TWELVES = [(p, 0, 768, 384) for p in range(2)] + [
    (p, BASE[p] + at, 384, 256) for at in (0, 896) for p in range(3)
]


def finish_send_kernel(info, *refs):
    k_ac, k_b, g_ac, g_b, s0, s1, s2, send, own, twelve = refs
    sums, n = (s0, s1, s2), s0.shape[1]
    s0[...] = k_ac[:, :n].astype(F32) + g_ac[:, :n].astype(F32)
    s2[...] = k_ac[:, n:].astype(F32) + g_ac[:, n:].astype(F32)
    s1[...] = k_b[...].astype(F32) + g_b[...].astype(F32)
    here = 0
    for p, at, n, width in TWELVES:
        ref = sums[p]
        twelve[0:8, here : here + n] = ref[:, at : at + n]
        twelve[8:12, here : here + width] = ref[0:4, at + n : at + n + width]
        twelve[8:12, here + width : here + n] = ref[4:8, at + n : at + n + n - width]
        here += n
    vec = s2[:, 1792:]
    twelve[0:8, 3840:] = vec
    twelve[8:12, 3840:] = pltpu.roll(vec, 112, 1)[0:4]
    first = first_core(info, (6, 3968))
    send[...] = jnp.where(first, twelve[6:12], twelve[0:6])
    own[...] = jnp.where(first, twelve[0:6], twelve[6:12])


def finish_kernel(
    info, s0, s1, s2, own, got, qkv, out_self, query, kv, out_cross, up, down, gain, bias, down_bias
):
    sums = (s0, s1, s2)
    first = first_core(info, (6, 3840))
    low = jnp.where(first, own[:, :3840], got[:, :3840])
    high = jnp.where(first, got[:, :3840], own[:, :3840])
    for ref, begin, blocks, width in (
        (up, 0, 1, 1536), (kv, 1536, 2, 384), (query, 2304, 1, 384), (qkv, 2688, 3, 384),
    ):
        for i in range(blocks):
            at = begin + i * width
            ref[:, 2 * i * width : (2 * i + 1) * width] = low[:, at : at + width]
            ref[:, (2 * i + 1) * width : (2 * i + 2) * width] = high[:, at : at + width]
    for p in range(3):
        lanes = slice(256 * p, 256 * p + 256)
        out_cross[:, lanes] = sums[p][0:6, BASE[p] + 640 : BASE[p] + 896]
        out_self[:, lanes] = sums[p][0:6, BASE[p] + 1536 : BASE[p] + 1792]
    for p in range(2):
        for k in range(3):
            at = 1152 + 384 * k
            down[8 * k : 8 * k + 8, 384 * p : 384 * p + 384] = sums[p][:, at : at + 384]
    total = jnp.concatenate([own[:, 3840:] + got[:, 3840:], jnp.zeros((122, 128), F32)], 0)
    across = jnp.transpose(total)
    gain[...] = across[0:4, 0:6]
    bias[...] = across[4:8, 0:6]
    down_bias[...] = across[8:9, 0:6]


def finish_send(info, keeps, gots, widths):
    return staged(
        "finish_send",
        finish_send_kernel,
        (info,),
        (*keeps, *gots),
        [shape((8, n), F32) for n in widths] + [shape((6, 3968), F32)] * 2,
        1e6,
        [pltpu.VMEM((16, 3968), F32)],
        mib=8,
    )


def finish(info, sums, own, got):
    return staged(
        "finish",
        finish_kernel,
        (info,),
        (*sums, own, got),
        [
            shape(dims, F32)
            for dims in (
                (6, 2304), (6, 768), (6, 768), (6, 1536), (6, 768), (6, 3072), (24, 768), (4, 6), (4, 6),
                (1, 6),
            )
        ],
        1e6,
        mib=8,
    )


def text_finish_kernel(vec, text, stream, mine, got, out_mine, out_got, grad, out):
    xhat, inv = normalize(text[...].astype(F32))
    grad[...] = stream[...] + norm_back(mine[...] + got[...], vec[0:1], xhat, inv)
    out[...] = out_mine[...] + out_got[...]


def text_finish(vec, text, stream, mine, got, out_mine, out_got):
    return staged(
        "text_finish",
        text_finish_kernel,
        (),
        (vec, text, stream, mine, got, out_mine, out_got),
        [shape((128, 768), F32)] * 2,
        1e6,
        mib=8,
    )


def image_finish_kernel(pick, v0, v1, v2, v3, out):
    values = [v[...].astype(F32) for v in (v0, v1, v2, v3)]
    for image in range(4):
        total = values[3]
        for turn in range(3):
            total = jnp.where(pick[turn] == image, values[turn], total)
        out[:, image, :] = total


def image_finish(pick, values):
    out = staged(
        "image_finish",
        image_finish_kernel,
        (pick,),
        values,
        [shape((188, 4, 768), F32)],
        1e6,
    )[0]
    return jnp.transpose(out, (1, 0, 2))


def combine_kernel(plan, *refs):
    at = 0
    ins = []
    for keeps, gots in plan:
        ins.append((refs[at : at + len(keeps)], refs[at + len(keeps) : at + len(keeps) + len(gots)]))
        at += len(keeps) + len(gots)
    outs = refs[at:]
    for p, (keeps, gots) in enumerate(ins):
        here = 0
        edges = []
        for ref in keeps:
            edges.append((here, here + ref.shape[1], ref))
            here += ref.shape[1]
        here = 0
        for ref in gots:
            for low, high, keep in edges:
                a, b = max(low, here), min(high, here + ref.shape[1])
                if a >= b:
                    continue
                total = keep[:, a - low : b - low].astype(F32) + ref[:, a - here : b - here].astype(F32)
                half = total.shape[0] // 2
                outs[2 * p][:, a:b] = total[:half].astype(BF)
                outs[2 * p + 1][:, a:b] = total[half:].astype(BF)
            here += ref.shape[1]


def combine(parts):
    plan, args, outs = [], [], []
    for keeps, gots in parts:
        plan.append(([k.shape[1] for k in keeps], [g.shape[1] for g in gots]))
        args += [*keeps, *gots]
        rows, width = keeps[0].shape[0], sum(k.shape[1] for k in keeps)
        outs += [shape((rows // 2, width), BF)] * 2
    got = staged(
        "combine", lambda *refs: combine_kernel(plan, *refs), (), args, outs, 1e6
    )
    return [(got[2 * p], got[2 * p + 1]) for p in range(len(parts))]


def regroup_kernel(k_a, g_a, k_bc, g_bc, keep_ac, send_ac, keep_b, send_b):
    first = k_a[...].astype(F32) + g_a[...].astype(F32)
    second = k_bc[...].astype(F32) + g_bc[...].astype(F32)
    n, m, half = k_a.shape[1], keep_b.shape[1], k_a.shape[0] // 2
    for rows, ac, b in ((slice(0, half), keep_ac, keep_b), (slice(half, 2 * half), send_ac, send_b)):
        ac[:, :n] = first[rows].astype(BF)
        ac[:, n:] = second[rows, m:].astype(BF)
        b[...] = second[rows, :m].astype(BF)


def regroup(k_a, g_a, k_bc, g_bc, m):
    half, n = k_a.shape[0] // 2, k_a.shape[1]
    widths = (n + k_bc.shape[1] - m, n + k_bc.shape[1] - m, m, m)
    got = staged(
        "regroup",
        regroup_kernel,
        (),
        (k_a, g_a, k_bc, g_bc),
        [shape((half, w), BF) for w in widths],
        1e6,
    )
    return [(got[0], got[1]), (got[2], got[3])]


def send_step(step, values, parts=(0, 1, 2)):
    v0, v1 = ((1, 3), (3, 1))[step % 2]
    return [
        lax.ppermute(v, BOTH, xor_pairs(ORDERS[p][step // 2], v0, v1)) for v, p in zip(values, parts)
    ]


def after(value, *others):
    return lax.optimization_barrier((value, *others))[0]


def image_moves(images, way):
    once = [(core + i, core + (i + 16 * way) % 64) for core in (0, 64) for i in range(64)]
    first, second, third = images
    return [
        lax.ppermute(first, BOTH, once),
        move_on(second),
        lax.ppermute(third, BOTH, [(j, i) for i, j in once]),
    ]


def move_on(image):
    route = [(i, (i + 16) % 64) for i in range(64)]
    return lax.ppermute(image, BOTH, route + [(64 + j, 64 + i) for i, j in route])


def on_device(
    text_input,
    image_tokens,
    output_grad,
    segment_starts,
    caption_image,
    image_counts,
    norm_gain,
    norm_bias,
    self_qkv,
    self_out,
    cross_q,
    cross_kv,
    cross_out,
    up_weight,
    up_bias,
    down_weight,
    down_bias,
):
    core = lax.axis_index("seq")
    chip = lax.axis_index("batch")
    first = core == 0

    def ordered(own, other, axis):
        return jnp.where(
            first, jnp.concatenate([own, other], axis), jnp.concatenate([other, own], axis)
        )

    place = jnp.stack([core, chip]).astype(jnp.int32)
    weights = (self_qkv, cross_kv, cross_q, up_weight)
    vectors = (norm_gain, norm_bias, down_bias[None])
    got = swap(pack_swap(place, weights, vectors))
    slot = pack_slots(
        place, weights, vectors, got, self_out, cross_out, down_weight, up_bias[None]
    )
    gathered = lax.all_gather(slot, "batch", axis=0, tiled=True)

    late_text, late_grad = after(text_input, slot), after(output_grad, slot)
    text = ordered(late_text, swap(late_text), 1).reshape(256, 768)
    grad = ordered(late_grad, swap(late_grad), 1).reshape(256, 768)

    group_images = after(caption_image, slot).reshape(64, 8)
    my_captions = lax.dynamic_index_in_dim(group_images, chip, 0, keepdims=False)
    limits = jnp.take(image_counts, my_captions).reshape(4, 2)
    limits = jnp.where(first, jnp.concatenate([limits[:, 0], limits[:, 1]]), jnp.concatenate([limits[:, 1], limits[:, 0]]))
    turns = jnp.arange(4)
    targets = (chip - turns * 16) % 64
    wanted = group_images[targets, 2 * turns + core]
    local_pick = wanted - (core * 64 + chip) * 4
    outgoing = image_pick(after(local_pick, slot), image_tokens)
    received = [outgoing[0], *image_moves(outgoing[1:], -1)]
    received[2] = move_on(received[2])
    own_images = image_stack(received)
    other_images = swap(own_images)
    info = jnp.concatenate(
        [core[None], segment_starts.reshape(8), limits, jnp.zeros((15,), jnp.int32)]
    ).astype(jnp.int32)

    column_index = indices(after(place, slot))

    gathered, info, grad, text, column_index, own_images, other_images = lax.optimization_barrier(
        (gathered, info, grad, text, column_index, own_images, other_images)
    )
    w_qkv, w_kv, w_query, w_up, w_self, w_cross, w_down, vec, b_up = unpack(gathered)
    part, joined, mixed_self, normed_one = self_forward(info, vec, w_qkv, w_self, text)
    got = swap(part)
    kv, image_normed = image_forward(vec, w_kv, own_images, other_images)
    after_self, normed_two, q_cross, mixed_cross, part = cross_forward(
        info, vec, text, part, got, kv, w_query, w_cross
    )
    after_cross, normed_three, active, hidden_low, text_mine, text_other, part, sum3 = feed(
        info, vec, b_up, after_self, part, swap(part), w_up, w_down, grad
    )
    text_got = swap(text_other)
    got = swap(part)

    grads = feed_grads(normed_three, active, hidden_low, grad, column_index)
    keep_one, up_rows = grads[0:2], grads[4]
    got_one = send_step(0, grads[2:4], (0, 1))
    stream_two, cross_low, dq, dkv, part, sum1 = cross_backward(
        info, vec, after(grad, keep_one[0]), part, got, after_cross, w_cross, q_cross, kv, w_query, after_self
    )
    got = swap(part)
    image_send = image_part(dkv, w_kv)[0]
    *rows_back, sum2 = image_backward(vec, dkv, w_kv, swap(image_send), own_images)
    returned = [rows_back[0], *image_moves(rows_back[1:], 1)]
    k_keep, v_keep, k_send, v_send = image_grads(
        image_normed, after(dkv, sum2), mixed_cross, cross_low, column_index
    )
    returned[2] = move_on(after(returned[2], k_keep))
    q_keep, q_send = query_grads(
        normed_two, after(dq, k_keep), mixed_cross, cross_low, column_index
    )
    keep_two, early = [k_keep, v_keep, q_keep], [k_send, v_send, q_send]
    stream_one, self_low, d_joined, one_mine, one_other, sum0 = self_backward(
        info, vec, after(stream_two, q_keep), part, got, after_self, w_self, joined,
        w_qkv, text,
    )
    self_low, *late = lax.optimization_barrier((self_low, *returned[1:], *got_one))
    returned, got_one = returned[:1] + late[:3], late[3:]
    grads = self_grads(
        normed_one, d_joined, mixed_self, self_low, (sum0, sum1, sum2, sum3), grad, up_rows,
        column_index, early,
    )
    keep_three = grads[0:3]
    got_two = send_step(0, grads[3:6])
    one_got = swap(one_other)
    image_grad = image_finish(after(local_pick, grads[3]), returned)
    text_grad, text_output = text_finish(
        after(vec, grads[3]), text_input.reshape(128, 768), stream_one, one_mine, one_got, text_mine,
        text_got,
    )
    got_two, image_grad, text_grad = lax.optimization_barrier((got_two, image_grad, text_grad))
    pairs = []
    for p in range(3):
        keeps, gots = [keep_two[p], keep_three[p]], [got_two[p]]
        if p < 2:
            keeps, gots = [keep_one[p], *keeps], [got_one[p], *gots]
        pairs += combine([(keeps, gots)])
    a_got, b_got, c_got = send_step(1, [v for _, v in pairs])
    saved = pairs
    pairs = combine([([pairs[0][0]], [a_got])])
    pairs += combine([([saved[1][0], saved[2][0]], [b_got, c_got])])
    for step in (2, 3):
        got_step = send_step(step, [v for _, v in pairs], (0, 1))
        if step == 2:
            pairs = combine([([k], [g]) for (k, _), g in zip(pairs, got_step)])
    pairs = regroup(*[v for (k, _), g in zip(pairs, got_step) for v in (k, g)], saved[1][0].shape[1])
    got_step = send_step(4, [v for _, v in pairs], (0, 1))
    pairs = combine([([k], [g]) for (k, _), g in zip(pairs, got_step)])
    got_step = send_step(5, [v for _, v in pairs], (0, 1))
    *sums, send, own = finish_send(
        place, [k for k, _ in pairs], got_step, [k.shape[1] for k, _ in saved]
    )

    text_grad, text_output = text_grad.reshape(2, 64, 768), text_output.reshape(2, 64, 768)

    (
        qkv_grad, self_grad, query_grad, kv_grad, cross_grad, up_grad, down_grad, gain_grad, bias_grad,
        down_bias_grad,
    ) = finish(place, sums, own, swap(send))
    up_bias_grad = sums[2][0, 1856:1880]
    return (
        text_output,
        text_grad,
        image_grad,
        gain_grad,
        bias_grad,
        qkv_grad,
        self_grad,
        query_grad,
        kv_grad,
        cross_grad,
        up_grad,
        up_bias_grad,
        down_grad,
        down_bias_grad[0],
    )


def solution(mesh):
    rows = P("batch", "seq", None)
    shard = P(BOTH, None)
    wide = P(None, BOTH)
    return jax.shard_map(
        on_device,
        mesh=mesh,
        in_specs=(
            rows, P(BOTH, None, None), rows, P("batch", None), P(), P(), wide, wide,
            shard, shard, shard, shard, shard, shard, P(BOTH), shard, P(BOTH),
        ),
        out_specs=(
            rows, rows, P(BOTH, None, None), wide, wide,
            shard, shard, shard, shard, shard, shard, P(BOTH), shard, P(BOTH),
        ),
        check_vma=False,
    )
```

```python
import math

import jax
import jax.numpy as jnp
from jax import lax
from jax.experimental import pallas as pl
from jax.experimental.pallas import tpu as pltpu
from jax.sharding import PartitionSpec as P

HEADS = 12
HEAD_DIM = 64
EPSILON = 1e-05
MASKED_SCORE = -1e30
BF = jnp.bfloat16
F32 = jnp.float32
BOTH = ("seq", "batch")
STRIDE = {"z": 16, "y": 4, "x": 1}
ORDERS = (("x", "z", "y"), ("y", "x", "z"), ("z", "x", "y"))


def xor_pairs(axis, value0, value1):
    step, out = STRIDE[axis], []
    for core, value in ((0, value0), (1, value1)):
        for chip in range(64):
            at = chip // step % 4
            out.append((core * 64 + chip, core * 64 + chip + ((at ^ value) - at) * step))
    return out


def swap(value):
    return lax.ppermute(value, "seq", [(0, 1), (1, 0)])


def mm(a, b):
    return jnp.dot(a, b, preferred_element_type=F32)


def mm_t(a, b):
    return lax.dot_general(a, b, (((1,), (1,)), ((), ())), preferred_element_type=F32)


def t_mm(a, b):
    return lax.dot_general(a, b, (((0,), (0,)), ((), ())), preferred_element_type=F32)


def normalize(values):
    center = jnp.mean(values, -1, keepdims=True)
    centred = values - center
    spread = jnp.mean(centred * centred, -1, keepdims=True)
    inv = lax.rsqrt(spread + EPSILON)
    return centred * inv, inv


def norm_back(grad, gain, xhat, inv):
    scaled = grad * gain
    return inv * (
        scaled
        - jnp.mean(scaled, -1, keepdims=True)
        - xhat * jnp.mean(scaled * xhat, -1, keepdims=True)
    )


VMEM = pl.BlockSpec(memory_space=pltpu.VMEM)
SMEM = pl.BlockSpec(memory_space=pltpu.SMEM)
HBM = pl.BlockSpec(memory_space=pltpu.HBM)


def shape(dims, dtype):
    return jax.ShapeDtypeStruct(dims, dtype)


def cost(flops, moved):
    return pl.CostEstimate(
        flops=int(flops / 64), bytes_accessed=int(moved / 64), transcendentals=0
    )


def params(mib):
    return pltpu.CompilerParams(vmem_limit_bytes=mib * 1024 * 1024)


def staged(name, kernel, scalars, ins, outs, work, scratch=(), mib=16):
    moved = sum(math.prod(v.shape) * v.dtype.itemsize for v in (*ins, *outs))
    return pl.pallas_call(
        kernel,
        out_shape=tuple(outs),
        in_specs=[SMEM] * len(scalars) + [VMEM] * len(ins),
        out_specs=(VMEM,) * len(outs),
        scratch_shapes=list(scratch),
        compiler_params=params(mib),
        cost_estimate=cost(work, moved),
        name=name,
    )(*scalars, *ins)


def placed(columns, i, size):
    place = lax.broadcasted_iota(jnp.int32, (512, size), 1)
    return (place == columns[:, i : i + 1]).astype(F32).astype(BF)


def segment_of(info, row, dims, axis):
    place = lax.broadcasted_iota(jnp.int32, dims, axis)
    total = jnp.full(dims, -1, jnp.int32)
    for j in range(4):
        total = total + (place >= info[1 + 4 * row + j]).astype(jnp.int32)
    return total


def low_lanes():
    return lax.broadcasted_iota(jnp.int32, (1, 128), 1) < 64


def stacked(pair):
    left = low_lanes()
    zero = jnp.zeros_like(pair)
    return jnp.concatenate([jnp.where(left, pair, zero), jnp.where(left, zero, pair)], 0)


def merged(two):
    n = two.shape[0] // 2
    return jnp.where(low_lanes(), two[:n], two[n:])


def softmax(scores, allowed):
    scores = jnp.where(allowed, scores, MASKED_SCORE)
    weights = jnp.exp(scores - jnp.max(scores, -1, keepdims=True))
    return weights * (1.0 / jnp.sum(weights, -1, keepdims=True))


def softmax_back(probs, dprobs):
    return (probs * (dprobs - jnp.sum(probs * dprobs, -1, keepdims=True))).astype(BF)


def self_allowed(info, row):
    at = segment_of(info, row, (128, 128), 0)
    key = segment_of(info, row, (128, 128), 1)
    i = lax.broadcasted_iota(jnp.int32, (128, 128), 0)
    j = lax.broadcasted_iota(jnp.int32, (128, 128), 1)
    allowed = (at == key) & (j <= i)
    return jnp.concatenate([allowed, allowed], 0)


def cross_allowed(info, row):
    core = info[0]
    lane = lax.broadcasted_iota(jnp.int32, (1, 768), 1)
    key = jnp.full((1, 768), -1, jnp.int32)
    images = (2 * row, 2 * row + 1, 4 + 2 * row, 5 + 2 * row)
    captions = (core, 2 + core, 1 - core, 3 - core)
    for block in range(4):
        limit = info[9 + images[block]]
        key = jnp.where(
            (lane >= 192 * block) & (lane < 192 * block + limit), captions[block], key
        )
    at = segment_of(info, row, (128, 1), 0)
    return jnp.concatenate([at, at], 0) == key


def row_keys(kv, row, lanes):
    return jnp.concatenate(
        [kv[384 * row : 384 * row + 384, lanes], kv[768 + 384 * row : 1152 + 384 * row, lanes]], 0
    )


def lanes_of():
    lane = lax.broadcasted_iota(jnp.int32, (128, 1536), 0)
    unit = lax.broadcasted_iota(jnp.int32, (128, 1536), 1)
    return (lane == 64 + lax.rem(unit, 24)).astype(F32).astype(BF)


def own_lanes():
    chip = lax.broadcasted_iota(jnp.int32, (64, 1536), 0) * 24
    unit = lax.broadcasted_iota(jnp.int32, (64, 1536), 1)
    return (unit >= chip) & (unit < chip + 24)


def self_forward_kernel(info, vec, w_qkv, w_out, text, part, joined, mixed, normed):
    xhat, _ = normalize(text[...].astype(F32))
    normed[...] = (xhat * vec[0:1] + vec[4:5]).astype(BF)
    joined[...] = mm(normed[...], w_qkv[...]).astype(BF)
    for row in range(2):
        allowed = self_allowed(info, row)
        at = slice(128 * row, 128 * row + 128)
        for j in range(3):
            q = stacked(joined[at, 128 * j : 128 * j + 128]) * 0.125
            k = joined[at, 384 + 128 * j : 512 + 128 * j]
            v = joined[at, 768 + 128 * j : 896 + 128 * j]
            probs = softmax(mm_t(q, k), allowed)
            mixed[at, 128 * j : 128 * j + 128] = merged(mm(probs.astype(BF), v)).astype(BF)
    part[...] = mm(mixed[...], w_out[...])


def self_forward(info, vec, w_qkv, w_out, text):
    return staged(
        "self_forward",
        self_forward_kernel,
        (info,),
        (vec, w_qkv, w_out, text),
        (
            shape((256, 768), F32),
            shape((256, 1152), BF),
            shape((256, 384), BF),
            shape((256, 768), BF),
        ),
        2e9,
    )


def rows_of_six(first, last, shift):
    row = lax.broadcasted_iota(jnp.int32, (192, 256), 0)
    place = lax.broadcasted_iota(jnp.int32, (192, 256), 1)
    chip = lax.div(row, 6)
    r = row - 6 * chip
    hit = (place == 8 * chip + r + shift) & (r >= first) & (r <= last)
    return hit.astype(F32).astype(BF)


def unpack_kernel(
    gathered, w_qkv, w_kv, w_query, w_up, w_self, w_cross, w_down, vec, b_up, g, sems
):
    spans = ((4608, 1152), (0, 1152), (6912, 2432), (5760, 1152), (1152, 1152), (2304, 2304))
    loads = [
        pltpu.make_async_copy(gathered.at[:, pl.ds(at, n)], g.at[:, pl.ds(at, n)], sems.at[i])
        for i, (at, n) in enumerate(spans)
    ]
    loads[0].start()
    loads[1].start()
    low, high = rows_of_six(0, 5, 0), rows_of_six(0, 1, 6)
    both = jnp.concatenate([low, high], 0)
    left, right = rows_of_six(2, 5, -2), rows_of_six(2, 5, 2)

    def natural(at, n, begin, rest, outs):
        for half in range(2):
            here = slice(256 * half, 256 * half + 256)
            there = slice(192 * half, 192 * half + 192)
            rows = mm(both, g[here, at : at + n])
            outs[0][there] = rows[:192].astype(BF)
            there = slice(outs[2] + 192 * half, outs[2] + 192 * half + 192)
            outs[1][there] = (rows[192:] + mm(rest, g[here, begin : begin + n])).astype(BF)

    loads[0].wait()
    loads[1].wait()
    for i in (2, 3, 4):
        loads[i].start()
    natural(0, 1152, 4608, left, (w_qkv, w_qkv, 384))
    loads[2].wait()
    loads[5].start()
    tail = g[:, 6912:7040]
    lane = lax.broadcasted_iota(jnp.int32, (1, 128), 1)
    one = jnp.where(lane < 16, tail.astype(F32), 0.0).astype(BF)
    two = jnp.where((lane >= 16) & (lane < 32), tail.astype(F32), 0.0).astype(BF)
    halves = [slice(0, 256), slice(256, 512)]
    rows = [mm(low, one[h]) for h in halves]
    rows += [mm(high, one[h]) + mm(left, two[h]) for h in halves]
    across = jnp.transpose(jnp.concatenate(rows, 0))
    vec[...] = across[:16] + across[16:32]
    chip = lax.broadcasted_iota(jnp.int32, (64, 512), 0)
    place = lax.broadcasted_iota(jnp.int32, (64, 512), 1)
    of_chip = mm((place == 8 * chip).astype(F32).astype(BF), tail).astype(BF)
    b_up[...] = jnp.sum(jnp.where(own_lanes(), mm(of_chip, lanes_of()), 0.0), 0, keepdims=True)
    slabs = [
        g[:, 7040 + 768 * k : 7808 + 768 * k].astype(F32).reshape(64, 1, 8, 768) for k in range(3)
    ]
    w_down[...] = jnp.concatenate(slabs, 1).reshape(1536, 768).astype(BF)
    loads[3].wait()
    loads[4].wait()
    natural(1152, 768, 5760, left, (w_kv, w_kv, 384))
    natural(1920, 384, 6528, left, (w_query, w_query, 384))
    loads[5].wait()
    natural(2304, 1536, 4608, right, (w_up, w_up, 384))
    natural(3840, 768, 6144, right, (w_self, w_cross, 0))


def unpack(gathered):
    outs = ((768, 1152), (768, 768), (768, 384), (768, 1536), (384, 768), (384, 768), (1536, 768))
    return pl.pallas_call(
        unpack_kernel,
        out_shape=(
            *[shape(o, BF) for o in outs],
            shape((16, 768), F32),
            shape((1, 1536), F32),
        ),
        in_specs=[HBM],
        out_specs=(VMEM,) * 9,
        scratch_shapes=[pltpu.VMEM((512, 9344), BF), pltpu.SemaphoreType.DMA((6,))],
        compiler_params=params(46),
        cost_estimate=cost(4e9, 20e6),
        name="unpack",
    )(gathered)


def natural_row(at_slot, twelfth):
    return at_slot * 6 + twelfth + jnp.where(twelfth >= 6, 378, 0)


def index_kernel(place, columns):
    core, chip = place[0], place[1]

    def target_of(order, slot):
        first = slot * 0 + core == 0
        target = 0
        for axis, digit in zip(order, (slot >> 4, (slot >> 2) & 3, slot & 3)):
            step = STRIDE[axis]
            here = lax.rem(lax.div(chip, step), 4)
            other = jnp.where(
                first, jnp.where(digit == 1, 3, jnp.maximum(digit, 1) - 1), digit ^ (digit >> 1)
            )
            target = target + (here ^ other) * step
        return target

    def out_pick(at_slot, eight):
        return jnp.where(eight < 6, at_slot * 6 + eight, -1)

    at = lax.broadcasted_iota(jnp.int32, (512, 1), 0)
    eight = at & 7
    targets = [target_of(order, at >> 3) for order in ORDERS]
    values = []
    for target in targets:
        values += [natural_row(target, eight), natural_row(target, 8 + (eight & 3)) - 384]
    values += [out_pick(target, eight) for target in targets]
    values += [target * 8 + eight for target in targets] + [jnp.where(eight == 0, targets[2], -1)]
    for i in range(16):
        columns[:, i : i + 1] = values[i] if i < len(values) else at * 0


def indices(place):
    return staged(
        "indices",
        index_kernel,
        (place,),
        (),
        [shape((512, 16), jnp.int32)],
        1e6,
    )[0]


def image_pick_kernel(pick, tokens, *outs):
    for turn, out in enumerate(outs):
        out[...] = tokens[pick[turn]]


def image_pick(pick, tokens):
    return staged(
        "image_pick", image_pick_kernel, (pick,), (tokens,), [shape((188, 768), BF)] * 4, 1e6
    )


def image_stack_kernel(v0, v1, v2, v3, out, wide):
    wide[188:192] = jnp.zeros((4, 768), F32)
    for turn, value in enumerate((v0, v1, v2, v3)):
        wide[0:188] = value[...].astype(F32)
        out[192 * turn : 192 * turn + 192] = wide[...].astype(BF)


def image_stack(values):
    return staged(
        "image_stack",
        image_stack_kernel,
        (),
        values,
        [shape((768, 768), BF)],
        1e6,
        [pltpu.VMEM((192, 768), F32)],
    )[0]


def image_forward_kernel(vec, w_kv, own, other, kv, normed):
    row = lax.broadcasted_iota(jnp.int32, (192, 1), 0)
    for image in range(8):
        source, here = (own, 192 * image) if image < 4 else (other, 192 * image - 768)
        xhat, _ = normalize(source[here : here + 192].astype(F32))
        at = slice(192 * image, 192 * image + 192)
        normed[at] = jnp.where(row < 188, xhat * vec[2:3] + vec[6:7], 0.0).astype(BF)
        kv[at] = mm(normed[at], w_kv[...]).astype(BF)


def image_forward(vec, w_kv, own, other):
    return staged(
        "image_forward",
        image_forward_kernel,
        (),
        (vec, w_kv, own, other),
        (shape((1536, 768), BF), shape((1536, 768), BF)),
        2e9,
    )


def cross_forward_kernel(
    info, vec, text, mine, got, w_query, kv, w_out, after, normed, queries, mixed, part
):
    after[...] = text[...].astype(F32) + (mine[...] + got[...])
    xhat, _ = normalize(after[...])
    normed[...] = (xhat * vec[1:2] + vec[5:6]).astype(BF)
    queries[...] = mm(normed[...], w_query[...]).astype(BF)
    for row in range(2):
        allowed = cross_allowed(info, row)
        at = slice(128 * row, 128 * row + 128)
        for j in range(3):
            lanes = slice(128 * j, 128 * j + 128)
            q = stacked(queries[at, lanes]) * 0.125
            k = row_keys(kv, row, lanes)
            v = row_keys(kv, row, slice(384 + 128 * j, 512 + 128 * j))
            probs = softmax(mm_t(q, k), allowed)
            mixed[at, lanes] = merged(mm(probs.astype(BF), v)).astype(BF)
    part[...] = mm(mixed[...], w_out[...])


def cross_forward(info, vec, text, mine, got, kv, w_query, w_out):
    return staged(
        "cross_forward",
        cross_forward_kernel,
        (info,),
        (vec, text, mine, got, w_query, kv, w_out),
        (shape((256, 768), F32), shape((256, 768), BF), shape((256, 384), BF), shape((256, 384), BF), shape((256, 768), F32)),
        3e9,
    )


def feed_kernel(
    info, vec, b_up, before, mine, got, w_up, w_down, grad,
    after, normed, active, hidden_low, to_mine, to_other, back, sums,
    part,
):
    after[...] = before[...] + (mine[...] + got[...])
    xhat, _ = normalize(after[...])
    normed[...] = (xhat * vec[3:4] + vec[7:8]).astype(BF)
    part[...] = jnp.zeros((256, 768), F32)
    for k in range(3):
        lanes = slice(512 * k, 512 * k + 512)
        down = w_down[lanes]
        hidden = mm(normed[...], w_up[:, lanes]) + b_up[:, lanes]
        cdf = 0.5 * (1.0 + lax.erf(hidden * 0.7071067811865476))
        active[:, lanes] = (hidden * cdf).astype(BF)
        slope = cdf + hidden * (jnp.exp(-0.5 * hidden * hidden) * 0.3989422804014327)
        part[...] += mm(active[:, lanes], down)
        hidden_low[:, lanes] = (mm_t(grad[...], down) * slope).astype(BF)
    back[...] = mm_t(hidden_low[...], w_up[...])
    sums[...] = jnp.concatenate(
        [
            jnp.sum(back[...] * xhat, 0, keepdims=True),
            jnp.sum(back[...], 0, keepdims=True),
            jnp.zeros((6, 768), F32),
        ],
        0,
    )
    core = info[0]
    bias = vec[8:9]
    for row in range(2):
        at = pl.ds(pl.multiple_of(128 * row + 64 * core, 64), 64)
        to_mine[64 * row : 64 * row + 64] = after[at] + part[at] + bias
        at = pl.ds(pl.multiple_of(128 * row + 64 * (1 - core), 64), 64)
        to_other[64 * row : 64 * row + 64] = part[at]


def feed(info, vec, b_up, before, mine, got, w_up, w_down, grad):
    return staged(
        "feed",
        feed_kernel,
        (info,),
        (vec, b_up, before, mine, got, w_up, w_down, grad),
        (shape((256, 768), F32), shape((256, 768), BF), shape((256, 1536), BF), shape((256, 1536), BF), shape((128, 768), F32), shape((128, 768), F32), shape((256, 768), F32), shape((8, 768), F32)),
        3e9,
        [pltpu.VMEM((256, 768), F32)],
    )


def laid_out(weight, qa, qb, width):
    top = mm(qa, weight)
    rest = mm(qb, weight[384:])
    n = weight.shape[1]
    upper = lax.broadcasted_iota(jnp.int32, (512, 1), 0) % 8 < 4
    tail = rest[:, width:]
    if n - width < width:
        tail = jnp.concatenate([tail, jnp.zeros((512, 2 * width - n), F32)], 1)
    return top, jnp.where(upper, rest[:, :width], tail)


def put(keep, send, lanes, value):
    keep[:, lanes] = value[:256].astype(BF)
    send[:, lanes] = value[256:].astype(BF)


def feed_grads_kernel(normed, active, hidden_low, grad, index, *outs):
    keeps, sends, up_rows = outs[0:2], outs[2:4], outs[4]
    d_up = t_mm(normed[...], hidden_low[...]).astype(BF)
    total = jnp.sum(hidden_low[...].astype(F32), 0, keepdims=True)
    of_chip = mm_t(jnp.where(own_lanes(), total, 0.0).astype(BF), lanes_of()).astype(BF)
    up_rows[...] = mm(placed(index, 12, 64), of_chip)
    for p in range(2):
        qa, qb = placed(index, 2 * p, 768), placed(index, 2 * p + 1, 384)
        top, rest = laid_out(d_up[:, 768 * p : 768 * p + 768], qa, qb, 384)
        put(keeps[p], sends[p], slice(0, 768), top)
        put(keeps[p], sends[p], slice(768, 1152), rest)
    d_down = t_mm(active[...], grad[...]).reshape(64, 3, 8, 768)
    slabs = [placed(index, 9 + p, 512) for p in range(2)]
    for k in range(3):
        rows = d_down[:, k].reshape(512, 768).astype(BF)
        for p, slab in enumerate(slabs):
            moved = mm(slab, rows[:, 384 * p : 384 * p + 384])
            put(keeps[p], sends[p], slice(1152 + 384 * k, 1536 + 384 * k), moved)


def feed_grads(normed, active, hidden_low, grad, index):
    return staged(
        "feed_grads",
        feed_grads_kernel,
        (),
        (normed, active, hidden_low, grad, index),
        (*[shape((256, 2304), BF)] * 4, shape((512, 128), F32)),
        6e9,
    )


def cross_backward_kernel(
    info, vec, grad, mine, got, after, w_out, queries, kv, w_query, before,
    stream, low, dq, dkv, back, sums,
):
    xhat, inv = normalize(after[...])
    step = norm_back(mine[...] + got[...], vec[3:4], xhat, inv)
    stream[...] = grad[...].astype(F32) + step
    low[...] = stream[...].astype(BF)
    mixed_grad = mm_t(low[...], w_out[...]).astype(BF)
    for row in range(2):
        allowed = cross_allowed(info, row)
        at = slice(128 * row, 128 * row + 128)
        for j in range(3):
            lanes = slice(128 * j, 128 * j + 128)
            value_lanes = slice(384 + 128 * j, 512 + 128 * j)
            q = stacked(queries[at, lanes]) * 0.125
            do = stacked(mixed_grad[at, lanes])
            k = row_keys(kv, row, lanes)
            v = row_keys(kv, row, value_lanes)
            probs = softmax(mm_t(q, k), allowed)
            ds = softmax_back(probs, mm_t(do, v))
            dq[at, lanes] = (merged(mm(ds, k)) * 0.125).astype(BF)
            dk = t_mm(ds, q).astype(BF)
            dv = t_mm(probs.astype(BF), do).astype(BF)
            for value, where in ((dk, lanes), (dv, value_lanes)):
                dkv[384 * row : 384 * row + 384, where] = value[:384]
                dkv[768 + 384 * row : 1152 + 384 * row, where] = value[384:]
    back[...] = mm_t(dq[...], w_query[...])
    xhat, _ = normalize(before[...])
    sums[...] = jnp.concatenate(
        [
            jnp.sum(back[...] * xhat, 0, keepdims=True),
            jnp.sum(back[...], 0, keepdims=True),
            jnp.zeros((6, 768), F32),
        ],
        0,
    )


def cross_backward(info, vec, grad, mine, got, after, w_out, queries, kv, w_query, before):
    return staged(
        "cross_backward",
        cross_backward_kernel,
        (info,),
        (vec, grad, mine, got, after, w_out, queries, kv, w_query, before),
        (shape((256, 768), F32), shape((256, 768), BF), shape((256, 384), BF), shape((1536, 768), BF), shape((256, 768), F32), shape((8, 768), F32)),
        5e9,
    )


def cross_part(p, weight, mixed, low, index, keep, send):
    qa, qb = placed(index, 2 * p, 768), placed(index, 2 * p + 1, 384)
    top, rest = laid_out(weight, qa, qb, 256)
    put(keep, send, slice(0, 384), top)
    put(keep, send, slice(384, 640), rest)
    d_out = t_mm(mixed[...], low[:, 256 * p : 256 * p + 256]).astype(BF)
    put(keep, send, slice(640, 896), mm(placed(index, 6 + p, 384), d_out))


def image_grads_kernel(image_normed, dkv, mixed, low, index, keep0, keep1, send0, send1):
    d_kv = t_mm(image_normed[...], dkv[...]).astype(BF)
    cross_part(0, d_kv[:, :384], mixed, low, index, keep0, send0)
    cross_part(1, d_kv[:, 384:], mixed, low, index, keep1, send1)


def image_grads(image_normed, dkv, mixed, low, index):
    return staged(
        "image_grads",
        image_grads_kernel,
        (),
        (image_normed, dkv, mixed, low, index),
        [shape((256, 896), BF)] * 4,
        4e9,
    )


def query_grads_kernel(normed, dq, mixed, low, index, keep, send):
    d_query = t_mm(normed[...], dq[...]).astype(BF)
    cross_part(2, d_query, mixed, low, index, keep, send)


def query_grads(normed, dq, mixed, low, index):
    return staged(
        "query_grads",
        query_grads_kernel,
        (),
        (normed, dq, mixed, low, index),
        [shape((256, 896), BF)] * 2,
        1e9,
    )


def image_part_kernel(dkv, w_kv, out):
    out[...] = mm_t(dkv[768:], w_kv[...]).astype(BF)


def image_part(dkv, w_kv):
    return staged(
        "image_part",
        image_part_kernel,
        (),
        (dkv, w_kv),
        (shape((768, 768), BF),),
        1e9,
    )


def image_backward_kernel(vec, dkv, w_kv, got, own, out, low1, low2, low3, sums):
    total = [jnp.zeros((1, 768), F32)] * 2
    for image, result in enumerate((out, low1, low2, low3)):
        at = slice(192 * image, 192 * image + 192)
        dy = mm_t(dkv[at], w_kv[...]) + got[at].astype(F32)
        xhat, inv = normalize(own[at].astype(F32))
        total = [
            total[0] + jnp.sum(dy * xhat, 0, keepdims=True),
            total[1] + jnp.sum(dy, 0, keepdims=True),
        ]
        result[...] = norm_back(dy, vec[2:3], xhat, inv)[:188].astype(result.dtype)
    sums[...] = jnp.concatenate(total + [jnp.zeros((6, 768), F32)], 0)


def image_backward(vec, dkv, w_kv, got, own):
    return staged(
        "image_backward",
        image_backward_kernel,
        (),
        (vec, dkv, w_kv, got, own),
        (shape((188, 768), F32), *[shape((188, 768), BF)] * 3, shape((8, 768), F32)),
        1e9,
    )


def self_backward_kernel(
    info, vec, stream_in, mine, got, before, w_out, joined, w_qkv, text,
    stream_mine, low, d_joined, to_mine, to_other, sums,
    stream, back,
):
    xhat, inv = normalize(before[...])
    stream[...] = stream_in[...] + norm_back(mine[...] + got[...], vec[1:2], xhat, inv)
    low[...] = stream[...].astype(BF)
    mixed_grad = mm_t(low[...], w_out[...]).astype(BF)
    for row in range(2):
        allowed = self_allowed(info, row)
        at = slice(128 * row, 128 * row + 128)
        for j in range(3):
            lanes = [slice(384 * i + 128 * j, 384 * i + 128 * j + 128) for i in range(3)]
            q = stacked(joined[at, lanes[0]]) * 0.125
            k = joined[at, lanes[1]]
            v = joined[at, lanes[2]]
            do = stacked(mixed_grad[at, lanes[0]])
            probs = softmax(mm_t(q, k), allowed)
            ds = softmax_back(probs, mm_t(do, v))
            d_joined[at, lanes[0]] = (merged(mm(ds, k)) * 0.125).astype(BF)
            d_joined[at, lanes[1]] = t_mm(ds, q).astype(BF)
            d_joined[at, lanes[2]] = t_mm(probs.astype(BF), do).astype(BF)
    back[...] = mm_t(d_joined[...], w_qkv[...])
    xhat, _ = normalize(text[...].astype(F32))
    sums[...] = jnp.concatenate(
        [
            jnp.sum(back[...] * xhat, 0, keepdims=True),
            jnp.sum(back[...], 0, keepdims=True),
            jnp.zeros((6, 768), F32),
        ],
        0,
    )
    core = info[0]
    for row in range(2):
        at = pl.ds(pl.multiple_of(128 * row + 64 * core, 64), 64)
        stream_mine[64 * row : 64 * row + 64] = stream[at]
        to_mine[64 * row : 64 * row + 64] = back[at]
        at = pl.ds(pl.multiple_of(128 * row + 64 * (1 - core), 64), 64)
        to_other[64 * row : 64 * row + 64] = back[at]


def self_backward(info, vec, stream_in, mine, got, before, w_out, joined, w_qkv, text):
    return staged(
        "self_backward",
        self_backward_kernel,
        (info,),
        (vec, stream_in, mine, got, before, w_out, joined, w_qkv, text),
        (shape((128, 768), F32), shape((256, 768), BF), shape((256, 1152), BF), shape((128, 768), F32), shape((128, 768), F32), shape((8, 768), F32)),
        3e9,
        [pltpu.VMEM((256, 768), F32), pltpu.VMEM((256, 768), F32)],
    )


def self_grads_kernel(
    normed, d_joined, mixed, low, sum0, sum1, sum2, sum3, grad, up_rows,
    index, e0, e1, e2, *outs,
):
    keeps, sends = outs[0:3], outs[3:6]
    for send, early in zip(sends, (e0, e1, e2)):
        send[:, :896] = early[...]
    d_qkv = t_mm(normed[...], d_joined[...]).astype(BF)
    d_out = t_mm(mixed[...], low[...]).astype(BF)
    for p in range(3):
        qa, qb = placed(index, 2 * p, 768), placed(index, 2 * p + 1, 384)
        o = placed(index, 6 + p, 384)
        top, rest = laid_out(d_qkv[:, 384 * p : 384 * p + 384], qa, qb, 256)
        moved = mm(o, d_out[:, 256 * p : 256 * p + 256])
        for at, value in ((0, top), (384, rest), (640, moved)):
            n = value.shape[1]
            keeps[p][:, at : at + n] = value[:256].astype(BF)
            sends[p][:, 896 + at : 896 + at + n] = value[256:].astype(BF)
    down_sum = jnp.sum(grad[...].astype(F32), 0, keepdims=True) * 0.5
    rows = [s[i : i + 1] for i in range(2) for s in (sum0, sum1, sum2, sum3)]
    rows = jnp.concatenate(rows + [down_sum, jnp.zeros((7, 768), F32)], 0).astype(BF)
    zero = jnp.zeros((16, 768), BF)
    first = jnp.concatenate([rows] + [zero] * 7, 0)
    second = jnp.concatenate([zero, rows] + [zero] * 6, 0)
    value = mm_t(qa, first) + mm_t(qb, second[:, 384:]) + up_rows[...]
    keeps[2][:, 896:1024] = value[:256].astype(BF)
    sends[2][:, 1792:1920] = value[256:].astype(BF)


def self_grads(normed, d_joined, mixed, low, sums, grad, up_rows, index, early):
    return staged(
        "self_grads",
        self_grads_kernel,
        (),
        (normed, d_joined, mixed, low, *sums, grad, up_rows, index, *early),
        (*[shape((256, n), BF) for n in (896, 896, 1024, 1792, 1792, 1920)],),
        3e9,
    )


def first_core(info, dims):
    return lax.broadcasted_iota(jnp.int32, dims, 0) * 0 + info[0] == 0


BLOCKS = ((0, 3, 384), (1, 2, 384), (2, 1, 384), (3, 1, 1536))


def halves_into(core, refs, target, sem):
    copies, here = [], 0
    for which, blocks, width in BLOCKS:
        for i in range(blocks):
            at = pl.multiple_of(2 * i * width + core * width, 128)
            copies.append(
                pltpu.make_async_copy(
                    refs[which].at[:, pl.ds(at, width)], target.at[:, pl.ds(here, width)],
                    sem.at[len(copies)],
                )
            )
            here += width
    return copies


def vector_rows(gain, bias, down_bias):
    total = jnp.zeros((6, 128), F32)
    for at, ref in ((0, gain), (4, bias), (8, down_bias)):
        n = ref.shape[0]
        i = lax.broadcasted_iota(jnp.int32, (n, 128), 0) + at
        j = lax.broadcasted_iota(jnp.int32, (n, 128), 1)
        total = total + t_mm(ref[...], ((i == j) | (i + 16 == j)).astype(F32).astype(BF))
    return total


def pack_swap_kernel(info, qkv, kv, query, up, gain, bias, down_bias, send, half, sem):
    copies = halves_into(1 - info[0], (qkv, kv, query, up), half, sem)
    for c in copies:
        c.start()
    send[:, 3840:] = vector_rows(gain, bias, down_bias).astype(BF)
    for c in copies:
        c.wait()
    send[:, :3840] = half[...]


def pack_slots_kernel(
    info, qkv, kv, query, up, self_out, cross_out, down, got, gain, bias, down_bias, up_bias,
    slot, twelve, half, outs, slabs, theirs, sem, sems,
):
    copies = halves_into(info[0], (qkv, kv, query, up), half, sem)
    others = [
        pltpu.make_async_copy(self_out, outs.at[0], sems.at[0]),
        pltpu.make_async_copy(cross_out, outs.at[1], sems.at[1]),
        pltpu.make_async_copy(down, slabs, sems.at[2]),
    ]
    sent = pltpu.make_async_copy(got, theirs, sems.at[3])
    sent.start()
    for c in copies + others:
        c.start()
    first = first_core(info, (6, 128))
    mine = vector_rows(gain, bias, down_bias)
    sent.wait()
    other = theirs[:, 3840:].astype(F32)
    twelve[0:6, 4608:] = jnp.where(first, mine, other)
    twelve[6:12, 4608:] = jnp.where(first, other, mine)
    twelve[12:16, 4608:] = jnp.zeros((4, 128), F32)
    lane = lax.broadcasted_iota(jnp.int32, (8, 128), 1)
    row = lax.broadcasted_iota(jnp.int32, (8, 128), 0)
    vec = jnp.where(lane < 16, twelve[0:8, 4608:], 0.0)
    vec = vec + jnp.where((lane >= 16) & (lane < 32), twelve[8:16, 4608:], 0.0)
    i = lax.broadcasted_iota(jnp.int32, (24, 128), 0)
    j = lax.broadcasted_iota(jnp.int32, (24, 128), 1)
    units = mm(up_bias[...], (i + 64 == j).astype(F32).astype(BF))
    slot[:, 6912:7040] = (vec + jnp.where(row == 0, units, 0.0)).astype(BF)
    for c in copies:
        c.wait()
    first = first_core(info, (6, 3840))
    mine = half[...].astype(F32)
    other = theirs[:, :3840].astype(F32)
    twelve[0:6, :3840] = jnp.where(first, mine, other)
    twelve[6:12, :3840] = jnp.where(first, other, mine)
    for c in others:
        c.wait()
    twelve[0:6, 3840:4608] = outs[0].astype(F32)
    twelve[6:12, 3840:4608] = outs[1].astype(F32)
    slot[:, :4608] = twelve[0:8, :4608].astype(BF)
    twelve[0:4, :2304] = twelve[8:12, :2304]
    twelve[4:8, :2304] = twelve[8:12, 2304:4608]
    slot[:, 4608:6912] = twelve[0:8, :2304].astype(BF)
    wide = slabs[...].astype(F32)
    for k in range(3):
        at = 7040 + 768 * k
        slot[:, at : at + 768] = wide[8 * k : 8 * k + 8].astype(BF)


def packed(name, kernel, info, far, near, out, scratch):
    return pl.pallas_call(
        kernel,
        out_shape=out,
        in_specs=[SMEM] + [HBM] * len(far) + [VMEM] * len(near),
        out_specs=VMEM,
        scratch_shapes=scratch,
        compiler_params=params(60),
        cost_estimate=cost(1e6, 1e6),
        name=name,
    )(info, *far, *near)


def pack_swap(info, weights, vectors):
    return packed(
        "pack_swap",
        pack_swap_kernel,
        info,
        weights,
        vectors,
        shape((6, 3968), BF),
        [pltpu.VMEM((6, 3840), BF), pltpu.SemaphoreType.DMA((7,))],
    )


def pack_slots(info, weights, vectors, got, self_out, cross_out, down, up_bias):
    return packed(
        "pack_slots",
        pack_slots_kernel,
        info,
        (*weights, self_out, cross_out, down, got),
        (*vectors, up_bias),
        shape((8, 9344), BF),
        [
            pltpu.VMEM((16, 4736), F32),
            pltpu.VMEM((6, 3840), BF),
            pltpu.VMEM((2, 6, 768), BF),
            pltpu.VMEM((24, 768), BF),
            pltpu.VMEM((6, 3968), BF),
            pltpu.SemaphoreType.DMA((7,)),
            pltpu.SemaphoreType.DMA((4,)),
        ],
    )


BASE = (2304, 2304, 0)
TWELVES = [(p, 0, 768, 384) for p in range(2)] + [
    (p, BASE[p] + at, 384, 256) for at in (0, 896) for p in range(3)
]


def finish_send_kernel(info, *refs):
    k_ac, k_b, g_ac, g_b, s0, s1, s2, send, own, twelve = refs
    sums, n = (s0, s1, s2), s0.shape[1]
    s0[...] = k_ac[:, :n].astype(F32) + g_ac[:, :n].astype(F32)
    s2[...] = k_ac[:, n:].astype(F32) + g_ac[:, n:].astype(F32)
    s1[...] = k_b[...].astype(F32) + g_b[...].astype(F32)
    here = 0
    for p, at, n, width in TWELVES:
        ref = sums[p]
        twelve[0:8, here : here + n] = ref[:, at : at + n]
        twelve[8:12, here : here + width] = ref[0:4, at + n : at + n + width]
        twelve[8:12, here + width : here + n] = ref[4:8, at + n : at + n + n - width]
        here += n
    vec = s2[:, 1792:]
    twelve[0:8, 3840:] = vec
    twelve[8:12, 3840:] = pltpu.roll(vec, 112, 1)[0:4]
    first = first_core(info, (6, 3968))
    send[...] = jnp.where(first, twelve[6:12], twelve[0:6])
    own[...] = jnp.where(first, twelve[0:6], twelve[6:12])


def finish_kernel(
    info, s0, s1, s2, own, got, qkv, out_self, query, kv, out_cross, up, down, gain, bias, down_bias
):
    sums = (s0, s1, s2)
    first = first_core(info, (6, 3840))
    low = jnp.where(first, own[:, :3840], got[:, :3840])
    high = jnp.where(first, got[:, :3840], own[:, :3840])
    for ref, begin, blocks, width in (
        (up, 0, 1, 1536), (kv, 1536, 2, 384), (query, 2304, 1, 384), (qkv, 2688, 3, 384),
    ):
        for i in range(blocks):
            at = begin + i * width
            ref[:, 2 * i * width : (2 * i + 1) * width] = low[:, at : at + width]
            ref[:, (2 * i + 1) * width : (2 * i + 2) * width] = high[:, at : at + width]
    for p in range(3):
        lanes = slice(256 * p, 256 * p + 256)
        out_cross[:, lanes] = sums[p][0:6, BASE[p] + 640 : BASE[p] + 896]
        out_self[:, lanes] = sums[p][0:6, BASE[p] + 1536 : BASE[p] + 1792]
    for p in range(2):
        for k in range(3):
            at = 1152 + 384 * k
            down[8 * k : 8 * k + 8, 384 * p : 384 * p + 384] = sums[p][:, at : at + 384]
    total = jnp.concatenate([own[:, 3840:] + got[:, 3840:], jnp.zeros((122, 128), F32)], 0)
    across = jnp.transpose(total)
    gain[...] = across[0:4, 0:6]
    bias[...] = across[4:8, 0:6]
    down_bias[...] = across[8:9, 0:6]


def finish_send(info, keeps, gots, widths):
    return staged(
        "finish_send",
        finish_send_kernel,
        (info,),
        (*keeps, *gots),
        [shape((8, n), F32) for n in widths] + [shape((6, 3968), F32)] * 2,
        1e6,
        [pltpu.VMEM((16, 3968), F32)],
        mib=8,
    )


def finish(info, sums, own, got):
    return staged(
        "finish",
        finish_kernel,
        (info,),
        (*sums, own, got),
        [
            shape(dims, F32)
            for dims in (
                (6, 2304), (6, 768), (6, 768), (6, 1536), (6, 768), (6, 3072), (24, 768), (4, 6), (4, 6),
                (1, 6),
            )
        ],
        1e6,
        mib=8,
    )


def text_finish_kernel(vec, text, stream, mine, got, out_mine, out_got, grad, out):
    xhat, inv = normalize(text[...].astype(F32))
    grad[...] = stream[...] + norm_back(mine[...] + got[...], vec[0:1], xhat, inv)
    out[...] = out_mine[...] + out_got[...]


def text_finish(vec, text, stream, mine, got, out_mine, out_got):
    return staged(
        "text_finish",
        text_finish_kernel,
        (),
        (vec, text, stream, mine, got, out_mine, out_got),
        [shape((128, 768), F32)] * 2,
        1e6,
        mib=8,
    )


def image_finish_kernel(pick, v0, v1, v2, v3, out):
    values = [v[...].astype(F32) for v in (v0, v1, v2, v3)]
    for image in range(4):
        total = values[3]
        for turn in range(3):
            total = jnp.where(pick[turn] == image, values[turn], total)
        out[:, image, :] = total


def image_finish(pick, values):
    out = staged(
        "image_finish",
        image_finish_kernel,
        (pick,),
        values,
        [shape((188, 4, 768), F32)],
        1e6,
    )[0]
    return jnp.transpose(out, (1, 0, 2))


def combine_kernel(plan, *refs):
    at = 0
    ins = []
    for keeps, gots in plan:
        ins.append((refs[at : at + len(keeps)], refs[at + len(keeps) : at + len(keeps) + len(gots)]))
        at += len(keeps) + len(gots)
    outs = refs[at:]
    for p, (keeps, gots) in enumerate(ins):
        here = 0
        edges = []
        for ref in keeps:
            edges.append((here, here + ref.shape[1], ref))
            here += ref.shape[1]
        here = 0
        for ref in gots:
            for low, high, keep in edges:
                a, b = max(low, here), min(high, here + ref.shape[1])
                if a >= b:
                    continue
                total = keep[:, a - low : b - low].astype(F32) + ref[:, a - here : b - here].astype(F32)
                half = total.shape[0] // 2
                outs[2 * p][:, a:b] = total[:half].astype(BF)
                outs[2 * p + 1][:, a:b] = total[half:].astype(BF)
            here += ref.shape[1]


def combine(parts):
    plan, args, outs = [], [], []
    for keeps, gots in parts:
        plan.append(([k.shape[1] for k in keeps], [g.shape[1] for g in gots]))
        args += [*keeps, *gots]
        rows, width = keeps[0].shape[0], sum(k.shape[1] for k in keeps)
        outs += [shape((rows // 2, width), BF)] * 2
    got = staged(
        "combine", lambda *refs: combine_kernel(plan, *refs), (), args, outs, 1e6
    )
    return [(got[2 * p], got[2 * p + 1]) for p in range(len(parts))]


def regroup_kernel(k_a, g_a, k_bc, g_bc, keep_ac, send_ac, keep_b, send_b):
    first = k_a[...].astype(F32) + g_a[...].astype(F32)
    second = k_bc[...].astype(F32) + g_bc[...].astype(F32)
    n, m, half = k_a.shape[1], keep_b.shape[1], k_a.shape[0] // 2
    for rows, ac, b in ((slice(0, half), keep_ac, keep_b), (slice(half, 2 * half), send_ac, send_b)):
        ac[:, :n] = first[rows].astype(BF)
        ac[:, n:] = second[rows, m:].astype(BF)
        b[...] = second[rows, :m].astype(BF)


def regroup(k_a, g_a, k_bc, g_bc, m):
    half, n = k_a.shape[0] // 2, k_a.shape[1]
    widths = (n + k_bc.shape[1] - m, n + k_bc.shape[1] - m, m, m)
    got = staged(
        "regroup",
        regroup_kernel,
        (),
        (k_a, g_a, k_bc, g_bc),
        [shape((half, w), BF) for w in widths],
        1e6,
    )
    return [(got[0], got[1]), (got[2], got[3])]


def send_step(step, values, parts=(0, 1, 2)):
    v0, v1 = ((1, 3), (3, 1))[step % 2]
    return [
        lax.ppermute(v, BOTH, xor_pairs(ORDERS[p][step // 2], v0, v1)) for v, p in zip(values, parts)
    ]


def after(value, *others):
    return lax.optimization_barrier((value, *others))[0]


def image_moves(images, way):
    once = [(core + i, core + (i + 16 * way) % 64) for core in (0, 64) for i in range(64)]
    first, second, third = images
    return [
        lax.ppermute(first, BOTH, once),
        move_on(second),
        lax.ppermute(third, BOTH, [(j, i) for i, j in once]),
    ]


def move_on(image):
    route = [(i, (i + 16) % 64) for i in range(64)]
    return lax.ppermute(image, BOTH, route + [(64 + j, 64 + i) for i, j in route])


def on_device(
    text_input,
    image_tokens,
    output_grad,
    segment_starts,
    caption_image,
    image_counts,
    norm_gain,
    norm_bias,
    self_qkv,
    self_out,
    cross_q,
    cross_kv,
    cross_out,
    up_weight,
    up_bias,
    down_weight,
    down_bias,
):
    core = lax.axis_index("seq")
    chip = lax.axis_index("batch")
    first = core == 0

    def ordered(own, other, axis):
        return jnp.where(
            first, jnp.concatenate([own, other], axis), jnp.concatenate([other, own], axis)
        )

    place = jnp.stack([core, chip]).astype(jnp.int32)
    weights = (self_qkv, cross_kv, cross_q, up_weight)
    vectors = (norm_gain, norm_bias, down_bias[None])
    got = swap(pack_swap(place, weights, vectors))
    slot = pack_slots(
        place, weights, vectors, got, self_out, cross_out, down_weight, up_bias[None]
    )
    gathered = lax.all_gather(slot, "batch", axis=0, tiled=True)

    late_text, late_grad = after(text_input, slot), after(output_grad, slot)
    text = ordered(late_text, swap(late_text), 1).reshape(256, 768)
    grad = ordered(late_grad, swap(late_grad), 1).reshape(256, 768)

    group_images = after(caption_image, slot).reshape(64, 8)
    my_captions = lax.dynamic_index_in_dim(group_images, chip, 0, keepdims=False)
    limits = jnp.take(image_counts, my_captions).reshape(4, 2)
    limits = jnp.where(first, jnp.concatenate([limits[:, 0], limits[:, 1]]), jnp.concatenate([limits[:, 1], limits[:, 0]]))
    turns = jnp.arange(4)
    targets = (chip - turns * 16) % 64
    wanted = group_images[targets, 2 * turns + core]
    local_pick = wanted - (core * 64 + chip) * 4
    outgoing = image_pick(after(local_pick, slot), image_tokens)
    received = [outgoing[0], *image_moves(outgoing[1:], -1)]
    received[2] = move_on(received[2])
    own_images = image_stack(received)
    other_images = swap(own_images)
    info = jnp.concatenate(
        [core[None], segment_starts.reshape(8), limits, jnp.zeros((15,), jnp.int32)]
    ).astype(jnp.int32)

    column_index = indices(after(place, slot))

    gathered, info, grad, text, column_index, own_images, other_images = lax.optimization_barrier(
        (gathered, info, grad, text, column_index, own_images, other_images)
    )
    w_qkv, w_kv, w_query, w_up, w_self, w_cross, w_down, vec, b_up = unpack(gathered)
    part, joined, mixed_self, normed_one = self_forward(info, vec, w_qkv, w_self, text)
    got = swap(part)
    kv, image_normed = image_forward(vec, w_kv, own_images, other_images)
    after_self, normed_two, q_cross, mixed_cross, part = cross_forward(
        info, vec, text, part, got, kv, w_query, w_cross
    )
    after_cross, normed_three, active, hidden_low, text_mine, text_other, part, sum3 = feed(
        info, vec, b_up, after_self, part, swap(part), w_up, w_down, grad
    )
    text_got = swap(text_other)
    got = swap(part)

    grads = feed_grads(normed_three, active, hidden_low, grad, column_index)
    keep_one, up_rows = grads[0:2], grads[4]
    got_one = send_step(0, grads[2:4], (0, 1))
    stream_two, cross_low, dq, dkv, part, sum1 = cross_backward(
        info, vec, after(grad, keep_one[0]), part, got, after_cross, w_cross, q_cross, kv, w_query, after_self
    )
    got = swap(part)
    image_send = image_part(dkv, w_kv)[0]
    *rows_back, sum2 = image_backward(vec, dkv, w_kv, swap(image_send), own_images)
    returned = [rows_back[0], *image_moves(rows_back[1:], 1)]
    k_keep, v_keep, k_send, v_send = image_grads(
        image_normed, after(dkv, sum2), mixed_cross, cross_low, column_index
    )
    q_keep, q_send = query_grads(
        normed_two, after(dq, k_keep), mixed_cross, cross_low, column_index
    )
    returned[2] = move_on(after(returned[2], q_keep))
    keep_two, early = [k_keep, v_keep, q_keep], [k_send, v_send, q_send]
    stream_one, self_low, d_joined, one_mine, one_other, sum0 = self_backward(
        info, vec, after(stream_two, q_keep), part, got, after_self, w_self, joined,
        w_qkv, text,
    )
    self_low, *late = lax.optimization_barrier((self_low, *returned[1:], *got_one))
    returned, got_one = returned[:1] + late[:3], late[3:]
    grads = self_grads(
        normed_one, d_joined, mixed_self, self_low, (sum0, sum1, sum2, sum3), grad, up_rows,
        column_index, early,
    )
    keep_three = grads[0:3]
    got_two = send_step(0, grads[3:6])
    one_got = swap(one_other)
    image_grad = image_finish(after(local_pick, grads[3]), returned)
    text_grad, text_output = text_finish(
        after(vec, grads[3]), text_input.reshape(128, 768), stream_one, one_mine, one_got, text_mine,
        text_got,
    )
    got_two, image_grad, text_grad = lax.optimization_barrier((got_two, image_grad, text_grad))
    pairs = []
    for p in range(3):
        keeps, gots = [keep_two[p], keep_three[p]], [got_two[p]]
        if p < 2:
            keeps, gots = [keep_one[p], *keeps], [got_one[p], *gots]
        pairs += combine([(keeps, gots)])
    a_got, b_got, c_got = send_step(1, [v for _, v in pairs])
    saved = pairs
    pairs = combine([([pairs[0][0]], [a_got])])
    pairs += combine([([saved[1][0], saved[2][0]], [b_got, c_got])])
    for step in (2, 3):
        got_step = send_step(step, [v for _, v in pairs], (0, 1))
        if step == 2:
            pairs = combine([([k], [g]) for (k, _), g in zip(pairs, got_step)])
    pairs = regroup(*[v for (k, _), g in zip(pairs, got_step) for v in (k, g)], saved[1][0].shape[1])
    got_step = send_step(4, [v for _, v in pairs], (0, 1))
    pairs = combine([([k], [g]) for (k, _), g in zip(pairs, got_step)])
    got_step = send_step(5, [v for _, v in pairs], (0, 1))
    *sums, send, own = finish_send(
        place, [k for k, _ in pairs], got_step, [k.shape[1] for k, _ in saved]
    )

    text_grad, text_output = text_grad.reshape(2, 64, 768), text_output.reshape(2, 64, 768)

    (
        qkv_grad, self_grad, query_grad, kv_grad, cross_grad, up_grad, down_grad, gain_grad, bias_grad,
        down_bias_grad,
    ) = finish(place, sums, own, swap(send))
    up_bias_grad = sums[2][0, 1856:1880]
    return (
        text_output,
        text_grad,
        image_grad,
        gain_grad,
        bias_grad,
        qkv_grad,
        self_grad,
        query_grad,
        kv_grad,
        cross_grad,
        up_grad,
        up_bias_grad,
        down_grad,
        down_bias_grad[0],
    )


def solution(mesh):
    rows = P("batch", "seq", None)
    shard = P(BOTH, None)
    wide = P(None, BOTH)
    return jax.shard_map(
        on_device,
        mesh=mesh,
        in_specs=(
            rows, P(BOTH, None, None), rows, P("batch", None), P(), P(), wide, wide,
            shard, shard, shard, shard, shard, shard, P(BOTH), shard, P(BOTH),
        ),
        out_specs=(
            rows, rows, P(BOTH, None, None), wide, wide,
            shard, shard, shard, shard, shard, shard, P(BOTH), shard, P(BOTH),
        ),
        check_vma=False,
    )
```

```python
import math

import jax
import jax.numpy as jnp
from jax import lax
from jax.experimental import pallas as pl
from jax.experimental.pallas import tpu as pltpu
from jax.sharding import PartitionSpec as P

HEADS = 12
HEAD_DIM = 64
EPSILON = 1e-05
MASKED_SCORE = -1e30
BF = jnp.bfloat16
F32 = jnp.float32
BOTH = ("seq", "batch")
STRIDE = {"z": 16, "y": 4, "x": 1}
ORDERS = (("x", "z", "y"), ("y", "x", "z"), ("z", "x", "y"))


def xor_pairs(axis, value0, value1):
    step, out = STRIDE[axis], []
    for core, value in ((0, value0), (1, value1)):
        for chip in range(64):
            at = chip // step % 4
            out.append((core * 64 + chip, core * 64 + chip + ((at ^ value) - at) * step))
    return out


def swap(value):
    return lax.ppermute(value, "seq", [(0, 1), (1, 0)])


def mm(a, b):
    return jnp.dot(a, b, preferred_element_type=F32)


def mm_t(a, b):
    return lax.dot_general(a, b, (((1,), (1,)), ((), ())), preferred_element_type=F32)


def t_mm(a, b):
    return lax.dot_general(a, b, (((0,), (0,)), ((), ())), preferred_element_type=F32)


def normalize(values):
    center = jnp.mean(values, -1, keepdims=True)
    centred = values - center
    spread = jnp.mean(centred * centred, -1, keepdims=True)
    inv = lax.rsqrt(spread + EPSILON)
    return centred * inv, inv


def norm_back(grad, gain, xhat, inv):
    scaled = grad * gain
    return inv * (
        scaled
        - jnp.mean(scaled, -1, keepdims=True)
        - xhat * jnp.mean(scaled * xhat, -1, keepdims=True)
    )


VMEM = pl.BlockSpec(memory_space=pltpu.VMEM)
SMEM = pl.BlockSpec(memory_space=pltpu.SMEM)
HBM = pl.BlockSpec(memory_space=pltpu.HBM)


def shape(dims, dtype):
    return jax.ShapeDtypeStruct(dims, dtype)


def cost(flops, moved):
    return pl.CostEstimate(
        flops=int(flops / 64), bytes_accessed=int(moved / 64), transcendentals=0
    )


def params(mib):
    return pltpu.CompilerParams(vmem_limit_bytes=mib * 1024 * 1024)


def staged(name, kernel, scalars, ins, outs, work, scratch=(), mib=16):
    moved = sum(math.prod(v.shape) * v.dtype.itemsize for v in (*ins, *outs))
    return pl.pallas_call(
        kernel,
        out_shape=tuple(outs),
        in_specs=[SMEM] * len(scalars) + [VMEM] * len(ins),
        out_specs=(VMEM,) * len(outs),
        scratch_shapes=list(scratch),
        compiler_params=params(mib),
        cost_estimate=cost(work, moved),
        name=name,
    )(*scalars, *ins)


def placed(columns, i, size):
    place = lax.broadcasted_iota(jnp.int32, (512, size), 1)
    return (place == columns[:, i : i + 1]).astype(F32).astype(BF)


def segment_of(info, row, dims, axis):
    place = lax.broadcasted_iota(jnp.int32, dims, axis)
    total = jnp.full(dims, -1, jnp.int32)
    for j in range(4):
        total = total + (place >= info[1 + 4 * row + j]).astype(jnp.int32)
    return total


def low_lanes():
    return lax.broadcasted_iota(jnp.int32, (1, 128), 1) < 64


def stacked(pair):
    left = low_lanes()
    zero = jnp.zeros_like(pair)
    return jnp.concatenate([jnp.where(left, pair, zero), jnp.where(left, zero, pair)], 0)


def merged(two):
    n = two.shape[0] // 2
    return jnp.where(low_lanes(), two[:n], two[n:])


def softmax(scores, allowed):
    scores = jnp.where(allowed, scores, MASKED_SCORE)
    weights = jnp.exp(scores - jnp.max(scores, -1, keepdims=True))
    return weights * (1.0 / jnp.sum(weights, -1, keepdims=True))


def softmax_back(probs, dprobs):
    return (probs * (dprobs - jnp.sum(probs * dprobs, -1, keepdims=True))).astype(BF)


def self_allowed(info, row):
    at = segment_of(info, row, (128, 128), 0)
    key = segment_of(info, row, (128, 128), 1)
    i = lax.broadcasted_iota(jnp.int32, (128, 128), 0)
    j = lax.broadcasted_iota(jnp.int32, (128, 128), 1)
    allowed = (at == key) & (j <= i)
    return jnp.concatenate([allowed, allowed], 0)


def cross_allowed(info, row):
    core = info[0]
    lane = lax.broadcasted_iota(jnp.int32, (1, 768), 1)
    key = jnp.full((1, 768), -1, jnp.int32)
    images = (2 * row, 2 * row + 1, 4 + 2 * row, 5 + 2 * row)
    captions = (core, 2 + core, 1 - core, 3 - core)
    for block in range(4):
        limit = info[9 + images[block]]
        key = jnp.where(
            (lane >= 192 * block) & (lane < 192 * block + limit), captions[block], key
        )
    at = segment_of(info, row, (128, 1), 0)
    return jnp.concatenate([at, at], 0) == key


def row_keys(kv, row, lanes):
    return jnp.concatenate(
        [kv[384 * row : 384 * row + 384, lanes], kv[768 + 384 * row : 1152 + 384 * row, lanes]], 0
    )


def lanes_of():
    lane = lax.broadcasted_iota(jnp.int32, (128, 1536), 0)
    unit = lax.broadcasted_iota(jnp.int32, (128, 1536), 1)
    return (lane == 64 + lax.rem(unit, 24)).astype(F32).astype(BF)


def own_lanes():
    chip = lax.broadcasted_iota(jnp.int32, (64, 1536), 0) * 24
    unit = lax.broadcasted_iota(jnp.int32, (64, 1536), 1)
    return (unit >= chip) & (unit < chip + 24)


def self_forward_kernel(info, vec, w_qkv, w_out, text, part, joined, mixed, normed):
    xhat, _ = normalize(text[...].astype(F32))
    normed[...] = (xhat * vec[0:1] + vec[4:5]).astype(BF)
    joined[...] = mm(normed[...], w_qkv[...]).astype(BF)
    for row in range(2):
        allowed = self_allowed(info, row)
        at = slice(128 * row, 128 * row + 128)
        for j in range(3):
            q = stacked(joined[at, 128 * j : 128 * j + 128]) * 0.125
            k = joined[at, 384 + 128 * j : 512 + 128 * j]
            v = joined[at, 768 + 128 * j : 896 + 128 * j]
            probs = softmax(mm_t(q, k), allowed)
            mixed[at, 128 * j : 128 * j + 128] = merged(mm(probs.astype(BF), v)).astype(BF)
    part[...] = mm(mixed[...], w_out[...])


def self_forward(info, vec, w_qkv, w_out, text):
    return staged(
        "self_forward",
        self_forward_kernel,
        (info,),
        (vec, w_qkv, w_out, text),
        (
            shape((256, 768), F32),
            shape((256, 1152), BF),
            shape((256, 384), BF),
            shape((256, 768), BF),
        ),
        2e9,
    )


def rows_of_six(first, last, shift):
    row = lax.broadcasted_iota(jnp.int32, (192, 256), 0)
    place = lax.broadcasted_iota(jnp.int32, (192, 256), 1)
    chip = lax.div(row, 6)
    r = row - 6 * chip
    hit = (place == 8 * chip + r + shift) & (r >= first) & (r <= last)
    return hit.astype(F32).astype(BF)


def unpack_kernel(
    gathered, w_qkv, w_kv, w_query, w_up, w_self, w_cross, w_down, vec, b_up, g, sems
):
    spans = ((4608, 1152), (0, 1152), (6912, 2432), (5760, 1152), (1152, 1152), (2304, 2304))
    loads = [
        pltpu.make_async_copy(gathered.at[:, pl.ds(at, n)], g.at[:, pl.ds(at, n)], sems.at[i])
        for i, (at, n) in enumerate(spans)
    ]
    loads[0].start()
    loads[1].start()
    low, high = rows_of_six(0, 5, 0), rows_of_six(0, 1, 6)
    both = jnp.concatenate([low, high], 0)
    left, right = rows_of_six(2, 5, -2), rows_of_six(2, 5, 2)

    def natural(at, n, begin, rest, outs):
        for half in range(2):
            here = slice(256 * half, 256 * half + 256)
            there = slice(192 * half, 192 * half + 192)
            rows = mm(both, g[here, at : at + n])
            outs[0][there] = rows[:192].astype(BF)
            there = slice(outs[2] + 192 * half, outs[2] + 192 * half + 192)
            outs[1][there] = (rows[192:] + mm(rest, g[here, begin : begin + n])).astype(BF)

    loads[0].wait()
    loads[1].wait()
    for i in (2, 3, 4):
        loads[i].start()
    natural(0, 1152, 4608, left, (w_qkv, w_qkv, 384))
    loads[2].wait()
    loads[5].start()
    tail = g[:, 6912:7040]
    lane = lax.broadcasted_iota(jnp.int32, (1, 128), 1)
    one = jnp.where(lane < 16, tail.astype(F32), 0.0).astype(BF)
    two = jnp.where((lane >= 16) & (lane < 32), tail.astype(F32), 0.0).astype(BF)
    halves = [slice(0, 256), slice(256, 512)]
    rows = [mm(low, one[h]) for h in halves]
    rows += [mm(high, one[h]) + mm(left, two[h]) for h in halves]
    across = jnp.transpose(jnp.concatenate(rows, 0))
    vec[...] = across[:16] + across[16:32]
    chip = lax.broadcasted_iota(jnp.int32, (64, 512), 0)
    place = lax.broadcasted_iota(jnp.int32, (64, 512), 1)
    of_chip = mm((place == 8 * chip).astype(F32).astype(BF), tail).astype(BF)
    b_up[...] = jnp.sum(jnp.where(own_lanes(), mm(of_chip, lanes_of()), 0.0), 0, keepdims=True)
    slabs = [
        g[:, 7040 + 768 * k : 7808 + 768 * k].astype(F32).reshape(64, 1, 8, 768) for k in range(3)
    ]
    w_down[...] = jnp.concatenate(slabs, 1).reshape(1536, 768).astype(BF)
    loads[3].wait()
    loads[4].wait()
    natural(1152, 768, 5760, left, (w_kv, w_kv, 384))
    natural(1920, 384, 6528, left, (w_query, w_query, 384))
    loads[5].wait()
    natural(2304, 1536, 4608, right, (w_up, w_up, 384))
    natural(3840, 768, 6144, right, (w_self, w_cross, 0))


def unpack(gathered):
    outs = ((768, 1152), (768, 768), (768, 384), (768, 1536), (384, 768), (384, 768), (1536, 768))
    return pl.pallas_call(
        unpack_kernel,
        out_shape=(
            *[shape(o, BF) for o in outs],
            shape((16, 768), F32),
            shape((1, 1536), F32),
        ),
        in_specs=[HBM],
        out_specs=(VMEM,) * 9,
        scratch_shapes=[pltpu.VMEM((512, 9344), BF), pltpu.SemaphoreType.DMA((6,))],
        compiler_params=params(46),
        cost_estimate=cost(4e9, 20e6),
        name="unpack",
    )(gathered)


def natural_row(at_slot, twelfth):
    return at_slot * 6 + twelfth + jnp.where(twelfth >= 6, 378, 0)


def index_kernel(place, columns):
    core, chip = place[0], place[1]

    def target_of(order, slot):
        first = slot * 0 + core == 0
        target = 0
        for axis, digit in zip(order, (slot >> 4, (slot >> 2) & 3, slot & 3)):
            step = STRIDE[axis]
            here = lax.rem(lax.div(chip, step), 4)
            other = jnp.where(
                first, jnp.where(digit == 1, 3, jnp.maximum(digit, 1) - 1), digit ^ (digit >> 1)
            )
            target = target + (here ^ other) * step
        return target

    def out_pick(at_slot, eight):
        return jnp.where(eight < 6, at_slot * 6 + eight, -1)

    at = lax.broadcasted_iota(jnp.int32, (512, 1), 0)
    eight = at & 7
    targets = [target_of(order, at >> 3) for order in ORDERS]
    values = []
    for target in targets:
        values += [natural_row(target, eight), natural_row(target, 8 + (eight & 3)) - 384]
    values += [out_pick(target, eight) for target in targets]
    values += [target * 8 + eight for target in targets] + [jnp.where(eight == 0, targets[2], -1)]
    for i in range(16):
        columns[:, i : i + 1] = values[i] if i < len(values) else at * 0


def indices(place):
    return staged(
        "indices",
        index_kernel,
        (place,),
        (),
        [shape((512, 16), jnp.int32)],
        1e6,
    )[0]


def image_pick_kernel(pick, tokens, *outs):
    for turn, out in enumerate(outs):
        out[...] = tokens[pick[turn]]


def image_pick(pick, tokens):
    return staged(
        "image_pick", image_pick_kernel, (pick,), (tokens,), [shape((188, 768), BF)] * 4, 1e6
    )


def image_stack_kernel(v0, v1, v2, v3, out, wide):
    wide[188:192] = jnp.zeros((4, 768), F32)
    for turn, value in enumerate((v0, v1, v2, v3)):
        wide[0:188] = value[...].astype(F32)
        out[192 * turn : 192 * turn + 192] = wide[...].astype(BF)


def image_stack(values):
    return staged(
        "image_stack",
        image_stack_kernel,
        (),
        values,
        [shape((768, 768), BF)],
        1e6,
        [pltpu.VMEM((192, 768), F32)],
    )[0]


def image_forward_kernel(vec, w_kv, own, other, kv, normed):
    row = lax.broadcasted_iota(jnp.int32, (192, 1), 0)
    for image in range(8):
        source, here = (own, 192 * image) if image < 4 else (other, 192 * image - 768)
        xhat, _ = normalize(source[here : here + 192].astype(F32))
        at = slice(192 * image, 192 * image + 192)
        normed[at] = jnp.where(row < 188, xhat * vec[2:3] + vec[6:7], 0.0).astype(BF)
        kv[at] = mm(normed[at], w_kv[...]).astype(BF)


def image_forward(vec, w_kv, own, other):
    return staged(
        "image_forward",
        image_forward_kernel,
        (),
        (vec, w_kv, own, other),
        (shape((1536, 768), BF), shape((1536, 768), BF)),
        2e9,
    )


def cross_forward_kernel(
    info, vec, text, mine, got, w_query, kv, w_out, after, normed, queries, mixed, part
):
    after[...] = text[...].astype(F32) + (mine[...] + got[...])
    xhat, _ = normalize(after[...])
    normed[...] = (xhat * vec[1:2] + vec[5:6]).astype(BF)
    queries[...] = mm(normed[...], w_query[...]).astype(BF)
    for row in range(2):
        allowed = cross_allowed(info, row)
        at = slice(128 * row, 128 * row + 128)
        for j in range(3):
            lanes = slice(128 * j, 128 * j + 128)
            q = stacked(queries[at, lanes]) * 0.125
            k = row_keys(kv, row, lanes)
            v = row_keys(kv, row, slice(384 + 128 * j, 512 + 128 * j))
            probs = softmax(mm_t(q, k), allowed)
            mixed[at, lanes] = merged(mm(probs.astype(BF), v)).astype(BF)
    part[...] = mm(mixed[...], w_out[...])


def cross_forward(info, vec, text, mine, got, kv, w_query, w_out):
    return staged(
        "cross_forward",
        cross_forward_kernel,
        (info,),
        (vec, text, mine, got, w_query, kv, w_out),
        (shape((256, 768), F32), shape((256, 768), BF), shape((256, 384), BF), shape((256, 384), BF), shape((256, 768), F32)),
        3e9,
    )


def feed_kernel(
    info, vec, b_up, before, mine, got, w_up, w_down, grad,
    after, normed, active, hidden_low, to_mine, to_other, back, sums,
    part,
):
    after[...] = before[...] + (mine[...] + got[...])
    xhat, _ = normalize(after[...])
    normed[...] = (xhat * vec[3:4] + vec[7:8]).astype(BF)
    part[...] = jnp.zeros((256, 768), F32)
    for k in range(3):
        lanes = slice(512 * k, 512 * k + 512)
        down = w_down[lanes]
        hidden = mm(normed[...], w_up[:, lanes]) + b_up[:, lanes]
        cdf = 0.5 * (1.0 + lax.erf(hidden * 0.7071067811865476))
        active[:, lanes] = (hidden * cdf).astype(BF)
        slope = cdf + hidden * (jnp.exp(-0.5 * hidden * hidden) * 0.3989422804014327)
        part[...] += mm(active[:, lanes], down)
        hidden_low[:, lanes] = (mm_t(grad[...], down) * slope).astype(BF)
    back[...] = mm_t(hidden_low[...], w_up[...])
    sums[...] = jnp.concatenate(
        [
            jnp.sum(back[...] * xhat, 0, keepdims=True),
            jnp.sum(back[...], 0, keepdims=True),
            jnp.zeros((6, 768), F32),
        ],
        0,
    )
    core = info[0]
    bias = vec[8:9]
    for row in range(2):
        at = pl.ds(pl.multiple_of(128 * row + 64 * core, 64), 64)
        to_mine[64 * row : 64 * row + 64] = after[at] + part[at] + bias
        at = pl.ds(pl.multiple_of(128 * row + 64 * (1 - core), 64), 64)
        to_other[64 * row : 64 * row + 64] = part[at]


def feed(info, vec, b_up, before, mine, got, w_up, w_down, grad):
    return staged(
        "feed",
        feed_kernel,
        (info,),
        (vec, b_up, before, mine, got, w_up, w_down, grad),
        (shape((256, 768), F32), shape((256, 768), BF), shape((256, 1536), BF), shape((256, 1536), BF), shape((128, 768), F32), shape((128, 768), F32), shape((256, 768), F32), shape((8, 768), F32)),
        3e9,
        [pltpu.VMEM((256, 768), F32)],
    )


def laid_out(weight, qa, qb, width):
    top = mm(qa, weight)
    rest = mm(qb, weight[384:])
    n = weight.shape[1]
    upper = lax.broadcasted_iota(jnp.int32, (512, 1), 0) % 8 < 4
    tail = rest[:, width:]
    if n - width < width:
        tail = jnp.concatenate([tail, jnp.zeros((512, 2 * width - n), F32)], 1)
    return top, jnp.where(upper, rest[:, :width], tail)


def put(keep, send, lanes, value):
    keep[:, lanes] = value[:256].astype(BF)
    send[:, lanes] = value[256:].astype(BF)


def feed_grads_kernel(normed, active, hidden_low, grad, index, *outs):
    keeps, sends, up_rows = outs[0:2], outs[2:4], outs[4]
    d_up = t_mm(normed[...], hidden_low[...]).astype(BF)
    total = jnp.sum(hidden_low[...].astype(F32), 0, keepdims=True)
    of_chip = mm_t(jnp.where(own_lanes(), total, 0.0).astype(BF), lanes_of()).astype(BF)
    up_rows[...] = mm(placed(index, 12, 64), of_chip)
    for p in range(2):
        qa, qb = placed(index, 2 * p, 768), placed(index, 2 * p + 1, 384)
        top, rest = laid_out(d_up[:, 768 * p : 768 * p + 768], qa, qb, 384)
        put(keeps[p], sends[p], slice(0, 768), top)
        put(keeps[p], sends[p], slice(768, 1152), rest)
    d_down = t_mm(active[...], grad[...]).reshape(64, 3, 8, 768)
    slabs = [placed(index, 9 + p, 512) for p in range(2)]
    for k in range(3):
        rows = d_down[:, k].reshape(512, 768).astype(BF)
        for p, slab in enumerate(slabs):
            moved = mm(slab, rows[:, 384 * p : 384 * p + 384])
            put(keeps[p], sends[p], slice(1152 + 384 * k, 1536 + 384 * k), moved)


def feed_grads(normed, active, hidden_low, grad, index):
    return staged(
        "feed_grads",
        feed_grads_kernel,
        (),
        (normed, active, hidden_low, grad, index),
        (*[shape((256, 2304), BF)] * 4, shape((512, 128), F32)),
        6e9,
    )


def cross_backward_kernel(
    info, vec, grad, mine, got, after, w_out, queries, kv, w_query, before,
    stream, low, dq, dkv, back, sums,
):
    xhat, inv = normalize(after[...])
    step = norm_back(mine[...] + got[...], vec[3:4], xhat, inv)
    stream[...] = grad[...].astype(F32) + step
    low[...] = stream[...].astype(BF)
    mixed_grad = mm_t(low[...], w_out[...]).astype(BF)
    for row in range(2):
        allowed = cross_allowed(info, row)
        at = slice(128 * row, 128 * row + 128)
        for j in range(3):
            lanes = slice(128 * j, 128 * j + 128)
            value_lanes = slice(384 + 128 * j, 512 + 128 * j)
            q = stacked(queries[at, lanes]) * 0.125
            do = stacked(mixed_grad[at, lanes])
            k = row_keys(kv, row, lanes)
            v = row_keys(kv, row, value_lanes)
            probs = softmax(mm_t(q, k), allowed)
            ds = softmax_back(probs, mm_t(do, v))
            dq[at, lanes] = (merged(mm(ds, k)) * 0.125).astype(BF)
            dk = t_mm(ds, q).astype(BF)
            dv = t_mm(probs.astype(BF), do).astype(BF)
            for value, where in ((dk, lanes), (dv, value_lanes)):
                dkv[384 * row : 384 * row + 384, where] = value[:384]
                dkv[768 + 384 * row : 1152 + 384 * row, where] = value[384:]
    back[...] = mm_t(dq[...], w_query[...])
    xhat, _ = normalize(before[...])
    sums[...] = jnp.concatenate(
        [
            jnp.sum(back[...] * xhat, 0, keepdims=True),
            jnp.sum(back[...], 0, keepdims=True),
            jnp.zeros((6, 768), F32),
        ],
        0,
    )


def cross_backward(info, vec, grad, mine, got, after, w_out, queries, kv, w_query, before):
    return staged(
        "cross_backward",
        cross_backward_kernel,
        (info,),
        (vec, grad, mine, got, after, w_out, queries, kv, w_query, before),
        (shape((256, 768), F32), shape((256, 768), BF), shape((256, 384), BF), shape((1536, 768), BF), shape((256, 768), F32), shape((8, 768), F32)),
        5e9,
    )


def cross_part(p, weight, mixed, low, index, keep, send):
    qa, qb = placed(index, 2 * p, 768), placed(index, 2 * p + 1, 384)
    top, rest = laid_out(weight, qa, qb, 256)
    put(keep, send, slice(0, 384), top)
    put(keep, send, slice(384, 640), rest)
    d_out = t_mm(mixed[...], low[:, 256 * p : 256 * p + 256]).astype(BF)
    put(keep, send, slice(640, 896), mm(placed(index, 6 + p, 384), d_out))


def image_grads_kernel(image_normed, dkv, mixed, low, index, keep0, keep1, send0, send1):
    d_kv = t_mm(image_normed[...], dkv[...]).astype(BF)
    cross_part(0, d_kv[:, :384], mixed, low, index, keep0, send0)
    cross_part(1, d_kv[:, 384:], mixed, low, index, keep1, send1)


def image_grads(image_normed, dkv, mixed, low, index):
    return staged(
        "image_grads",
        image_grads_kernel,
        (),
        (image_normed, dkv, mixed, low, index),
        [shape((256, 896), BF)] * 4,
        4e9,
    )


def query_grads_kernel(normed, dq, mixed, low, index, keep, send):
    d_query = t_mm(normed[...], dq[...]).astype(BF)
    cross_part(2, d_query, mixed, low, index, keep, send)


def query_grads(normed, dq, mixed, low, index):
    return staged(
        "query_grads",
        query_grads_kernel,
        (),
        (normed, dq, mixed, low, index),
        [shape((256, 896), BF)] * 2,
        1e9,
    )


def image_part_kernel(dkv, w_kv, out):
    out[...] = mm_t(dkv[768:], w_kv[...]).astype(BF)


def image_part(dkv, w_kv):
    return staged(
        "image_part",
        image_part_kernel,
        (),
        (dkv, w_kv),
        (shape((768, 768), BF),),
        1e9,
    )


def image_backward_kernel(vec, dkv, w_kv, got, own, out, low1, low2, low3, sums):
    total = [jnp.zeros((1, 768), F32)] * 2
    for image, result in enumerate((out, low1, low2, low3)):
        at = slice(192 * image, 192 * image + 192)
        dy = mm_t(dkv[at], w_kv[...]) + got[at].astype(F32)
        xhat, inv = normalize(own[at].astype(F32))
        total = [
            total[0] + jnp.sum(dy * xhat, 0, keepdims=True),
            total[1] + jnp.sum(dy, 0, keepdims=True),
        ]
        result[...] = norm_back(dy, vec[2:3], xhat, inv)[:188].astype(result.dtype)
    sums[...] = jnp.concatenate(total + [jnp.zeros((6, 768), F32)], 0)


def image_backward(vec, dkv, w_kv, got, own):
    return staged(
        "image_backward",
        image_backward_kernel,
        (),
        (vec, dkv, w_kv, got, own),
        (shape((188, 768), F32), *[shape((188, 768), BF)] * 3, shape((8, 768), F32)),
        1e9,
    )


def self_backward_kernel(
    info, vec, stream_in, mine, got, before, w_out, joined, w_qkv, text,
    stream_mine, low, d_joined, to_mine, to_other, sums,
    stream, back,
):
    xhat, inv = normalize(before[...])
    stream[...] = stream_in[...] + norm_back(mine[...] + got[...], vec[1:2], xhat, inv)
    low[...] = stream[...].astype(BF)
    mixed_grad = mm_t(low[...], w_out[...]).astype(BF)
    for row in range(2):
        allowed = self_allowed(info, row)
        at = slice(128 * row, 128 * row + 128)
        for j in range(3):
            lanes = [slice(384 * i + 128 * j, 384 * i + 128 * j + 128) for i in range(3)]
            q = stacked(joined[at, lanes[0]]) * 0.125
            k = joined[at, lanes[1]]
            v = joined[at, lanes[2]]
            do = stacked(mixed_grad[at, lanes[0]])
            probs = softmax(mm_t(q, k), allowed)
            ds = softmax_back(probs, mm_t(do, v))
            d_joined[at, lanes[0]] = (merged(mm(ds, k)) * 0.125).astype(BF)
            d_joined[at, lanes[1]] = t_mm(ds, q).astype(BF)
            d_joined[at, lanes[2]] = t_mm(probs.astype(BF), do).astype(BF)
    back[...] = mm_t(d_joined[...], w_qkv[...])
    xhat, _ = normalize(text[...].astype(F32))
    sums[...] = jnp.concatenate(
        [
            jnp.sum(back[...] * xhat, 0, keepdims=True),
            jnp.sum(back[...], 0, keepdims=True),
            jnp.zeros((6, 768), F32),
        ],
        0,
    )
    core = info[0]
    for row in range(2):
        at = pl.ds(pl.multiple_of(128 * row + 64 * core, 64), 64)
        stream_mine[64 * row : 64 * row + 64] = stream[at]
        to_mine[64 * row : 64 * row + 64] = back[at]
        at = pl.ds(pl.multiple_of(128 * row + 64 * (1 - core), 64), 64)
        to_other[64 * row : 64 * row + 64] = back[at]


def self_backward(info, vec, stream_in, mine, got, before, w_out, joined, w_qkv, text):
    return staged(
        "self_backward",
        self_backward_kernel,
        (info,),
        (vec, stream_in, mine, got, before, w_out, joined, w_qkv, text),
        (shape((128, 768), F32), shape((256, 768), BF), shape((256, 1152), BF), shape((128, 768), F32), shape((128, 768), F32), shape((8, 768), F32)),
        3e9,
        [pltpu.VMEM((256, 768), F32), pltpu.VMEM((256, 768), F32)],
    )


def self_grads_kernel(
    normed, d_joined, mixed, low, sum0, sum1, sum2, sum3, grad, up_rows,
    index, e0, e1, e2, *outs,
):
    keeps, sends = outs[0:3], outs[3:6]
    for send, early in zip(sends, (e0, e1, e2)):
        send[:, :896] = early[...]
    d_qkv = t_mm(normed[...], d_joined[...]).astype(BF)
    d_out = t_mm(mixed[...], low[...]).astype(BF)
    for p in range(3):
        qa, qb = placed(index, 2 * p, 768), placed(index, 2 * p + 1, 384)
        o = placed(index, 6 + p, 384)
        top, rest = laid_out(d_qkv[:, 384 * p : 384 * p + 384], qa, qb, 256)
        moved = mm(o, d_out[:, 256 * p : 256 * p + 256])
        for at, value in ((0, top), (384, rest), (640, moved)):
            n = value.shape[1]
            keeps[p][:, at : at + n] = value[:256].astype(BF)
            sends[p][:, 896 + at : 896 + at + n] = value[256:].astype(BF)
    down_sum = jnp.sum(grad[...].astype(F32), 0, keepdims=True) * 0.5
    rows = [s[i : i + 1] for i in range(2) for s in (sum0, sum1, sum2, sum3)]
    rows = jnp.concatenate(rows + [down_sum, jnp.zeros((7, 768), F32)], 0).astype(BF)
    zero = jnp.zeros((16, 768), BF)
    first = jnp.concatenate([rows] + [zero] * 7, 0)
    second = jnp.concatenate([zero, rows] + [zero] * 6, 0)
    value = mm_t(qa, first) + mm_t(qb, second[:, 384:]) + up_rows[...]
    keeps[2][:, 896:1024] = value[:256].astype(BF)
    sends[2][:, 1792:1920] = value[256:].astype(BF)


def self_grads(normed, d_joined, mixed, low, sums, grad, up_rows, index, early):
    return staged(
        "self_grads",
        self_grads_kernel,
        (),
        (normed, d_joined, mixed, low, *sums, grad, up_rows, index, *early),
        (*[shape((256, n), BF) for n in (896, 896, 1024, 1792, 1792, 1920)],),
        3e9,
    )


def first_core(info, dims):
    return lax.broadcasted_iota(jnp.int32, dims, 0) * 0 + info[0] == 0


BLOCKS = ((0, 3, 384), (1, 2, 384), (2, 1, 384), (3, 1, 1536))


def halves_into(core, refs, target, sem):
    copies, here = [], 0
    for which, blocks, width in BLOCKS:
        for i in range(blocks):
            at = pl.multiple_of(2 * i * width + core * width, 128)
            copies.append(
                pltpu.make_async_copy(
                    refs[which].at[:, pl.ds(at, width)], target.at[:, pl.ds(here, width)],
                    sem.at[len(copies)],
                )
            )
            here += width
    return copies


def vector_rows(gain, bias, down_bias):
    total = jnp.zeros((6, 128), F32)
    for at, ref in ((0, gain), (4, bias), (8, down_bias)):
        n = ref.shape[0]
        i = lax.broadcasted_iota(jnp.int32, (n, 128), 0) + at
        j = lax.broadcasted_iota(jnp.int32, (n, 128), 1)
        total = total + t_mm(ref[...], ((i == j) | (i + 16 == j)).astype(F32).astype(BF))
    return total


def pack_swap_kernel(info, qkv, kv, query, up, gain, bias, down_bias, send, half, sem):
    copies = halves_into(1 - info[0], (qkv, kv, query, up), half, sem)
    for c in copies:
        c.start()
    send[:, 3840:] = vector_rows(gain, bias, down_bias).astype(BF)
    for c in copies:
        c.wait()
    send[:, :3840] = half[...]


def pack_slots_kernel(
    info, qkv, kv, query, up, self_out, cross_out, down, got, gain, bias, down_bias, up_bias,
    slot, twelve, half, outs, slabs, theirs, sem, sems,
):
    copies = halves_into(info[0], (qkv, kv, query, up), half, sem)
    others = [
        pltpu.make_async_copy(self_out, outs.at[0], sems.at[0]),
        pltpu.make_async_copy(cross_out, outs.at[1], sems.at[1]),
        pltpu.make_async_copy(down, slabs, sems.at[2]),
    ]
    sent = pltpu.make_async_copy(got, theirs, sems.at[3])
    sent.start()
    for c in copies + others:
        c.start()
    first = first_core(info, (6, 128))
    mine = vector_rows(gain, bias, down_bias)
    sent.wait()
    other = theirs[:, 3840:].astype(F32)
    twelve[0:6, 4608:] = jnp.where(first, mine, other)
    twelve[6:12, 4608:] = jnp.where(first, other, mine)
    twelve[12:16, 4608:] = jnp.zeros((4, 128), F32)
    lane = lax.broadcasted_iota(jnp.int32, (8, 128), 1)
    row = lax.broadcasted_iota(jnp.int32, (8, 128), 0)
    vec = jnp.where(lane < 16, twelve[0:8, 4608:], 0.0)
    vec = vec + jnp.where((lane >= 16) & (lane < 32), twelve[8:16, 4608:], 0.0)
    i = lax.broadcasted_iota(jnp.int32, (24, 128), 0)
    j = lax.broadcasted_iota(jnp.int32, (24, 128), 1)
    units = mm(up_bias[...], (i + 64 == j).astype(F32).astype(BF))
    slot[:, 6912:7040] = (vec + jnp.where(row == 0, units, 0.0)).astype(BF)
    for c in copies:
        c.wait()
    first = first_core(info, (6, 3840))
    mine = half[...].astype(F32)
    other = theirs[:, :3840].astype(F32)
    twelve[0:6, :3840] = jnp.where(first, mine, other)
    twelve[6:12, :3840] = jnp.where(first, other, mine)
    for c in others:
        c.wait()
    twelve[0:6, 3840:4608] = outs[0].astype(F32)
    twelve[6:12, 3840:4608] = outs[1].astype(F32)
    slot[:, :4608] = twelve[0:8, :4608].astype(BF)
    twelve[0:4, :2304] = twelve[8:12, :2304]
    twelve[4:8, :2304] = twelve[8:12, 2304:4608]
    slot[:, 4608:6912] = twelve[0:8, :2304].astype(BF)
    wide = slabs[...].astype(F32)
    for k in range(3):
        at = 7040 + 768 * k
        slot[:, at : at + 768] = wide[8 * k : 8 * k + 8].astype(BF)


def packed(name, kernel, info, far, near, out, scratch):
    return pl.pallas_call(
        kernel,
        out_shape=out,
        in_specs=[SMEM] + [HBM] * len(far) + [VMEM] * len(near),
        out_specs=VMEM,
        scratch_shapes=scratch,
        compiler_params=params(60),
        cost_estimate=cost(1e6, 1e6),
        name=name,
    )(info, *far, *near)


def pack_swap(info, weights, vectors):
    return packed(
        "pack_swap",
        pack_swap_kernel,
        info,
        weights,
        vectors,
        shape((6, 3968), BF),
        [pltpu.VMEM((6, 3840), BF), pltpu.SemaphoreType.DMA((7,))],
    )


def pack_slots(info, weights, vectors, got, self_out, cross_out, down, up_bias):
    return packed(
        "pack_slots",
        pack_slots_kernel,
        info,
        (*weights, self_out, cross_out, down, got),
        (*vectors, up_bias),
        shape((8, 9344), BF),
        [
            pltpu.VMEM((16, 4736), F32),
            pltpu.VMEM((6, 3840), BF),
            pltpu.VMEM((2, 6, 768), BF),
            pltpu.VMEM((24, 768), BF),
            pltpu.VMEM((6, 3968), BF),
            pltpu.SemaphoreType.DMA((7,)),
            pltpu.SemaphoreType.DMA((4,)),
        ],
    )


BASE = (2304, 2304, 0)
TWELVES = [(p, 0, 768, 384) for p in range(2)] + [
    (p, BASE[p] + at, 384, 256) for at in (0, 896) for p in range(3)
]


def finish_send_kernel(info, *refs):
    k_ac, k_b, g_ac, g_b, s0, s1, s2, send, own, twelve = refs
    sums, n = (s0, s1, s2), s0.shape[1]
    s0[...] = k_ac[:, :n].astype(F32) + g_ac[:, :n].astype(F32)
    s2[...] = k_ac[:, n:].astype(F32) + g_ac[:, n:].astype(F32)
    s1[...] = k_b[...].astype(F32) + g_b[...].astype(F32)
    here = 0
    for p, at, n, width in TWELVES:
        ref = sums[p]
        twelve[0:8, here : here + n] = ref[:, at : at + n]
        twelve[8:12, here : here + width] = ref[0:4, at + n : at + n + width]
        twelve[8:12, here + width : here + n] = ref[4:8, at + n : at + n + n - width]
        here += n
    vec = s2[:, 1792:]
    twelve[0:8, 3840:] = vec
    twelve[8:12, 3840:] = pltpu.roll(vec, 112, 1)[0:4]
    first = first_core(info, (6, 3968))
    send[...] = jnp.where(first, twelve[6:12], twelve[0:6])
    own[...] = jnp.where(first, twelve[0:6], twelve[6:12])


def finish_kernel(
    info, s0, s1, s2, own, got, qkv, out_self, query, kv, out_cross, up, down, gain, bias, down_bias
):
    sums = (s0, s1, s2)
    first = first_core(info, (6, 3840))
    low = jnp.where(first, own[:, :3840], got[:, :3840])
    high = jnp.where(first, got[:, :3840], own[:, :3840])
    for ref, begin, blocks, width in (
        (up, 0, 1, 1536), (kv, 1536, 2, 384), (query, 2304, 1, 384), (qkv, 2688, 3, 384),
    ):
        for i in range(blocks):
            at = begin + i * width
            ref[:, 2 * i * width : (2 * i + 1) * width] = low[:, at : at + width]
            ref[:, (2 * i + 1) * width : (2 * i + 2) * width] = high[:, at : at + width]
    for p in range(3):
        lanes = slice(256 * p, 256 * p + 256)
        out_cross[:, lanes] = sums[p][0:6, BASE[p] + 640 : BASE[p] + 896]
        out_self[:, lanes] = sums[p][0:6, BASE[p] + 1536 : BASE[p] + 1792]
    for p in range(2):
        for k in range(3):
            at = 1152 + 384 * k
            down[8 * k : 8 * k + 8, 384 * p : 384 * p + 384] = sums[p][:, at : at + 384]
    total = jnp.concatenate([own[:, 3840:] + got[:, 3840:], jnp.zeros((122, 128), F32)], 0)
    across = jnp.transpose(total)
    gain[...] = across[0:4, 0:6]
    bias[...] = across[4:8, 0:6]
    down_bias[...] = across[8:9, 0:6]


def finish_send(info, keeps, gots, widths):
    return staged(
        "finish_send",
        finish_send_kernel,
        (info,),
        (*keeps, *gots),
        [shape((8, n), F32) for n in widths] + [shape((6, 3968), F32)] * 2,
        1e6,
        [pltpu.VMEM((16, 3968), F32)],
        mib=8,
    )


def finish(info, sums, own, got):
    return staged(
        "finish",
        finish_kernel,
        (info,),
        (*sums, own, got),
        [
            shape(dims, F32)
            for dims in (
                (6, 2304), (6, 768), (6, 768), (6, 1536), (6, 768), (6, 3072), (24, 768), (4, 6), (4, 6),
                (1, 6),
            )
        ],
        1e6,
        mib=8,
    )


def text_finish_kernel(vec, text, stream, mine, got, out_mine, out_got, grad, out):
    xhat, inv = normalize(text[...].astype(F32))
    grad[...] = stream[...] + norm_back(mine[...] + got[...], vec[0:1], xhat, inv)
    out[...] = out_mine[...] + out_got[...]


def text_finish(vec, text, stream, mine, got, out_mine, out_got):
    return staged(
        "text_finish",
        text_finish_kernel,
        (),
        (vec, text, stream, mine, got, out_mine, out_got),
        [shape((128, 768), F32)] * 2,
        1e6,
        mib=8,
    )


def image_finish_kernel(pick, v0, v1, v2, v3, out):
    values = [v[...].astype(F32) for v in (v0, v1, v2, v3)]
    for image in range(4):
        total = values[3]
        for turn in range(3):
            total = jnp.where(pick[turn] == image, values[turn], total)
        out[:, image, :] = total


def image_finish(pick, values):
    out = staged(
        "image_finish",
        image_finish_kernel,
        (pick,),
        values,
        [shape((188, 4, 768), F32)],
        1e6,
    )[0]
    return jnp.transpose(out, (1, 0, 2))


def combine_kernel(plan, *refs):
    at = 0
    ins = []
    for keeps, gots in plan:
        ins.append((refs[at : at + len(keeps)], refs[at + len(keeps) : at + len(keeps) + len(gots)]))
        at += len(keeps) + len(gots)
    outs = refs[at:]
    for p, (keeps, gots) in enumerate(ins):
        here = 0
        edges = []
        for ref in keeps:
            edges.append((here, here + ref.shape[1], ref))
            here += ref.shape[1]
        here = 0
        for ref in gots:
            for low, high, keep in edges:
                a, b = max(low, here), min(high, here + ref.shape[1])
                if a >= b:
                    continue
                total = keep[:, a - low : b - low].astype(F32) + ref[:, a - here : b - here].astype(F32)
                half = total.shape[0] // 2
                outs[2 * p][:, a:b] = total[:half].astype(BF)
                outs[2 * p + 1][:, a:b] = total[half:].astype(BF)
            here += ref.shape[1]


def combine(parts):
    plan, args, outs = [], [], []
    for keeps, gots in parts:
        plan.append(([k.shape[1] for k in keeps], [g.shape[1] for g in gots]))
        args += [*keeps, *gots]
        rows, width = keeps[0].shape[0], sum(k.shape[1] for k in keeps)
        outs += [shape((rows // 2, width), BF)] * 2
    got = staged(
        "combine", lambda *refs: combine_kernel(plan, *refs), (), args, outs, 1e6
    )
    return [(got[2 * p], got[2 * p + 1]) for p in range(len(parts))]


def regroup_kernel(k_a, g_a, k_bc, g_bc, keep_ac, send_ac, keep_b, send_b):
    first = k_a[...].astype(F32) + g_a[...].astype(F32)
    second = k_bc[...].astype(F32) + g_bc[...].astype(F32)
    n, m, half = k_a.shape[1], keep_b.shape[1], k_a.shape[0] // 2
    for rows, ac, b in ((slice(0, half), keep_ac, keep_b), (slice(half, 2 * half), send_ac, send_b)):
        ac[:, :n] = first[rows].astype(BF)
        ac[:, n:] = second[rows, m:].astype(BF)
        b[...] = second[rows, :m].astype(BF)


def regroup(k_a, g_a, k_bc, g_bc, m):
    half, n = k_a.shape[0] // 2, k_a.shape[1]
    widths = (n + k_bc.shape[1] - m, n + k_bc.shape[1] - m, m, m)
    got = staged(
        "regroup",
        regroup_kernel,
        (),
        (k_a, g_a, k_bc, g_bc),
        [shape((half, w), BF) for w in widths],
        1e6,
    )
    return [(got[0], got[1]), (got[2], got[3])]


def send_step(step, values, parts=(0, 1, 2)):
    v0, v1 = ((1, 3), (3, 1))[step % 2]
    return [
        lax.ppermute(v, BOTH, xor_pairs(ORDERS[p][step // 2], v0, v1)) for v, p in zip(values, parts)
    ]


def after(value, *others):
    return lax.optimization_barrier((value, *others))[0]


def image_moves(images, way):
    once = [(core + i, core + (i + 16 * way) % 64) for core in (0, 64) for i in range(64)]
    first, second, third = images
    return [
        lax.ppermute(first, BOTH, once),
        move_on(second),
        lax.ppermute(third, BOTH, [(j, i) for i, j in once]),
    ]


def move_on(image):
    route = [(i, (i + 16) % 64) for i in range(64)]
    return lax.ppermute(image, BOTH, route + [(64 + j, 64 + i) for i, j in route])


def on_device(
    text_input,
    image_tokens,
    output_grad,
    segment_starts,
    caption_image,
    image_counts,
    norm_gain,
    norm_bias,
    self_qkv,
    self_out,
    cross_q,
    cross_kv,
    cross_out,
    up_weight,
    up_bias,
    down_weight,
    down_bias,
):
    core = lax.axis_index("seq")
    chip = lax.axis_index("batch")
    first = core == 0

    def ordered(own, other, axis):
        return jnp.where(
            first, jnp.concatenate([own, other], axis), jnp.concatenate([other, own], axis)
        )

    place = jnp.stack([core, chip]).astype(jnp.int32)
    weights = (self_qkv, cross_kv, cross_q, up_weight)
    vectors = (norm_gain, norm_bias, down_bias[None])
    got = swap(pack_swap(place, weights, vectors))
    slot = pack_slots(
        place, weights, vectors, got, self_out, cross_out, down_weight, up_bias[None]
    )
    gathered = lax.all_gather(slot, "batch", axis=0, tiled=True)

    late_text, late_grad = after(text_input, slot), after(output_grad, slot)
    text = ordered(late_text, swap(late_text), 1).reshape(256, 768)
    grad = ordered(late_grad, swap(late_grad), 1).reshape(256, 768)

    group_images = after(caption_image, slot).reshape(64, 8)
    my_captions = lax.dynamic_index_in_dim(group_images, chip, 0, keepdims=False)
    limits = jnp.take(image_counts, my_captions).reshape(4, 2)
    limits = jnp.where(first, jnp.concatenate([limits[:, 0], limits[:, 1]]), jnp.concatenate([limits[:, 1], limits[:, 0]]))
    turns = jnp.arange(4)
    targets = (chip - turns * 16) % 64
    wanted = group_images[targets, 2 * turns + core]
    local_pick = wanted - (core * 64 + chip) * 4
    outgoing = image_pick(after(local_pick, slot), image_tokens)
    received = [outgoing[0], *image_moves(outgoing[1:], -1)]
    received[2] = move_on(received[2])
    own_images = image_stack(received)
    other_images = swap(own_images)
    info = jnp.concatenate(
        [core[None], segment_starts.reshape(8), limits, jnp.zeros((15,), jnp.int32)]
    ).astype(jnp.int32)

    column_index = indices(after(place, slot))

    gathered, info, grad, text, column_index, own_images, other_images = lax.optimization_barrier(
        (gathered, info, grad, text, column_index, own_images, other_images)
    )
    w_qkv, w_kv, w_query, w_up, w_self, w_cross, w_down, vec, b_up = unpack(gathered)
    part, joined, mixed_self, normed_one = self_forward(info, vec, w_qkv, w_self, text)
    got = swap(part)
    kv, image_normed = image_forward(vec, w_kv, own_images, other_images)
    after_self, normed_two, q_cross, mixed_cross, part = cross_forward(
        info, vec, text, part, got, kv, w_query, w_cross
    )
    after_cross, normed_three, active, hidden_low, text_mine, text_other, part, sum3 = feed(
        info, vec, b_up, after_self, part, swap(part), w_up, w_down, grad
    )
    text_got = swap(text_other)
    got = swap(part)

    grads = feed_grads(normed_three, active, hidden_low, grad, column_index)
    keep_one, up_rows = grads[0:2], grads[4]
    got_one = send_step(0, grads[2:4], (0, 1))
    stream_two, cross_low, dq, dkv, part, sum1 = cross_backward(
        info, vec, after(grad, keep_one[0]), part, got, after_cross, w_cross, q_cross, kv, w_query, after_self
    )
    got = swap(part)
    image_send = image_part(dkv, w_kv)[0]
    *rows_back, sum2 = image_backward(vec, dkv, w_kv, swap(image_send), own_images)
    returned = [rows_back[0], *image_moves(rows_back[1:], 1)]
    k_keep, v_keep, k_send, v_send = image_grads(
        image_normed, after(dkv, sum2), mixed_cross, cross_low, column_index
    )
    q_keep, q_send = query_grads(
        normed_two, after(dq, k_keep, got), mixed_cross, cross_low, column_index
    )
    returned[2] = move_on(after(returned[2], q_keep))
    keep_two, early = [k_keep, v_keep, q_keep], [k_send, v_send, q_send]
    stream_one, self_low, d_joined, one_mine, one_other, sum0 = self_backward(
        info, vec, after(stream_two, q_keep), part, got, after_self, w_self, joined,
        w_qkv, text,
    )
    self_low, *late = lax.optimization_barrier((self_low, *returned[1:], *got_one))
    returned, got_one = returned[:1] + late[:3], late[3:]
    grads = self_grads(
        normed_one, d_joined, mixed_self, self_low, (sum0, sum1, sum2, sum3), grad, up_rows,
        column_index, early,
    )
    keep_three = grads[0:3]
    got_two = send_step(0, grads[3:6])
    one_got = swap(one_other)
    image_grad = image_finish(after(local_pick, grads[3]), returned)
    text_grad, text_output = text_finish(
        after(vec, grads[3]), text_input.reshape(128, 768), stream_one, one_mine, one_got, text_mine,
        text_got,
    )
    got_two, image_grad, text_grad = lax.optimization_barrier((got_two, image_grad, text_grad))
    pairs = []
    for p in range(3):
        keeps, gots = [keep_two[p], keep_three[p]], [got_two[p]]
        if p < 2:
            keeps, gots = [keep_one[p], *keeps], [got_one[p], *gots]
        pairs += combine([(keeps, gots)])
    a_got, b_got, c_got = send_step(1, [v for _, v in pairs])
    saved = pairs
    pairs = combine([([pairs[0][0]], [a_got])])
    pairs += combine([([saved[1][0], saved[2][0]], [b_got, c_got])])
    for step in (2, 3):
        got_step = send_step(step, [v for _, v in pairs], (0, 1))
        if step == 2:
            pairs = combine([([k], [g]) for (k, _), g in zip(pairs, got_step)])
    pairs = regroup(*[v for (k, _), g in zip(pairs, got_step) for v in (k, g)], saved[1][0].shape[1])
    got_step = send_step(4, [v for _, v in pairs], (0, 1))
    pairs = combine([([k], [g]) for (k, _), g in zip(pairs, got_step)])
    got_step = send_step(5, [v for _, v in pairs], (0, 1))
    *sums, send, own = finish_send(
        place, [k for k, _ in pairs], got_step, [k.shape[1] for k, _ in saved]
    )

    text_grad, text_output = text_grad.reshape(2, 64, 768), text_output.reshape(2, 64, 768)

    (
        qkv_grad, self_grad, query_grad, kv_grad, cross_grad, up_grad, down_grad, gain_grad, bias_grad,
        down_bias_grad,
    ) = finish(place, sums, own, swap(send))
    up_bias_grad = sums[2][0, 1856:1880]
    return (
        text_output,
        text_grad,
        image_grad,
        gain_grad,
        bias_grad,
        qkv_grad,
        self_grad,
        query_grad,
        kv_grad,
        cross_grad,
        up_grad,
        up_bias_grad,
        down_grad,
        down_bias_grad[0],
    )


def solution(mesh):
    rows = P("batch", "seq", None)
    shard = P(BOTH, None)
    wide = P(None, BOTH)
    return jax.shard_map(
        on_device,
        mesh=mesh,
        in_specs=(
            rows, P(BOTH, None, None), rows, P("batch", None), P(), P(), wide, wide,
            shard, shard, shard, shard, shard, shard, P(BOTH), shard, P(BOTH),
        ),
        out_specs=(
            rows, rows, P(BOTH, None, None), wide, wide,
            shard, shard, shard, shard, shard, shard, P(BOTH), shard, P(BOTH),
        ),
        check_vma=False,
    )
```
